32 devices in a mesh: blk: 4 (over x, core), site: 8 (over z, y).
Axes of the slice: x: 2, y: 2, z: 4, core: 2. Of those that a mesh axis runs over, the one named last changes fastest.
Arguments:
- modes: bfloat16 [2, 1, 256, 12, 1024], P(None, None, 'blk', None, 'site'), may hold values from -0.75 to 0.75
- momenta: int32 [4, 3], replicated, may hold values from -2 to 2
Outputs:
- meson_field: float32 [128, 256, 256], P('site', 'blk')
The draws below stay inside these ranges and needn't reach their ends.
All inputs are finite; a program needn't handle non-finite values.
Results may differ from the reference program's by a relative error of at most 0.0027.
Values may be sent and summed in bfloat16 or wider, within the bound.
No kernel may reach another device: no remote copies, remote signals or barrier semaphores. Data moves between devices by JAX's collectives and lax.ppermute only.
A program may use at most 128 MiB of HBM per device.

```python
import math
import jax
import jax.numpy as jnp
from jax import lax

NM = 256
LEXT = 48
NP = 4
NT = 1
SITES = 1024
BLOCKS = 4
BLOCK = 64


def with_ends(drawn, stream_key, smallest, largest):
    place = [jax.random.randint(jax.random.fold_in(stream_key, axis), (), 0, length) for axis, length in enumerate(drawn.shape)]
    longest = drawn.shape.index(max(drawn.shape))
    beside = place[:longest] + [(place[longest] + 1) % drawn.shape[longest]] + place[longest + 1:]
    return drawn.at[tuple(place)].set(smallest).at[tuple(beside)].set(largest)


def steps_of(key, shape, shards, low, largest):
    gain, own = 1.0, jax.random.fold_in(key, 6)
    for dim, shards_of in shards:
        draws = jnp.exp(jax.random.uniform(jax.random.fold_in(own, dim), (shards_of,), jnp.float32, low / len(shards), largest / len(shards)))
        gain = gain * jnp.repeat(draws, shape[dim] // shards_of).reshape([-1 if axis == dim else 1 for axis in range(len(shape))])
    return gain


def noise(key, shape, spread, bound, pieces=(), held_as=jnp.bfloat16):
    gain = steps_of(key, shape, pieces, -0.22, 0.18) if pieces else 1.0
    values = jax.random.normal(key, shape, jnp.float32) * spread * gain
    return jnp.minimum(jnp.maximum(values, -bound), bound).astype(held_as)


def setup_inputs(seed: int = 0) -> dict:
    seeds = jax.random.split(jax.random.key(seed), 3)
    return {
        "modes": noise(seeds[0], (2, NT, NM, 12, SITES), ((3 * SITES) ** -0.25), 0.75, ((2, 4), (4, 8))),
        "momenta": with_ends(jax.random.randint(seeds[1], (NP, 3), -2, 3), jax.random.fold_in(seeds[1], 1), -2, 2).astype(jnp.int32),
    }


TWO_PI = 2.0 * math.pi


def phase_table(momenta, first_site, site_count, extent):
    flat = first_site + jnp.arange(site_count, dtype=jnp.int32)
    coords = jnp.stack([flat % extent, (flat // extent) % extent, flat // (extent * extent)], 0)
    turns = jnp.mod(jnp.sum(momenta[:, :, None] * coords[None, :, :], axis=1), extent)
    angle = turns.astype(jnp.float32) * (TWO_PI / extent)
    return jnp.stack([jnp.cos(angle), jnp.sin(angle)], 1)


def reference(modes, momenta):
    half = BLOCKS // 2
    weights = phase_table(momenta, jnp.int32(0), SITES, LEXT)
    fields = modes.reshape(2, NT, NM, 4, 3, SITES)

    def one_pair(index):
        step = index // NP
        moment = index % NP
        field = lax.dynamic_index_in_dim(fields, step, 1, keepdims=False)
        weight = lax.dynamic_index_in_dim(weights, moment, 0, keepdims=False)
        phased = (field.astype(jnp.float32)[:, None] * weight[None, :, None, None, None, :]).astype(jnp.bfloat16)
        return jnp.einsum("awisxn,bjrxn->wabisjr", phased.astype(jnp.float32), field.astype(jnp.float32))

    products = lax.map(one_pair, jnp.arange(NT * NP, dtype=jnp.int32))
    real_part = products[:, :, 0, 0] + products[:, :, 1, 1]
    imag_part = products[:, :, 0, 1] - products[:, :, 1, 0]
    direct = jnp.stack([real_part[:, 0] + imag_part[:, 1], imag_part[:, 0] - real_part[:, 1]], 0)
    mirror = jnp.stack([real_part[:, 0] - imag_part[:, 1], -(imag_part[:, 0] + real_part[:, 1])], 0)
    direct = jnp.transpose(direct, (1, 3, 5, 0, 2, 4)).reshape(NT * NP * 32, NM, NM)
    mirror = jnp.transpose(mirror, (1, 5, 3, 0, 4, 2)).reshape(NT * NP * 32, NM, NM)
    owners = jnp.arange(NM) // BLOCK
    distance = jnp.mod(owners[:, None] - owners[None, :], BLOCKS)
    return jnp.where((distance <= half)[None], direct, mirror)
```

```python
import functools
import math

import jax
import jax.numpy as jnp
from jax import lax
from jax.experimental import pallas as pl
from jax.experimental.pallas import tpu as pltpu
from jax.sharding import Mesh, PartitionSpec as P

LEXT = 48

TWO_PI = 2.0 * math.pi


def phase_table(momenta, first_site, site_count, extent):
    flat = first_site + jnp.arange(site_count, dtype=jnp.int32)
    coords = jnp.stack([flat % extent, flat // extent % extent, flat // (extent * extent)], 0)
    turns = jnp.mod(jnp.sum(momenta[:, :, None] * coords[None, :, :], axis=1), extent)
    angle = turns.astype(jnp.float32) * (TWO_PI / extent)
    return jnp.stack([jnp.cos(angle), jnp.sin(angle)], 1)


def left_sides(left_ref, weights_ref):
    spins, depth = left_ref.shape[2], left_ref.shape[4]
    half = depth // 2
    cosine = jnp.tile(weights_ref[0, 0:1], (1, depth // weights_ref.shape[-1]))
    sine = jnp.tile(weights_ref[0, 1:2], (1, depth // weights_ref.shape[-1]))
    cosine_rows = [[], []]
    sine_rows = [[], []]
    for spin in range(spins):
        own = left_ref[0, 0, spin].astype(jnp.float32)
        by_cos = (own * cosine).astype(jnp.bfloat16)
        by_sin = (own * sine).astype(jnp.bfloat16)
        cosine_rows[0].append(by_cos)
        cosine_rows[1].append(jnp.concatenate([-by_cos[:, half:], by_cos[:, :half]], 1))
        sine_rows[0].append(jnp.concatenate([-by_sin[:, half:], by_sin[:, :half]], 1))
        sine_rows[1].append(-by_sin)
    return (
        jnp.concatenate(cosine_rows[0] + cosine_rows[1], 0),
        jnp.concatenate(sine_rows[0] + sine_rows[1], 0),
    )


def add_terms(place_ref, weights_ref, left_ref, right_ref, field_ref):
    @pl.when(pl.program_id(0) == 0)
    def _():
        field_ref[...] = jnp.zeros_like(field_ref)

    spins = left_ref.shape[2]
    groups, columns, per_block, depth = right_ref.shape[0], *right_ref.shape[2:]
    left_cos, left_sin = left_sides(left_ref, weights_ref)
    dims = (((1,), (1,)), ((), ()))
    for column in range(columns):
        right = right_ref[:, 0, column].reshape(groups * per_block, depth)
        term = lax.dot_general(
            left_cos, right, dims, preferred_element_type=jnp.float32
        ) + lax.dot_general(left_sin, right, dims, preferred_element_type=jnp.float32)
        for part in range(2):
            for spin in range(spins):
                start = (part * spins + spin) * per_block
                field_ref[(spin * columns + column) * 2 + part] += term[start : start + per_block]


def add_terms_and_place(
    place_ref, weights_ref, left_ref, right_ref, near_ref, field_ref, total_ref
):
    add_terms(place_ref, weights_ref, left_ref, right_ref, total_ref)

    @pl.when(pl.program_id(0) == pl.num_programs(0) - 1)
    def _():
        per_block = near_ref.shape[1]
        first = place_ref[3] == 0
        for row in range(near_ref.shape[0]):
            near, far = near_ref[row], total_ref[row]
            even, odd = jnp.where(first, near, far), jnp.where(first, far, near)
            pieces = []
            for start in range(0, near.shape[1], per_block):
                pieces += [even[:, start : start + per_block], odd[:, start : start + per_block]]
            field_ref[row] = jnp.concatenate(pieces, 1)


def shards(modes, momenta):
    groups = lax.axis_size("pair")
    sites = lax.axis_size("site")
    slots, steps, per_block, spin_colour, site_count = modes.shape
    nmom = momenta.shape[0]
    share = steps * nmom * 32 // sites
    columns = min(4, share // 2)
    spins = share // (2 * columns)
    owned = lax.axis_index("site") * (share // 2)
    place = jnp.stack(
        [
            lax.axis_index("pair"),
            owned // 4 % 4 // spins,
            owned % 4 // columns,
            lax.axis_index("core"),
        ]
    ).astype(jnp.int32)

    packed = jnp.transpose(modes.reshape(slots, per_block, 4, 3, site_count), (2, 1, 0, 3, 4))
    packed = packed.reshape(4, per_block, slots * 3 * site_count)
    depth = packed.shape[-1]
    near = lax.all_gather(packed, ("pair", "site"))
    near = near.reshape(groups, sites, 4, per_block, depth)
    far = lax.ppermute(near, "core", [(0, 1), (1, 0)])

    mine = lax.dynamic_slice_in_dim(momenta, owned // 16, 1, 0)
    weights = phase_table(mine, jnp.int32(0), sites * site_count, LEXT)[0]
    weights = jnp.transpose(weights.reshape(2, sites, site_count), (1, 0, 2))

    wide = groups * per_block
    in_specs = [
        pl.BlockSpec((1, 2, site_count), lambda m, place: (m, 0, 0)),
        pl.BlockSpec(
            (1, 1, spins, per_block, depth), lambda m, place: (place[0], m, place[1], 0, 0)
        ),
        pl.BlockSpec(
            (groups, 1, columns, per_block, depth), lambda m, place: (0, m, place[2], 0, 0)
        ),
    ]
    estimate = pl.CostEstimate(
        flops=4 * share * per_block * wide * depth * sites,
        bytes_accessed=wide * sites * 4 * depth * 2,
        transcendentals=0,
    )
    params = pltpu.CompilerParams(vmem_limit_bytes=56 * 1024 * 1024)
    half = pl.pallas_call(
        add_terms,
        grid_spec=pltpu.PrefetchScalarGridSpec(
            num_scalar_prefetch=1,
            grid=(sites,),
            in_specs=in_specs,
            out_specs=pl.BlockSpec((share, per_block, wide), lambda m, place: (0, 0, 0)),
        ),
        out_shape=jax.ShapeDtypeStruct((share, per_block, wide), jnp.float32),
        compiler_params=params,
        cost_estimate=estimate,
    )(place, weights, near, near)
    return pl.pallas_call(
        add_terms_and_place,
        grid_spec=pltpu.PrefetchScalarGridSpec(
            num_scalar_prefetch=1,
            grid=(sites,),
            in_specs=in_specs
            + [pl.BlockSpec((share, per_block, wide), lambda m, place: (0, 0, 0))],
            out_specs=pl.BlockSpec((share, per_block, 2 * wide), lambda m, place: (0, 0, 0)),
            scratch_shapes=[pltpu.VMEM((share, per_block, wide), jnp.float32)],
        ),
        out_shape=jax.ShapeDtypeStruct((share, per_block, 2 * wide), jnp.float32),
        compiler_params=params,
        cost_estimate=estimate,
    )(place, weights, near, far, half)


def solution(mesh):
    count = mesh.shape["blk"]
    split = Mesh(mesh.devices.reshape(count // 2, 2, -1), ("pair", "core", "site"))
    placed = (P(None, None, ("pair", "core"), None, "site"), P())
    return jax.shard_map(
        shards,
        mesh=split,
        in_specs=placed,
        out_specs=P("site", ("pair", "core"), None),
        check_vma=False,
    )
```

```python
import functools
import math

import jax
import jax.numpy as jnp
from jax import lax
from jax.experimental import pallas as pl
from jax.experimental.pallas import tpu as pltpu
from jax.sharding import Mesh, PartitionSpec as P

LEXT = 48

TWO_PI = 2.0 * math.pi


def phase_table(momenta, first_site, site_count, extent):
    flat = first_site + jnp.arange(site_count, dtype=jnp.int32)
    coords = jnp.stack([flat % extent, flat // extent % extent, flat // (extent * extent)], 0)
    turns = jnp.mod(jnp.sum(momenta[:, :, None] * coords[None, :, :], axis=1), extent)
    angle = turns.astype(jnp.float32) * (TWO_PI / extent)
    return jnp.stack([jnp.cos(angle), jnp.sin(angle)], 1)


def left_sides(left_ref, weights_ref):
    spins, depth = left_ref.shape[2], left_ref.shape[4]
    half = depth // 2
    cosine = jnp.tile(weights_ref[0, 0:1], (1, depth // weights_ref.shape[-1]))
    sine = jnp.tile(weights_ref[0, 1:2], (1, depth // weights_ref.shape[-1]))
    cosine_rows = [[], []]
    sine_rows = [[], []]
    for spin in range(spins):
        own = left_ref[0, 0, spin].astype(jnp.float32)
        by_cos = (own * cosine).astype(jnp.bfloat16)
        by_sin = (own * sine).astype(jnp.bfloat16)
        cosine_rows[0].append(by_cos)
        cosine_rows[1].append(jnp.concatenate([-by_cos[:, half:], by_cos[:, :half]], 1))
        sine_rows[0].append(jnp.concatenate([-by_sin[:, half:], by_sin[:, :half]], 1))
        sine_rows[1].append(-by_sin)
    return (
        jnp.concatenate(cosine_rows[0] + cosine_rows[1], 0),
        jnp.concatenate(sine_rows[0] + sine_rows[1], 0),
    )


def add_terms(weights_ref, left_ref, right_refs, total_refs, width):
    left_cos, left_sin = left_sides(left_ref, weights_ref)
    dims = (((1,), (1,)), ((), ()))
    for right_ref, total_ref in zip(right_refs, total_refs):
        groups, columns, per_block, depth = right_ref.shape[0], *right_ref.shape[2:]
        for chunk in range(columns // width):
            right = right_ref[:, 0, chunk * width : (chunk + 1) * width]
            right = right.reshape(groups * width * per_block, depth)
            term = lax.dot_general(left_cos, right, dims, preferred_element_type=jnp.float32)
            term += lax.dot_general(left_sin, right, dims, preferred_element_type=jnp.float32)
            total_ref[chunk] += term


def start_kernel(width, place_ref, weights_ref, left_ref, near_ref, far_ref, near_out, far_out):
    @pl.when(pl.program_id(0) == 0)
    def _():
        near_out[...] = jnp.zeros_like(near_out)
        far_out[...] = jnp.zeros_like(far_out)

    add_terms(weights_ref, left_ref, [near_ref, far_ref], [near_out, far_out], width)


def next_kernel(
    width, place_ref, weights_ref, left_ref, near_ref, far_ref, near_in, far_in, near_out, far_out
):
    @pl.when(pl.program_id(0) == 0)
    def _():
        near_out[...] = near_in[...]
        far_out[...] = far_in[...]

    add_terms(weights_ref, left_ref, [near_ref, far_ref], [near_out, far_out], width)


def near_kernel(width, place_ref, weights_ref, left_ref, near_ref, near_in, near_out):
    @pl.when(pl.program_id(0) == 0)
    def _():
        near_out[...] = near_in[...]

    add_terms(weights_ref, left_ref, [near_ref], [near_out], width)


def last_kernel(
    width, place_ref, weights_ref, left_ref, far_ref, near_in, far_in, field_ref, far_total
):
    @pl.when(pl.program_id(0) == 0)
    def _():
        far_total[...] = far_in[...]

    add_terms(weights_ref, left_ref, [far_ref], [far_total], width)

    @pl.when(pl.program_id(0) == pl.num_programs(0) - 1)
    def _():
        spins = left_ref.shape[2]
        groups, columns, per_block = far_ref.shape[0], far_ref.shape[2], far_ref.shape[3]
        first = place_ref[3] == 0
        for chunk in range(columns // width):
            near, far = near_in[chunk], far_total[chunk]
            even, odd = jnp.where(first, near, far), jnp.where(first, far, near)
            for part in range(2):
                for spin in range(spins):
                    top = (part * spins + spin) * per_block
                    rows = slice(top, top + per_block)
                    for inner in range(width):
                        pieces = []
                        for group in range(groups):
                            start = (group * width + inner) * per_block
                            across = slice(start, start + per_block)
                            pieces += [even[rows, across], odd[rows, across]]
                        row = (spin * columns + chunk * width + inner) * 2 + part
                        field_ref[row] = jnp.concatenate(pieces, 1)


def shards(modes, momenta):
    groups, deep, flat = (lax.axis_size(name) for name in ("pair", "deep", "flat"))
    sites = deep * flat
    slots, steps, per_block, spin_colour, site_count = modes.shape
    share = steps * momenta.shape[0] * 32 // sites
    columns = min(4, share // 2)
    spins = share // (2 * columns)
    width = max(1, min(columns, 256 // (groups * per_block)))
    level = lax.axis_index("deep")
    owned = (level * flat + lax.axis_index("flat")) * (share // 2)
    place = [
        lax.axis_index("pair"),
        owned // 4 % 4 // spins,
        owned % 4 // columns,
        lax.axis_index("core"),
    ]
    place = jnp.stack(place + [jnp.bitwise_xor(level, d) for d in range(deep)]).astype(jnp.int32)

    packed = jnp.transpose(modes.reshape(slots, per_block, 4, 3, site_count), (2, 1, 0, 3, 4))
    packed = packed.reshape(4, per_block, slots * 3 * site_count)
    depth = packed.shape[-1]
    pieces = [packed]
    for d in range(1, deep):
        pieces.append(lax.ppermute(packed, "deep", [(i, i ^ d) for i in range(deep)]))

    nears = [
        lax.all_gather(piece, ("pair", "flat")).reshape(groups, flat, 4, per_block, depth)
        for piece in pieces
    ]

    def both(near):
        return [near, lax.ppermute(near, "core", [(0, 1), (1, 0)])]

    mine = lax.dynamic_slice_in_dim(momenta, owned // 16, 1, 0)
    weights = phase_table(mine, jnp.int32(0), sites * site_count, LEXT)[0]
    weights = jnp.transpose(weights.reshape(2, sites, site_count), (1, 0, 2))

    tall, wide = 2 * spins * per_block, groups * width * per_block
    total_shape = (columns // width, tall, wide)
    field_shape = (share, per_block, 2 * groups * per_block)
    total_spec = pl.BlockSpec(total_shape, lambda m, place: (0, 0, 0))
    total = jax.ShapeDtypeStruct(total_shape, jnp.float32)

    def call(kernel, d, near, rights, totals, out_specs, out_shape, scratch=()):
        in_specs = [
            pl.BlockSpec((1, 2, site_count), lambda m, place: (place[4 + d] * flat + m, 0, 0)),
            pl.BlockSpec(
                (1, 1, spins, per_block, depth), lambda m, place: (place[0], m, place[1], 0, 0)
            ),
        ]
        right_spec = pl.BlockSpec(
            (groups, 1, columns, per_block, depth), lambda m, place: (0, m, place[2], 0, 0)
        )
        in_specs += [right_spec] * len(rights) + [total_spec] * len(totals)
        return pl.pallas_call(
            functools.partial(kernel, width),
            grid_spec=pltpu.PrefetchScalarGridSpec(
                num_scalar_prefetch=1,
                grid=(flat,),
                in_specs=in_specs,
                out_specs=out_specs,
                scratch_shapes=scratch,
            ),
            out_shape=out_shape,
            compiler_params=pltpu.CompilerParams(vmem_limit_bytes=48 * 1024 * 1024),
            cost_estimate=pl.CostEstimate(
                flops=4 * tall * groups * per_block * columns * depth * flat * len(rights),
                bytes_accessed=groups * flat * 4 * per_block * depth * 2 * len(rights),
                transcendentals=0,
            ),
        )(place, weights, near, *rights, *totals)

    totals = call(
        start_kernel, 0, nears[0], both(nears[0]), [], [total_spec] * 2, [total] * 2
    )
    for d in range(1, deep - 1):
        near, totals = lax.optimization_barrier((nears[d], totals))
        totals = call(next_kernel, d, near, both(near), totals, [total_spec] * 2, [total] * 2)
    near, totals = lax.optimization_barrier((nears[deep - 1], totals))
    near, far = both(near)
    near_total = call(near_kernel, deep - 1, near, [near], totals[:1], total_spec, total)
    return call(
        last_kernel,
        deep - 1,
        near,
        [far],
        [near_total, totals[1]],
        pl.BlockSpec(field_shape, lambda m, place: (0, 0, 0)),
        jax.ShapeDtypeStruct(field_shape, jnp.float32),
        [pltpu.VMEM(total_shape, jnp.float32)],
    )


def solution(mesh):
    count, sites = mesh.shape["blk"], mesh.shape["site"]
    flat = 2 ** (int(math.log2(sites)) // 2)
    split = Mesh(
        mesh.devices.reshape(count // 2, 2, sites // flat, flat), ("pair", "core", "deep", "flat")
    )
    placed = (P(None, None, ("pair", "core"), None, ("deep", "flat")), P())
    return jax.shard_map(
        shards,
        mesh=split,
        in_specs=placed,
        out_specs=P(("deep", "flat"), ("pair", "core"), None),
        check_vma=False,
    )
```

```python
import functools
import math

import jax
import jax.numpy as jnp
from jax import lax
from jax.experimental import pallas as pl
from jax.experimental.pallas import tpu as pltpu
from jax.sharding import Mesh, PartitionSpec as P

LEXT = 48

TWO_PI = 2.0 * math.pi

AXES = ("pair", "core", "deep", "flat")


def phase_table(momenta, first_site, site_count, extent):
    flat = first_site + jnp.arange(site_count, dtype=jnp.int32)
    coords = jnp.stack([flat % extent, flat // extent % extent, flat // (extent * extent)], 0)
    turns = jnp.mod(jnp.sum(momenta[:, :, None] * coords[None, :, :], axis=1), extent)
    angle = turns.astype(jnp.float32) * (TWO_PI / extent)
    return jnp.stack([jnp.cos(angle), jnp.sin(angle)], 1)


def left_sides(owns, weights):
    depth = owns[0].shape[1]
    half = depth // 2
    cosine = jnp.tile(weights[0:1], (1, depth // weights.shape[1]))
    sine = jnp.tile(weights[1:2], (1, depth // weights.shape[1]))
    cosine_rows = [[], []]
    sine_rows = [[], []]
    for own in owns:
        own = own.astype(jnp.float32)
        by_cos = (own * cosine).astype(jnp.bfloat16)
        by_sin = (own * sine).astype(jnp.bfloat16)
        cosine_rows[0].append(by_cos)
        cosine_rows[1].append(jnp.concatenate([-by_cos[:, half:], by_cos[:, :half]], 1))
        sine_rows[0].append(jnp.concatenate([-by_sin[:, half:], by_sin[:, :half]], 1))
        sine_rows[1].append(-by_sin)
    return (
        jnp.concatenate(cosine_rows[0] + cosine_rows[1], 0),
        jnp.concatenate(sine_rows[0] + sine_rows[1], 0),
    )


def product(left_cos, left_sin, right):
    dims = (((1,), (1,)), ((), ()))
    term = lax.dot_general(left_cos, right, dims, preferred_element_type=jnp.float32)
    return term + lax.dot_general(left_sin, right, dims, preferred_element_type=jnp.float32)


def add_shards(names, has_totals, last, place_ref, weights_ref, *refs):
    refs = list(refs)
    held = {name: refs.pop(0) for name in names}
    steps = sorted({name[2] for name in names})
    sources = {}
    for dz in steps:
        for kind in ("O", "A", "B"):
            key = ("near", kind, dz)
            sources[key] = held[key] if key in held else refs.pop(0)
    totals_in = refs.pop(0) if has_totals else None
    out_ref, left_ref = refs.pop(0), refs.pop(0)
    totals_ref = refs.pop(0) if last else out_ref
    pair, core, level, beside, first_s, flat = (place_ref[i] for i in range(6))
    spins, per_block = left_ref.shape[2] // (2 * out_ref.shape[1]), out_ref.shape[1]
    if not last:
        per_block = sources[("near", "O", steps[0])].shape[1]
        spins = left_ref.shape[2] // (2 * per_block)

    if has_totals:
        totals_ref[...] = totals_in[...]
    else:
        totals_ref[...] = jnp.zeros_like(totals_ref)

    for slot, dz in enumerate(steps):
        shard = jnp.bitwise_xor(level, dz) * flat
        here = [sources[("near", "O", dz)][first_s + s] for s in range(spins)]
        there = []
        for s in range(spins):
            by_a = sources[("near", "A", dz)][first_s + s]
            by_b = sources[("near", "B", dz)][first_s + s]
            there.append(jnp.where(core == 0, by_b, by_a))
        for dy, owns in enumerate((here, there)):
            weights = weights_ref[shard + jnp.bitwise_xor(beside, dy)]
            left_cos, left_sin = left_sides(owns, weights)
            left_ref[2 * slot + dy, 0] = left_cos
            left_ref[2 * slot + dy, 1] = left_sin

    for side, kind, dz in names:
        right_ref = held[(side, kind, dz)]
        right = right_ref[...].reshape(-1, right_ref.shape[2])
        turn = core if side == "near" else 1 - core
        dx, dy = {"O": (0, 0), "A": (1 - turn, turn), "B": (turn, 1 - turn), "AB": (1, 1)}[kind]
        slot = 2 * steps.index(dz) + dy
        totals_ref[0 if side == "near" else 1, dx] += product(
            left_ref[slot, 0], left_ref[slot, 1], right
        )

    if last:
        columns = totals_ref.shape[3] // per_block
        for part in range(2):
            for spin in range(spins):
                top = (part * spins + spin) * per_block
                for column in range(columns):
                    across = pl.ds(column * per_block, per_block)
                    pieces = [
                        totals_ref[
                            jnp.bitwise_xor(core, c),
                            jnp.bitwise_xor(pair, p),
                            pl.ds(top, per_block),
                            across,
                        ]
                        for p in range(2)
                        for c in range(2)
                    ]
                    row = (spin * columns + column) * 2 + part
                    out_ref[row] = jnp.concatenate(pieces, 1)


def swap_in_windows(packed, place, weights, share):
    shape = tuple(lax.axis_size(name) for name in AXES)
    columns, per_block, depth = packed.shape
    spins = share // (2 * columns)
    tall, wide = 2 * spins * per_block, columns * per_block
    strides = (shape[1] * shape[2] * shape[3], shape[2] * shape[3], shape[3], 1)

    def move(array, target):
        pairs = []
        for p in range(shape[0]):
            for c in range(shape[1]):
                for z in range(shape[2]):
                    for y in range(shape[3]):
                        ends = (p, c, z, y), target(p, c, z, y)
                        pairs.append(
                            tuple(sum(a * b for a, b in zip(end, strides)) for end in ends)
                        )
        return lax.ppermute(array, AXES, pairs)

    def hop_a(array):
        return move(array, lambda p, c, z, y: (p ^ 1, c, z, y) if c == 0 else (p, c, z, y ^ 1))

    def hop_b(array):
        return move(array, lambda p, c, z, y: (p, c, z, y ^ 1) if c == 0 else (p ^ 1, c, z, y))

    def hop_z(array, by):
        return move(array, lambda p, c, z, y: (p, c, z ^ by, y))

    def swap(array):
        return move(array, lambda p, c, z, y: (p, c ^ 1, z, y))

    got = {("near", "O", 0): packed}
    totals = None

    def add(names, totals, last=False):
        steps = sorted({name[2] for name in names})
        extra = [
            ("near", kind, dz)
            for dz in steps
            for kind in ("O", "A", "B")
            if ("near", kind, dz) not in names
        ]
        operands = [place, weights] + [got[name] for name in list(names) + extra]
        if totals is not None:
            operands.append(totals)
        total_shape = (2, 2, tall, wide)
        out = (share, per_block, 4 * per_block) if last else total_shape
        scratch = [pltpu.VMEM((2 * len(steps), 2, tall, depth), jnp.bfloat16)]
        if last:
            scratch.append(pltpu.VMEM(total_shape, jnp.float32))
        return pl.pallas_call(
            functools.partial(add_shards, tuple(names), totals is not None, last),
            in_specs=[pl.BlockSpec(memory_space=pltpu.SMEM)]
            + [pl.BlockSpec(memory_space=pltpu.VMEM)] * (len(operands) - 1),
            out_specs=pl.BlockSpec(memory_space=pltpu.VMEM),
            out_shape=jax.ShapeDtypeStruct(out, jnp.float32),
            scratch_shapes=scratch,
            compiler_params=pltpu.CompilerParams(vmem_limit_bytes=40 * 1024 * 1024),
            cost_estimate=pl.CostEstimate(
                flops=4 * tall * wide * depth * len(names),
                bytes_accessed=wide * depth * 2 * len(names) + 8 * 4 * tall * wide,
                transcendentals=0,
            ),
        )(*operands)

    def near(kind, dz):
        return got[("near", kind, dz)]

    windows = [
        (
            {
                ("near", "A", 0): lambda: hop_a(near("O", 0)),
                ("near", "B", 0): lambda: hop_b(near("O", 0)),
                ("near", "O", 1): lambda: hop_z(near("O", 0), 1),
            },
            [("O", 0)],
            [],
        ),
        (
            {
                ("near", "O", 2): lambda: hop_z(near("O", 0), 2),
                ("near", "AB", 0): lambda: hop_b(near("A", 0)),
                ("near", "A", 1): lambda: hop_a(near("O", 1)),
                ("near", "B", 1): lambda: hop_b(near("O", 1)),
            },
            [("A", 0), ("B", 0), ("O", 1)],
            [("near", "O", 0), ("near", "A", 0), ("near", "B", 0), ("far", "O", 0)],
        ),
        (
            {
                ("near", "A", 2): lambda: hop_a(near("O", 2)),
                ("near", "B", 2): lambda: hop_b(near("O", 2)),
                ("near", "O", 3): lambda: hop_z(near("O", 2), 1),
            },
            [("AB", 0), ("A", 1), ("B", 1), ("O", 2)],
            [("near", "AB", 0), ("near", "O", 1), ("near", "A", 1), ("near", "B", 1)]
            + [("far", "A", 0), ("far", "B", 0), ("far", "O", 1)],
        ),
        (
            {
                ("near", "AB", 2): lambda: hop_b(near("A", 2)),
                ("near", "A", 3): lambda: hop_a(near("O", 3)),
                ("near", "B", 3): lambda: hop_b(near("O", 3)),
                ("near", "AB", 1): lambda: hop_z(near("AB", 0), 1),
            },
            [("A", 2), ("B", 2), ("O", 3)],
            [("far", "AB", 0), ("far", "A", 1), ("far", "B", 1)]
            + [("near", "O", 2), ("near", "A", 2), ("near", "B", 2), ("far", "O", 2)],
        ),
        (
            {("near", "AB", 3): lambda: hop_b(near("A", 3))},
            [("AB", 1), ("AB", 2), ("A", 3), ("B", 3)],
            [("near", "O", 3), ("near", "A", 3), ("near", "B", 3), ("near", "AB", 1)]
            + [("near", "AB", 2), ("far", "A", 2), ("far", "B", 2), ("far", "O", 3)],
        ),
        (
            {},
            [("AB", 3)],
            [("near", "AB", 3), ("far", "AB", 1), ("far", "AB", 2), ("far", "A", 3)]
            + [("far", "B", 3)],
        ),
    ]
    for travels, swaps, names in windows:
        new = {name: start() for name, start in travels.items()}
        for kind, dz in swaps:
            new[("far", kind, dz)] = swap(near(kind, dz))
        if names:
            totals = add(names, totals)
        got.update(new)
        got, totals = lax.optimization_barrier((got, totals))
    return add([("far", "AB", 3)], totals, last=True)


def add_terms(place_ref, weights_ref, left_ref, right_ref, field_ref):
    @pl.when(pl.program_id(0) == 0)
    def _():
        field_ref[...] = jnp.zeros_like(field_ref)

    spins = left_ref.shape[2]
    groups, columns, per_block, depth = right_ref.shape[0], *right_ref.shape[2:]
    owns = [left_ref[0, 0, spin] for spin in range(spins)]
    left_cos, left_sin = left_sides(owns, weights_ref[0])
    for column in range(columns):
        right = right_ref[:, 0, column].reshape(groups * per_block, depth)
        term = product(left_cos, left_sin, right)
        for part in range(2):
            for spin in range(spins):
                start = (part * spins + spin) * per_block
                field_ref[(spin * columns + column) * 2 + part] += term[start : start + per_block]


def gather_whole(packed, place, weights, share):
    groups, _, deep, flat = (lax.axis_size(name) for name in AXES)
    sites = deep * flat
    _, per_block, depth = packed.shape
    columns = min(4, share // 2)
    spins = share // (2 * columns)
    near = lax.all_gather(packed, ("pair", "deep", "flat"))
    near = near.reshape(groups, sites, 4, per_block, depth)
    far = lax.ppermute(near, "core", [(0, 1), (1, 0)])
    wide = groups * per_block

    def half(right):
        return pl.pallas_call(
            add_terms,
            grid_spec=pltpu.PrefetchScalarGridSpec(
                num_scalar_prefetch=1,
                grid=(sites,),
                in_specs=[
                    pl.BlockSpec((1, 2, weights.shape[2]), lambda m, place: (m, 0, 0)),
                    pl.BlockSpec(
                        (1, 1, spins, per_block, depth),
                        lambda m, place: (place[0], m, place[4] // spins, 0, 0),
                    ),
                    pl.BlockSpec(
                        (groups, 1, columns, per_block, depth),
                        lambda m, place: (0, m, place[6] // columns, 0, 0),
                    ),
                ],
                out_specs=pl.BlockSpec((share, per_block, wide), lambda m, place: (0, 0, 0)),
            ),
            out_shape=jax.ShapeDtypeStruct((share, per_block, wide), jnp.float32),
            compiler_params=pltpu.CompilerParams(vmem_limit_bytes=40 * 1024 * 1024),
        )(place, weights, near, right)

    sides = [half(right).reshape(share, per_block, groups, per_block) for right in (near, far)]
    first = lax.axis_index("core") == 0
    even, odd = (jnp.where(first, a, b) for a, b in (sides, sides[::-1]))
    return jnp.stack([even, odd], 3).reshape(share, per_block, 2 * wide)


def shards(modes, momenta):
    groups, _, deep, flat = (lax.axis_size(name) for name in AXES)
    sites = deep * flat
    slots, steps, per_block, spin_colour, site_count = modes.shape
    share = steps * momenta.shape[0] * 32 // sites
    owned = (lax.axis_index("deep") * flat + lax.axis_index("flat")) * (share // 2)
    place = [lax.axis_index(name) for name in AXES]
    place = jnp.stack(place + [owned // 4 % 4, jnp.int32(flat), owned % 4]).astype(jnp.int32)

    packed = jnp.transpose(modes.reshape(slots, per_block, 4, 3, site_count), (2, 1, 0, 3, 4))
    packed = packed.reshape(4, per_block, slots * 3 * site_count)

    mine = lax.dynamic_slice_in_dim(momenta, owned // 16, 1, 0)
    weights = phase_table(mine, jnp.int32(0), sites * site_count, LEXT)[0]
    weights = jnp.transpose(weights.reshape(2, sites, site_count), (1, 0, 2))

    if (groups, deep, flat) == (2, 4, 2) and share in (8, 16, 32):
        return swap_in_windows(packed, place, weights, share)
    return gather_whole(packed, place, weights, share)


def solution(mesh):
    count, sites = mesh.shape["blk"], mesh.shape["site"]
    flat = 2 ** (int(math.log2(sites)) // 2)
    split = Mesh(mesh.devices.reshape(count // 2, 2, sites // flat, flat), AXES)
    placed = (P(None, None, ("pair", "core"), None, ("deep", "flat")), P())
    return jax.shard_map(
        shards,
        mesh=split,
        in_specs=placed,
        out_specs=P(("deep", "flat"), ("pair", "core"), None),
        check_vma=False,
    )
```

```python
import functools
import math

import jax
import jax.numpy as jnp
from jax import lax
from jax.experimental import pallas as pl
from jax.experimental.pallas import tpu as pltpu
from jax.sharding import Mesh, PartitionSpec as P

LEXT = 48

TWO_PI = 2.0 * math.pi

AXES = ("pair", "core", "deep", "flat")


def phase_table(momenta, first_site, site_count, extent):
    flat = first_site + jnp.arange(site_count, dtype=jnp.int32)
    coords = jnp.stack([flat % extent, flat // extent % extent, flat // (extent * extent)], 0)
    turns = jnp.mod(jnp.sum(momenta[:, :, None] * coords[None, :, :], axis=1), extent)
    angle = turns.astype(jnp.float32) * (TWO_PI / extent)
    return jnp.stack([jnp.cos(angle), jnp.sin(angle)], 1)


def left_sides(owns, weights):
    depth = owns[0].shape[1]
    half = depth // 2
    cosine = jnp.tile(weights[0:1], (1, depth // weights.shape[1]))
    sine = jnp.tile(weights[1:2], (1, depth // weights.shape[1]))
    cosine_rows = [[], []]
    sine_rows = [[], []]
    for own in owns:
        own = own.astype(jnp.float32)
        by_cos = (own * cosine).astype(jnp.bfloat16)
        by_sin = (own * sine).astype(jnp.bfloat16)
        cosine_rows[0].append(by_cos)
        cosine_rows[1].append(jnp.concatenate([-by_cos[:, half:], by_cos[:, :half]], 1))
        sine_rows[0].append(jnp.concatenate([-by_sin[:, half:], by_sin[:, :half]], 1))
        sine_rows[1].append(-by_sin)
    return (
        jnp.concatenate(cosine_rows[0] + cosine_rows[1], 0),
        jnp.concatenate(sine_rows[0] + sine_rows[1], 0),
    )


def product(left_cos, left_sin, right):
    dims = (((1,), (1,)), ((), ()))
    term = lax.dot_general(left_cos, right, dims, preferred_element_type=jnp.float32)
    return term + lax.dot_general(left_sin, right, dims, preferred_element_type=jnp.float32)


def add_shards(names, where, has_totals, last, place_ref, weights_ref, *refs):
    refs = list(refs)
    scratch_ref = refs.pop() if last else None
    left_ref, out_ref = refs.pop(), refs.pop()
    totals_in = refs.pop() if has_totals else None
    totals_ref = scratch_ref if last else out_ref

    def shard(name):
        index, slot = where[name]
        return refs[index] if slot is None else refs[index].at[slot]

    pair, core, level, beside, first_s, flat = (place_ref[i] for i in range(6))
    columns, per_block, _ = shard(names[0]).shape
    spins = left_ref.shape[2] // (2 * per_block)

    if has_totals:
        totals_ref[...] = totals_in[...]
    else:
        totals_ref[...] = jnp.zeros_like(totals_ref)

    slots = left_slots(names)
    for slot, (dy, dz) in enumerate(slots):
        site = jnp.bitwise_xor(level, dz) * flat + jnp.bitwise_xor(beside, dy)
        if dy == 0:
            owns = [shard(("near", "O", dz))[first_s + s] for s in range(spins)]
        else:
            owns = [
                jnp.where(
                    core == 0,
                    shard(("near", "B", dz))[first_s + s],
                    shard(("near", "A", dz))[first_s + s],
                )
                for s in range(spins)
            ]
        left_ref[slot, 0], left_ref[slot, 1] = left_sides(owns, weights_ref[site])

    for side, kind, dz in names:
        right = shard((side, kind, dz))[...].reshape(columns * per_block, -1)
        turn = core if side == "near" else 1 - core
        dx, dy = {"O": (0, 0), "A": (1 - turn, turn), "B": (turn, 1 - turn), "AB": (1, 1)}[kind]
        if kind in ("O", "AB"):
            slot = slots.index((dy, dz))
        else:
            slot = slots.index((0, dz)) + dy
        totals_ref[0 if side == "near" else 1, dx] += product(
            left_ref[slot, 0], left_ref[slot, 1], right
        )

    if last:
        for part in range(2):
            for spin in range(spins):
                top = (part * spins + spin) * per_block
                for column in range(columns):
                    across = pl.ds(column * per_block, per_block)
                    pieces = [
                        totals_ref[
                            jnp.bitwise_xor(core, c),
                            jnp.bitwise_xor(pair, p),
                            pl.ds(top, per_block),
                            across,
                        ]
                        for p in range(2)
                        for c in range(2)
                    ]
                    row = (spin * columns + column) * 2 + part
                    out_ref[row] = jnp.concatenate(pieces, 1)


def route_second(place_ref, *refs):
    stack_ref, both_ref, relayed_ref, mixed_ref = refs[6:]
    ab0_ref, o1_ref, o2_ref = refs[3:6]
    for slot in range(6):
        stack_ref[slot] = refs[slot][...]
    both_ref[0] = o1_ref[...]
    both_ref[1] = o2_ref[...]
    relayed_ref[0] = ab0_ref[...]
    relayed_ref[1] = o2_ref[...]
    mixed_ref[...] = jnp.where(place_ref[1] == 0, o2_ref[...], ab0_ref[...])


def route_third(z1_ref, a12_ref, b12_ref, ab2_ref, stack_ref, o3_ref):
    for slot, ref in enumerate((z1_ref, a12_ref, b12_ref)):
        stack_ref[2 * slot] = ref[0]
        stack_ref[2 * slot + 1] = ref[1]
    stack_ref[6] = ab2_ref[...]
    o3_ref[...] = z1_ref[1]


def left_slots(names):
    needed = set()
    for _, kind, dz in names:
        needed |= {"O": {(0, dz)}, "AB": {(1, dz)}}.get(kind, {(0, dz), (1, dz)})
    return sorted(needed, key=lambda slot: (slot[1], slot[0]))


def swap_in_windows(packed, place, weights, share):
    shape = tuple(lax.axis_size(name) for name in AXES)
    columns, per_block, depth = packed.shape
    spins = share // (2 * columns)
    tall, wide = 2 * spins * per_block, columns * per_block
    strides = (shape[1] * shape[2] * shape[3], shape[2] * shape[3], shape[3], 1)

    def move(array, target):
        pairs = []
        for p in range(shape[0]):
            for c in range(shape[1]):
                for z in range(shape[2]):
                    for y in range(shape[3]):
                        ends = (p, c, z, y), target(p, c, z, y)
                        pairs.append(
                            tuple(sum(a * b for a, b in zip(end, strides)) for end in ends)
                        )
        return lax.ppermute(array, AXES, pairs)

    def hop_a(array):
        return move(array, lambda p, c, z, y: (p ^ 1, c, z, y) if c == 0 else (p, c, z, y ^ 1))

    def hop_b(array):
        return move(array, lambda p, c, z, y: (p, c, z, y ^ 1) if c == 0 else (p ^ 1, c, z, y))

    def hop_ab(array):
        return move(array, lambda p, c, z, y: (p ^ 1, c, z, y ^ 1))

    def hop_z(array, by):
        return move(array, lambda p, c, z, y: (p, c, z ^ by, y))

    def hop_mixed(array):
        return move(
            array, lambda p, c, z, y: (p ^ 1, c, z, y ^ 1) if c == 0 else (p, c, z ^ 2, y)
        )

    def swap(array):
        return move(array, lambda p, c, z, y: (p, c ^ 1, z, y))

    arrays = {}
    where = {}

    def put(key, array, side, kinds):
        arrays[key] = array
        for slot, (kind, dz) in enumerate(kinds):
            where[(side, kind, dz)] = (key, slot if len(kinds) > 1 else None)

    def near(kind, dz):
        key, slot = where[("near", kind, dz)]
        return arrays[key] if slot is None else arrays[key][slot]

    def add(names, totals, last=False):
        slots = left_slots(names)
        uses = list(names)
        for dy, dz in slots:
            uses += [("near", kind, dz) for kind in (("A", "B") if dy else ("O",))]
        keys = sorted({where[name][0] for name in uses})
        places = {name: (keys.index(where[name][0]), where[name][1]) for name in uses}
        operands = [place, weights] + [arrays[key] for key in keys]
        if totals is not None:
            operands.append(totals)
        total_shape = (2, 2, tall, wide)
        out = (share, per_block, 4 * per_block) if last else total_shape
        scratch = [pltpu.VMEM((len(slots), 2, tall, depth), jnp.bfloat16)]
        if last:
            scratch.append(pltpu.VMEM(total_shape, jnp.float32))
        return pl.pallas_call(
            functools.partial(add_shards, tuple(names), places, totals is not None, last),
            in_specs=[pl.BlockSpec(memory_space=pltpu.SMEM)]
            + [pl.BlockSpec(memory_space=pltpu.VMEM)] * (len(operands) - 1),
            out_specs=pl.BlockSpec(memory_space=pltpu.VMEM),
            out_shape=jax.ShapeDtypeStruct(out, jnp.float32),
            scratch_shapes=scratch,
            compiler_params=pltpu.CompilerParams(vmem_limit_bytes=40 * 1024 * 1024),
            cost_estimate=pl.CostEstimate(
                flops=4 * tall * wide * depth * len(names),
                bytes_accessed=wide * depth * 2 * len(names) + 8 * 4 * tall * wide,
                transcendentals=0,
            ),
        )(*operands)

    def fence(totals):
        nonlocal arrays
        arrays, totals = lax.optimization_barrier((arrays, totals))
        return totals

    put("o0", packed, "near", [("O", 0)])

    new = [hop_a(packed), hop_b(packed), hop_ab(packed), hop_z(packed, 1), hop_z(packed, 2)]
    for key, array, kind in zip(
        ("a0", "b0", "ab0", "o1", "o2"), new, (("A", 0), ("B", 0), ("AB", 0), ("O", 1), ("O", 2))
    ):
        put(key, array, "near", [kind])
    place, weights = fence((place, weights))

    def route(kernel, operands, counts):
        block = pl.BlockSpec(memory_space=pltpu.VMEM)
        first = pl.BlockSpec(memory_space=pltpu.SMEM) if operands[0] is place else block
        shapes = [(count,) * (count > 1) + packed.shape for count in counts]
        routed = pl.pallas_call(
            kernel,
            in_specs=[first] + [block] * (len(operands) - 1),
            out_specs=[block] * len(counts),
            out_shape=[jax.ShapeDtypeStruct(shape, packed.dtype) for shape in shapes],
            compiler_params=pltpu.CompilerParams(vmem_limit_bytes=24 * 1024 * 1024),
        )(*operands)
        return fence(routed)

    first = [("O", 0), ("A", 0), ("B", 0), ("AB", 0), ("O", 1), ("O", 2)]
    stack, both, relayed, mixed = route(
        route_second, [place] + [near(*kind) for kind in first], (6, 2, 2, 1)
    )
    new = [hop_z(relayed, 1), hop_a(both), hop_b(both), hop_mixed(mixed), swap(stack)]
    totals = add([("near", *kind) for kind in first], None)
    put("z1", new[0], "near", [("AB", 1), ("O", 3)])
    put("a12", new[1], "near", [("A", 1), ("A", 2)])
    put("b12", new[2], "near", [("B", 1), ("B", 2)])
    put("ab2", new[3], "near", [("AB", 2)])
    put("far1", new[4], "far", first)
    totals = fence(totals)

    second = [("AB", 1), ("O", 3), ("A", 1), ("A", 2), ("B", 1), ("B", 2), ("AB", 2)]
    arrived = [arrays[key] for key in ("z1", "a12", "b12", "ab2")]
    stack, start = route(route_third, arrived, (7, 1))
    new = [hop_z(near("AB", 2), 1), hop_a(start), hop_b(start), swap(stack)]
    totals = add([("near", *kind) for kind in second] + [("far", *kind) for kind in first], totals)
    put("ab3", new[0], "near", [("AB", 3)])
    put("a3", new[1], "near", [("A", 3)])
    put("b3", new[2], "near", [("B", 3)])
    put("far2", new[3], "far", second)
    totals = fence(totals)

    third = [("A", 3), ("B", 3), ("AB", 3)]
    new = [swap(near(*kind)) for kind in third]
    totals = add([("near", *kind) for kind in third] + [("far", *kind) for kind in second], totals)
    for kind, array in zip(third, new):
        put("far " + kind[0], array, "far", [kind])
    totals = fence(totals)
    return add([("far", *kind) for kind in third], totals, last=True)


def add_terms(place_ref, weights_ref, left_ref, right_ref, field_ref):
    @pl.when(pl.program_id(0) == 0)
    def _():
        field_ref[...] = jnp.zeros_like(field_ref)

    spins = left_ref.shape[2]
    groups, columns, per_block, depth = right_ref.shape[0], *right_ref.shape[2:]
    owns = [left_ref[0, 0, spin] for spin in range(spins)]
    left_cos, left_sin = left_sides(owns, weights_ref[0])
    for column in range(columns):
        right = right_ref[:, 0, column].reshape(groups * per_block, depth)
        term = product(left_cos, left_sin, right)
        for part in range(2):
            for spin in range(spins):
                start = (part * spins + spin) * per_block
                field_ref[(spin * columns + column) * 2 + part] += term[start : start + per_block]


def gather_whole(packed, place, weights, share):
    groups, _, deep, flat = (lax.axis_size(name) for name in AXES)
    sites = deep * flat
    _, per_block, depth = packed.shape
    columns = min(4, share // 2)
    spins = share // (2 * columns)
    near = lax.all_gather(packed, ("pair", "deep", "flat"))
    near = near.reshape(groups, sites, 4, per_block, depth)
    far = lax.ppermute(near, "core", [(0, 1), (1, 0)])
    wide = groups * per_block

    def half(right):
        return pl.pallas_call(
            add_terms,
            grid_spec=pltpu.PrefetchScalarGridSpec(
                num_scalar_prefetch=1,
                grid=(sites,),
                in_specs=[
                    pl.BlockSpec((1, 2, weights.shape[2]), lambda m, place: (m, 0, 0)),
                    pl.BlockSpec(
                        (1, 1, spins, per_block, depth),
                        lambda m, place: (place[0], m, place[4] // spins, 0, 0),
                    ),
                    pl.BlockSpec(
                        (groups, 1, columns, per_block, depth),
                        lambda m, place: (0, m, place[6] // columns, 0, 0),
                    ),
                ],
                out_specs=pl.BlockSpec((share, per_block, wide), lambda m, place: (0, 0, 0)),
            ),
            out_shape=jax.ShapeDtypeStruct((share, per_block, wide), jnp.float32),
            compiler_params=pltpu.CompilerParams(vmem_limit_bytes=40 * 1024 * 1024),
        )(place, weights, near, right)

    sides = [half(right).reshape(share, per_block, groups, per_block) for right in (near, far)]
    first = lax.axis_index("core") == 0
    even, odd = (jnp.where(first, a, b) for a, b in (sides, sides[::-1]))
    return jnp.stack([even, odd], 3).reshape(share, per_block, 2 * wide)


def shards(modes, momenta):
    groups, _, deep, flat = (lax.axis_size(name) for name in AXES)
    sites = deep * flat
    slots, steps, per_block, spin_colour, site_count = modes.shape
    share = steps * momenta.shape[0] * 32 // sites
    owned = (lax.axis_index("deep") * flat + lax.axis_index("flat")) * (share // 2)
    place = [lax.axis_index(name) for name in AXES]
    place = jnp.stack(place + [owned // 4 % 4, jnp.int32(flat), owned % 4]).astype(jnp.int32)

    packed = jnp.transpose(modes.reshape(slots, per_block, 4, 3, site_count), (2, 1, 0, 3, 4))
    packed = packed.reshape(4, per_block, slots * 3 * site_count)

    mine = lax.dynamic_slice_in_dim(momenta, owned // 16, 1, 0)
    weights = phase_table(mine, jnp.int32(0), sites * site_count, LEXT)[0]
    weights = jnp.transpose(weights.reshape(2, sites, site_count), (1, 0, 2))

    if (groups, deep, flat) == (2, 4, 2) and share in (8, 16, 32):
        return swap_in_windows(packed, place, weights, share)
    return gather_whole(packed, place, weights, share)


def solution(mesh):
    count, sites = mesh.shape["blk"], mesh.shape["site"]
    flat = 2 ** (int(math.log2(sites)) // 2)
    split = Mesh(mesh.devices.reshape(count // 2, 2, sites // flat, flat), AXES)
    placed = (P(None, None, ("pair", "core"), None, ("deep", "flat")), P())
    return jax.shard_map(
        shards,
        mesh=split,
        in_specs=placed,
        out_specs=P(("deep", "flat"), ("pair", "core"), None),
        check_vma=False,
    )
```

```python
import functools
import math

import jax
import jax.numpy as jnp
from jax import lax
from jax.experimental import pallas as pl
from jax.experimental.pallas import tpu as pltpu
from jax.sharding import Mesh, PartitionSpec as P

LEXT = 48

TWO_PI = 2.0 * math.pi

AXES = ("pair", "core", "deep", "flat")


def phase_table(momenta, first_site, site_count, extent):
    flat = first_site + jnp.arange(site_count, dtype=jnp.int32)
    coords = jnp.stack([flat % extent, flat // extent % extent, flat // (extent * extent)], 0)
    turns = jnp.mod(jnp.sum(momenta[:, :, None] * coords[None, :, :], axis=1), extent)
    angle = turns.astype(jnp.float32) * (TWO_PI / extent)
    return jnp.stack([jnp.cos(angle), jnp.sin(angle)], 1)


def left_sides(owns, weights):
    depth = owns[0].shape[1]
    half = depth // 2
    cosine = jnp.tile(weights[0:1], (1, depth // weights.shape[1]))
    sine = jnp.tile(weights[1:2], (1, depth // weights.shape[1]))
    cosine_rows = [[], []]
    sine_rows = [[], []]
    for own in owns:
        own = own.astype(jnp.float32)
        by_cos = (own * cosine).astype(jnp.bfloat16)
        by_sin = (own * sine).astype(jnp.bfloat16)
        cosine_rows[0].append(by_cos)
        cosine_rows[1].append(jnp.concatenate([-by_cos[:, half:], by_cos[:, :half]], 1))
        sine_rows[0].append(jnp.concatenate([-by_sin[:, half:], by_sin[:, :half]], 1))
        sine_rows[1].append(-by_sin)
    return (
        jnp.concatenate(cosine_rows[0] + cosine_rows[1], 0),
        jnp.concatenate(sine_rows[0] + sine_rows[1], 0),
    )


def product(left_cos, left_sin, right):
    dims = (((1,), (1,)), ((), ()))
    term = lax.dot_general(left_cos, right, dims, preferred_element_type=jnp.float32)
    return term + lax.dot_general(left_sin, right, dims, preferred_element_type=jnp.float32)


def add_shards(names, where, has_totals, last, place_ref, weights_ref, *refs):
    refs = list(refs)
    scratch_ref = refs.pop() if last else None
    left_ref, out_ref = refs.pop(), refs.pop()
    totals_in = refs.pop() if has_totals else None
    totals_ref = scratch_ref if last else out_ref

    def shard(name):
        index, slot = where[name]
        return refs[index] if slot is None else refs[index].at[slot]

    pair, core, level, beside, first_s, flat = (place_ref[i] for i in range(6))
    columns, per_block, _ = shard(names[0]).shape
    spins = left_ref.shape[2] // (2 * per_block)

    if has_totals:
        totals_ref[...] = totals_in[...]
    else:
        totals_ref[...] = jnp.zeros_like(totals_ref)

    slots = left_slots(names)
    for slot, (dy, dz) in enumerate(slots):
        site = jnp.bitwise_xor(level, dz) * flat + jnp.bitwise_xor(beside, dy)
        if dy == 0:
            owns = [shard(("near", "O", dz))[first_s + s] for s in range(spins)]
        else:
            owns = [
                jnp.where(
                    core == 0,
                    shard(("near", "B", dz))[first_s + s],
                    shard(("near", "A", dz))[first_s + s],
                )
                for s in range(spins)
            ]
        left_ref[slot, 0], left_ref[slot, 1] = left_sides(owns, weights_ref[site])

    for side, kind, dz in names:
        right = shard((side, kind, dz))[...].reshape(columns * per_block, -1)
        turn = core if side == "near" else 1 - core
        dx, dy = {"O": (0, 0), "A": (1 - turn, turn), "B": (turn, 1 - turn), "AB": (1, 1)}[kind]
        if kind in ("O", "AB"):
            slot = slots.index((dy, dz))
        else:
            slot = slots.index((0, dz)) + dy
        totals_ref[0 if side == "near" else 1, dx] += product(
            left_ref[slot, 0], left_ref[slot, 1], right
        )

    if last:
        for part in range(2):
            for spin in range(spins):
                top = (part * spins + spin) * per_block
                for column in range(columns):
                    across = pl.ds(column * per_block, per_block)
                    pieces = [
                        totals_ref[
                            jnp.bitwise_xor(core, c),
                            jnp.bitwise_xor(pair, p),
                            pl.ds(top, per_block),
                            across,
                        ]
                        for p in range(2)
                        for c in range(2)
                    ]
                    row = (spin * columns + column) * 2 + part
                    out_ref[row] = jnp.concatenate(pieces, 1)


def route_second(place_ref, *refs):
    stack_ref, both_ref, relayed_ref, mixed_ref = refs[6:]
    ab0_ref, o1_ref, o2_ref = refs[3:6]
    for slot in range(6):
        stack_ref[slot] = refs[slot][...]
    both_ref[0] = o1_ref[...]
    both_ref[1] = o2_ref[...]
    relayed_ref[0] = ab0_ref[...]
    relayed_ref[1] = o2_ref[...]
    mixed_ref[...] = jnp.where(place_ref[1] == 0, o2_ref[...], ab0_ref[...])


def route_third(z1_ref, a12_ref, b12_ref, ab2_ref, stack_ref, o3_ref):
    for slot, ref in enumerate((z1_ref, a12_ref, b12_ref)):
        stack_ref[2 * slot] = ref[0]
        stack_ref[2 * slot + 1] = ref[1]
    stack_ref[6] = ab2_ref[...]
    o3_ref[...] = z1_ref[1]


def left_slots(names):
    needed = set()
    for _, kind, dz in names:
        needed |= {"O": {(0, dz)}, "AB": {(1, dz)}}.get(kind, {(0, dz), (1, dz)})
    return sorted(needed, key=lambda slot: (slot[1], slot[0]))


def swap_in_windows(packed, place, weights, share):
    shape = tuple(lax.axis_size(name) for name in AXES)
    columns, per_block, depth = packed.shape
    spins = share // (2 * columns)
    tall, wide = 2 * spins * per_block, columns * per_block
    strides = (shape[1] * shape[2] * shape[3], shape[2] * shape[3], shape[3], 1)

    def move(array, target):
        pairs = []
        for p in range(shape[0]):
            for c in range(shape[1]):
                for z in range(shape[2]):
                    for y in range(shape[3]):
                        ends = (p, c, z, y), target(p, c, z, y)
                        pairs.append(
                            tuple(sum(a * b for a, b in zip(end, strides)) for end in ends)
                        )
        return lax.ppermute(array, AXES, pairs)

    def hop_a(array):
        return move(array, lambda p, c, z, y: (p ^ 1, c, z, y) if c == 0 else (p, c, z, y ^ 1))

    def hop_b(array):
        return move(array, lambda p, c, z, y: (p, c, z, y ^ 1) if c == 0 else (p ^ 1, c, z, y))

    def hop_ab(array):
        return move(array, lambda p, c, z, y: (p ^ 1, c, z, y ^ 1))

    def hop_z(array, by):
        return move(array, lambda p, c, z, y: (p, c, z ^ by, y))

    def hop_mixed(array):
        return move(
            array, lambda p, c, z, y: (p ^ 1, c, z, y ^ 1) if c == 0 else (p, c, z ^ 2, y)
        )

    def swap(array):
        return move(array, lambda p, c, z, y: (p, c ^ 1, z, y))

    arrays = {}
    where = {}

    def put(key, array, side, kinds):
        arrays[key] = array
        for slot, (kind, dz) in enumerate(kinds):
            where[(side, kind, dz)] = (key, slot if len(kinds) > 1 else None)

    def near(kind, dz):
        key, slot = where[("near", kind, dz)]
        return arrays[key] if slot is None else arrays[key][slot]

    def add(names, totals, last=False):
        slots = left_slots(names)
        uses = list(names)
        for dy, dz in slots:
            uses += [("near", kind, dz) for kind in (("A", "B") if dy else ("O",))]
        keys = sorted({where[name][0] for name in uses})
        places = {name: (keys.index(where[name][0]), where[name][1]) for name in uses}
        operands = [place, weights] + [arrays[key] for key in keys]
        if totals is not None:
            operands.append(totals)
        total_shape = (2, 2, tall, wide)
        out = (share, per_block, 4 * per_block) if last else total_shape
        scratch = [pltpu.VMEM((len(slots), 2, tall, depth), jnp.bfloat16)]
        if last:
            scratch.append(pltpu.VMEM(total_shape, jnp.float32))
        return pl.pallas_call(
            functools.partial(add_shards, tuple(names), places, totals is not None, last),
            in_specs=[pl.BlockSpec(memory_space=pltpu.SMEM)]
            + [pl.BlockSpec(memory_space=pltpu.VMEM)] * (len(operands) - 1),
            out_specs=pl.BlockSpec(memory_space=pltpu.VMEM),
            out_shape=jax.ShapeDtypeStruct(out, jnp.float32),
            scratch_shapes=scratch,
            compiler_params=pltpu.CompilerParams(vmem_limit_bytes=40 * 1024 * 1024),
            cost_estimate=pl.CostEstimate(
                flops=4 * tall * wide * depth * len(names),
                bytes_accessed=wide * depth * 2 * len(names) + 8 * 4 * tall * wide,
                transcendentals=0,
            ),
        )(*operands)

    def fence(totals):
        nonlocal arrays
        arrays, totals = lax.optimization_barrier((arrays, totals))
        return totals

    put("0", packed, "near", [("O", 0)])

    first = [("O", 2), ("A", 0), ("O", 1), ("AB", 0), ("B", 0)]
    new = [hop_z(packed, 2), hop_a(packed), hop_z(packed, 1), hop_ab(packed), hop_b(packed)]
    for order, (kind, array) in enumerate(zip(first, new)):
        put("1" + "abcde"[order], array, "near", [kind])
    place, weights = fence((place, weights))

    def route(kernel, operands, counts):
        block = pl.BlockSpec(memory_space=pltpu.VMEM)
        first = pl.BlockSpec(memory_space=pltpu.SMEM) if operands[0] is place else block
        shapes = [(count,) * (count > 1) + packed.shape for count in counts]
        routed = pl.pallas_call(
            kernel,
            in_specs=[first] + [block] * (len(operands) - 1),
            out_specs=[block] * len(counts),
            out_shape=[jax.ShapeDtypeStruct(shape, packed.dtype) for shape in shapes],
            compiler_params=pltpu.CompilerParams(vmem_limit_bytes=24 * 1024 * 1024),
        )(*operands)
        return fence(routed)

    first = [("O", 0), ("A", 0), ("B", 0), ("AB", 0), ("O", 1), ("O", 2)]
    stack, both, relayed, mixed = route(
        route_second, [place] + [near(*kind) for kind in first], (6, 2, 2, 1)
    )
    second = [("AB", 1), ("O", 3), ("A", 1), ("A", 2), ("B", 1), ("B", 2), ("AB", 2)]
    totals = add([("near", *kind) for kind in first], None)
    put("2a", hop_a(both), "near", second[2:4])
    put("2b", hop_z(relayed, 1), "near", second[0:2])
    put("2c", hop_b(both), "near", second[4:6])
    put("2d", hop_mixed(mixed), "near", second[6:7])
    put("2e", swap(stack), "far", first)
    totals = fence(totals)

    arrived = [arrays[key] for key in ("2b", "2a", "2c", "2d")]
    stack, start = route(route_third, arrived, (7, 1))
    third = [("AB", 3), ("A", 3), ("B", 3)]
    new = [hop_z(near("AB", 2), 1), hop_a(start), hop_b(start)]
    put("3d", swap(stack), "far", second)
    totals = add([("near", *kind) for kind in second] + [("far", *kind) for kind in first], totals)
    totals = add([("far", *kind) for kind in second], totals)
    for order, (kind, array) in enumerate(zip(third, new)):
        put("3" + "abc"[order], array, "near", [kind])
    totals = fence(totals)

    new = [swap(near(*kind)) for kind in third]
    totals = add([("near", *kind) for kind in third], totals)
    for order, (kind, array) in enumerate(zip(third, new)):
        put("4" + "abc"[order], array, "far", [kind])
    totals = fence(totals)
    return add([("far", *kind) for kind in third], totals, last=True)


def add_terms(place_ref, weights_ref, left_ref, right_ref, field_ref):
    @pl.when(pl.program_id(0) == 0)
    def _():
        field_ref[...] = jnp.zeros_like(field_ref)

    spins = left_ref.shape[2]
    groups, columns, per_block, depth = right_ref.shape[0], *right_ref.shape[2:]
    owns = [left_ref[0, 0, spin] for spin in range(spins)]
    left_cos, left_sin = left_sides(owns, weights_ref[0])
    for column in range(columns):
        right = right_ref[:, 0, column].reshape(groups * per_block, depth)
        term = product(left_cos, left_sin, right)
        for part in range(2):
            for spin in range(spins):
                start = (part * spins + spin) * per_block
                field_ref[(spin * columns + column) * 2 + part] += term[start : start + per_block]


def gather_whole(packed, place, weights, share):
    groups, _, deep, flat = (lax.axis_size(name) for name in AXES)
    sites = deep * flat
    _, per_block, depth = packed.shape
    columns = min(4, share // 2)
    spins = share // (2 * columns)
    near = lax.all_gather(packed, ("pair", "deep", "flat"))
    near = near.reshape(groups, sites, 4, per_block, depth)
    far = lax.ppermute(near, "core", [(0, 1), (1, 0)])
    wide = groups * per_block

    def half(right):
        return pl.pallas_call(
            add_terms,
            grid_spec=pltpu.PrefetchScalarGridSpec(
                num_scalar_prefetch=1,
                grid=(sites,),
                in_specs=[
                    pl.BlockSpec((1, 2, weights.shape[2]), lambda m, place: (m, 0, 0)),
                    pl.BlockSpec(
                        (1, 1, spins, per_block, depth),
                        lambda m, place: (place[0], m, place[4] // spins, 0, 0),
                    ),
                    pl.BlockSpec(
                        (groups, 1, columns, per_block, depth),
                        lambda m, place: (0, m, place[6] // columns, 0, 0),
                    ),
                ],
                out_specs=pl.BlockSpec((share, per_block, wide), lambda m, place: (0, 0, 0)),
            ),
            out_shape=jax.ShapeDtypeStruct((share, per_block, wide), jnp.float32),
            compiler_params=pltpu.CompilerParams(vmem_limit_bytes=40 * 1024 * 1024),
        )(place, weights, near, right)

    sides = [half(right).reshape(share, per_block, groups, per_block) for right in (near, far)]
    first = lax.axis_index("core") == 0
    even, odd = (jnp.where(first, a, b) for a, b in (sides, sides[::-1]))
    return jnp.stack([even, odd], 3).reshape(share, per_block, 2 * wide)


def shards(modes, momenta):
    groups, _, deep, flat = (lax.axis_size(name) for name in AXES)
    sites = deep * flat
    slots, steps, per_block, spin_colour, site_count = modes.shape
    share = steps * momenta.shape[0] * 32 // sites
    owned = (lax.axis_index("deep") * flat + lax.axis_index("flat")) * (share // 2)
    place = [lax.axis_index(name) for name in AXES]
    place = jnp.stack(place + [owned // 4 % 4, jnp.int32(flat), owned % 4]).astype(jnp.int32)

    packed = jnp.transpose(modes.reshape(slots, per_block, 4, 3, site_count), (2, 1, 0, 3, 4))
    packed = packed.reshape(4, per_block, slots * 3 * site_count)

    mine = lax.dynamic_slice_in_dim(momenta, owned // 16, 1, 0)
    weights = phase_table(mine, jnp.int32(0), sites * site_count, LEXT)[0]
    weights = jnp.transpose(weights.reshape(2, sites, site_count), (1, 0, 2))

    if (groups, deep, flat) == (2, 4, 2) and share in (8, 16, 32):
        return swap_in_windows(packed, place, weights, share)
    return gather_whole(packed, place, weights, share)


def solution(mesh):
    count, sites = mesh.shape["blk"], mesh.shape["site"]
    flat = 2 ** (int(math.log2(sites)) // 2)
    split = Mesh(mesh.devices.reshape(count // 2, 2, sites // flat, flat), AXES)
    placed = (P(None, None, ("pair", "core"), None, ("deep", "flat")), P())
    return jax.shard_map(
        shards,
        mesh=split,
        in_specs=placed,
        out_specs=P(("deep", "flat"), ("pair", "core"), None),
        check_vma=False,
    )
```

```python
import functools
import math

import jax
import jax.numpy as jnp
from jax import lax
from jax.experimental import pallas as pl
from jax.experimental.pallas import tpu as pltpu
from jax.sharding import Mesh, PartitionSpec as P

LEXT = 48

TWO_PI = 2.0 * math.pi

AXES = ("pair", "core", "deep", "flat")


def phase_table(momenta, first_site, site_count, extent):
    flat = first_site + jnp.arange(site_count, dtype=jnp.int32)
    coords = jnp.stack([flat % extent, flat // extent % extent, flat // (extent * extent)], 0)
    turns = jnp.mod(jnp.sum(momenta[:, :, None] * coords[None, :, :], axis=1), extent)
    angle = turns.astype(jnp.float32) * (TWO_PI / extent)
    return jnp.stack([jnp.cos(angle), jnp.sin(angle)], 1)


def left_sides(owns, weights):
    depth = owns[0].shape[1]
    half = depth // 2
    cosine = jnp.tile(weights[0:1], (1, depth // weights.shape[1]))
    sine = jnp.tile(weights[1:2], (1, depth // weights.shape[1]))
    cosine_rows = [[], []]
    sine_rows = [[], []]
    for own in owns:
        own = own.astype(jnp.float32)
        by_cos = (own * cosine).astype(jnp.bfloat16)
        by_sin = (own * sine).astype(jnp.bfloat16)
        cosine_rows[0].append(by_cos)
        cosine_rows[1].append(jnp.concatenate([-by_cos[:, half:], by_cos[:, :half]], 1))
        sine_rows[0].append(jnp.concatenate([-by_sin[:, half:], by_sin[:, :half]], 1))
        sine_rows[1].append(-by_sin)
    return (
        jnp.concatenate(cosine_rows[0] + cosine_rows[1], 0),
        jnp.concatenate(sine_rows[0] + sine_rows[1], 0),
    )


def product(left_cos, left_sin, right):
    dims = (((1,), (1,)), ((), ()))
    term = lax.dot_general(left_cos, right, dims, preferred_element_type=jnp.float32)
    return term + lax.dot_general(left_sin, right, dims, preferred_element_type=jnp.float32)


def add_shards(names, where, has_totals, last, place_ref, weights_ref, *refs):
    refs = list(refs)
    scratch_ref = refs.pop() if last else None
    left_ref, out_ref = refs.pop(), refs.pop()
    totals_in = refs.pop() if has_totals else None
    totals_ref = scratch_ref if last else out_ref

    def shard(name):
        index, slot = where[name]
        return refs[index] if slot is None else refs[index].at[slot]

    pair, core, level, beside, first_s, flat = (place_ref[i] for i in range(6))
    columns, per_block, _ = shard(names[0]).shape
    spins = left_ref.shape[2] // (2 * per_block)

    if has_totals:
        totals_ref[...] = totals_in[...]
    else:
        totals_ref[...] = jnp.zeros_like(totals_ref)

    slots = left_slots(names)
    for slot, (dy, dz) in enumerate(slots):
        site = jnp.bitwise_xor(level, dz) * flat + jnp.bitwise_xor(beside, dy)
        if dy == 0:
            owns = [shard(("near", "O", dz))[first_s + s] for s in range(spins)]
        else:
            owns = [
                jnp.where(
                    core == 0,
                    shard(("near", "B", dz))[first_s + s],
                    shard(("near", "A", dz))[first_s + s],
                )
                for s in range(spins)
            ]
        left_ref[slot, 0], left_ref[slot, 1] = left_sides(owns, weights_ref[site])

    for side, kind, dz in names:
        right = shard((side, kind, dz))[...].reshape(columns * per_block, -1)
        turn = core if side == "near" else 1 - core
        dx, dy = {"O": (0, 0), "A": (1 - turn, turn), "B": (turn, 1 - turn), "AB": (1, 1)}[kind]
        if kind in ("O", "AB"):
            slot = slots.index((dy, dz))
        else:
            slot = slots.index((0, dz)) + dy
        totals_ref[0 if side == "near" else 1, dx] += product(
            left_ref[slot, 0], left_ref[slot, 1], right
        )

    if last:
        for part in range(2):
            for spin in range(spins):
                top = (part * spins + spin) * per_block
                for column in range(columns):
                    across = pl.ds(column * per_block, per_block)
                    pieces = [
                        totals_ref[
                            jnp.bitwise_xor(core, c),
                            jnp.bitwise_xor(pair, p),
                            pl.ds(top, per_block),
                            across,
                        ]
                        for p in range(2)
                        for c in range(2)
                    ]
                    row = (spin * columns + column) * 2 + part
                    out_ref[row] = jnp.concatenate(pieces, 1)


def route_second(place_ref, *refs):
    ab0_ref, o1_ref, o2_ref, stack_ref, both_ref, relayed_ref, mixed_ref = refs
    for slot in range(3):
        stack_ref[slot] = refs[slot][...]
    both_ref[0] = o1_ref[...]
    both_ref[1] = o2_ref[...]
    relayed_ref[0] = ab0_ref[...]
    relayed_ref[1] = o2_ref[...]
    mixed_ref[...] = jnp.where(place_ref[1] == 0, o2_ref[...], ab0_ref[...])


def route_third(z1_ref, a12_ref, b12_ref, ab2_ref, stack_ref, o3_ref):
    for slot, ref in enumerate((z1_ref, a12_ref, b12_ref)):
        stack_ref[2 * slot] = ref[0]
        stack_ref[2 * slot + 1] = ref[1]
    stack_ref[6] = ab2_ref[...]
    o3_ref[...] = z1_ref[1]


def left_slots(names):
    needed = set()
    for _, kind, dz in names:
        needed |= {"O": {(0, dz)}, "AB": {(1, dz)}}.get(kind, {(0, dz), (1, dz)})
    return sorted(needed, key=lambda slot: (slot[1], slot[0]))


def swap_in_windows(packed, place, weights, share):
    shape = tuple(lax.axis_size(name) for name in AXES)
    columns, per_block, depth = packed.shape
    spins = share // (2 * columns)
    tall, wide = 2 * spins * per_block, columns * per_block
    strides = (shape[1] * shape[2] * shape[3], shape[2] * shape[3], shape[3], 1)

    def move(array, target):
        pairs = []
        for p in range(shape[0]):
            for c in range(shape[1]):
                for z in range(shape[2]):
                    for y in range(shape[3]):
                        ends = (p, c, z, y), target(p, c, z, y)
                        pairs.append(
                            tuple(sum(a * b for a, b in zip(end, strides)) for end in ends)
                        )
        return lax.ppermute(array, AXES, pairs)

    def hop_a(array):
        return move(array, lambda p, c, z, y: (p ^ 1, c, z, y) if c == 0 else (p, c, z, y ^ 1))

    def hop_b(array):
        return move(array, lambda p, c, z, y: (p, c, z, y ^ 1) if c == 0 else (p ^ 1, c, z, y))

    def hop_ab(array):
        return move(array, lambda p, c, z, y: (p ^ 1, c, z, y ^ 1))

    def hop_z(array, by):
        return move(array, lambda p, c, z, y: (p, c, z ^ by, y))

    def hop_mixed(array):
        return move(
            array, lambda p, c, z, y: (p ^ 1, c, z, y ^ 1) if c == 0 else (p, c, z ^ 2, y)
        )

    def swap(array):
        return move(array, lambda p, c, z, y: (p, c ^ 1, z, y))

    arrays = {}
    where = {}

    def put(key, array, side, kinds):
        arrays[key] = array
        for slot, (kind, dz) in enumerate(kinds):
            where[(side, kind, dz)] = (key, slot if len(kinds) > 1 else None)

    def near(kind, dz):
        key, slot = where[("near", kind, dz)]
        return arrays[key] if slot is None else arrays[key][slot]

    def add(names, totals, last=False):
        slots = left_slots(names)
        uses = list(names)
        for dy, dz in slots:
            uses += [("near", kind, dz) for kind in (("A", "B") if dy else ("O",))]
        keys = sorted({where[name][0] for name in uses})
        places = {name: (keys.index(where[name][0]), where[name][1]) for name in uses}
        operands = [place, weights] + [arrays[key] for key in keys]
        if totals is not None:
            operands.append(totals)
        total_shape = (2, 2, tall, wide)
        out = (share, per_block, 4 * per_block) if last else total_shape
        scratch = [pltpu.VMEM((len(slots), 2, tall, depth), jnp.bfloat16)]
        if last:
            scratch.append(pltpu.VMEM(total_shape, jnp.float32))
        return pl.pallas_call(
            functools.partial(add_shards, tuple(names), places, totals is not None, last),
            in_specs=[pl.BlockSpec(memory_space=pltpu.SMEM)]
            + [pl.BlockSpec(memory_space=pltpu.VMEM)] * (len(operands) - 1),
            out_specs=pl.BlockSpec(memory_space=pltpu.VMEM),
            out_shape=jax.ShapeDtypeStruct(out, jnp.float32),
            scratch_shapes=scratch,
            compiler_params=pltpu.CompilerParams(vmem_limit_bytes=40 * 1024 * 1024),
            cost_estimate=pl.CostEstimate(
                flops=4 * tall * wide * depth * len(names),
                bytes_accessed=wide * depth * 2 * len(names) + 8 * 4 * tall * wide,
                transcendentals=0,
            ),
        )(*operands)

    def fence(totals):
        nonlocal arrays
        arrays, totals = lax.optimization_barrier((arrays, totals))
        return totals

    put("0", packed, "near", [("O", 0)])

    early = [("O", 0), ("A", 0), ("B", 0)]
    new = [hop_z(packed, 2), hop_a(packed), hop_z(packed, 1), hop_b(packed)]
    put("1b", new[1], "near", [("A", 0)])
    put("1d", new[3], "near", [("B", 0)])
    totals, place, weights = fence((None, place, weights))
    totals = add([("near", *kind) for kind in early], None)
    totals = fence(totals)
    for order, kind in enumerate(early):
        put("1f" + "abc"[order], swap(near(*kind)), "far", [kind])
    put("1e", hop_b(near("A", 0)), "near", [("AB", 0)])
    put("1a", new[0], "near", [("O", 2)])
    put("1c", new[2], "near", [("O", 1)])
    totals = fence(totals)

    def route(kernel, operands, counts):
        block = pl.BlockSpec(memory_space=pltpu.VMEM)
        first = pl.BlockSpec(memory_space=pltpu.SMEM) if operands[0] is place else block
        shapes = [(count,) * (count > 1) + packed.shape for count in counts]
        routed = pl.pallas_call(
            kernel,
            in_specs=[first] + [block] * (len(operands) - 1),
            out_specs=[block] * len(counts),
            out_shape=[jax.ShapeDtypeStruct(shape, packed.dtype) for shape in shapes],
            compiler_params=pltpu.CompilerParams(vmem_limit_bytes=24 * 1024 * 1024),
        )(*operands)
        return fence(routed)

    first = [("AB", 0), ("O", 1), ("O", 2)]
    stack, both, relayed, mixed = route(
        route_second, [place] + [near(*kind) for kind in first], (3, 2, 2, 1)
    )
    second = [("AB", 1), ("O", 3), ("A", 1), ("A", 2), ("B", 1), ("B", 2), ("AB", 2)]
    totals = add(
        [("near", *kind) for kind in first] + [("far", *kind) for kind in early], totals
    )
    put("2a", hop_z(relayed, 1), "near", second[0:2])
    put("2b", hop_a(both), "near", second[2:4])
    put("2c", hop_b(both), "near", second[4:6])
    put("2d", hop_mixed(mixed), "near", second[6:7])
    put("2e", swap(stack), "far", first)
    totals = fence(totals)

    arrived = [arrays[key] for key in ("2a", "2b", "2c", "2d")]
    stack, start = route(route_third, arrived, (7, 1))
    third = [("AB", 3), ("A", 3), ("B", 3)]
    new = [hop_z(near("AB", 2), 1), hop_a(start), hop_b(start)]
    put("3d", swap(stack), "far", second)
    totals = add([("near", *kind) for kind in second] + [("far", *kind) for kind in first], totals)
    totals = add([("far", *kind) for kind in second], totals)
    for order, (kind, array) in enumerate(zip(third, new)):
        put("3" + "abc"[order], array, "near", [kind])
    totals = fence(totals)

    new = [swap(near(*kind)) for kind in third]
    totals = add([("near", *kind) for kind in third], totals)
    for order, (kind, array) in enumerate(zip(third, new)):
        put("4" + "abc"[order], array, "far", [kind])
    totals = fence(totals)
    return add([("far", *kind) for kind in third], totals, last=True)


def add_terms(place_ref, weights_ref, left_ref, right_ref, field_ref):
    @pl.when(pl.program_id(0) == 0)
    def _():
        field_ref[...] = jnp.zeros_like(field_ref)

    spins = left_ref.shape[2]
    groups, columns, per_block, depth = right_ref.shape[0], *right_ref.shape[2:]
    owns = [left_ref[0, 0, spin] for spin in range(spins)]
    left_cos, left_sin = left_sides(owns, weights_ref[0])
    for column in range(columns):
        right = right_ref[:, 0, column].reshape(groups * per_block, depth)
        term = product(left_cos, left_sin, right)
        for part in range(2):
            for spin in range(spins):
                start = (part * spins + spin) * per_block
                field_ref[(spin * columns + column) * 2 + part] += term[start : start + per_block]


def gather_whole(packed, place, weights, share):
    groups, _, deep, flat = (lax.axis_size(name) for name in AXES)
    sites = deep * flat
    _, per_block, depth = packed.shape
    columns = min(4, share // 2)
    spins = share // (2 * columns)
    near = lax.all_gather(packed, ("pair", "deep", "flat"))
    near = near.reshape(groups, sites, 4, per_block, depth)
    far = lax.ppermute(near, "core", [(0, 1), (1, 0)])
    wide = groups * per_block

    def half(right):
        return pl.pallas_call(
            add_terms,
            grid_spec=pltpu.PrefetchScalarGridSpec(
                num_scalar_prefetch=1,
                grid=(sites,),
                in_specs=[
                    pl.BlockSpec((1, 2, weights.shape[2]), lambda m, place: (m, 0, 0)),
                    pl.BlockSpec(
                        (1, 1, spins, per_block, depth),
                        lambda m, place: (place[0], m, place[4] // spins, 0, 0),
                    ),
                    pl.BlockSpec(
                        (groups, 1, columns, per_block, depth),
                        lambda m, place: (0, m, place[6] // columns, 0, 0),
                    ),
                ],
                out_specs=pl.BlockSpec((share, per_block, wide), lambda m, place: (0, 0, 0)),
            ),
            out_shape=jax.ShapeDtypeStruct((share, per_block, wide), jnp.float32),
            compiler_params=pltpu.CompilerParams(vmem_limit_bytes=40 * 1024 * 1024),
        )(place, weights, near, right)

    sides = [half(right).reshape(share, per_block, groups, per_block) for right in (near, far)]
    first = lax.axis_index("core") == 0
    even, odd = (jnp.where(first, a, b) for a, b in (sides, sides[::-1]))
    return jnp.stack([even, odd], 3).reshape(share, per_block, 2 * wide)


def shards(modes, momenta):
    groups, _, deep, flat = (lax.axis_size(name) for name in AXES)
    sites = deep * flat
    slots, steps, per_block, spin_colour, site_count = modes.shape
    share = steps * momenta.shape[0] * 32 // sites
    owned = (lax.axis_index("deep") * flat + lax.axis_index("flat")) * (share // 2)
    place = [lax.axis_index(name) for name in AXES]
    place = jnp.stack(place + [owned // 4 % 4, jnp.int32(flat), owned % 4]).astype(jnp.int32)

    packed = jnp.transpose(modes.reshape(slots, per_block, 4, 3, site_count), (2, 1, 0, 3, 4))
    packed = packed.reshape(4, per_block, slots * 3 * site_count)

    mine = lax.dynamic_slice_in_dim(momenta, owned // 16, 1, 0)
    weights = phase_table(mine, jnp.int32(0), sites * site_count, LEXT)[0]
    weights = jnp.transpose(weights.reshape(2, sites, site_count), (1, 0, 2))

    if (groups, deep, flat) == (2, 4, 2) and share in (8, 16, 32):
        return swap_in_windows(packed, place, weights, share)
    return gather_whole(packed, place, weights, share)


def solution(mesh):
    count, sites = mesh.shape["blk"], mesh.shape["site"]
    flat = 2 ** (int(math.log2(sites)) // 2)
    split = Mesh(mesh.devices.reshape(count // 2, 2, sites // flat, flat), AXES)
    placed = (P(None, None, ("pair", "core"), None, ("deep", "flat")), P())
    return jax.shard_map(
        shards,
        mesh=split,
        in_specs=placed,
        out_specs=P(("deep", "flat"), ("pair", "core"), None),
        check_vma=False,
    )
```

```python
import functools
import math

import jax
import jax.numpy as jnp
from jax import lax
from jax.experimental import pallas as pl
from jax.experimental.pallas import tpu as pltpu
from jax.sharding import Mesh, PartitionSpec as P

LEXT = 48

TWO_PI = 2.0 * math.pi

AXES = ("pair", "core", "deep", "flat")


def phase_table(momenta, first_site, site_count, extent):
    flat = first_site + jnp.arange(site_count, dtype=jnp.int32)
    coords = jnp.stack([flat % extent, flat // extent % extent, flat // (extent * extent)], 0)
    turns = jnp.mod(jnp.sum(momenta[:, :, None] * coords[None, :, :], axis=1), extent)
    angle = turns.astype(jnp.float32) * (TWO_PI / extent)
    return jnp.stack([jnp.cos(angle), jnp.sin(angle)], 1)


def left_sides(owns, weights):
    depth = owns[0].shape[1]
    half = depth // 2
    cosine = jnp.tile(weights[0:1], (1, depth // weights.shape[1]))
    sine = jnp.tile(weights[1:2], (1, depth // weights.shape[1]))
    cosine_rows = [[], []]
    sine_rows = [[], []]
    for own in owns:
        own = own.astype(jnp.float32)
        by_cos = (own * cosine).astype(jnp.bfloat16)
        by_sin = (own * sine).astype(jnp.bfloat16)
        cosine_rows[0].append(by_cos)
        cosine_rows[1].append(jnp.concatenate([-by_cos[:, half:], by_cos[:, :half]], 1))
        sine_rows[0].append(jnp.concatenate([-by_sin[:, half:], by_sin[:, :half]], 1))
        sine_rows[1].append(-by_sin)
    return (
        jnp.concatenate(cosine_rows[0] + cosine_rows[1], 0),
        jnp.concatenate(sine_rows[0] + sine_rows[1], 0),
    )


def product(left_cos, left_sin, right):
    dims = (((1,), (1,)), ((), ()))
    term = lax.dot_general(left_cos, right, dims, preferred_element_type=jnp.float32)
    return term + lax.dot_general(left_sin, right, dims, preferred_element_type=jnp.float32)


def add_shards(names, where, has_totals, last, place_ref, weights_ref, *refs):
    refs = list(refs)
    if last:
        far_ref, out_ref, totals_in, left_ref = (refs.pop() for _ in range(4))
    else:
        left_ref, out_ref = refs.pop(), refs.pop()
        totals_in = refs.pop() if has_totals else None

    def shard(name):
        index, slot = where[name]
        return refs[index] if slot is None else refs[index].at[slot]

    pair, core, level, beside, first_s, flat = (place_ref[i] for i in range(6))
    columns, per_block, _ = shard(names[0]).shape
    spins = left_ref.shape[2] // (2 * per_block)

    slots = left_slots(names)
    if last:
        far_ref[...] = totals_in[1]
    else:
        if has_totals:
            out_ref[...] = totals_in[...]
        else:
            out_ref[...] = jnp.zeros_like(out_ref)
        for slot, (dy, dz) in enumerate(slots):
            site = jnp.bitwise_xor(level, dz) * flat + jnp.bitwise_xor(beside, dy)
            if dy == 0:
                owns = [shard(("near", "O", dz))[first_s + s] for s in range(spins)]
            else:
                owns = [
                    jnp.where(
                        core == 0,
                        shard(("near", "B", dz))[first_s + s],
                        shard(("near", "A", dz))[first_s + s],
                    )
                    for s in range(spins)
                ]
            left_ref[slot, 0], left_ref[slot, 1] = left_sides(owns, weights_ref[site])

    for side, kind, dz in names:
        right = shard((side, kind, dz))[...].reshape(columns * per_block, -1)
        turn = core if side == "near" else 1 - core
        dx, dy = {"O": (0, 0), "A": (1 - turn, turn), "B": (turn, 1 - turn), "AB": (1, 1)}[kind]
        if kind in ("O", "AB"):
            slot = slots.index((dy, dz))
        else:
            slot = slots.index((0, dz)) + dy
        term = product(left_ref[slot, 0], left_ref[slot, 1], right)
        if last:
            far_ref[dx] += term
        else:
            out_ref[0 if side == "near" else 1, dx] += term

    if last:
        lane = lax.broadcasted_iota(jnp.int32, (per_block, 2 * per_block), 1)
        for part in range(2):
            for spin in range(spins):
                top = (part * spins + spin) * per_block
                for column in range(0, columns, 2):
                    across = pl.ds(column * per_block, 2 * per_block)
                    for p in range(2):
                        dx = jnp.bitwise_xor(pair, p)
                        near = totals_in[0, dx, pl.ds(top, per_block), across]
                        far = far_ref[dx, pl.ds(top, per_block), across]
                        even = jnp.where(core == 0, near, far)
                        odd = jnp.where(core == 0, far, near)
                        row = (spin * columns + column) * 2 + part
                        place = pl.ds(p * 2 * per_block, 2 * per_block)
                        out_ref[row, :, place] = jnp.where(
                            lane < per_block, even, pltpu.roll(odd, per_block, 1)
                        )
                        out_ref[row + 2, :, place] = jnp.where(
                            lane < per_block, pltpu.roll(even, per_block, 1), odd
                        )


def route_second(place_ref, *refs):
    ab0_ref, o1_ref, o2_ref, stack_ref, both_ref, relayed_ref, mixed_ref = refs[3:]
    for slot in range(6):
        stack_ref[slot] = refs[slot][...]
    both_ref[0] = o1_ref[...]
    both_ref[1] = o2_ref[...]
    relayed_ref[0] = ab0_ref[...]
    relayed_ref[1] = o2_ref[...]
    mixed_ref[...] = jnp.where(place_ref[1] == 0, o2_ref[...], ab0_ref[...])


def route_third(z1_ref, a12_ref, b12_ref, ab2_ref, stack_ref, o3_ref):
    for slot, ref in enumerate((z1_ref, a12_ref, b12_ref)):
        stack_ref[2 * slot] = ref[0]
        stack_ref[2 * slot + 1] = ref[1]
    stack_ref[6] = ab2_ref[...]
    o3_ref[...] = z1_ref[1]


def left_slots(names):
    needed = set()
    for _, kind, dz in names:
        needed |= {"O": {(0, dz)}, "AB": {(1, dz)}}.get(kind, {(0, dz), (1, dz)})
    return sorted(needed, key=lambda slot: (slot[1], slot[0]))


def swap_in_windows(packed, place, weights, share):
    shape = tuple(lax.axis_size(name) for name in AXES)
    columns, per_block, depth = packed.shape
    spins = share // (2 * columns)
    tall, wide = 2 * spins * per_block, columns * per_block
    strides = (shape[1] * shape[2] * shape[3], shape[2] * shape[3], shape[3], 1)

    def move(array, target):
        pairs = []
        for p in range(shape[0]):
            for c in range(shape[1]):
                for z in range(shape[2]):
                    for y in range(shape[3]):
                        ends = (p, c, z, y), target(p, c, z, y)
                        pairs.append(
                            tuple(sum(a * b for a, b in zip(end, strides)) for end in ends)
                        )
        return lax.ppermute(array, AXES, pairs)

    def hop_a(array):
        return move(array, lambda p, c, z, y: (p ^ 1, c, z, y) if c == 0 else (p, c, z, y ^ 1))

    def hop_b(array):
        return move(array, lambda p, c, z, y: (p, c, z, y ^ 1) if c == 0 else (p ^ 1, c, z, y))

    def hop_ab(array):
        return move(array, lambda p, c, z, y: (p ^ 1, c, z, y ^ 1))

    def hop_z(array, by):
        return move(array, lambda p, c, z, y: (p, c, z ^ by, y))

    def hop_mixed(array):
        return move(
            array, lambda p, c, z, y: (p ^ 1, c, z, y ^ 1) if c == 0 else (p, c, z ^ 2, y)
        )

    def swap(array):
        return move(array, lambda p, c, z, y: (p, c ^ 1, z, y))

    arrays = {}
    where = {}

    def put(key, array, side, kinds):
        arrays[key] = array
        for slot, (kind, dz) in enumerate(kinds):
            where[(side, kind, dz)] = (key, slot if len(kinds) > 1 else None)

    def near(kind, dz):
        key, slot = where[("near", kind, dz)]
        return arrays[key] if slot is None else arrays[key][slot]

    def add(names, totals, keep=False, left=None):
        last = left is not None
        slots = left_slots(names)
        uses = list(names)
        for dy, dz in [] if last else slots:
            uses += [("near", kind, dz) for kind in (("A", "B") if dy else ("O",))]
        keys = sorted({where[name][0] for name in uses})
        places = {name: (keys.index(where[name][0]), where[name][1]) for name in uses}
        operands = [place, weights] + [arrays[key] for key in keys]
        operands += [each for each in (left, totals) if each is not None]
        total_shape = (2, 2, tall, wide)
        left_shape = (len(slots), 2, tall, depth)
        block = pl.BlockSpec(memory_space=pltpu.VMEM)
        out_shape = [jax.ShapeDtypeStruct(total_shape, jnp.float32)]
        scratch = [pltpu.VMEM(left_shape, jnp.bfloat16)]
        if last:
            out_shape = [jax.ShapeDtypeStruct((share, per_block, 4 * per_block), jnp.float32)]
            scratch = [pltpu.VMEM(total_shape[1:], jnp.float32)]
        if keep:
            out_shape.append(jax.ShapeDtypeStruct(left_shape, jnp.bfloat16))
            scratch = []
        out = pl.pallas_call(
            functools.partial(add_shards, tuple(names), places, totals is not None, last),
            in_specs=[pl.BlockSpec(memory_space=pltpu.SMEM)] + [block] * (len(operands) - 1),
            out_specs=[block] * len(out_shape),
            out_shape=out_shape,
            scratch_shapes=scratch,
            compiler_params=pltpu.CompilerParams(vmem_limit_bytes=40 * 1024 * 1024),
            cost_estimate=pl.CostEstimate(
                flops=4 * tall * wide * depth * len(names),
                bytes_accessed=wide * depth * 2 * len(names) + 8 * 4 * tall * wide,
                transcendentals=0,
            ),
        )(*operands)
        return out if keep else out[0]

    def fence(totals):
        nonlocal arrays
        arrays, totals = lax.optimization_barrier((arrays, totals))
        return totals

    put("9", packed, "near", [("O", 0)])

    put("1a", hop_z(packed, 2), "near", [("O", 2)])
    put("1b", hop_z(packed, 1), "near", [("O", 1)])
    put("1c", hop_b(packed), "near", [("B", 0)])
    put("1d", hop_a(packed), "near", [("A", 0)])
    put("1e", hop_b(near("A", 0)), "near", [("AB", 0)])
    place, weights = fence((place, weights))

    def route(kernel, operands, counts):
        block = pl.BlockSpec(memory_space=pltpu.VMEM)
        first = pl.BlockSpec(memory_space=pltpu.SMEM) if operands[0] is place else block
        shapes = [(count,) * (count > 1) + packed.shape for count in counts]
        routed = pl.pallas_call(
            kernel,
            in_specs=[first] + [block] * (len(operands) - 1),
            out_specs=[block] * len(counts),
            out_shape=[jax.ShapeDtypeStruct(shape, packed.dtype) for shape in shapes],
            compiler_params=pltpu.CompilerParams(vmem_limit_bytes=24 * 1024 * 1024),
        )(*operands)
        return fence(routed)

    first = [("O", 0), ("A", 0), ("B", 0), ("AB", 0), ("O", 1), ("O", 2)]
    stack, both, relayed, mixed = route(
        route_second, [place] + [near(*kind) for kind in first], (6, 2, 2, 1)
    )
    second = [("AB", 1), ("O", 3), ("A", 1), ("A", 2), ("B", 1), ("B", 2), ("AB", 2)]
    totals = add([("near", *kind) for kind in first], None)
    put("2a", hop_z(relayed, 1), "near", second[0:2])
    put("2b", hop_a(both), "near", second[2:4])
    put("2c", hop_b(both), "near", second[4:6])
    put("2d", hop_mixed(mixed), "near", second[6:7])
    put("2e", swap(stack), "far", first)
    totals = fence(totals)

    arrived = [arrays[key] for key in ("2a", "2b", "2c", "2d")]
    stack, start = route(route_third, arrived, (7, 1))
    third = [("AB", 3), ("A", 3), ("B", 3)]
    new = [hop_z(near("AB", 2), 1), hop_a(start), hop_b(start)]
    put("3d", swap(stack), "far", second)
    totals = add([("near", *kind) for kind in second] + [("far", *kind) for kind in first], totals)
    totals = add([("far", *kind) for kind in second], totals)
    for order, (kind, array) in enumerate(zip(third, new)):
        put("3" + "abc"[order], array, "near", [kind])
    totals = fence(totals)

    new = [swap(near(*kind)) for kind in third]
    totals, left = add([("near", *kind) for kind in third], totals, keep=True)
    for order, (kind, array) in enumerate(zip(third, new)):
        put("4" + "abc"[order], array, "far", [kind])
    totals, left = fence((totals, left))
    return add([("far", *kind) for kind in third], totals, left=left)


def add_terms(place_ref, weights_ref, left_ref, right_ref, field_ref):
    @pl.when(pl.program_id(0) == 0)
    def _():
        field_ref[...] = jnp.zeros_like(field_ref)

    spins = left_ref.shape[2]
    groups, columns, per_block, depth = right_ref.shape[0], *right_ref.shape[2:]
    owns = [left_ref[0, 0, spin] for spin in range(spins)]
    left_cos, left_sin = left_sides(owns, weights_ref[0])
    for column in range(columns):
        right = right_ref[:, 0, column].reshape(groups * per_block, depth)
        term = product(left_cos, left_sin, right)
        for part in range(2):
            for spin in range(spins):
                start = (part * spins + spin) * per_block
                field_ref[(spin * columns + column) * 2 + part] += term[start : start + per_block]


def gather_whole(packed, place, weights, share):
    groups, _, deep, flat = (lax.axis_size(name) for name in AXES)
    sites = deep * flat
    _, per_block, depth = packed.shape
    columns = min(4, share // 2)
    spins = share // (2 * columns)
    near = lax.all_gather(packed, ("pair", "deep", "flat"))
    near = near.reshape(groups, sites, 4, per_block, depth)
    far = lax.ppermute(near, "core", [(0, 1), (1, 0)])
    wide = groups * per_block

    def half(right):
        return pl.pallas_call(
            add_terms,
            grid_spec=pltpu.PrefetchScalarGridSpec(
                num_scalar_prefetch=1,
                grid=(sites,),
                in_specs=[
                    pl.BlockSpec((1, 2, weights.shape[2]), lambda m, place: (m, 0, 0)),
                    pl.BlockSpec(
                        (1, 1, spins, per_block, depth),
                        lambda m, place: (place[0], m, place[4] // spins, 0, 0),
                    ),
                    pl.BlockSpec(
                        (groups, 1, columns, per_block, depth),
                        lambda m, place: (0, m, place[6] // columns, 0, 0),
                    ),
                ],
                out_specs=pl.BlockSpec((share, per_block, wide), lambda m, place: (0, 0, 0)),
            ),
            out_shape=jax.ShapeDtypeStruct((share, per_block, wide), jnp.float32),
            compiler_params=pltpu.CompilerParams(vmem_limit_bytes=40 * 1024 * 1024),
        )(place, weights, near, right)

    sides = [half(right).reshape(share, per_block, groups, per_block) for right in (near, far)]
    first = lax.axis_index("core") == 0
    even, odd = (jnp.where(first, a, b) for a, b in (sides, sides[::-1]))
    return jnp.stack([even, odd], 3).reshape(share, per_block, 2 * wide)


def shards(modes, momenta):
    groups, _, deep, flat = (lax.axis_size(name) for name in AXES)
    sites = deep * flat
    slots, steps, per_block, spin_colour, site_count = modes.shape
    share = steps * momenta.shape[0] * 32 // sites
    owned = (lax.axis_index("deep") * flat + lax.axis_index("flat")) * (share // 2)
    place = [lax.axis_index(name) for name in AXES]
    place = jnp.stack(place + [owned // 4 % 4, jnp.int32(flat), owned % 4]).astype(jnp.int32)

    packed = jnp.transpose(modes.reshape(slots, per_block, 4, 3, site_count), (2, 1, 0, 3, 4))
    packed = packed.reshape(4, per_block, slots * 3 * site_count)

    mine = lax.dynamic_slice_in_dim(momenta, owned // 16, 1, 0)
    weights = phase_table(mine, jnp.int32(0), sites * site_count, LEXT)[0]
    weights = jnp.transpose(weights.reshape(2, sites, site_count), (1, 0, 2))

    if (groups, deep, flat) == (2, 4, 2) and share in (8, 16, 32):
        return swap_in_windows(packed, place, weights, share)
    return gather_whole(packed, place, weights, share)


def solution(mesh):
    count, sites = mesh.shape["blk"], mesh.shape["site"]
    flat = 2 ** (int(math.log2(sites)) // 2)
    split = Mesh(mesh.devices.reshape(count // 2, 2, sites // flat, flat), AXES)
    placed = (P(None, None, ("pair", "core"), None, ("deep", "flat")), P())
    return jax.shard_map(
        shards,
        mesh=split,
        in_specs=placed,
        out_specs=P(("deep", "flat"), ("pair", "core"), None),
        check_vma=False,
    )
```

```python
import functools
import math

import jax
import jax.numpy as jnp
from jax import lax
from jax.experimental import pallas as pl
from jax.experimental.pallas import tpu as pltpu
from jax.sharding import Mesh, PartitionSpec as P

LEXT = 48

TWO_PI = 2.0 * math.pi

AXES = ("pair", "core", "deep", "flat")


def phase_table(momenta, first_site, site_count, extent):
    flat = first_site + jnp.arange(site_count, dtype=jnp.int32)
    coords = jnp.stack([flat % extent, flat // extent % extent, flat // (extent * extent)], 0)
    turns = jnp.mod(jnp.sum(momenta[:, :, None] * coords[None, :, :], axis=1), extent)
    angle = turns.astype(jnp.float32) * (TWO_PI / extent)
    return jnp.stack([jnp.cos(angle), jnp.sin(angle)], 1)


def left_sides(owns, weights):
    depth = owns[0].shape[1]
    half = depth // 2
    cosine = jnp.tile(weights[0:1], (1, depth // weights.shape[1]))
    sine = jnp.tile(weights[1:2], (1, depth // weights.shape[1]))
    cosine_rows = [[], []]
    sine_rows = [[], []]
    for own in owns:
        own = own.astype(jnp.float32)
        by_cos = (own * cosine).astype(jnp.bfloat16)
        by_sin = (own * sine).astype(jnp.bfloat16)
        cosine_rows[0].append(by_cos)
        cosine_rows[1].append(jnp.concatenate([-by_cos[:, half:], by_cos[:, :half]], 1))
        sine_rows[0].append(jnp.concatenate([-by_sin[:, half:], by_sin[:, :half]], 1))
        sine_rows[1].append(-by_sin)
    return (
        jnp.concatenate(cosine_rows[0] + cosine_rows[1], 0),
        jnp.concatenate(sine_rows[0] + sine_rows[1], 0),
    )


def product(left_cos, left_sin, right):
    dims = (((1,), (1,)), ((), ()))
    term = lax.dot_general(left_cos, right, dims, preferred_element_type=jnp.float32)
    return term + lax.dot_general(left_sin, right, dims, preferred_element_type=jnp.float32)


def add_shards(names, where, has_totals, last, place_ref, weights_ref, *refs):
    refs = list(refs)
    if last:
        sems, row_ref, far_ref, out_ref, totals_in, left_ref = (refs.pop() for _ in range(6))
    else:
        left_ref, out_ref = refs.pop(), refs.pop()
        totals_in = refs.pop() if has_totals else None

    def shard(name):
        index, slot = where[name]
        return refs[index] if slot is None else refs[index].at[slot]

    pair, core, level, beside, first_s, flat = (place_ref[i] for i in range(6))
    columns, per_block, _ = shard(names[0]).shape
    spins = left_ref.shape[2] // (2 * per_block)

    slots = left_slots(names)
    if last:
        far_ref[...] = totals_in[1]
    else:
        if has_totals:
            out_ref[...] = totals_in[...]
        else:
            out_ref[...] = jnp.zeros_like(out_ref)
        for slot, (dy, dz) in enumerate(slots):
            site = jnp.bitwise_xor(level, dz) * flat + jnp.bitwise_xor(beside, dy)
            if dy == 0:
                owns = [shard(("near", "O", dz))[first_s + s] for s in range(spins)]
            else:
                owns = [
                    jnp.where(
                        core == 0,
                        shard(("near", "B", dz))[first_s + s],
                        shard(("near", "A", dz))[first_s + s],
                    )
                    for s in range(spins)
                ]
            left_ref[slot, 0], left_ref[slot, 1] = left_sides(owns, weights_ref[site])

    for side, kind, dz in names:
        right = shard((side, kind, dz))[...].reshape(columns * per_block, -1)
        turn = core if side == "near" else 1 - core
        dx, dy = {"O": (0, 0), "A": (1 - turn, turn), "B": (turn, 1 - turn), "AB": (1, 1)}[kind]
        if kind in ("O", "AB"):
            slot = slots.index((dy, dz))
        else:
            slot = slots.index((0, dz)) + dy
        term = product(left_ref[slot, 0], left_ref[slot, 1], right)
        if last:
            far_ref[dx] += term
        else:
            out_ref[0 if side == "near" else 1, dx] += term

    if last:
        lane = lax.broadcasted_iota(jnp.int32, (per_block, 2 * per_block), 1)
        copies = []
        for spin in range(spins):
            for column in range(0, columns, 2):
                first = (spin * columns + column) * 2
                across = pl.ds(column * per_block, 2 * per_block)
                for part in range(2):
                    top = (part * spins + spin) * per_block
                    for p in range(2):
                        dx = jnp.bitwise_xor(pair, p)
                        near = totals_in[0, dx, pl.ds(top, per_block), across]
                        far = far_ref[dx, pl.ds(top, per_block), across]
                        even = jnp.where(core == 0, near, far)
                        odd = jnp.where(core == 0, far, near)
                        place = pl.ds(p * 2 * per_block, 2 * per_block)
                        row_ref[first + part, :, place] = jnp.where(
                            lane < per_block, even, pltpu.roll(odd, per_block, 1)
                        )
                        row_ref[first + part + 2, :, place] = jnp.where(
                            lane < per_block, pltpu.roll(even, per_block, 1), odd
                        )
                rows = pl.ds(first, 4)
                copies.append(
                    pltpu.make_async_copy(row_ref.at[rows], out_ref.at[rows], sems.at[len(copies)])
                )
                copies[-1].start()
        for copy in copies:
            copy.wait()


def route_second(place_ref, *refs):
    ab0_ref, o1_ref, o2_ref, stack_ref, both_ref, mixed_ref = refs[3:]
    for slot in range(6):
        stack_ref[slot] = refs[slot][...]
    both_ref[0] = o1_ref[...]
    both_ref[1] = o2_ref[...]
    mixed_ref[...] = jnp.where(place_ref[1] == 0, o2_ref[...], ab0_ref[...])


def route_third(ab1_ref, o3_ref, ab2_ref, a12_ref, b12_ref, stack_ref):
    for slot, ref in enumerate((ab1_ref, o3_ref, ab2_ref)):
        stack_ref[slot] = ref[...]
    stack_ref[3:5] = a12_ref[...]
    stack_ref[5:7] = b12_ref[...]


def route_last(a3_ref, ab3_ref, stack_ref):
    stack_ref[0] = a3_ref[...]
    stack_ref[1] = ab3_ref[...]


def left_slots(names):
    needed = set()
    for _, kind, dz in names:
        needed |= {"O": {(0, dz)}, "AB": {(1, dz)}}.get(kind, {(0, dz), (1, dz)})
    return sorted(needed, key=lambda slot: (slot[1], slot[0]))


def swap_in_windows(packed, place, weights, share):
    shape = tuple(lax.axis_size(name) for name in AXES)
    columns, per_block, depth = packed.shape
    spins = share // (2 * columns)
    tall, wide = 2 * spins * per_block, columns * per_block
    strides = (shape[1] * shape[2] * shape[3], shape[2] * shape[3], shape[3], 1)

    def move(array, target):
        pairs = []
        for p in range(shape[0]):
            for c in range(shape[1]):
                for z in range(shape[2]):
                    for y in range(shape[3]):
                        ends = (p, c, z, y), target(p, c, z, y)
                        pairs.append(
                            tuple(sum(a * b for a, b in zip(end, strides)) for end in ends)
                        )
        return lax.ppermute(array, AXES, pairs)

    def hop_a(array):
        return move(array, lambda p, c, z, y: (p ^ 1, c, z, y) if c == 0 else (p, c, z, y ^ 1))

    def hop_b(array):
        return move(array, lambda p, c, z, y: (p, c, z, y ^ 1) if c == 0 else (p ^ 1, c, z, y))

    def hop_ab(array):
        return move(array, lambda p, c, z, y: (p ^ 1, c, z, y ^ 1))

    def hop_z(array, by):
        return move(array, lambda p, c, z, y: (p, c, z ^ by, y))

    def hop_mixed(array):
        return move(
            array, lambda p, c, z, y: (p ^ 1, c, z, y ^ 1) if c == 0 else (p, c, z ^ 2, y)
        )

    def swap(array):
        return move(array, lambda p, c, z, y: (p, c ^ 1, z, y))

    arrays = {}
    where = {}

    def put(key, array, side, kinds):
        arrays[key] = array
        for slot, (kind, dz) in enumerate(kinds):
            where[(side, kind, dz)] = (key, slot if len(kinds) > 1 else None)

    def near(kind, dz):
        key, slot = where[("near", kind, dz)]
        return arrays[key] if slot is None else arrays[key][slot]

    def add(names, totals, keep=False, left=None):
        last = left is not None
        slots = left_slots(names)
        uses = list(names)
        for dy, dz in [] if last else slots:
            uses += [("near", kind, dz) for kind in (("A", "B") if dy else ("O",))]
        keys = sorted({where[name][0] for name in uses})
        places = {name: (keys.index(where[name][0]), where[name][1]) for name in uses}
        operands = [place, weights] + [arrays[key] for key in keys]
        operands += [each for each in (left, totals) if each is not None]
        total_shape = (2, 2, tall, wide)
        left_shape = (len(slots), 2, tall, depth)
        block = pl.BlockSpec(memory_space=pltpu.VMEM)
        out_shape = [jax.ShapeDtypeStruct(total_shape, jnp.float32)]
        scratch = [pltpu.VMEM(left_shape, jnp.bfloat16)]
        out_specs = [block]
        if last:
            out_shape = [jax.ShapeDtypeStruct((share, per_block, 4 * per_block), jnp.float32)]
            out_specs = [pl.BlockSpec(memory_space=pl.ANY)]
            scratch = [
                pltpu.VMEM(total_shape[1:], jnp.float32),
                pltpu.VMEM(out_shape[0].shape, jnp.float32),
                pltpu.SemaphoreType.DMA((spins * columns // 2,)),
            ]
        if keep:
            out_shape.append(jax.ShapeDtypeStruct(left_shape, jnp.bfloat16))
            out_specs, scratch = [block] * 2, []
        out = pl.pallas_call(
            functools.partial(add_shards, tuple(names), places, totals is not None, last),
            in_specs=[pl.BlockSpec(memory_space=pltpu.SMEM)] + [block] * (len(operands) - 1),
            out_specs=out_specs,
            out_shape=out_shape,
            scratch_shapes=scratch,
            compiler_params=pltpu.CompilerParams(vmem_limit_bytes=40 * 1024 * 1024),
            cost_estimate=pl.CostEstimate(
                flops=4 * tall * wide * depth * len(names),
                bytes_accessed=wide * depth * 2 * len(names) + 8 * 4 * tall * wide,
                transcendentals=0,
            ),
        )(*operands)
        return out if keep else out[0]

    def fence(totals):
        nonlocal arrays
        arrays, totals = lax.optimization_barrier((arrays, totals))
        return totals

    put("9", packed, "near", [("O", 0)])

    put("1a", hop_z(packed, 2), "near", [("O", 2)])
    put("1b", hop_z(packed, 1), "near", [("O", 1)])
    put("1c", hop_b(packed), "near", [("B", 0)])
    put("1d", hop_a(packed), "near", [("A", 0)])
    put("1e", hop_b(near("A", 0)), "near", [("AB", 0)])
    place, weights = fence((place, weights))

    def route(kernel, operands, counts, weight=0):
        block = pl.BlockSpec(memory_space=pltpu.VMEM)
        first = pl.BlockSpec(memory_space=pltpu.SMEM) if operands[0] is place else block
        shapes = [(count,) * (count > 1) + packed.shape for count in counts]
        routed = pl.pallas_call(
            kernel,
            in_specs=[first] + [block] * (len(operands) - 1),
            out_specs=[block] * len(counts),
            out_shape=[jax.ShapeDtypeStruct(shape, packed.dtype) for shape in shapes],
            compiler_params=pltpu.CompilerParams(vmem_limit_bytes=24 * 1024 * 1024),
            cost_estimate=pl.CostEstimate(flops=weight, bytes_accessed=0, transcendentals=0),
        )(*operands)
        return fence(routed)

    first = [("O", 0), ("A", 0), ("B", 0), ("AB", 0), ("O", 1), ("O", 2)]
    second = [("AB", 1), ("O", 3), ("AB", 2), ("A", 1), ("A", 2), ("B", 1), ("B", 2)]
    third = [("A", 3), ("AB", 3), ("B", 3)]
    stack, both, mixed = route(route_second, [place] + [near(*kind) for kind in first], (6, 2, 1))
    totals = add([("near", *kind) for kind in first], None)
    o3, ab2, a12, b12 = hop_z(near("O", 2), 1), hop_mixed(mixed), hop_a(both), hop_b(both)
    put("2a", swap(stack), "far", first)
    totals = fence(totals)

    put("2b", hop_z(near("AB", 0), 1), "near", [("AB", 1)])
    totals = add([("far", *kind) for kind in first], totals)
    ab1 = arrays.pop("2b")
    put("2c", o3, "near", [("O", 3)])
    put("2d", ab2, "near", [("AB", 2)])
    totals = fence(totals)

    ab3, a3, o3 = hop_z(near("AB", 2), 1), hop_a(near("O", 3)), near("O", 3)
    arrays["2b"] = ab1
    put("2e", a12, "near", [("A", 1), ("A", 2)])
    put("2f", b12, "near", [("B", 1), ("B", 2)])
    totals = fence(totals)

    keys = ("2b", "2c", "2d", "2e", "2f")
    (stack,) = route(route_third, [arrays[key] for key in keys], (7,))
    b3, far2 = hop_b(near("O", 3)), swap(stack)
    totals = add([("near", *kind) for kind in second], totals)
    a3, ab3, totals = lax.optimization_barrier((a3, ab3, totals))
    (stack,) = route(route_last, [a3, ab3], (2,), weight=10**11)
    put("3a", stack, "near", third[:2])
    stack = swap(stack)
    put("3d", far2, "far", second)
    totals = add([("far", *kind) for kind in second], totals)
    put("3b", b3, "near", third[2:])
    totals = fence(totals)

    put("4a", stack, "far", third[:2])
    far3 = swap(near("B", 3))
    totals, left = add([("near", *kind) for kind in third], totals, keep=True)
    put("4b", far3, "far", third[2:])
    totals, left = fence((totals, left))
    return add([("far", *kind) for kind in third], totals, left=left)


def add_terms(place_ref, weights_ref, left_ref, right_ref, field_ref):
    @pl.when(pl.program_id(0) == 0)
    def _():
        field_ref[...] = jnp.zeros_like(field_ref)

    spins = left_ref.shape[2]
    groups, columns, per_block, depth = right_ref.shape[0], *right_ref.shape[2:]
    owns = [left_ref[0, 0, spin] for spin in range(spins)]
    left_cos, left_sin = left_sides(owns, weights_ref[0])
    for column in range(columns):
        right = right_ref[:, 0, column].reshape(groups * per_block, depth)
        term = product(left_cos, left_sin, right)
        for part in range(2):
            for spin in range(spins):
                start = (part * spins + spin) * per_block
                field_ref[(spin * columns + column) * 2 + part] += term[start : start + per_block]


def gather_whole(packed, place, weights, share):
    groups, _, deep, flat = (lax.axis_size(name) for name in AXES)
    sites = deep * flat
    _, per_block, depth = packed.shape
    columns = min(4, share // 2)
    spins = share // (2 * columns)
    near = lax.all_gather(packed, ("pair", "deep", "flat"))
    near = near.reshape(groups, sites, 4, per_block, depth)
    far = lax.ppermute(near, "core", [(0, 1), (1, 0)])
    wide = groups * per_block

    def half(right):
        return pl.pallas_call(
            add_terms,
            grid_spec=pltpu.PrefetchScalarGridSpec(
                num_scalar_prefetch=1,
                grid=(sites,),
                in_specs=[
                    pl.BlockSpec((1, 2, weights.shape[2]), lambda m, place: (m, 0, 0)),
                    pl.BlockSpec(
                        (1, 1, spins, per_block, depth),
                        lambda m, place: (place[0], m, place[4] // spins, 0, 0),
                    ),
                    pl.BlockSpec(
                        (groups, 1, columns, per_block, depth),
                        lambda m, place: (0, m, place[6] // columns, 0, 0),
                    ),
                ],
                out_specs=pl.BlockSpec((share, per_block, wide), lambda m, place: (0, 0, 0)),
            ),
            out_shape=jax.ShapeDtypeStruct((share, per_block, wide), jnp.float32),
            compiler_params=pltpu.CompilerParams(vmem_limit_bytes=40 * 1024 * 1024),
        )(place, weights, near, right)

    sides = [half(right).reshape(share, per_block, groups, per_block) for right in (near, far)]
    first = lax.axis_index("core") == 0
    even, odd = (jnp.where(first, a, b) for a, b in (sides, sides[::-1]))
    return jnp.stack([even, odd], 3).reshape(share, per_block, 2 * wide)


def shards(modes, momenta):
    groups, _, deep, flat = (lax.axis_size(name) for name in AXES)
    sites = deep * flat
    slots, steps, per_block, spin_colour, site_count = modes.shape
    share = steps * momenta.shape[0] * 32 // sites
    owned = (lax.axis_index("deep") * flat + lax.axis_index("flat")) * (share // 2)
    place = [lax.axis_index(name) for name in AXES]
    place = jnp.stack(place + [owned // 4 % 4, jnp.int32(flat), owned % 4]).astype(jnp.int32)

    packed = jnp.transpose(modes.reshape(slots, per_block, 4, 3, site_count), (2, 1, 0, 3, 4))
    packed = packed.reshape(4, per_block, slots * 3 * site_count)

    mine = lax.dynamic_slice_in_dim(momenta, owned // 16, 1, 0)
    weights = phase_table(mine, jnp.int32(0), sites * site_count, LEXT)[0]
    weights = jnp.transpose(weights.reshape(2, sites, site_count), (1, 0, 2))

    if (groups, deep, flat) == (2, 4, 2) and share in (8, 16, 32):
        return swap_in_windows(packed, place, weights, share)
    return gather_whole(packed, place, weights, share)


def solution(mesh):
    count, sites = mesh.shape["blk"], mesh.shape["site"]
    flat = 2 ** (int(math.log2(sites)) // 2)
    split = Mesh(mesh.devices.reshape(count // 2, 2, sites // flat, flat), AXES)
    placed = (P(None, None, ("pair", "core"), None, ("deep", "flat")), P())
    return jax.shard_map(
        shards,
        mesh=split,
        in_specs=placed,
        out_specs=P(("deep", "flat"), ("pair", "core"), None),
        check_vma=False,
    )
```

```python
import functools
import math

import jax
import jax.numpy as jnp
from jax import lax
from jax.experimental import pallas as pl
from jax.experimental.pallas import tpu as pltpu
from jax.sharding import Mesh, PartitionSpec as P

LEXT = 48

TWO_PI = 2.0 * math.pi

AXES = ("pair", "core", "deep", "flat")


def phase_table(momenta, first_site, site_count, extent):
    flat = first_site + jnp.arange(site_count, dtype=jnp.int32)
    coords = jnp.stack([flat % extent, flat // extent % extent, flat // (extent * extent)], 0)
    turns = jnp.mod(jnp.sum(momenta[:, :, None] * coords[None, :, :], axis=1), extent)
    angle = turns.astype(jnp.float32) * (TWO_PI / extent)
    return jnp.stack([jnp.cos(angle), jnp.sin(angle)], 1)


def left_sides(owns, weights):
    depth = owns[0].shape[1]
    half = depth // 2
    cosine = jnp.tile(weights[0:1], (1, depth // weights.shape[1]))
    sine = jnp.tile(weights[1:2], (1, depth // weights.shape[1]))
    cosine_rows = [[], []]
    sine_rows = [[], []]
    for own in owns:
        own = own.astype(jnp.float32)
        by_cos = (own * cosine).astype(jnp.bfloat16)
        by_sin = (own * sine).astype(jnp.bfloat16)
        cosine_rows[0].append(by_cos)
        cosine_rows[1].append(jnp.concatenate([-by_cos[:, half:], by_cos[:, :half]], 1))
        sine_rows[0].append(jnp.concatenate([-by_sin[:, half:], by_sin[:, :half]], 1))
        sine_rows[1].append(-by_sin)
    return (
        jnp.concatenate(cosine_rows[0] + cosine_rows[1], 0),
        jnp.concatenate(sine_rows[0] + sine_rows[1], 0),
    )


def product(left_cos, left_sin, right):
    dims = (((1,), (1,)), ((), ()))
    term = lax.dot_general(left_cos, right, dims, preferred_element_type=jnp.float32)
    return term + lax.dot_general(left_sin, right, dims, preferred_element_type=jnp.float32)


def add_shards(names, where, slots, has_totals, last, place_ref, weights_ref, *refs):
    refs = list(refs)
    if last:
        sems, row_ref, far_ref, out_ref, totals_in, left_ref = (refs.pop() for _ in range(6))
    else:
        left_ref, out_ref = refs.pop(), refs.pop()
        totals_in = refs.pop() if has_totals else None

    def shard(name):
        index, slot = where[name]
        return refs[index] if slot is None else refs[index].at[slot]

    pair, core, level, beside, first_s, flat = (place_ref[i] for i in range(6))
    columns, per_block, _ = shard(names[0]).shape
    spins = left_ref.shape[2] // (2 * per_block)

    if last:
        far_ref[...] = totals_in[1]
    else:
        if has_totals:
            out_ref[...] = totals_in[...]
        else:
            out_ref[...] = jnp.zeros_like(out_ref)
        for slot, (dy, dz) in enumerate(slots):
            site = jnp.bitwise_xor(level, dz) * flat + jnp.bitwise_xor(beside, dy)
            if dy == 0:
                owns = [shard(("near", "O", dz))[first_s + s] for s in range(spins)]
            else:
                owns = [
                    jnp.where(
                        core == 0,
                        shard(("near", "B", dz))[first_s + s],
                        shard(("near", "A", dz))[first_s + s],
                    )
                    for s in range(spins)
                ]
            left_ref[slot, 0], left_ref[slot, 1] = left_sides(owns, weights_ref[site])

    for side, kind, dz in names:
        right = shard((side, kind, dz))[...].reshape(columns * per_block, -1)
        turn = core if side == "near" else 1 - core
        dx, dy = {"O": (0, 0), "A": (1 - turn, turn), "B": (turn, 1 - turn), "AB": (1, 1)}[kind]
        if kind in ("O", "AB"):
            slot = slots.index((dy, dz))
        else:
            slot = slots.index((0, dz)) + dy
        term = product(left_ref[slot, 0], left_ref[slot, 1], right)
        if last:
            far_ref[dx] += term
        else:
            out_ref[0 if side == "near" else 1, dx] += term

    if last:
        lane = lax.broadcasted_iota(jnp.int32, (per_block, 2 * per_block), 1)
        copies = []
        for spin in range(spins):
            for column in range(0, columns, 2):
                first = (spin * columns + column) * 2
                across = pl.ds(column * per_block, 2 * per_block)
                for part in range(2):
                    top = (part * spins + spin) * per_block
                    for p in range(2):
                        dx = jnp.bitwise_xor(pair, p)
                        near = totals_in[0, dx, pl.ds(top, per_block), across]
                        far = far_ref[dx, pl.ds(top, per_block), across]
                        even = jnp.where(core == 0, near, far)
                        odd = jnp.where(core == 0, far, near)
                        place = pl.ds(p * 2 * per_block, 2 * per_block)
                        row_ref[first + part, :, place] = jnp.where(
                            lane < per_block, even, pltpu.roll(odd, per_block, 1)
                        )
                        row_ref[first + part + 2, :, place] = jnp.where(
                            lane < per_block, pltpu.roll(even, per_block, 1), odd
                        )
                rows = pl.ds(first, 4)
                copies.append(
                    pltpu.make_async_copy(row_ref.at[rows], out_ref.at[rows], sems.at[len(copies)])
                )
                copies[-1].start()
        for copy in copies:
            copy.wait()


def route_second(*refs):
    stack_ref, both_ref = refs[6:]
    for slot in range(6):
        stack_ref[slot] = refs[slot][...]
    both_ref[0] = refs[4][...]
    both_ref[1] = refs[5][...]


def route_third(o3_ref, a12_ref, b12_ref, stack_ref):
    stack_ref[0] = o3_ref[...]
    stack_ref[1:3] = a12_ref[...]
    stack_ref[3:5] = b12_ref[...]


def route_fourth(a3_ref, ab2_ref, o3_ref, stack_ref, both_ref):
    stack_ref[0] = a3_ref[...]
    stack_ref[1] = ab2_ref[...]
    both_ref[0] = a3_ref[...]
    both_ref[1] = o3_ref[...]


def left_slots(names):
    needed = set()
    for _, kind, dz in names:
        needed |= {"O": {(0, dz)}, "AB": {(1, dz)}}.get(kind, {(0, dz), (1, dz)})
    return sorted(needed, key=lambda slot: (slot[1], slot[0]))


def swap_in_windows(packed, place, weights, share):
    shape = tuple(lax.axis_size(name) for name in AXES)
    columns, per_block, depth = packed.shape
    spins = share // (2 * columns)
    tall, wide = 2 * spins * per_block, columns * per_block
    strides = (shape[1] * shape[2] * shape[3], shape[2] * shape[3], shape[3], 1)

    def move(array, target):
        pairs = []
        for p in range(shape[0]):
            for c in range(shape[1]):
                for z in range(shape[2]):
                    for y in range(shape[3]):
                        ends = (p, c, z, y), target(p, c, z, y)
                        pairs.append(
                            tuple(sum(a * b for a, b in zip(end, strides)) for end in ends)
                        )
        return lax.ppermute(array, AXES, pairs)

    def hop_a(array):
        return move(array, lambda p, c, z, y: (p ^ 1, c, z, y) if c == 0 else (p, c, z, y ^ 1))

    def hop_b(array):
        return move(array, lambda p, c, z, y: (p, c, z, y ^ 1) if c == 0 else (p ^ 1, c, z, y))

    def hop_z(array, by):
        return move(array, lambda p, c, z, y: (p, c, z ^ by, y))

    def swap(array):
        return move(array, lambda p, c, z, y: (p, c ^ 1, z, y))

    arrays = {}
    where = {}

    def put(key, array, side, kinds):
        arrays[key] = array
        for slot, (kind, dz) in enumerate(kinds):
            where[(side, kind, dz)] = (key, slot if len(kinds) > 1 else None)

    def near(kind, dz):
        key, slot = where[("near", kind, dz)]
        return arrays[key] if slot is None else arrays[key][slot]

    def add(names, totals, keep=False, left=None, slots=None):
        last = left is not None
        slots = slots or left_slots(names)
        uses = list(names)
        for dy, dz in [] if last else slots:
            uses += [("near", kind, dz) for kind in (("A", "B") if dy else ("O",))]
        keys = sorted({where[name][0] for name in uses})
        places = {name: (keys.index(where[name][0]), where[name][1]) for name in uses}
        operands = [place, weights] + [arrays[key] for key in keys]
        operands += [each for each in (left, totals) if each is not None]
        total_shape = (2, 2, tall, wide)
        left_shape = (len(slots), 2, tall, depth)
        block = pl.BlockSpec(memory_space=pltpu.VMEM)
        out_shape = [jax.ShapeDtypeStruct(total_shape, jnp.float32)]
        scratch = [pltpu.VMEM(left_shape, jnp.bfloat16)]
        out_specs = [block]
        if last:
            out_shape = [jax.ShapeDtypeStruct((share, per_block, 4 * per_block), jnp.float32)]
            out_specs = [pl.BlockSpec(memory_space=pl.ANY)]
            scratch = [
                pltpu.VMEM(total_shape[1:], jnp.float32),
                pltpu.VMEM(out_shape[0].shape, jnp.float32),
                pltpu.SemaphoreType.DMA((spins * columns // 2,)),
            ]
        if keep:
            out_shape.append(jax.ShapeDtypeStruct(left_shape, jnp.bfloat16))
            out_specs, scratch = [block] * 2, []
        out = pl.pallas_call(
            functools.partial(add_shards, tuple(names), places, slots, totals is not None, last),
            in_specs=[pl.BlockSpec(memory_space=pltpu.SMEM)] + [block] * (len(operands) - 1),
            out_specs=out_specs,
            out_shape=out_shape,
            scratch_shapes=scratch,
            compiler_params=pltpu.CompilerParams(vmem_limit_bytes=40 * 1024 * 1024),
            cost_estimate=pl.CostEstimate(
                flops=4 * tall * wide * depth * len(names),
                bytes_accessed=wide * depth * 2 * len(names) + 8 * 4 * tall * wide,
                transcendentals=0,
            ),
        )(*operands)
        return out if keep else out[0]

    def fence(totals):
        nonlocal arrays
        arrays, totals = lax.optimization_barrier((arrays, totals))
        return totals

    put("9", packed, "near", [("O", 0)])

    put("1a", hop_z(packed, 2), "near", [("O", 2)])
    put("1b", hop_z(packed, 1), "near", [("O", 1)])
    put("1c", hop_b(packed), "near", [("B", 0)])
    put("1d", hop_a(packed), "near", [("A", 0)])
    put("1e", hop_b(near("A", 0)), "near", [("AB", 0)])
    place, weights = fence((place, weights))

    def route(kernel, operands, counts, weight=0):
        block = pl.BlockSpec(memory_space=pltpu.VMEM)
        shapes = [(count,) * (count > 1) + packed.shape for count in counts]
        routed = pl.pallas_call(
            kernel,
            in_specs=[block] * len(operands),
            out_specs=[block] * len(counts),
            out_shape=[jax.ShapeDtypeStruct(shape, packed.dtype) for shape in shapes],
            compiler_params=pltpu.CompilerParams(vmem_limit_bytes=24 * 1024 * 1024),
            cost_estimate=pl.CostEstimate(flops=weight, bytes_accessed=0, transcendentals=0),
        )(*operands)
        return fence(routed)

    first = [("O", 0), ("A", 0), ("B", 0), ("AB", 0), ("O", 1), ("O", 2)]
    second = [("O", 3), ("A", 1), ("A", 2), ("B", 1), ("B", 2)]
    third = [("A", 3), ("AB", 2)]
    fourth = [("AB", 3), ("B", 3), ("AB", 1)]
    stack, both = route(route_second, [near(*kind) for kind in first], (6, 2))
    totals = add([("near", *kind) for kind in first], None)
    o3, a12, b12 = hop_z(near("O", 2), 1), hop_a(both), hop_b(both)
    put("2a", swap(stack), "far", first)
    totals = fence(totals)

    ab2 = hop_z(near("AB", 0), 2)
    totals = add([("far", *kind) for kind in first], totals)
    put("2b", o3, "near", second[:1])
    totals = fence(totals)

    a3 = hop_a(near("O", 3))
    put("2c", a12, "near", second[1:3])
    put("2d", b12, "near", second[3:5])
    totals = fence(totals)

    (stack,) = route(route_third, [arrays[key] for key in ("2b", "2c", "2d")], (5,))
    far2 = swap(stack)
    put("3b", ab2, "near", third[1:])
    totals = add([("near", *kind) for kind in second + third[1:]], totals)
    a3, totals = lax.optimization_barrier((a3, totals))
    stack, both = route(route_fourth, [a3, ab2, near("O", 3)], (2, 2), weight=10**11)
    put("3a", a3, "near", third[:1])
    totals = fence(totals)

    b3, ab1, far3 = hop_b(both), hop_z(near("AB", 0), 1), swap(stack)
    put("3d", far2, "far", second)
    totals = add([("far", *kind) for kind in second], totals)
    put("3e", far3, "far", third)
    put("4a", b3, "near", fourth[:2])
    put("4b", ab1, "near", fourth[2:])
    totals = fence(totals)

    new = [swap(arrays["4a"]), swap(arrays["4b"])]
    names = [("near", *kind) for kind in fourth + third[:1]] + [("far", *kind) for kind in third]
    totals, left = add(names, totals, keep=True)
    put("5a", new[0], "far", fourth[:2])
    put("5b", new[1], "far", fourth[2:])
    totals, left = fence((totals, left))
    return add([("far", *kind) for kind in fourth], totals, left=left, slots=left_slots(names))


def add_terms(place_ref, weights_ref, left_ref, right_ref, field_ref):
    @pl.when(pl.program_id(0) == 0)
    def _():
        field_ref[...] = jnp.zeros_like(field_ref)

    spins = left_ref.shape[2]
    groups, columns, per_block, depth = right_ref.shape[0], *right_ref.shape[2:]
    owns = [left_ref[0, 0, spin] for spin in range(spins)]
    left_cos, left_sin = left_sides(owns, weights_ref[0])
    for column in range(columns):
        right = right_ref[:, 0, column].reshape(groups * per_block, depth)
        term = product(left_cos, left_sin, right)
        for part in range(2):
            for spin in range(spins):
                start = (part * spins + spin) * per_block
                field_ref[(spin * columns + column) * 2 + part] += term[start : start + per_block]


def gather_whole(packed, place, weights, share):
    groups, _, deep, flat = (lax.axis_size(name) for name in AXES)
    sites = deep * flat
    _, per_block, depth = packed.shape
    columns = min(4, share // 2)
    spins = share // (2 * columns)
    near = lax.all_gather(packed, ("pair", "deep", "flat"))
    near = near.reshape(groups, sites, 4, per_block, depth)
    far = lax.ppermute(near, "core", [(0, 1), (1, 0)])
    wide = groups * per_block

    def half(right):
        return pl.pallas_call(
            add_terms,
            grid_spec=pltpu.PrefetchScalarGridSpec(
                num_scalar_prefetch=1,
                grid=(sites,),
                in_specs=[
                    pl.BlockSpec((1, 2, weights.shape[2]), lambda m, place: (m, 0, 0)),
                    pl.BlockSpec(
                        (1, 1, spins, per_block, depth),
                        lambda m, place: (place[0], m, place[4] // spins, 0, 0),
                    ),
                    pl.BlockSpec(
                        (groups, 1, columns, per_block, depth),
                        lambda m, place: (0, m, place[6] // columns, 0, 0),
                    ),
                ],
                out_specs=pl.BlockSpec((share, per_block, wide), lambda m, place: (0, 0, 0)),
            ),
            out_shape=jax.ShapeDtypeStruct((share, per_block, wide), jnp.float32),
            compiler_params=pltpu.CompilerParams(vmem_limit_bytes=40 * 1024 * 1024),
        )(place, weights, near, right)

    sides = [half(right).reshape(share, per_block, groups, per_block) for right in (near, far)]
    first = lax.axis_index("core") == 0
    even, odd = (jnp.where(first, a, b) for a, b in (sides, sides[::-1]))
    return jnp.stack([even, odd], 3).reshape(share, per_block, 2 * wide)


def shards(modes, momenta):
    groups, _, deep, flat = (lax.axis_size(name) for name in AXES)
    sites = deep * flat
    slots, steps, per_block, spin_colour, site_count = modes.shape
    share = steps * momenta.shape[0] * 32 // sites
    owned = (lax.axis_index("deep") * flat + lax.axis_index("flat")) * (share // 2)
    place = [lax.axis_index(name) for name in AXES]
    place = jnp.stack(place + [owned // 4 % 4, jnp.int32(flat), owned % 4]).astype(jnp.int32)

    packed = jnp.transpose(modes.reshape(slots, per_block, 4, 3, site_count), (2, 1, 0, 3, 4))
    packed = packed.reshape(4, per_block, slots * 3 * site_count)

    mine = lax.dynamic_slice_in_dim(momenta, owned // 16, 1, 0)
    weights = phase_table(mine, jnp.int32(0), sites * site_count, LEXT)[0]
    weights = jnp.transpose(weights.reshape(2, sites, site_count), (1, 0, 2))

    if (groups, deep, flat) == (2, 4, 2) and share in (8, 16, 32):
        return swap_in_windows(packed, place, weights, share)
    return gather_whole(packed, place, weights, share)


def solution(mesh):
    count, sites = mesh.shape["blk"], mesh.shape["site"]
    flat = 2 ** (int(math.log2(sites)) // 2)
    split = Mesh(mesh.devices.reshape(count // 2, 2, sites // flat, flat), AXES)
    placed = (P(None, None, ("pair", "core"), None, ("deep", "flat")), P())
    return jax.shard_map(
        shards,
        mesh=split,
        in_specs=placed,
        out_specs=P(("deep", "flat"), ("pair", "core"), None),
        check_vma=False,
    )
```

```python
import functools
import math

import jax
import jax.numpy as jnp
from jax import lax
from jax.experimental import pallas as pl
from jax.experimental.pallas import tpu as pltpu
from jax.sharding import Mesh, PartitionSpec as P

LEXT = 48

TWO_PI = 2.0 * math.pi

AXES = ("pair", "core", "deep", "flat")


def phase_table(momenta, first_site, site_count, extent):
    flat = first_site + jnp.arange(site_count, dtype=jnp.int32)
    coords = jnp.stack([flat % extent, flat // extent % extent, flat // (extent * extent)], 0)
    turns = jnp.mod(jnp.sum(momenta[:, :, None] * coords[None, :, :], axis=1), extent)
    angle = turns.astype(jnp.float32) * (TWO_PI / extent)
    return jnp.stack([jnp.cos(angle), jnp.sin(angle)], 1)


def left_sides(owns, weights):
    depth = owns[0].shape[1]
    half = depth // 2
    cosine = jnp.tile(weights[0:1], (1, depth // weights.shape[1]))
    sine = jnp.tile(weights[1:2], (1, depth // weights.shape[1]))
    cosine_rows = [[], []]
    sine_rows = [[], []]
    for own in owns:
        own = own.astype(jnp.float32)
        by_cos = (own * cosine).astype(jnp.bfloat16)
        by_sin = (own * sine).astype(jnp.bfloat16)
        cosine_rows[0].append(by_cos)
        cosine_rows[1].append(jnp.concatenate([-by_cos[:, half:], by_cos[:, :half]], 1))
        sine_rows[0].append(jnp.concatenate([-by_sin[:, half:], by_sin[:, :half]], 1))
        sine_rows[1].append(-by_sin)
    return (
        jnp.concatenate(cosine_rows[0] + cosine_rows[1], 0),
        jnp.concatenate(sine_rows[0] + sine_rows[1], 0),
    )


def product(left_cos, left_sin, right):
    dims = (((1,), (1,)), ((), ()))
    term = lax.dot_general(left_cos, right, dims, preferred_element_type=jnp.float32)
    return term + lax.dot_general(left_sin, right, dims, preferred_element_type=jnp.float32)


def add_shards(names, where, has_totals, half, last, place_ref, weights_ref, *refs):
    refs = list(refs)
    if half or last:
        sems, row_ref = refs.pop(), refs.pop()
    if last:
        far_ref, field_ref, _, totals_in, left_ref = (refs.pop() for _ in range(5))
    elif half:
        field_ref, left_ref, out_ref, totals_in = (refs.pop() for _ in range(4))
    else:
        left_ref, out_ref = refs.pop(), refs.pop()
        totals_in = refs.pop() if has_totals else None

    def shard(name):
        index, slot = where[name]
        return refs[index] if slot is None else refs[index].at[slot]

    pair, core, level, beside, first_s, flat = (place_ref[i] for i in range(6))
    columns, per_block, _ = shard(names[0]).shape
    spins = left_ref.shape[2] // (2 * per_block)

    def send_columns(dx, near, far):
        lane = lax.broadcasted_iota(jnp.int32, (per_block, 2 * per_block), 1)
        start = pl.multiple_of(jnp.bitwise_xor(pair, dx) * (2 * per_block), 2 * per_block)
        copies = []
        for spin in range(spins):
            for column in range(0, columns, 2):
                first = (spin * columns + column) * 2
                across = slice(column * per_block, (column + 2) * per_block)
                for part in range(2):
                    top = (part * spins + spin) * per_block
                    one = near(slice(top, top + per_block), across)
                    two = far(slice(top, top + per_block), across)
                    even = jnp.where(core == 0, one, two)
                    odd = jnp.where(core == 0, two, one)
                    row_ref[first + part] = jnp.where(
                        lane < per_block, even, pltpu.roll(odd, per_block, 1)
                    )
                    row_ref[first + part + 2] = jnp.where(
                        lane < per_block, pltpu.roll(even, per_block, 1), odd
                    )
                rows = pl.ds(first, 4)
                target = field_ref.at[rows, :, pl.ds(start, 2 * per_block)]
                copies.append(
                    pltpu.make_async_copy(row_ref.at[rows], target, sems.at[len(copies)])
                )
                copies[-1].start()
        return copies

    slots = left_slots(names)
    if last:
        far_ref[...] = totals_in[1, 1] + product(
            left_ref[0, 0], left_ref[0, 1], shard(names[0])[...].reshape(columns * per_block, -1)
        )
        copies = send_columns(
            1, lambda rows, across: totals_in[0, 1, rows, across],
            lambda rows, across: far_ref[rows, across],
        )
        for copy in copies:
            copy.wait()
        return

    copies = []
    if half:
        copies = send_columns(
            0, lambda rows, across: totals_in[0, 0, rows, across],
            lambda rows, across: totals_in[1, 0, rows, across],
        )
    if has_totals:
        out_ref[...] = totals_in[...]
    else:
        out_ref[...] = jnp.zeros_like(out_ref)
    for slot, (dy, dz) in enumerate(slots):
        site = jnp.bitwise_xor(level, dz) * flat + jnp.bitwise_xor(beside, dy)
        if dy == 0:
            owns = [shard(("near", "O", dz))[first_s + s] for s in range(spins)]
        else:
            owns = [
                jnp.where(
                    core == 0,
                    shard(("near", "B", dz))[first_s + s],
                    shard(("near", "A", dz))[first_s + s],
                )
                for s in range(spins)
            ]
        left_ref[slot, 0], left_ref[slot, 1] = left_sides(owns, weights_ref[site])

    for side, kind, dz in names:
        right = shard((side, kind, dz))[...].reshape(columns * per_block, -1)
        turn = core if side == "near" else 1 - core
        dx, dy = {"O": (0, 0), "A": (1 - turn, turn), "B": (turn, 1 - turn), "AB": (1, 1)}[kind]
        if kind in ("O", "AB"):
            slot = slots.index((dy, dz))
        else:
            slot = slots.index((0, dz)) + dy
        out_ref[0 if side == "near" else 1, dx] += product(
            left_ref[slot, 0], left_ref[slot, 1], right
        )
    for copy in copies:
        copy.wait()


def route_second(*refs):
    stack_ref, both_ref = refs[6:]
    for slot in range(6):
        stack_ref[slot] = refs[slot][...]
    both_ref[0] = refs[4][...]
    both_ref[1] = refs[5][...]


def route_third(o3_ref, a12_ref, b12_ref, stack_ref):
    stack_ref[0] = o3_ref[...]
    stack_ref[1:3] = a12_ref[...]
    stack_ref[3:5] = b12_ref[...]


def route_fourth(*refs):
    for slot in range(4):
        refs[4][slot] = refs[slot][...]


def left_slots(names):
    needed = set()
    for _, kind, dz in names:
        needed |= {"O": {(0, dz)}, "AB": {(1, dz)}}.get(kind, {(0, dz), (1, dz)})
    return sorted(needed, key=lambda slot: (slot[1], slot[0]))


def swap_in_windows(packed, place, weights, share):
    shape = tuple(lax.axis_size(name) for name in AXES)
    columns, per_block, depth = packed.shape
    spins = share // (2 * columns)
    tall, wide = 2 * spins * per_block, columns * per_block
    strides = (shape[1] * shape[2] * shape[3], shape[2] * shape[3], shape[3], 1)

    def move(array, target):
        pairs = []
        for p in range(shape[0]):
            for c in range(shape[1]):
                for z in range(shape[2]):
                    for y in range(shape[3]):
                        ends = (p, c, z, y), target(p, c, z, y)
                        pairs.append(
                            tuple(sum(a * b for a, b in zip(end, strides)) for end in ends)
                        )
        return lax.ppermute(array, AXES, pairs)

    def hop_a(array):
        return move(array, lambda p, c, z, y: (p ^ 1, c, z, y) if c == 0 else (p, c, z, y ^ 1))

    def hop_b(array):
        return move(array, lambda p, c, z, y: (p, c, z, y ^ 1) if c == 0 else (p ^ 1, c, z, y))

    def hop_z(array, by):
        return move(array, lambda p, c, z, y: (p, c, z ^ by, y))

    def swap(array):
        return move(array, lambda p, c, z, y: (p, c ^ 1, z, y))

    arrays = {}
    where = {}

    def put(key, array, side, kinds):
        arrays[key] = array
        for slot, (kind, dz) in enumerate(kinds):
            where[(side, kind, dz)] = (key, slot if len(kinds) > 1 else None)

    def near(kind, dz):
        key, slot = where[("near", kind, dz)]
        return arrays[key] if slot is None else arrays[key][slot]

    def add(names, totals, half=False, left=None, field=None):
        last = left is not None
        slots = left_slots(names)
        uses = list(names)
        for dy, dz in [] if last else slots:
            uses += [("near", kind, dz) for kind in (("A", "B") if dy else ("O",))]
        keys = sorted({where[name][0] for name in uses})
        places = {name: (keys.index(where[name][0]), where[name][1]) for name in uses}
        operands = [place, weights] + [arrays[key] for key in keys]
        operands += [each for each in (left, totals, field) if each is not None]
        total_shape = (2, 2, tall, wide)
        left_shape = (len(slots), 2, tall, depth)
        field_shape = (share, per_block, 4 * per_block)
        block, apart = (pl.BlockSpec(memory_space=space) for space in (pltpu.VMEM, pltpu.HBM))
        in_specs = [pl.BlockSpec(memory_space=pltpu.SMEM)] + [block] * (len(operands) - 1)
        out_shape, out_specs = [jax.ShapeDtypeStruct(total_shape, jnp.float32)], [block]
        scratch, aliases = [pltpu.VMEM(left_shape, jnp.bfloat16)], {}
        if half:
            out_shape.append(jax.ShapeDtypeStruct(left_shape, jnp.bfloat16))
            out_specs.append(block)
            scratch = []
        if last:
            out_shape, out_specs, scratch = [], [], [pltpu.VMEM(total_shape[2:], jnp.float32)]
            in_specs[-1] = apart
            aliases = {len(operands) - 1: 0}
        if half or last:
            out_shape.append(jax.ShapeDtypeStruct(field_shape, jnp.float32))
            out_specs.append(apart)
            scratch.append(pltpu.VMEM((*field_shape[:2], 2 * per_block), jnp.float32))
            scratch.append(pltpu.SemaphoreType.DMA((spins * columns // 2,)))
        out = pl.pallas_call(
            functools.partial(add_shards, tuple(names), places, totals is not None, half, last),
            in_specs=in_specs,
            out_specs=out_specs,
            out_shape=out_shape,
            scratch_shapes=scratch,
            input_output_aliases=aliases,
            compiler_params=pltpu.CompilerParams(vmem_limit_bytes=40 * 1024 * 1024),
            cost_estimate=pl.CostEstimate(
                flops=4 * tall * wide * depth * len(names),
                bytes_accessed=wide * depth * 2 * len(names) + 8 * 4 * tall * wide,
                transcendentals=0,
            ),
        )(*operands)
        return out if half else out[0]

    def fence(totals):
        nonlocal arrays
        arrays, totals = lax.optimization_barrier((arrays, totals))
        return totals

    put("9", packed, "near", [("O", 0)])

    put("1a", hop_z(packed, 2), "near", [("O", 2)])
    put("1b", hop_z(packed, 1), "near", [("O", 1)])
    put("1c", hop_b(packed), "near", [("B", 0)])
    put("1d", hop_a(packed), "near", [("A", 0)])
    put("1e", hop_b(near("A", 0)), "near", [("AB", 0)])
    place, weights = fence((place, weights))

    def route(kernel, operands, counts, weight=0):
        block = pl.BlockSpec(memory_space=pltpu.VMEM)
        shapes = [(count,) * (count > 1) + packed.shape for count in counts]
        routed = pl.pallas_call(
            kernel,
            in_specs=[block] * len(operands),
            out_specs=[block] * len(counts),
            out_shape=[jax.ShapeDtypeStruct(shape, packed.dtype) for shape in shapes],
            compiler_params=pltpu.CompilerParams(vmem_limit_bytes=24 * 1024 * 1024),
            cost_estimate=pl.CostEstimate(flops=weight, bytes_accessed=0, transcendentals=0),
        )(*operands)
        return fence(routed)

    first = [("O", 0), ("A", 0), ("B", 0), ("AB", 0), ("O", 1), ("O", 2)]
    second = [("O", 3), ("A", 1), ("A", 2), ("B", 1), ("B", 2)]
    third = [("A", 3), ("B", 3), ("AB", 1), ("AB", 2)]
    fourth = [("AB", 3)]
    stack, both = route(route_second, [near(*kind) for kind in first], (6, 2))
    totals = add([("near", *kind) for kind in first], None)
    o3, a12, b12 = hop_z(near("O", 2), 1), hop_a(both), hop_b(both)
    put("2a", swap(stack), "far", first)
    totals = fence(totals)

    ab2 = hop_z(near("AB", 0), 2)
    totals = add([("far", *kind) for kind in first], totals)
    put("2b", o3, "near", second[:1])
    put("2c", a12, "near", second[1:3])
    put("2d", b12, "near", second[3:5])
    totals = fence(totals)

    (stack,) = route(route_third, [arrays[key] for key in ("2b", "2c", "2d")], (5,))
    a3, b3, ab1 = hop_a(near("O", 3)), hop_b(near("O", 3)), hop_z(near("AB", 0), 1)
    far2 = swap(stack)
    put("3d", ab2, "near", third[3:])
    totals = add([("near", *kind) for kind in second + third[3:]], totals)
    a3, b3, ab1, totals = lax.optimization_barrier((a3, b3, ab1, totals))
    (stack,) = route(route_fourth, [a3, b3, ab1, ab2], (4,), weight=10**11)
    put("3a", a3, "near", third[:1])
    put("3b", b3, "near", third[1:2])
    put("3c", ab1, "near", third[2:3])
    totals = fence(totals)

    ab3, far3 = hop_b(near("A", 3)), swap(stack)
    put("3e", far2, "far", second)
    names = [("near", *kind) for kind in third[:3]] + [("far", *kind) for kind in second]
    totals = add(names, totals)
    put("3f", far3, "far", third)
    totals = add([("far", *kind) for kind in third], totals)
    put("4a", ab3, "near", fourth)
    totals = fence(totals)

    far4 = swap(arrays["4a"])
    totals, left, field = add([("near", *kind) for kind in fourth], totals, half=True)
    put("4b", far4, "far", fourth)
    totals, left, field = fence((totals, left, field))
    return add([("far", *kind) for kind in fourth], totals, left=left, field=field)


def add_terms(place_ref, weights_ref, left_ref, right_ref, field_ref):
    @pl.when(pl.program_id(0) == 0)
    def _():
        field_ref[...] = jnp.zeros_like(field_ref)

    spins = left_ref.shape[2]
    groups, columns, per_block, depth = right_ref.shape[0], *right_ref.shape[2:]
    owns = [left_ref[0, 0, spin] for spin in range(spins)]
    left_cos, left_sin = left_sides(owns, weights_ref[0])
    for column in range(columns):
        right = right_ref[:, 0, column].reshape(groups * per_block, depth)
        term = product(left_cos, left_sin, right)
        for part in range(2):
            for spin in range(spins):
                start = (part * spins + spin) * per_block
                field_ref[(spin * columns + column) * 2 + part] += term[start : start + per_block]


def gather_whole(packed, place, weights, share):
    groups, _, deep, flat = (lax.axis_size(name) for name in AXES)
    sites = deep * flat
    _, per_block, depth = packed.shape
    columns = min(4, share // 2)
    spins = share // (2 * columns)
    near = lax.all_gather(packed, ("pair", "deep", "flat"))
    near = near.reshape(groups, sites, 4, per_block, depth)
    far = lax.ppermute(near, "core", [(0, 1), (1, 0)])
    wide = groups * per_block

    def half(right):
        return pl.pallas_call(
            add_terms,
            grid_spec=pltpu.PrefetchScalarGridSpec(
                num_scalar_prefetch=1,
                grid=(sites,),
                in_specs=[
                    pl.BlockSpec((1, 2, weights.shape[2]), lambda m, place: (m, 0, 0)),
                    pl.BlockSpec(
                        (1, 1, spins, per_block, depth),
                        lambda m, place: (place[0], m, place[4] // spins, 0, 0),
                    ),
                    pl.BlockSpec(
                        (groups, 1, columns, per_block, depth),
                        lambda m, place: (0, m, place[6] // columns, 0, 0),
                    ),
                ],
                out_specs=pl.BlockSpec((share, per_block, wide), lambda m, place: (0, 0, 0)),
            ),
            out_shape=jax.ShapeDtypeStruct((share, per_block, wide), jnp.float32),
            compiler_params=pltpu.CompilerParams(vmem_limit_bytes=40 * 1024 * 1024),
        )(place, weights, near, right)

    sides = [half(right).reshape(share, per_block, groups, per_block) for right in (near, far)]
    first = lax.axis_index("core") == 0
    even, odd = (jnp.where(first, a, b) for a, b in (sides, sides[::-1]))
    return jnp.stack([even, odd], 3).reshape(share, per_block, 2 * wide)


def shards(modes, momenta):
    groups, _, deep, flat = (lax.axis_size(name) for name in AXES)
    sites = deep * flat
    slots, steps, per_block, spin_colour, site_count = modes.shape
    share = steps * momenta.shape[0] * 32 // sites
    owned = (lax.axis_index("deep") * flat + lax.axis_index("flat")) * (share // 2)
    place = [lax.axis_index(name) for name in AXES]
    place = jnp.stack(place + [owned // 4 % 4, jnp.int32(flat), owned % 4]).astype(jnp.int32)

    packed = jnp.transpose(modes.reshape(slots, per_block, 4, 3, site_count), (2, 1, 0, 3, 4))
    packed = packed.reshape(4, per_block, slots * 3 * site_count)

    mine = lax.dynamic_slice_in_dim(momenta, owned // 16, 1, 0)
    weights = phase_table(mine, jnp.int32(0), sites * site_count, LEXT)[0]
    weights = jnp.transpose(weights.reshape(2, sites, site_count), (1, 0, 2))

    if (groups, deep, flat) == (2, 4, 2) and share in (8, 16, 32):
        return swap_in_windows(packed, place, weights, share)
    return gather_whole(packed, place, weights, share)


def solution(mesh):
    count, sites = mesh.shape["blk"], mesh.shape["site"]
    flat = 2 ** (int(math.log2(sites)) // 2)
    split = Mesh(mesh.devices.reshape(count // 2, 2, sites // flat, flat), AXES)
    placed = (P(None, None, ("pair", "core"), None, ("deep", "flat")), P())
    return jax.shard_map(
        shards,
        mesh=split,
        in_specs=placed,
        out_specs=P(("deep", "flat"), ("pair", "core"), None),
        check_vma=False,
    )
```

```python
import functools
import math

import jax
import jax.numpy as jnp
from jax import lax
from jax.experimental import pallas as pl
from jax.experimental.pallas import tpu as pltpu
from jax.sharding import Mesh, PartitionSpec as P

LEXT = 48

TWO_PI = 2.0 * math.pi

AXES = ("pair", "core", "deep", "flat")


def phase_table(momenta, first_site, site_count, extent):
    flat = first_site + jnp.arange(site_count, dtype=jnp.int32)
    coords = jnp.stack([flat % extent, flat // extent % extent, flat // (extent * extent)], 0)
    turns = jnp.mod(jnp.sum(momenta[:, :, None] * coords[None, :, :], axis=1), extent)
    angle = turns.astype(jnp.float32) * (TWO_PI / extent)
    return jnp.stack([jnp.cos(angle), jnp.sin(angle)], 1)


def left_sides(owns, weights):
    depth = owns[0].shape[1]
    half = depth // 2
    cosine = jnp.tile(weights[0:1], (1, depth // weights.shape[1]))
    sine = jnp.tile(weights[1:2], (1, depth // weights.shape[1]))
    cosine_rows = [[], []]
    sine_rows = [[], []]
    for own in owns:
        own = own.astype(jnp.float32)
        by_cos = (own * cosine).astype(jnp.bfloat16)
        by_sin = (own * sine).astype(jnp.bfloat16)
        cosine_rows[0].append(by_cos)
        cosine_rows[1].append(jnp.concatenate([-by_cos[:, half:], by_cos[:, :half]], 1))
        sine_rows[0].append(jnp.concatenate([-by_sin[:, half:], by_sin[:, :half]], 1))
        sine_rows[1].append(-by_sin)
    return jnp.concatenate(cosine_rows[0] + cosine_rows[1] + sine_rows[0] + sine_rows[1], 0)


def product(left, right):
    dims = (((1,), (1,)), ((), ()))
    terms = lax.dot_general(left, right, dims, preferred_element_type=jnp.float32)
    half = terms.shape[0] // 2
    return terms[:half] + terms[half:]


def add_shards(names, where, has_totals, last, place_ref, weights_ref, *refs):
    refs = list(refs)
    if last:
        sems, row_ref, far_ref, out_ref, totals_in, left_ref = (refs.pop() for _ in range(6))
    else:
        left_ref, out_ref = refs.pop(), refs.pop()
        totals_in = refs.pop() if has_totals else None

    def shard(name):
        index, slot = where[name]
        return refs[index] if slot is None else refs[index].at[slot]

    pair, core, level, beside, first_s, flat = (place_ref[i] for i in range(6))
    columns, per_block, _ = shard(names[0]).shape
    spins = left_ref.shape[1] // (4 * per_block)

    slots = left_slots(names)
    if last:
        far_ref[...] = totals_in[1]
    else:
        if has_totals:
            out_ref[...] = totals_in[...]
        else:
            out_ref[...] = jnp.zeros_like(out_ref)
        for slot, (dy, dz) in enumerate(slots):
            site = jnp.bitwise_xor(level, dz) * flat + jnp.bitwise_xor(beside, dy)
            if dy == 0:
                owns = [shard(("near", "O", dz))[first_s + s] for s in range(spins)]
            else:
                owns = [
                    jnp.where(
                        core == 0,
                        shard(("near", "B", dz))[first_s + s],
                        shard(("near", "A", dz))[first_s + s],
                    )
                    for s in range(spins)
                ]
            left_ref[slot] = left_sides(owns, weights_ref[site])

    for side, kind, dz in names:
        right = shard((side, kind, dz))[...].reshape(columns * per_block, -1)
        turn = core if side == "near" else 1 - core
        dx, dy = {"O": (0, 0), "A": (1 - turn, turn), "B": (turn, 1 - turn), "AB": (1, 1)}[kind]
        if kind in ("O", "AB"):
            slot = slots.index((dy, dz))
        else:
            slot = slots.index((0, dz)) + dy
        term = product(left_ref[slot], right)
        if last:
            far_ref[dx] += term
        else:
            out_ref[0 if side == "near" else 1, dx] += term

    if last:
        lane = lax.broadcasted_iota(jnp.int32, (per_block, 2 * per_block), 1)
        copies = []
        for spin in range(spins):
            for column in range(0, columns, 2):
                first = (spin * columns + column) * 2
                across = pl.ds(column * per_block, 2 * per_block)
                for part in range(2):
                    top = (part * spins + spin) * per_block
                    for p in range(2):
                        dx = jnp.bitwise_xor(pair, p)
                        near = totals_in[0, dx, pl.ds(top, per_block), across]
                        far = far_ref[dx, pl.ds(top, per_block), across]
                        even = jnp.where(core == 0, near, far)
                        odd = jnp.where(core == 0, far, near)
                        place = pl.ds(p * 2 * per_block, 2 * per_block)
                        row_ref[first + part, :, place] = jnp.where(
                            lane < per_block, even, pltpu.roll(odd, per_block, 1)
                        )
                        row_ref[first + part + 2, :, place] = jnp.where(
                            lane < per_block, pltpu.roll(even, per_block, 1), odd
                        )
                rows = pl.ds(first, 4)
                copies.append(
                    pltpu.make_async_copy(row_ref.at[rows], out_ref.at[rows], sems.at[len(copies)])
                )
                copies[-1].start()
        for copy in copies:
            copy.wait()


def route_second(place_ref, *refs):
    ab0_ref, o1_ref, o2_ref, stack_ref, both_ref, mixed_ref = refs[3:]
    for slot in range(6):
        stack_ref[slot] = refs[slot][...]
    both_ref[0] = o1_ref[...]
    both_ref[1] = o2_ref[...]

    @pl.when(place_ref[1] == 0)
    def _():
        mixed_ref[...] = o2_ref[...]

    @pl.when(place_ref[1] != 0)
    def _():
        mixed_ref[...] = ab0_ref[...]


def route_third(ab1_ref, o3_ref, ab2_ref, a12_ref, b12_ref, stack_ref):
    for slot, ref in enumerate((ab1_ref, ab2_ref, o3_ref)):
        stack_ref[slot] = ref[...]
    stack_ref[3:5] = a12_ref[...]
    stack_ref[5:7] = b12_ref[...]


def route_last(a3_ref, ab3_ref, stack_ref):
    stack_ref[0] = a3_ref[...]
    stack_ref[1] = ab3_ref[...]


def left_slots(names):
    needed = set()
    for _, kind, dz in names:
        needed |= {"O": {(0, dz)}, "AB": {(1, dz)}}.get(kind, {(0, dz), (1, dz)})
    return sorted(needed, key=lambda slot: (slot[1], slot[0]))


def swap_in_windows(packed, place, weights, share):
    shape = tuple(lax.axis_size(name) for name in AXES)
    columns, per_block, depth = packed.shape
    spins = share // (2 * columns)
    tall, wide = 2 * spins * per_block, columns * per_block
    strides = (shape[1] * shape[2] * shape[3], shape[2] * shape[3], shape[3], 1)

    def move(array, target):
        pairs = []
        for p in range(shape[0]):
            for c in range(shape[1]):
                for z in range(shape[2]):
                    for y in range(shape[3]):
                        ends = (p, c, z, y), target(p, c, z, y)
                        pairs.append(
                            tuple(sum(a * b for a, b in zip(end, strides)) for end in ends)
                        )
        return lax.ppermute(array, AXES, pairs)

    def hop_a(array):
        return move(array, lambda p, c, z, y: (p ^ 1, c, z, y) if c == 0 else (p, c, z, y ^ 1))

    def hop_b(array):
        return move(array, lambda p, c, z, y: (p, c, z, y ^ 1) if c == 0 else (p ^ 1, c, z, y))

    def hop_ab(array):
        return move(array, lambda p, c, z, y: (p ^ 1, c, z, y ^ 1))

    def hop_z(array, by):
        return move(array, lambda p, c, z, y: (p, c, z ^ by, y))

    def hop_mixed(array):
        return move(
            array, lambda p, c, z, y: (p ^ 1, c, z, y ^ 1) if c == 0 else (p, c, z ^ 2, y)
        )

    def swap(array):
        return move(array, lambda p, c, z, y: (p, c ^ 1, z, y))

    arrays = {}
    where = {}

    def put(key, array, side, kinds):
        arrays[key] = array
        for slot, (kind, dz) in enumerate(kinds):
            where[(side, kind, dz)] = (key, slot if len(kinds) > 1 else None)

    def near(kind, dz):
        key, slot = where[("near", kind, dz)]
        return arrays[key] if slot is None else arrays[key][slot]

    def add(names, totals, keep=False, left=None, weight=1):
        last = left is not None
        slots = left_slots(names)
        uses = list(names)
        for dy, dz in [] if last else slots:
            uses += [("near", kind, dz) for kind in (("A", "B") if dy else ("O",))]
        keys = sorted({where[name][0] for name in uses})
        places = {name: (keys.index(where[name][0]), where[name][1]) for name in uses}
        operands = [place, weights] + [arrays[key] for key in keys]
        operands += [each for each in (left, totals) if each is not None]
        total_shape = (2, 2, tall, wide)
        left_shape = (len(slots), 2 * tall, depth)
        block = pl.BlockSpec(memory_space=pltpu.VMEM)
        out_shape = [jax.ShapeDtypeStruct(total_shape, jnp.float32)]
        scratch = [pltpu.VMEM(left_shape, jnp.bfloat16)]
        out_specs = [block]
        if last:
            out_shape = [jax.ShapeDtypeStruct((share, per_block, 4 * per_block), jnp.float32)]
            out_specs = [pl.BlockSpec(memory_space=pl.ANY)]
            scratch = [
                pltpu.VMEM(total_shape[1:], jnp.float32),
                pltpu.VMEM(out_shape[0].shape, jnp.float32),
                pltpu.SemaphoreType.DMA((spins * columns // 2,)),
            ]
        if keep:
            out_shape.append(jax.ShapeDtypeStruct(left_shape, jnp.bfloat16))
            out_specs, scratch = [block] * 2, []
        out = pl.pallas_call(
            functools.partial(add_shards, tuple(names), places, totals is not None, last),
            in_specs=[pl.BlockSpec(memory_space=pltpu.SMEM)] + [block] * (len(operands) - 1),
            out_specs=out_specs,
            out_shape=out_shape,
            scratch_shapes=scratch,
            compiler_params=pltpu.CompilerParams(vmem_limit_bytes=40 * 1024 * 1024),
            cost_estimate=pl.CostEstimate(
                flops=4 * tall * wide * depth * len(names) * weight,
                bytes_accessed=wide * depth * 2 * len(names) + 8 * 4 * tall * wide,
                transcendentals=0,
            ),
        )(*operands)
        return out if keep else out[0]

    def fence(totals):
        nonlocal arrays
        arrays, totals = lax.optimization_barrier((arrays, totals))
        return totals

    put("9", packed, "near", [("O", 0)])

    put("1a", hop_z(packed, 2), "near", [("O", 2)])
    put("1b", hop_z(packed, 1), "near", [("O", 1)])
    put("1c", hop_b(packed), "near", [("B", 0)])
    put("1d", hop_a(packed), "near", [("A", 0)])
    put("1e", hop_b(near("A", 0)), "near", [("AB", 0)])
    place, weights = fence((place, weights))

    def route(kernel, operands, counts, weight=0):
        block = pl.BlockSpec(memory_space=pltpu.VMEM)
        first = pl.BlockSpec(memory_space=pltpu.SMEM) if operands[0] is place else block
        shapes = [(count,) * (count > 1) + packed.shape for count in counts]
        routed = pl.pallas_call(
            kernel,
            in_specs=[first] + [block] * (len(operands) - 1),
            out_specs=[block] * len(counts),
            out_shape=[jax.ShapeDtypeStruct(shape, packed.dtype) for shape in shapes],
            compiler_params=pltpu.CompilerParams(vmem_limit_bytes=24 * 1024 * 1024),
            cost_estimate=pl.CostEstimate(flops=weight, bytes_accessed=0, transcendentals=0),
        )(*operands)
        return fence(routed)

    first = [("O", 0), ("A", 0), ("B", 0), ("AB", 0), ("O", 1), ("O", 2)]
    second = [("AB", 1), ("AB", 2), ("O", 3), ("A", 1), ("A", 2), ("B", 1), ("B", 2)]
    third = [("A", 3), ("AB", 3), ("B", 3)]
    stack, both, mixed = route(route_second, [place] + [near(*kind) for kind in first], (6, 2, 1))
    totals = add([("near", *kind) for kind in first], None)
    o3, ab2, a12, b12 = hop_z(near("O", 2), 1), hop_mixed(mixed), hop_a(both), hop_b(both)
    put("2a", swap(stack), "far", first)
    totals = fence(totals)

    put("2b", hop_z(near("AB", 0), 1), "near", [("AB", 1)])
    totals = add([("far", *kind) for kind in first], totals)
    ab1 = arrays.pop("2b")
    put("2c", o3, "near", [("O", 3)])
    put("2d", ab2, "near", [("AB", 2)])
    totals = fence(totals)

    ab3, a3, o3 = hop_z(near("AB", 2), 1), hop_a(near("O", 3)), near("O", 3)
    totals = add([("near", "O", 3)], totals, weight=45)
    arrays["2b"] = ab1
    put("2e", a12, "near", [("A", 1), ("A", 2)])
    put("2f", b12, "near", [("B", 1), ("B", 2)])
    totals = fence(totals)

    keys = ("2b", "2c", "2d", "2e", "2f")
    (stack,) = route(route_third, [arrays[key] for key in keys], (7,))
    b3, far2 = hop_b(near("O", 3)), swap(stack)
    names = [("near", *kind) for kind in second if kind != ("O", 3)]
    totals = add(names, totals)
    a3, ab3, totals = lax.optimization_barrier((a3, ab3, totals))
    (stack,) = route(route_last, [a3, ab3], (2,), weight=10**11)
    put("3a", stack, "near", third[:2])
    stack = swap(stack)
    put("3d", far2, "far", second)
    totals = add([("far", *kind) for kind in second], totals)
    put("3b", b3, "near", third[2:])
    totals = fence(totals)

    put("4a", stack, "far", third[:2])
    far3 = swap(near("B", 3))
    totals, left = add([("near", *kind) for kind in third], totals, keep=True)
    put("4b", far3, "far", third[2:])
    totals, left = fence((totals, left))
    return add([("far", *kind) for kind in third], totals, left=left)


def add_terms(place_ref, weights_ref, left_ref, right_ref, field_ref):
    @pl.when(pl.program_id(0) == 0)
    def _():
        field_ref[...] = jnp.zeros_like(field_ref)

    spins = left_ref.shape[2]
    groups, columns, per_block, depth = right_ref.shape[0], *right_ref.shape[2:]
    owns = [left_ref[0, 0, spin] for spin in range(spins)]
    left = left_sides(owns, weights_ref[0])
    for column in range(columns):
        right = right_ref[:, 0, column].reshape(groups * per_block, depth)
        term = product(left, right)
        for part in range(2):
            for spin in range(spins):
                start = (part * spins + spin) * per_block
                field_ref[(spin * columns + column) * 2 + part] += term[start : start + per_block]


def gather_whole(packed, place, weights, share):
    groups, _, deep, flat = (lax.axis_size(name) for name in AXES)
    sites = deep * flat
    _, per_block, depth = packed.shape
    columns = min(4, share // 2)
    spins = share // (2 * columns)
    near = lax.all_gather(packed, ("pair", "deep", "flat"))
    near = near.reshape(groups, sites, 4, per_block, depth)
    far = lax.ppermute(near, "core", [(0, 1), (1, 0)])
    wide = groups * per_block

    def half(right):
        return pl.pallas_call(
            add_terms,
            grid_spec=pltpu.PrefetchScalarGridSpec(
                num_scalar_prefetch=1,
                grid=(sites,),
                in_specs=[
                    pl.BlockSpec((1, 2, weights.shape[2]), lambda m, place: (m, 0, 0)),
                    pl.BlockSpec(
                        (1, 1, spins, per_block, depth),
                        lambda m, place: (place[0], m, place[4] // spins, 0, 0),
                    ),
                    pl.BlockSpec(
                        (groups, 1, columns, per_block, depth),
                        lambda m, place: (0, m, place[6] // columns, 0, 0),
                    ),
                ],
                out_specs=pl.BlockSpec((share, per_block, wide), lambda m, place: (0, 0, 0)),
            ),
            out_shape=jax.ShapeDtypeStruct((share, per_block, wide), jnp.float32),
            compiler_params=pltpu.CompilerParams(vmem_limit_bytes=40 * 1024 * 1024),
        )(place, weights, near, right)

    sides = [half(right).reshape(share, per_block, groups, per_block) for right in (near, far)]
    first = lax.axis_index("core") == 0
    even, odd = (jnp.where(first, a, b) for a, b in (sides, sides[::-1]))
    return jnp.stack([even, odd], 3).reshape(share, per_block, 2 * wide)


def shards(modes, momenta):
    groups, _, deep, flat = (lax.axis_size(name) for name in AXES)
    sites = deep * flat
    slots, steps, per_block, spin_colour, site_count = modes.shape
    share = steps * momenta.shape[0] * 32 // sites
    owned = (lax.axis_index("deep") * flat + lax.axis_index("flat")) * (share // 2)
    place = [lax.axis_index(name) for name in AXES]
    place = jnp.stack(place + [owned // 4 % 4, jnp.int32(flat), owned % 4]).astype(jnp.int32)

    packed = jnp.transpose(modes.reshape(slots, per_block, 4, 3, site_count), (2, 1, 0, 3, 4))
    packed = packed.reshape(4, per_block, slots * 3 * site_count)

    mine = lax.dynamic_slice_in_dim(momenta, owned // 16, 1, 0)
    weights = phase_table(mine, jnp.int32(0), sites * site_count, LEXT)[0]
    weights = jnp.transpose(weights.reshape(2, sites, site_count), (1, 0, 2))

    if (groups, deep, flat) == (2, 4, 2) and share in (8, 16, 32):
        return swap_in_windows(packed, place, weights, share)
    return gather_whole(packed, place, weights, share)


def solution(mesh):
    count, sites = mesh.shape["blk"], mesh.shape["site"]
    flat = 2 ** (int(math.log2(sites)) // 2)
    split = Mesh(mesh.devices.reshape(count // 2, 2, sites // flat, flat), AXES)
    placed = (P(None, None, ("pair", "core"), None, ("deep", "flat")), P())
    return jax.shard_map(
        shards,
        mesh=split,
        in_specs=placed,
        out_specs=P(("deep", "flat"), ("pair", "core"), None),
        check_vma=False,
    )
```

```python
import functools
import math

import jax
import jax.numpy as jnp
from jax import lax
from jax.experimental import pallas as pl
from jax.experimental.pallas import tpu as pltpu
from jax.sharding import Mesh, PartitionSpec as P

LEXT = 48

TWO_PI = 2.0 * math.pi

AXES = ("pair", "core", "deep", "flat")


def phase_table(momenta, first_site, site_count, extent):
    flat = first_site + jnp.arange(site_count, dtype=jnp.int32)
    coords = jnp.stack([flat % extent, flat // extent % extent, flat // (extent * extent)], 0)
    turns = jnp.mod(jnp.sum(momenta[:, :, None] * coords[None, :, :], axis=1), extent)
    angle = turns.astype(jnp.float32) * (TWO_PI / extent)
    return jnp.stack([jnp.cos(angle), jnp.sin(angle)], 1)


def left_sides(owns, weights):
    depth = owns[0].shape[1]
    half = depth // 2
    cosine = jnp.tile(weights[0:1], (1, depth // weights.shape[1]))
    sine = jnp.tile(weights[1:2], (1, depth // weights.shape[1]))
    cosine_rows = [[], []]
    sine_rows = [[], []]
    for own in owns:
        own = own.astype(jnp.float32)
        by_cos = (own * cosine).astype(jnp.bfloat16)
        by_sin = (own * sine).astype(jnp.bfloat16)
        cosine_rows[0].append(by_cos)
        cosine_rows[1].append(jnp.concatenate([-by_cos[:, half:], by_cos[:, :half]], 1))
        sine_rows[0].append(jnp.concatenate([-by_sin[:, half:], by_sin[:, :half]], 1))
        sine_rows[1].append(-by_sin)
    return jnp.concatenate(cosine_rows[0] + cosine_rows[1] + sine_rows[0] + sine_rows[1], 0)


def product(left, right):
    dims = (((1,), (1,)), ((), ()))
    terms = lax.dot_general(left, right, dims, preferred_element_type=jnp.float32)
    half = terms.shape[0] // 2
    return terms[:half] + terms[half:]


def add_shards(names, where, has_totals, last, share, weights_ref, *refs):
    refs = list(refs)
    if last:
        sems, row_ref, far_ref, out_ref, totals_in, left_ref = (refs.pop() for _ in range(6))
    else:
        left_ref, out_ref = refs.pop(), refs.pop()
        totals_in = refs.pop() if has_totals else None

    def shard(name):
        index, slot = where[name]
        return refs[index] if slot is None else refs[index].at[slot]

    pair, core, level, beside = (lax.axis_index(name) for name in AXES)
    flat = lax.axis_size("flat")
    columns, per_block, _ = shard(names[0]).shape
    first_s = lax.rem(lax.div((level * flat + beside) * (share // 2), 4), 4)
    spins = left_ref.shape[1] // (4 * per_block)

    slots = left_slots(names)
    if last:
        far_ref[...] = totals_in[1]
    else:
        if has_totals:
            out_ref[...] = totals_in[...]
        else:
            out_ref[...] = jnp.zeros_like(out_ref)
        for slot, (dy, dz) in enumerate(slots):
            site = jnp.bitwise_xor(level, dz) * flat + jnp.bitwise_xor(beside, dy)
            if dy == 0:
                owns = [shard(("near", "O", dz))[first_s + s] for s in range(spins)]
            else:
                owns = [
                    jnp.where(
                        core == 0,
                        shard(("near", "B", dz))[first_s + s],
                        shard(("near", "A", dz))[first_s + s],
                    )
                    for s in range(spins)
                ]
            left_ref[slot] = left_sides(owns, weights_ref[site])

    for side, kind, dz in names:
        right = shard((side, kind, dz))[...].reshape(columns * per_block, -1)
        turn = core if side == "near" else 1 - core
        dx, dy = {"O": (0, 0), "A": (1 - turn, turn), "B": (turn, 1 - turn), "AB": (1, 1)}[kind]
        if kind in ("O", "AB"):
            slot = slots.index((dy, dz))
        else:
            slot = slots.index((0, dz)) + dy
        term = product(left_ref[slot], right)
        if last:
            far_ref[dx] += term
        else:
            out_ref[0 if side == "near" else 1, dx] += term

    if last:
        lane = lax.broadcasted_iota(jnp.int32, (per_block, 2 * per_block), 1)
        copies = []
        for spin in range(spins):
            for column in range(0, columns, 2):
                first = (spin * columns + column) * 2
                across = pl.ds(column * per_block, 2 * per_block)
                for part in range(2):
                    top = (part * spins + spin) * per_block
                    for p in range(2):
                        dx = jnp.bitwise_xor(pair, p)
                        near = totals_in[0, dx, pl.ds(top, per_block), across]
                        far = far_ref[dx, pl.ds(top, per_block), across]
                        even = jnp.where(core == 0, near, far)
                        odd = jnp.where(core == 0, far, near)
                        place = pl.ds(p * 2 * per_block, 2 * per_block)
                        row_ref[first + part, :, place] = jnp.where(
                            lane < per_block, even, pltpu.roll(odd, per_block, 1)
                        )
                        row_ref[first + part + 2, :, place] = jnp.where(
                            lane < per_block, pltpu.roll(even, per_block, 1), odd
                        )
                rows = pl.ds(first, 4)
                copies.append(
                    pltpu.make_async_copy(row_ref.at[rows], out_ref.at[rows], sems.at[len(copies)])
                )
                copies[-1].start()
        for copy in copies:
            copy.wait()


def route_second(*refs):
    ab0_ref, o1_ref, o2_ref, stack_ref, both_ref, mixed_ref = refs[3:]
    core = lax.axis_index("core")
    for slot in range(6):
        stack_ref[slot] = refs[slot][...]
    both_ref[0] = o1_ref[...]
    both_ref[1] = o2_ref[...]

    @pl.when(core == 0)
    def _():
        mixed_ref[...] = o2_ref[...]

    @pl.when(core != 0)
    def _():
        mixed_ref[...] = ab0_ref[...]


def route_third(ab1_ref, o3_ref, ab2_ref, a12_ref, b12_ref, stack_ref):
    for slot, ref in enumerate((ab1_ref, ab2_ref, o3_ref)):
        stack_ref[slot] = ref[...]
    stack_ref[3:5] = a12_ref[...]
    stack_ref[5:7] = b12_ref[...]


def route_last(a3_ref, ab3_ref, stack_ref):
    stack_ref[0] = a3_ref[...]
    stack_ref[1] = ab3_ref[...]


def left_slots(names):
    needed = set()
    for _, kind, dz in names:
        needed |= {"O": {(0, dz)}, "AB": {(1, dz)}}.get(kind, {(0, dz), (1, dz)})
    return sorted(needed, key=lambda slot: (slot[1], slot[0]))


def swap_in_windows(packed, weights, share):
    shape = tuple(lax.axis_size(name) for name in AXES)
    columns, per_block, depth = packed.shape
    spins = share // (2 * columns)
    tall, wide = 2 * spins * per_block, columns * per_block
    strides = (shape[1] * shape[2] * shape[3], shape[2] * shape[3], shape[3], 1)

    def move(array, target):
        pairs = []
        for p in range(shape[0]):
            for c in range(shape[1]):
                for z in range(shape[2]):
                    for y in range(shape[3]):
                        ends = (p, c, z, y), target(p, c, z, y)
                        pairs.append(
                            tuple(sum(a * b for a, b in zip(end, strides)) for end in ends)
                        )
        return lax.ppermute(array, AXES, pairs)

    def hop_a(array):
        return move(array, lambda p, c, z, y: (p ^ 1, c, z, y) if c == 0 else (p, c, z, y ^ 1))

    def hop_b(array):
        return move(array, lambda p, c, z, y: (p, c, z, y ^ 1) if c == 0 else (p ^ 1, c, z, y))

    def hop_ab(array):
        return move(array, lambda p, c, z, y: (p ^ 1, c, z, y ^ 1))

    def hop_z(array, by):
        return move(array, lambda p, c, z, y: (p, c, z ^ by, y))

    def hop_mixed(array):
        return move(
            array, lambda p, c, z, y: (p ^ 1, c, z, y ^ 1) if c == 0 else (p, c, z ^ 2, y)
        )

    def swap(array):
        return move(array, lambda p, c, z, y: (p, c ^ 1, z, y))

    arrays = {}
    where = {}

    def put(key, array, side, kinds):
        arrays[key] = array
        for slot, (kind, dz) in enumerate(kinds):
            where[(side, kind, dz)] = (key, slot if len(kinds) > 1 else None)

    def near(kind, dz):
        key, slot = where[("near", kind, dz)]
        return arrays[key] if slot is None else arrays[key][slot]

    def add(names, totals, keep=False, left=None, weight=1):
        last = left is not None
        slots = left_slots(names)
        uses = list(names)
        for dy, dz in [] if last else slots:
            uses += [("near", kind, dz) for kind in (("A", "B") if dy else ("O",))]
        keys = sorted({where[name][0] for name in uses})
        places = {name: (keys.index(where[name][0]), where[name][1]) for name in uses}
        operands = [weights] + [arrays[key] for key in keys]
        operands += [each for each in (left, totals) if each is not None]
        total_shape = (2, 2, tall, wide)
        left_shape = (len(slots), 2 * tall, depth)
        block = pl.BlockSpec(memory_space=pltpu.VMEM)
        out_shape = [jax.ShapeDtypeStruct(total_shape, jnp.float32)]
        scratch = [pltpu.VMEM(left_shape, jnp.bfloat16)]
        out_specs = [block]
        if last:
            out_shape = [jax.ShapeDtypeStruct((share, per_block, 4 * per_block), jnp.float32)]
            out_specs = [pl.BlockSpec(memory_space=pl.ANY)]
            scratch = [
                pltpu.VMEM(total_shape[1:], jnp.float32),
                pltpu.VMEM(out_shape[0].shape, jnp.float32),
                pltpu.SemaphoreType.DMA((spins * columns // 2,)),
            ]
        if keep:
            out_shape.append(jax.ShapeDtypeStruct(left_shape, jnp.bfloat16))
            out_specs, scratch = [block] * 2, []
        out = pl.pallas_call(
            functools.partial(add_shards, tuple(names), places, totals is not None, last, share),
            in_specs=[block] * len(operands),
            out_specs=out_specs,
            out_shape=out_shape,
            scratch_shapes=scratch,
            compiler_params=pltpu.CompilerParams(vmem_limit_bytes=40 * 1024 * 1024),
            cost_estimate=pl.CostEstimate(
                flops=4 * tall * wide * depth * len(names) * weight,
                bytes_accessed=wide * depth * 2 * len(names) + 8 * 4 * tall * wide,
                transcendentals=0,
            ),
        )(*operands)
        return out if keep else out[0]

    def fence(totals):
        nonlocal arrays
        arrays, totals = lax.optimization_barrier((arrays, totals))
        return totals

    put("9", packed, "near", [("O", 0)])

    put("1a", hop_z(packed, 2), "near", [("O", 2)])
    put("1b", hop_z(packed, 1), "near", [("O", 1)])
    put("1c", hop_b(packed), "near", [("B", 0)])
    put("1d", hop_a(packed), "near", [("A", 0)])
    put("1e", hop_b(near("A", 0)), "near", [("AB", 0)])
    weights = fence(weights)

    def route(kernel, operands, counts, weight=0):
        block = pl.BlockSpec(memory_space=pltpu.VMEM)
        shapes = [(count,) * (count > 1) + packed.shape for count in counts]
        routed = pl.pallas_call(
            kernel,
            in_specs=[block] * len(operands),
            out_specs=[block] * len(counts),
            out_shape=[jax.ShapeDtypeStruct(shape, packed.dtype) for shape in shapes],
            compiler_params=pltpu.CompilerParams(vmem_limit_bytes=24 * 1024 * 1024),
            cost_estimate=pl.CostEstimate(flops=weight, bytes_accessed=0, transcendentals=0),
        )(*operands)
        return fence(routed)

    first = [("O", 0), ("A", 0), ("B", 0), ("AB", 0), ("O", 1), ("O", 2)]
    second = [("AB", 1), ("AB", 2), ("O", 3), ("A", 1), ("A", 2), ("B", 1), ("B", 2)]
    third = [("A", 3), ("AB", 3), ("B", 3)]
    stack, both, mixed = route(route_second, [near(*kind) for kind in first], (6, 2, 1))
    totals = add([("near", *kind) for kind in first], None)
    o3, ab2, a12, b12 = hop_z(near("O", 2), 1), hop_mixed(mixed), hop_a(both), hop_b(both)
    put("2a", swap(stack), "far", first)
    totals = fence(totals)

    put("2b", hop_z(near("AB", 0), 1), "near", [("AB", 1)])
    totals = add([("far", *kind) for kind in first], totals)
    ab1 = arrays.pop("2b")
    put("2c", o3, "near", [("O", 3)])
    put("2d", ab2, "near", [("AB", 2)])
    totals = fence(totals)

    ab3, a3, b3 = hop_z(near("AB", 2), 1), hop_a(near("O", 3)), hop_b(near("O", 3))
    totals = add([("near", "O", 3)], totals, weight=45)
    arrays["2b"] = ab1
    put("2e", a12, "near", [("A", 1), ("A", 2)])
    put("2f", b12, "near", [("B", 1), ("B", 2)])
    totals = fence(totals)

    keys = ("2b", "2c", "2d", "2e", "2f")
    (stack,) = route(route_third, [arrays[key] for key in keys], (7,))
    far2 = swap(stack)
    names = [("near", *kind) for kind in second if kind != ("O", 3)]
    totals = add(names, totals)
    a3, ab3, totals = lax.optimization_barrier((a3, ab3, totals))
    (stack,) = route(route_last, [a3, ab3], (2,), weight=10**11)
    put("3a", stack, "near", third[:2])
    stack = swap(stack)
    put("3d", far2, "far", second)
    totals = add([("far", *kind) for kind in second], totals)
    put("3b", b3, "near", third[2:])
    totals = fence(totals)

    put("4a", stack, "far", third[:2])
    far3 = swap(near("B", 3))
    totals, left = add([("near", *kind) for kind in third], totals, keep=True)
    put("4b", far3, "far", third[2:])
    totals, left = fence((totals, left))
    return add([("far", *kind) for kind in third], totals, left=left)


def add_terms(place_ref, weights_ref, left_ref, right_ref, field_ref):
    @pl.when(pl.program_id(0) == 0)
    def _():
        field_ref[...] = jnp.zeros_like(field_ref)

    spins = left_ref.shape[2]
    groups, columns, per_block, depth = right_ref.shape[0], *right_ref.shape[2:]
    owns = [left_ref[0, 0, spin] for spin in range(spins)]
    left = left_sides(owns, weights_ref[0])
    for column in range(columns):
        right = right_ref[:, 0, column].reshape(groups * per_block, depth)
        term = product(left, right)
        for part in range(2):
            for spin in range(spins):
                start = (part * spins + spin) * per_block
                field_ref[(spin * columns + column) * 2 + part] += term[start : start + per_block]


def gather_whole(packed, place, weights, share):
    groups, _, deep, flat = (lax.axis_size(name) for name in AXES)
    sites = deep * flat
    _, per_block, depth = packed.shape
    columns = min(4, share // 2)
    spins = share // (2 * columns)
    near = lax.all_gather(packed, ("pair", "deep", "flat"))
    near = near.reshape(groups, sites, 4, per_block, depth)
    far = lax.ppermute(near, "core", [(0, 1), (1, 0)])
    wide = groups * per_block

    def half(right):
        return pl.pallas_call(
            add_terms,
            grid_spec=pltpu.PrefetchScalarGridSpec(
                num_scalar_prefetch=1,
                grid=(sites,),
                in_specs=[
                    pl.BlockSpec((1, 2, weights.shape[2]), lambda m, place: (m, 0, 0)),
                    pl.BlockSpec(
                        (1, 1, spins, per_block, depth),
                        lambda m, place: (place[0], m, place[4] // spins, 0, 0),
                    ),
                    pl.BlockSpec(
                        (groups, 1, columns, per_block, depth),
                        lambda m, place: (0, m, place[6] // columns, 0, 0),
                    ),
                ],
                out_specs=pl.BlockSpec((share, per_block, wide), lambda m, place: (0, 0, 0)),
            ),
            out_shape=jax.ShapeDtypeStruct((share, per_block, wide), jnp.float32),
            compiler_params=pltpu.CompilerParams(vmem_limit_bytes=40 * 1024 * 1024),
        )(place, weights, near, right)

    sides = [half(right).reshape(share, per_block, groups, per_block) for right in (near, far)]
    first = lax.axis_index("core") == 0
    even, odd = (jnp.where(first, a, b) for a, b in (sides, sides[::-1]))
    return jnp.stack([even, odd], 3).reshape(share, per_block, 2 * wide)


def shards(modes, momenta):
    groups, _, deep, flat = (lax.axis_size(name) for name in AXES)
    sites = deep * flat
    slots, steps, per_block, spin_colour, site_count = modes.shape
    share = steps * momenta.shape[0] * 32 // sites
    owned = (lax.axis_index("deep") * flat + lax.axis_index("flat")) * (share // 2)
    place = [lax.axis_index(name) for name in AXES]
    place = jnp.stack(place + [owned // 4 % 4, jnp.int32(flat), owned % 4]).astype(jnp.int32)

    packed = jnp.transpose(modes.reshape(slots, per_block, 4, 3, site_count), (2, 1, 0, 3, 4))
    packed = packed.reshape(4, per_block, slots * 3 * site_count)

    mine = lax.dynamic_slice_in_dim(momenta, owned // 16, 1, 0)
    weights = phase_table(mine, jnp.int32(0), sites * site_count, LEXT)[0]
    weights = jnp.transpose(weights.reshape(2, sites, site_count), (1, 0, 2))

    if (groups, deep, flat) == (2, 4, 2) and share in (8, 16, 32):
        return swap_in_windows(packed, weights, share)
    return gather_whole(packed, place, weights, share)


def solution(mesh):
    count, sites = mesh.shape["blk"], mesh.shape["site"]
    flat = 2 ** (int(math.log2(sites)) // 2)
    split = Mesh(mesh.devices.reshape(count // 2, 2, sites // flat, flat), AXES)
    placed = (P(None, None, ("pair", "core"), None, ("deep", "flat")), P())
    return jax.shard_map(
        shards,
        mesh=split,
        in_specs=placed,
        out_specs=P(("deep", "flat"), ("pair", "core"), None),
        check_vma=False,
    )
```

```python
import functools
import math

import jax
import jax.numpy as jnp
from jax import lax
from jax.experimental import pallas as pl
from jax.experimental.pallas import tpu as pltpu
from jax.sharding import Mesh, PartitionSpec as P

LEXT = 48

TWO_PI = 2.0 * math.pi

AXES = ("pair", "core", "deep", "flat")


def phase_table(momenta, first_site, site_count, extent):
    flat = first_site + jnp.arange(site_count, dtype=jnp.int32)
    coords = jnp.stack([flat % extent, flat // extent % extent, flat // (extent * extent)], 0)
    turns = jnp.mod(jnp.sum(momenta[:, :, None] * coords[None, :, :], axis=1), extent)
    angle = turns.astype(jnp.float32) * (TWO_PI / extent)
    return jnp.stack([jnp.cos(angle), jnp.sin(angle)], 1)


def left_sides(owns, weights):
    depth = owns[0].shape[1]
    half = depth // 2
    cosine = jnp.tile(weights[0:1], (1, depth // weights.shape[1]))
    sine = jnp.tile(weights[1:2], (1, depth // weights.shape[1]))
    cosine_rows = [[], []]
    sine_rows = [[], []]
    for own in owns:
        own = own.astype(jnp.float32)
        by_cos = (own * cosine).astype(jnp.bfloat16)
        by_sin = (own * sine).astype(jnp.bfloat16)
        cosine_rows[0].append(by_cos)
        cosine_rows[1].append(jnp.concatenate([-by_cos[:, half:], by_cos[:, :half]], 1))
        sine_rows[0].append(jnp.concatenate([-by_sin[:, half:], by_sin[:, :half]], 1))
        sine_rows[1].append(-by_sin)
    return jnp.concatenate(cosine_rows[0] + cosine_rows[1] + sine_rows[0] + sine_rows[1], 0)


def product(left, right):
    dims = (((1,), (1,)), ((), ()))
    terms = lax.dot_general(left, right, dims, preferred_element_type=jnp.float32)
    half = terms.shape[0] // 2
    return terms[:half] + terms[half:]


def add_shards(names, where, slots, has_totals, given, last, share, weights_ref, *refs):
    refs = list(refs)
    if last:
        sems, row_ref, far_ref = (refs.pop() for _ in range(3))
    left_ref = None if given else refs.pop()
    out_ref = refs.pop()
    totals_in = refs.pop() if has_totals else None
    left_ref = refs.pop() if given else left_ref

    def shard(name):
        index, slot = where[name]
        return refs[index] if slot is None else refs[index].at[slot]

    def spin_rows(name, spin):
        ref = shard(name)
        tiles = [ref[part, spin * colours + x] for part in range(2) for x in range(colours)]
        return jnp.concatenate(tiles, 1)

    pair, core, level, beside = (lax.axis_index(name) for name in AXES)
    flat = lax.axis_size("flat")
    _, spin_colour, per_block, _ = shard(names[0]).shape
    columns, colours = 4, spin_colour // 4
    first_s = lax.rem(lax.div((level * flat + beside) * (share // 2), 4), 4)
    spins = left_ref.shape[1] // (4 * per_block)

    if last:
        far_ref[...] = totals_in[1]
    elif has_totals:
        out_ref[...] = totals_in[...]
    else:
        out_ref[...] = jnp.zeros_like(out_ref)
    if not given:
        for slot, (dy, dz) in enumerate(slots):
            site = jnp.bitwise_xor(level, dz) * flat + jnp.bitwise_xor(beside, dy)
            if dy == 0:
                owns = [spin_rows(("near", "O", dz), first_s + s) for s in range(spins)]
            else:
                owns = [
                    jnp.where(
                        core == 0,
                        spin_rows(("near", "B", dz), first_s + s),
                        spin_rows(("near", "A", dz), first_s + s),
                    )
                    for s in range(spins)
                ]
            left_ref[slot] = left_sides(owns, weights_ref[site])

    for side, kind, dz in names:
        right = jnp.concatenate([spin_rows((side, kind, dz), r) for r in range(columns)], 0)
        turn = core if side == "near" else 1 - core
        dx, dy = {"O": (0, 0), "A": (1 - turn, turn), "B": (turn, 1 - turn), "AB": (1, 1)}[kind]
        if kind in ("O", "AB"):
            slot = slots.index((dy, dz))
        else:
            slot = slots.index((0, dz)) + dy
        term = product(left_ref[slot], right)
        if last:
            far_ref[dx] += term
        else:
            out_ref[0 if side == "near" else 1, dx] += term

    if last:
        lane = lax.broadcasted_iota(jnp.int32, (per_block, 2 * per_block), 1)
        copies = []
        for spin in range(spins):
            for column in range(0, columns, 2):
                first = (spin * columns + column) * 2
                across = pl.ds(column * per_block, 2 * per_block)
                for part in range(2):
                    top = (part * spins + spin) * per_block
                    for p in range(2):
                        dx = jnp.bitwise_xor(pair, p)
                        near = totals_in[0, dx, pl.ds(top, per_block), across]
                        far = far_ref[dx, pl.ds(top, per_block), across]
                        even = jnp.where(core == 0, near, far)
                        odd = jnp.where(core == 0, far, near)
                        place = pl.ds(p * 2 * per_block, 2 * per_block)
                        row_ref[first + part, :, place] = jnp.where(
                            lane < per_block, even, pltpu.roll(odd, per_block, 1)
                        )
                        row_ref[first + part + 2, :, place] = jnp.where(
                            lane < per_block, pltpu.roll(even, per_block, 1), odd
                        )
                rows = pl.ds(first, 4)
                copies.append(
                    pltpu.make_async_copy(row_ref.at[rows], out_ref.at[rows], sems.at[len(copies)])
                )
                copies[-1].start()
        for copy in copies:
            copy.wait()


def route_second(*refs):
    ab0_ref, o1_ref, o2_ref, stack_ref, both_ref, mixed_ref = refs[3:]
    core = lax.axis_index("core")
    for slot in range(6):
        stack_ref[slot] = refs[slot][...]
    both_ref[0] = o1_ref[...]
    both_ref[1] = o2_ref[...]

    @pl.when(core == 0)
    def _():
        mixed_ref[...] = o2_ref[...]

    @pl.when(core != 0)
    def _():
        mixed_ref[...] = ab0_ref[...]


def route_third(ab1_ref, o3_ref, ab2_ref, a12_ref, b12_ref, stack_ref):
    for slot, ref in enumerate((ab1_ref, ab2_ref, o3_ref)):
        stack_ref[slot] = ref[...]
    stack_ref[3:5] = a12_ref[...]
    stack_ref[5:7] = b12_ref[...]


def route_last(a3_ref, ab3_ref, stack_ref):
    stack_ref[0] = a3_ref[...]
    stack_ref[1] = ab3_ref[...]


def left_slots(names):
    needed = set()
    for _, kind, dz in names:
        needed |= {"O": {(0, dz)}, "AB": {(1, dz)}}.get(kind, {(0, dz), (1, dz)})
    return sorted(needed, key=lambda slot: (slot[1], slot[0]))


def swap_in_windows(own, weights, share):
    shape = tuple(lax.axis_size(name) for name in AXES)
    columns, per_block = 4, own.shape[2]
    depth = own.size // (columns * per_block)
    spins = share // (2 * columns)
    tall, wide = 2 * spins * per_block, columns * per_block
    strides = (shape[1] * shape[2] * shape[3], shape[2] * shape[3], shape[3], 1)

    def move(array, target):
        pairs = []
        for p in range(shape[0]):
            for c in range(shape[1]):
                for z in range(shape[2]):
                    for y in range(shape[3]):
                        ends = (p, c, z, y), target(p, c, z, y)
                        pairs.append(
                            tuple(sum(a * b for a, b in zip(end, strides)) for end in ends)
                        )
        return lax.ppermute(array, AXES, pairs)

    def hop_a(array):
        return move(array, lambda p, c, z, y: (p ^ 1, c, z, y) if c == 0 else (p, c, z, y ^ 1))

    def hop_b(array):
        return move(array, lambda p, c, z, y: (p, c, z, y ^ 1) if c == 0 else (p ^ 1, c, z, y))

    def hop_ab(array):
        return move(array, lambda p, c, z, y: (p ^ 1, c, z, y ^ 1))

    def hop_z(array, by):
        return move(array, lambda p, c, z, y: (p, c, z ^ by, y))

    def hop_mixed(array):
        return move(
            array, lambda p, c, z, y: (p ^ 1, c, z, y ^ 1) if c == 0 else (p, c, z ^ 2, y)
        )

    def swap(array):
        return move(array, lambda p, c, z, y: (p, c ^ 1, z, y))

    arrays = {}
    where = {}

    def put(key, array, side, kinds):
        arrays[key] = array
        for slot, (kind, dz) in enumerate(kinds):
            where[(side, kind, dz)] = (key, slot if len(kinds) > 1 else None)

    def near(kind, dz):
        key, slot = where[("near", kind, dz)]
        return arrays[key] if slot is None else arrays[key][slot]

    def add(names, totals, keep=None, left=None, last=False, weight=1):
        given = left is not None
        slots, left = left if given else (keep or left_slots(names), None)
        uses = list(names)
        for dy, dz in [] if given else slots:
            uses += [("near", kind, dz) for kind in (("A", "B") if dy else ("O",))]
        keys = sorted({where[name][0] for name in uses})
        places = {name: (keys.index(where[name][0]), where[name][1]) for name in uses}
        operands = [weights] + [arrays[key] for key in keys]
        operands += [each for each in (left, totals) if each is not None]
        total_shape = (2, 2, tall, wide)
        left_shape = (len(slots), 2 * tall, depth)
        block = pl.BlockSpec(memory_space=pltpu.VMEM)
        out_shape = [jax.ShapeDtypeStruct(total_shape, jnp.float32)]
        scratch = [] if given or keep else [pltpu.VMEM(left_shape, jnp.bfloat16)]
        out_specs = [block]
        if last:
            out_shape = [jax.ShapeDtypeStruct((share, per_block, 4 * per_block), jnp.float32)]
            out_specs = [pl.BlockSpec(memory_space=pl.ANY)]
            scratch = [
                pltpu.VMEM(total_shape[1:], jnp.float32),
                pltpu.VMEM(out_shape[0].shape, jnp.float32),
                pltpu.SemaphoreType.DMA((spins * columns // 2,)),
            ]
        if keep:
            out_shape.append(jax.ShapeDtypeStruct(left_shape, jnp.bfloat16))
            out_specs.append(block)
        out = pl.pallas_call(
            functools.partial(
                add_shards, tuple(names), places, slots, totals is not None, given, last, share
            ),
            in_specs=[block] * len(operands),
            out_specs=out_specs,
            out_shape=out_shape,
            scratch_shapes=scratch,
            compiler_params=pltpu.CompilerParams(vmem_limit_bytes=40 * 1024 * 1024),
            cost_estimate=pl.CostEstimate(
                flops=4 * tall * wide * depth * len(names) * weight,
                bytes_accessed=wide * depth * 2 * len(names) + 8 * 4 * tall * wide,
                transcendentals=0,
            ),
        )(*operands)
        return (out[0], (slots, out[1])) if keep else out[0]

    def fence(totals):
        nonlocal arrays
        arrays, totals = lax.optimization_barrier((arrays, totals))
        return totals

    put("9", own, "near", [("O", 0)])

    put("1a", hop_z(own, 2), "near", [("O", 2)])
    put("1b", hop_z(own, 1), "near", [("O", 1)])
    put("1c", hop_b(own), "near", [("B", 0)])
    put("1d", hop_a(own), "near", [("A", 0)])
    put("1e", hop_b(near("A", 0)), "near", [("AB", 0)])
    weights = fence(weights)

    def route(kernel, operands, counts, weight=0):
        block = pl.BlockSpec(memory_space=pltpu.VMEM)
        shapes = [(count,) * (count > 1) + own.shape for count in counts]
        routed = pl.pallas_call(
            kernel,
            in_specs=[block] * len(operands),
            out_specs=[block] * len(counts),
            out_shape=[jax.ShapeDtypeStruct(shape, own.dtype) for shape in shapes],
            compiler_params=pltpu.CompilerParams(vmem_limit_bytes=24 * 1024 * 1024),
            cost_estimate=pl.CostEstimate(flops=weight, bytes_accessed=0, transcendentals=0),
        )(*operands)
        return fence(routed)

    first = [("O", 0), ("A", 0), ("B", 0), ("AB", 0), ("O", 1), ("O", 2)]
    second = [("AB", 1), ("AB", 2), ("O", 3), ("A", 1), ("A", 2), ("B", 1), ("B", 2)]
    third = [("A", 3), ("AB", 3), ("B", 3)]
    stack, both, mixed = route(route_second, [near(*kind) for kind in first], (6, 2, 1))
    totals = add([("near", *kind) for kind in first], None)
    o3, ab2, a12, b12 = hop_z(near("O", 2), 1), hop_mixed(mixed), hop_a(both), hop_b(both)
    put("2a", swap(stack), "far", first)
    totals = fence(totals)

    put("2b", hop_z(near("AB", 0), 1), "near", [("AB", 1)])
    totals = add([("far", *kind) for kind in first], totals)
    ab1 = arrays.pop("2b")
    put("2c", o3, "near", [("O", 3)])
    put("2d", ab2, "near", [("AB", 2)])
    totals = fence(totals)

    ab3, a3, b3 = hop_z(near("AB", 2), 1), hop_a(near("O", 3)), hop_b(near("O", 3))
    totals = add([("near", "O", 3)], totals, weight=45)
    arrays["2b"] = ab1
    put("2e", a12, "near", [("A", 1), ("A", 2)])
    put("2f", b12, "near", [("B", 1), ("B", 2)])
    totals = fence(totals)

    keys = ("2b", "2c", "2d", "2e", "2f")
    (stack,) = route(route_third, [arrays[key] for key in keys], (7,))
    far2 = swap(stack)
    names = [("near", *kind) for kind in second if kind != ("O", 3)]
    totals, (slots, left) = add(names, totals, keep=left_slots([("near", *kind) for kind in second]))
    a3, ab3, totals = lax.optimization_barrier((a3, ab3, totals))
    (stack,) = route(route_last, [a3, ab3], (2,), weight=10**11)
    put("3a", stack, "near", third[:2])
    stack = swap(stack)
    put("3d", far2, "far", second)
    totals = add([("far", *kind) for kind in second], totals, left=(slots, left))
    put("3b", b3, "near", third[2:])
    totals = fence(totals)

    put("4a", stack, "far", third[:2])
    far3 = swap(near("B", 3))
    names = [("near", *kind) for kind in third]
    totals, (slots, left) = add(names, totals, keep=left_slots(names))
    put("4b", far3, "far", third[2:])
    totals, left = fence((totals, left))
    return add([("far", *kind) for kind in third], totals, left=(slots, left), last=True)


def add_terms(place_ref, weights_ref, left_ref, right_ref, field_ref):
    @pl.when(pl.program_id(0) == 0)
    def _():
        field_ref[...] = jnp.zeros_like(field_ref)

    spins = left_ref.shape[2]
    groups, columns, per_block, depth = right_ref.shape[0], *right_ref.shape[2:]
    owns = [left_ref[0, 0, spin] for spin in range(spins)]
    left = left_sides(owns, weights_ref[0])
    for column in range(columns):
        right = right_ref[:, 0, column].reshape(groups * per_block, depth)
        term = product(left, right)
        for part in range(2):
            for spin in range(spins):
                start = (part * spins + spin) * per_block
                field_ref[(spin * columns + column) * 2 + part] += term[start : start + per_block]


def gather_whole(packed, place, weights, share):
    groups, _, deep, flat = (lax.axis_size(name) for name in AXES)
    sites = deep * flat
    _, per_block, depth = packed.shape
    columns = min(4, share // 2)
    spins = share // (2 * columns)
    near = lax.all_gather(packed, ("pair", "deep", "flat"))
    near = near.reshape(groups, sites, 4, per_block, depth)
    far = lax.ppermute(near, "core", [(0, 1), (1, 0)])
    wide = groups * per_block

    def half(right):
        return pl.pallas_call(
            add_terms,
            grid_spec=pltpu.PrefetchScalarGridSpec(
                num_scalar_prefetch=1,
                grid=(sites,),
                in_specs=[
                    pl.BlockSpec((1, 2, weights.shape[2]), lambda m, place: (m, 0, 0)),
                    pl.BlockSpec(
                        (1, 1, spins, per_block, depth),
                        lambda m, place: (place[0], m, place[4] // spins, 0, 0),
                    ),
                    pl.BlockSpec(
                        (groups, 1, columns, per_block, depth),
                        lambda m, place: (0, m, place[6] // columns, 0, 0),
                    ),
                ],
                out_specs=pl.BlockSpec((share, per_block, wide), lambda m, place: (0, 0, 0)),
            ),
            out_shape=jax.ShapeDtypeStruct((share, per_block, wide), jnp.float32),
            compiler_params=pltpu.CompilerParams(vmem_limit_bytes=40 * 1024 * 1024),
        )(place, weights, near, right)

    sides = [half(right).reshape(share, per_block, groups, per_block) for right in (near, far)]
    first = lax.axis_index("core") == 0
    even, odd = (jnp.where(first, a, b) for a, b in (sides, sides[::-1]))
    return jnp.stack([even, odd], 3).reshape(share, per_block, 2 * wide)


def shards(modes, momenta):
    groups, _, deep, flat = (lax.axis_size(name) for name in AXES)
    sites = deep * flat
    slots, steps, per_block, spin_colour, site_count = modes.shape
    share = steps * momenta.shape[0] * 32 // sites
    owned = (lax.axis_index("deep") * flat + lax.axis_index("flat")) * (share // 2)
    place = [lax.axis_index(name) for name in AXES]
    place = jnp.stack(place + [owned // 4 % 4, jnp.int32(flat), owned % 4]).astype(jnp.int32)

    mine = lax.dynamic_slice_in_dim(momenta, owned // 16, 1, 0)
    weights = phase_table(mine, jnp.int32(0), sites * site_count, LEXT)[0]
    weights = jnp.transpose(weights.reshape(2, sites, site_count), (1, 0, 2))

    if (groups, deep, flat) == (2, 4, 2) and steps == 1 and share in (8, 16, 32):
        own = jnp.transpose(modes[:, 0], (0, 2, 1, 3))
        return swap_in_windows(own, weights, share)
    packed = jnp.transpose(modes.reshape(slots, per_block, 4, 3, site_count), (2, 1, 0, 3, 4))
    packed = packed.reshape(4, per_block, slots * 3 * site_count)
    return gather_whole(packed, place, weights, share)


def solution(mesh):
    count, sites = mesh.shape["blk"], mesh.shape["site"]
    flat = 2 ** (int(math.log2(sites)) // 2)
    split = Mesh(mesh.devices.reshape(count // 2, 2, sites // flat, flat), AXES)
    placed = (P(None, None, ("pair", "core"), None, ("deep", "flat")), P())
    return jax.shard_map(
        shards,
        mesh=split,
        in_specs=placed,
        out_specs=P(("deep", "flat"), ("pair", "core"), None),
        check_vma=False,
    )
```

```python
import functools
import math

import jax
import jax.numpy as jnp
from jax import lax
from jax.experimental import pallas as pl
from jax.experimental.pallas import tpu as pltpu
from jax.sharding import Mesh, PartitionSpec as P

LEXT = 48

TWO_PI = 2.0 * math.pi

AXES = ("pair", "core", "deep", "flat")


def phase_table(momenta, first_site, site_count, extent):
    flat = first_site + jnp.arange(site_count, dtype=jnp.int32)
    coords = jnp.stack([flat % extent, flat // extent % extent, flat // (extent * extent)], 0)
    turns = jnp.mod(jnp.sum(momenta[:, :, None] * coords[None, :, :], axis=1), extent)
    angle = turns.astype(jnp.float32) * (TWO_PI / extent)
    return jnp.stack([jnp.cos(angle), jnp.sin(angle)], 1)


def left_sides(owns, weights):
    depth = owns[0].shape[1]
    half = depth // 2
    cosine = jnp.tile(weights[0:1], (1, depth // weights.shape[1]))
    sine = jnp.tile(weights[1:2], (1, depth // weights.shape[1]))
    cosine_rows = [[], []]
    sine_rows = [[], []]
    for own in owns:
        own = own.astype(jnp.float32)
        by_cos = (own * cosine).astype(jnp.bfloat16)
        by_sin = (own * sine).astype(jnp.bfloat16)
        cosine_rows[0].append(by_cos)
        cosine_rows[1].append(jnp.concatenate([-by_cos[:, half:], by_cos[:, :half]], 1))
        sine_rows[0].append(jnp.concatenate([-by_sin[:, half:], by_sin[:, :half]], 1))
        sine_rows[1].append(-by_sin)
    return jnp.concatenate(cosine_rows[0] + cosine_rows[1] + sine_rows[0] + sine_rows[1], 0)


def product(left, right):
    dims = (((1,), (1,)), ((), ()))
    terms = lax.dot_general(left, right, dims, preferred_element_type=jnp.float32)
    half = terms.shape[0] // 2
    return terms[:half] + terms[half:]


def add_shards(names, where, slots, has_totals, given, last, share, weights_ref, *refs):
    refs = list(refs)
    if last:
        sems, row_ref, far_ref = (refs.pop() for _ in range(3))
    left_ref = None if given else refs.pop()
    out_ref = refs.pop()
    totals_in = refs.pop() if has_totals else None
    left_ref = refs.pop() if given else left_ref

    def shard(name):
        index, slot = where[name]
        return refs[index] if slot is None else refs[index].at[slot]

    def spin_rows(name, spin):
        ref = shard(name)
        tiles = [ref[part, spin * colours + x] for part in range(2) for x in range(colours)]
        return jnp.concatenate(tiles, 1)

    pair, core, level, beside = (lax.axis_index(name) for name in AXES)
    flat = lax.axis_size("flat")
    _, spin_colour, per_block, _ = shard(names[0]).shape
    columns, colours = 4, spin_colour // 4
    first_s = lax.rem(lax.div((level * flat + beside) * (share // 2), 4), 4)
    spins = left_ref.shape[1] // (4 * per_block)

    if last:
        far_ref[...] = totals_in[1]
    elif has_totals:
        out_ref[...] = totals_in[...]
    else:
        out_ref[...] = jnp.zeros_like(out_ref)
    if not given:
        for slot, (dy, dz) in enumerate(slots):
            site = jnp.bitwise_xor(level, dz) * flat + jnp.bitwise_xor(beside, dy)
            if dy == 0:
                owns = [spin_rows(("near", "O", dz), first_s + s) for s in range(spins)]
            else:
                owns = [
                    jnp.where(
                        core == 0,
                        spin_rows(("near", "B", dz), first_s + s),
                        spin_rows(("near", "A", dz), first_s + s),
                    )
                    for s in range(spins)
                ]
            left_ref[slot] = left_sides(owns, weights_ref[site])

    for side, kind, dz in names:
        right = jnp.concatenate([spin_rows((side, kind, dz), r) for r in range(columns)], 0)
        turn = core if side == "near" else 1 - core
        dx, dy = {"O": (0, 0), "A": (1 - turn, turn), "B": (turn, 1 - turn), "AB": (1, 1)}[kind]
        if kind in ("O", "AB"):
            slot = slots.index((dy, dz))
        else:
            slot = slots.index((0, dz)) + dy
        term = product(left_ref[slot], right)
        if last:
            far_ref[dx] += term
        else:
            out_ref[0 if side == "near" else 1, dx] += term

    if last:
        lane = lax.broadcasted_iota(jnp.int32, (per_block, 2 * per_block), 1)
        copies = []
        for spin in range(spins):
            for column in range(0, columns, 2):
                first = (spin * columns + column) * 2
                across = pl.ds(column * per_block, 2 * per_block)
                for part in range(2):
                    top = (part * spins + spin) * per_block
                    for p in range(2):
                        dx = jnp.bitwise_xor(pair, p)
                        near = totals_in[0, dx, pl.ds(top, per_block), across]
                        far = far_ref[dx, pl.ds(top, per_block), across]
                        even = jnp.where(core == 0, near, far)
                        odd = jnp.where(core == 0, far, near)
                        place = pl.ds(p * 2 * per_block, 2 * per_block)
                        row_ref[first + part, :, place] = jnp.where(
                            lane < per_block, even, pltpu.roll(odd, per_block, 1)
                        )
                        row_ref[first + part + 2, :, place] = jnp.where(
                            lane < per_block, pltpu.roll(even, per_block, 1), odd
                        )
                rows = pl.ds(first, 4)
                copies.append(
                    pltpu.make_async_copy(row_ref.at[rows], out_ref.at[rows], sems.at[len(copies)])
                )
                copies[-1].start()
        for copy in copies:
            copy.wait()


def fetch(from_ref, to_ref, sem):
    copy = pltpu.make_async_copy(from_ref, to_ref, sem)
    copy.start()
    copy.wait()


def route_second(*refs):
    ab0_ref, o1_ref, o2_ref, stack_ref, both_ref, mixed_ref = refs[3:]
    core = lax.axis_index("core")
    for slot in range(6):
        stack_ref[slot] = refs[slot][...]
    both_ref[0] = o1_ref[...]
    both_ref[1] = o2_ref[...]

    @pl.when(core == 0)
    def _():
        mixed_ref[...] = o2_ref[...]

    @pl.when(core != 0)
    def _():
        mixed_ref[...] = ab0_ref[...]


def route_third(ab1_ref, o3_ref, ab2_ref, a12_ref, b12_ref, stack_ref):
    for slot, ref in enumerate((ab1_ref, ab2_ref, o3_ref)):
        stack_ref[slot] = ref[...]
    stack_ref[3:5] = a12_ref[...]
    stack_ref[5:7] = b12_ref[...]


def route_last(a3_ref, ab3_ref, stack_ref):
    stack_ref[0] = a3_ref[...]
    stack_ref[1] = ab3_ref[...]


def left_slots(names):
    needed = set()
    for _, kind, dz in names:
        needed |= {"O": {(0, dz)}, "AB": {(1, dz)}}.get(kind, {(0, dz), (1, dz)})
    return sorted(needed, key=lambda slot: (slot[1], slot[0]))


def swap_in_windows(own, weights, share):
    shape = tuple(lax.axis_size(name) for name in AXES)
    columns, per_block = 4, own.shape[2]
    depth = own.size // (columns * per_block)
    spins = share // (2 * columns)
    tall, wide = 2 * spins * per_block, columns * per_block
    strides = (shape[1] * shape[2] * shape[3], shape[2] * shape[3], shape[3], 1)

    def move(array, target):
        pairs = []
        for p in range(shape[0]):
            for c in range(shape[1]):
                for z in range(shape[2]):
                    for y in range(shape[3]):
                        ends = (p, c, z, y), target(p, c, z, y)
                        pairs.append(
                            tuple(sum(a * b for a, b in zip(end, strides)) for end in ends)
                        )
        return lax.ppermute(array, AXES, pairs)

    def hop_a(array):
        return move(array, lambda p, c, z, y: (p ^ 1, c, z, y) if c == 0 else (p, c, z, y ^ 1))

    def hop_b(array):
        return move(array, lambda p, c, z, y: (p, c, z, y ^ 1) if c == 0 else (p ^ 1, c, z, y))

    def hop_ab(array):
        return move(array, lambda p, c, z, y: (p ^ 1, c, z, y ^ 1))

    def hop_z(array, by):
        return move(array, lambda p, c, z, y: (p, c, z ^ by, y))

    def hop_mixed(array):
        return move(
            array, lambda p, c, z, y: (p ^ 1, c, z, y ^ 1) if c == 0 else (p, c, z ^ 2, y)
        )

    def swap(array):
        return move(array, lambda p, c, z, y: (p, c ^ 1, z, y))

    arrays = {}
    where = {}

    def put(key, array, side, kinds):
        arrays[key] = array
        for slot, (kind, dz) in enumerate(kinds):
            where[(side, kind, dz)] = (key, slot if len(kinds) > 1 else None)

    def near(kind, dz):
        key, slot = where[("near", kind, dz)]
        return arrays[key] if slot is None else arrays[key][slot]

    def add(names, totals, keep=None, left=None, last=False, weight=1):
        given = left is not None
        slots, left = left if given else (keep or left_slots(names), None)
        uses = list(names)
        for dy, dz in [] if given else slots:
            uses += [("near", kind, dz) for kind in (("A", "B") if dy else ("O",))]
        keys = sorted({where[name][0] for name in uses})
        places = {name: (keys.index(where[name][0]), where[name][1]) for name in uses}
        operands = [weights] + [arrays[key] for key in keys]
        operands += [each for each in (left, totals) if each is not None]
        total_shape = (2, 2, tall, wide)
        left_shape = (len(slots), 2 * tall, depth)
        block = pl.BlockSpec(memory_space=pltpu.VMEM)
        out_shape = [jax.ShapeDtypeStruct(total_shape, jnp.float32)]
        scratch = [] if given or keep else [pltpu.VMEM(left_shape, jnp.bfloat16)]
        out_specs = [block]
        if last:
            out_shape = [jax.ShapeDtypeStruct((share, per_block, 4 * per_block), jnp.float32)]
            out_specs = [pl.BlockSpec(memory_space=pl.ANY)]
            scratch = [
                pltpu.VMEM(total_shape[1:], jnp.float32),
                pltpu.VMEM(out_shape[0].shape, jnp.float32),
                pltpu.SemaphoreType.DMA((spins * columns // 2,)),
            ]
        if keep:
            out_shape.append(jax.ShapeDtypeStruct(left_shape, jnp.bfloat16))
            out_specs.append(block)
        out = pl.pallas_call(
            functools.partial(
                add_shards, tuple(names), places, slots, totals is not None, given, last, share
            ),
            in_specs=[block] * len(operands),
            out_specs=out_specs,
            out_shape=out_shape,
            scratch_shapes=scratch,
            compiler_params=pltpu.CompilerParams(vmem_limit_bytes=40 * 1024 * 1024),
            cost_estimate=pl.CostEstimate(
                flops=4 * tall * wide * depth * len(names) * weight,
                bytes_accessed=wide * depth * 2 * len(names) + 8 * 4 * tall * wide,
                transcendentals=0,
            ),
        )(*operands)
        return (out[0], (slots, out[1])) if keep else out[0]

    def fence(totals):
        nonlocal arrays
        arrays, totals = lax.optimization_barrier((arrays, totals))
        return totals

    put("1a", hop_z(own, 2), "near", [("O", 2)])
    put("1b", hop_a(own), "near", [("A", 0)])
    put("1c", hop_z(own, 1), "near", [("O", 1)])
    put("1d", hop_b(own), "near", [("B", 0)])
    put("1e", hop_b(near("A", 0)), "near", [("AB", 0)])
    held = pl.pallas_call(
        fetch,
        in_specs=[pl.BlockSpec(memory_space=pl.ANY)],
        out_specs=pl.BlockSpec(memory_space=pltpu.VMEM),
        out_shape=jax.ShapeDtypeStruct(own.shape, own.dtype),
        scratch_shapes=[pltpu.SemaphoreType.DMA],
    )(own)
    put("9", held, "near", [("O", 0)])
    weights = fence(weights)

    def route(kernel, operands, counts, weight=0):
        block = pl.BlockSpec(memory_space=pltpu.VMEM)
        shapes = [(count,) * (count > 1) + own.shape for count in counts]
        routed = pl.pallas_call(
            kernel,
            in_specs=[block] * len(operands),
            out_specs=[block] * len(counts),
            out_shape=[jax.ShapeDtypeStruct(shape, own.dtype) for shape in shapes],
            compiler_params=pltpu.CompilerParams(vmem_limit_bytes=24 * 1024 * 1024),
            cost_estimate=pl.CostEstimate(flops=weight, bytes_accessed=0, transcendentals=0),
        )(*operands)
        return fence(routed)

    first = [("O", 0), ("A", 0), ("B", 0), ("AB", 0), ("O", 1), ("O", 2)]
    second = [("AB", 1), ("AB", 2), ("O", 3), ("A", 1), ("A", 2), ("B", 1), ("B", 2)]
    third = [("A", 3), ("AB", 3), ("B", 3)]
    stack, both, mixed = route(route_second, [near(*kind) for kind in first], (6, 2, 1))
    totals = add([("near", *kind) for kind in first], None)
    o3, ab2, a12, b12 = hop_z(near("O", 2), 1), hop_mixed(mixed), hop_a(both), hop_b(both)
    put("2a", swap(stack), "far", first)
    totals = fence(totals)

    put("2b", hop_z(near("AB", 0), 1), "near", [("AB", 1)])
    totals = add([("far", *kind) for kind in first], totals)
    ab1 = arrays.pop("2b")
    put("2c", o3, "near", [("O", 3)])
    put("2d", ab2, "near", [("AB", 2)])
    totals = fence(totals)

    ab3, a3, b3 = hop_z(near("AB", 2), 1), hop_a(near("O", 3)), hop_b(near("O", 3))
    totals = add([("near", "O", 3)], totals, weight=45)
    arrays["2b"] = ab1
    put("2e", a12, "near", [("A", 1), ("A", 2)])
    put("2f", b12, "near", [("B", 1), ("B", 2)])
    totals = fence(totals)

    keys = ("2b", "2c", "2d", "2e", "2f")
    (stack,) = route(route_third, [arrays[key] for key in keys], (7,))
    far2 = swap(stack)
    names = [("near", *kind) for kind in second if kind != ("O", 3)]
    totals = add(names, totals)
    a3, ab3, totals = lax.optimization_barrier((a3, ab3, totals))
    (stack,) = route(route_last, [a3, ab3], (2,), weight=10**11)
    put("3a", stack, "near", third[:2])
    stack = swap(stack)
    put("3d", far2, "far", second)
    totals = add([("far", *kind) for kind in second], totals)
    put("3b", b3, "near", third[2:])
    totals = fence(totals)

    put("4a", stack, "far", third[:2])
    far3 = swap(near("B", 3))
    names = [("near", *kind) for kind in third]
    totals, (slots, left) = add(names, totals, keep=left_slots(names))
    put("4b", far3, "far", third[2:])
    totals, left = fence((totals, left))
    return add([("far", *kind) for kind in third], totals, left=(slots, left), last=True)


def add_terms(place_ref, weights_ref, left_ref, right_ref, field_ref):
    @pl.when(pl.program_id(0) == 0)
    def _():
        field_ref[...] = jnp.zeros_like(field_ref)

    spins = left_ref.shape[2]
    groups, columns, per_block, depth = right_ref.shape[0], *right_ref.shape[2:]
    owns = [left_ref[0, 0, spin] for spin in range(spins)]
    left = left_sides(owns, weights_ref[0])
    for column in range(columns):
        right = right_ref[:, 0, column].reshape(groups * per_block, depth)
        term = product(left, right)
        for part in range(2):
            for spin in range(spins):
                start = (part * spins + spin) * per_block
                field_ref[(spin * columns + column) * 2 + part] += term[start : start + per_block]


def gather_whole(packed, place, weights, share):
    groups, _, deep, flat = (lax.axis_size(name) for name in AXES)
    sites = deep * flat
    _, per_block, depth = packed.shape
    columns = min(4, share // 2)
    spins = share // (2 * columns)
    near = lax.all_gather(packed, ("pair", "deep", "flat"))
    near = near.reshape(groups, sites, 4, per_block, depth)
    far = lax.ppermute(near, "core", [(0, 1), (1, 0)])
    wide = groups * per_block

    def half(right):
        return pl.pallas_call(
            add_terms,
            grid_spec=pltpu.PrefetchScalarGridSpec(
                num_scalar_prefetch=1,
                grid=(sites,),
                in_specs=[
                    pl.BlockSpec((1, 2, weights.shape[2]), lambda m, place: (m, 0, 0)),
                    pl.BlockSpec(
                        (1, 1, spins, per_block, depth),
                        lambda m, place: (place[0], m, place[4] // spins, 0, 0),
                    ),
                    pl.BlockSpec(
                        (groups, 1, columns, per_block, depth),
                        lambda m, place: (0, m, place[6] // columns, 0, 0),
                    ),
                ],
                out_specs=pl.BlockSpec((share, per_block, wide), lambda m, place: (0, 0, 0)),
            ),
            out_shape=jax.ShapeDtypeStruct((share, per_block, wide), jnp.float32),
            compiler_params=pltpu.CompilerParams(vmem_limit_bytes=40 * 1024 * 1024),
        )(place, weights, near, right)

    sides = [half(right).reshape(share, per_block, groups, per_block) for right in (near, far)]
    first = lax.axis_index("core") == 0
    even, odd = (jnp.where(first, a, b) for a, b in (sides, sides[::-1]))
    return jnp.stack([even, odd], 3).reshape(share, per_block, 2 * wide)


def shards(modes, momenta):
    groups, _, deep, flat = (lax.axis_size(name) for name in AXES)
    sites = deep * flat
    slots, steps, per_block, spin_colour, site_count = modes.shape
    share = steps * momenta.shape[0] * 32 // sites
    owned = (lax.axis_index("deep") * flat + lax.axis_index("flat")) * (share // 2)
    place = [lax.axis_index(name) for name in AXES]
    place = jnp.stack(place + [owned // 4 % 4, jnp.int32(flat), owned % 4]).astype(jnp.int32)

    mine = lax.dynamic_slice_in_dim(momenta, owned // 16, 1, 0)
    weights = phase_table(mine, jnp.int32(0), sites * site_count, LEXT)[0]
    weights = jnp.transpose(weights.reshape(2, sites, site_count), (1, 0, 2))

    if (groups, deep, flat) == (2, 4, 2) and steps == 1 and share in (8, 16, 32):
        own = jnp.transpose(modes[:, 0], (0, 2, 1, 3))
        return swap_in_windows(own, weights, share)
    packed = jnp.transpose(modes.reshape(slots, per_block, 4, 3, site_count), (2, 1, 0, 3, 4))
    packed = packed.reshape(4, per_block, slots * 3 * site_count)
    return gather_whole(packed, place, weights, share)


def solution(mesh):
    count, sites = mesh.shape["blk"], mesh.shape["site"]
    flat = 2 ** (int(math.log2(sites)) // 2)
    split = Mesh(mesh.devices.reshape(count // 2, 2, sites // flat, flat), AXES)
    placed = (P(None, None, ("pair", "core"), None, ("deep", "flat")), P())
    return jax.shard_map(
        shards,
        mesh=split,
        in_specs=placed,
        out_specs=P(("deep", "flat"), ("pair", "core"), None),
        check_vma=False,
    )
```

```python
import functools
import math

import jax
import jax.numpy as jnp
from jax import lax
from jax.experimental import pallas as pl
from jax.experimental.pallas import tpu as pltpu
from jax.sharding import Mesh, PartitionSpec as P

LEXT = 48

TWO_PI = 2.0 * math.pi

AXES = ("pair", "core", "deep", "flat")


def phase_table(momenta, first_site, site_count, extent):
    flat = first_site + jnp.arange(site_count, dtype=jnp.int32)
    coords = jnp.stack([flat % extent, flat // extent % extent, flat // (extent * extent)], 0)
    turns = jnp.mod(jnp.sum(momenta[:, :, None] * coords[None, :, :], axis=1), extent)
    angle = turns.astype(jnp.float32) * (TWO_PI / extent)
    return jnp.stack([jnp.cos(angle), jnp.sin(angle)], 1)


def left_sides(owns, weights):
    depth = owns[0].shape[1]
    half = depth // 2
    cosine = jnp.tile(weights[0:1], (1, depth // weights.shape[1]))
    sine = jnp.tile(weights[1:2], (1, depth // weights.shape[1]))
    cosine_rows = [[], []]
    sine_rows = [[], []]
    for own in owns:
        own = own.astype(jnp.float32)
        by_cos = (own * cosine).astype(jnp.bfloat16)
        by_sin = (own * sine).astype(jnp.bfloat16)
        cosine_rows[0].append(by_cos)
        cosine_rows[1].append(jnp.concatenate([-by_cos[:, half:], by_cos[:, :half]], 1))
        sine_rows[0].append(jnp.concatenate([-by_sin[:, half:], by_sin[:, :half]], 1))
        sine_rows[1].append(-by_sin)
    return jnp.concatenate(cosine_rows[0] + cosine_rows[1] + sine_rows[0] + sine_rows[1], 0)


def product(left, right):
    dims = (((1,), (1,)), ((), ()))
    terms = lax.dot_general(left, right, dims, preferred_element_type=jnp.float32)
    half = terms.shape[0] // 2
    return terms[:half] + terms[half:]


def add_shards(names, where, slots, has_totals, given, last, share, weights_ref, *refs):
    refs = list(refs)
    if last:
        sems, row_ref, far_ref = (refs.pop() for _ in range(3))
    left_ref = None if given else refs.pop()
    out_ref = refs.pop()
    totals_in = refs.pop() if has_totals else None
    left_ref = refs.pop() if given else left_ref

    def shard(name):
        index, slot = where[name]
        return refs[index] if slot is None else refs[index].at[slot]

    def spin_rows(name, spin):
        ref = shard(name)
        tiles = [ref[part, spin * colours + x] for part in range(2) for x in range(colours)]
        return jnp.concatenate(tiles, 1)

    pair, core, level, beside = (lax.axis_index(name) for name in AXES)
    flat = lax.axis_size("flat")
    _, spin_colour, per_block, _ = shard(names[0]).shape
    columns, colours = 4, spin_colour // 4
    first_s = lax.rem(lax.div((level * flat + beside) * (share // 2), 4), 4)
    spins = left_ref.shape[1] // (4 * per_block)

    if last:
        far_ref[...] = totals_in[1]
    elif has_totals:
        out_ref[...] = totals_in[...]
    else:
        out_ref[...] = jnp.zeros_like(out_ref)
    if not given:
        for slot, (dy, dz) in enumerate(slots):
            site = jnp.bitwise_xor(level, dz) * flat + jnp.bitwise_xor(beside, dy)
            if dy == 0:
                owns = [spin_rows(("near", "O", dz), first_s + s) for s in range(spins)]
            else:
                owns = [
                    jnp.where(
                        core == 0,
                        spin_rows(("near", "B", dz), first_s + s),
                        spin_rows(("near", "A", dz), first_s + s),
                    )
                    for s in range(spins)
                ]
            left_ref[slot] = left_sides(owns, weights_ref[site])

    for side, kind, dz in names:
        right = jnp.concatenate([spin_rows((side, kind, dz), r) for r in range(columns)], 0)
        turn = core if side == "near" else 1 - core
        dx, dy = {"O": (0, 0), "A": (1 - turn, turn), "B": (turn, 1 - turn), "AB": (1, 1)}[kind]
        if kind in ("O", "AB"):
            slot = slots.index((dy, dz))
        else:
            slot = slots.index((0, dz)) + dy
        term = product(left_ref[slot], right)
        if last:
            far_ref[dx] += term
        else:
            out_ref[0 if side == "near" else 1, dx] += term

    if last:
        lane = lax.broadcasted_iota(jnp.int32, (per_block, 2 * per_block), 1)
        copies = []
        for spin in range(spins):
            for column in range(0, columns, 2):
                first = (spin * columns + column) * 2
                across = pl.ds(column * per_block, 2 * per_block)
                for part in range(2):
                    top = (part * spins + spin) * per_block
                    for p in range(2):
                        dx = jnp.bitwise_xor(pair, p)
                        near = totals_in[0, dx, pl.ds(top, per_block), across]
                        far = far_ref[dx, pl.ds(top, per_block), across]
                        even = jnp.where(core == 0, near, far)
                        odd = jnp.where(core == 0, far, near)
                        place = pl.ds(p * 2 * per_block, 2 * per_block)
                        row_ref[first + part, :, place] = jnp.where(
                            lane < per_block, even, pltpu.roll(odd, per_block, 1)
                        )
                        row_ref[first + part + 2, :, place] = jnp.where(
                            lane < per_block, pltpu.roll(even, per_block, 1), odd
                        )
                rows = pl.ds(first, 4)
                copies.append(
                    pltpu.make_async_copy(row_ref.at[rows], out_ref.at[rows], sems.at[len(copies)])
                )
                copies[-1].start()
        for copy in copies:
            copy.wait()


def route_second(*refs):
    ab0_ref, o1_ref, o2_ref, stack_ref, both_ref, mixed_ref = refs[2:]
    core = lax.axis_index("core")
    for slot in range(5):
        stack_ref[slot] = refs[slot][...]
    both_ref[0] = o1_ref[...]
    both_ref[1] = o2_ref[...]

    @pl.when(core == 0)
    def _():
        mixed_ref[...] = o2_ref[...]

    @pl.when(core != 0)
    def _():
        mixed_ref[...] = ab0_ref[...]


def route_third(ab1_ref, o3_ref, ab2_ref, a12_ref, b12_ref, stack_ref):
    for slot, ref in enumerate((ab1_ref, ab2_ref, o3_ref)):
        stack_ref[slot] = ref[...]
    stack_ref[3:5] = a12_ref[...]
    stack_ref[5:7] = b12_ref[...]


def route_last(a3_ref, ab3_ref, stack_ref):
    stack_ref[0] = a3_ref[...]
    stack_ref[1] = ab3_ref[...]


def left_slots(names):
    needed = set()
    for _, kind, dz in names:
        needed |= {"O": {(0, dz)}, "AB": {(1, dz)}}.get(kind, {(0, dz), (1, dz)})
    return sorted(needed, key=lambda slot: (slot[1], slot[0]))


def swap_in_windows(own, weights, share):
    shape = tuple(lax.axis_size(name) for name in AXES)
    columns, per_block = 4, own.shape[2]
    depth = own.size // (columns * per_block)
    spins = share // (2 * columns)
    tall, wide = 2 * spins * per_block, columns * per_block
    strides = (shape[1] * shape[2] * shape[3], shape[2] * shape[3], shape[3], 1)

    def move(array, target):
        pairs = []
        for p in range(shape[0]):
            for c in range(shape[1]):
                for z in range(shape[2]):
                    for y in range(shape[3]):
                        ends = (p, c, z, y), target(p, c, z, y)
                        pairs.append(
                            tuple(sum(a * b for a, b in zip(end, strides)) for end in ends)
                        )
        return lax.ppermute(array, AXES, pairs)

    def hop_a(array):
        return move(array, lambda p, c, z, y: (p ^ 1, c, z, y) if c == 0 else (p, c, z, y ^ 1))

    def hop_b(array):
        return move(array, lambda p, c, z, y: (p, c, z, y ^ 1) if c == 0 else (p ^ 1, c, z, y))

    def hop_ab(array):
        return move(array, lambda p, c, z, y: (p ^ 1, c, z, y ^ 1))

    def hop_z(array, by):
        return move(array, lambda p, c, z, y: (p, c, z ^ by, y))

    def hop_mixed(array):
        return move(
            array, lambda p, c, z, y: (p ^ 1, c, z, y ^ 1) if c == 0 else (p, c, z ^ 2, y)
        )

    def swap(array):
        return move(array, lambda p, c, z, y: (p, c ^ 1, z, y))

    arrays = {}
    where = {}

    def put(key, array, side, kinds):
        arrays[key] = array
        for slot, (kind, dz) in enumerate(kinds):
            where[(side, kind, dz)] = (key, slot if len(kinds) > 1 else None)

    def near(kind, dz):
        key, slot = where[("near", kind, dz)]
        return arrays[key] if slot is None else arrays[key][slot]

    def add(names, totals, keep=None, left=None, last=False, weight=1):
        given = left is not None
        slots, left = left if given else (keep or left_slots(names), None)
        uses = list(names)
        for dy, dz in [] if given else slots:
            uses += [("near", kind, dz) for kind in (("A", "B") if dy else ("O",))]
        keys = sorted({where[name][0] for name in uses})
        places = {name: (keys.index(where[name][0]), where[name][1]) for name in uses}
        operands = [weights] + [arrays[key] for key in keys]
        operands += [each for each in (left, totals) if each is not None]
        total_shape = (2, 2, tall, wide)
        left_shape = (len(slots), 2 * tall, depth)
        block = pl.BlockSpec(memory_space=pltpu.VMEM)
        out_shape = [jax.ShapeDtypeStruct(total_shape, jnp.float32)]
        scratch = [] if given or keep else [pltpu.VMEM(left_shape, jnp.bfloat16)]
        out_specs = [block]
        if last:
            out_shape = [jax.ShapeDtypeStruct((share, per_block, 4 * per_block), jnp.float32)]
            out_specs = [pl.BlockSpec(memory_space=pl.ANY)]
            scratch = [
                pltpu.VMEM(total_shape[1:], jnp.float32),
                pltpu.VMEM(out_shape[0].shape, jnp.float32),
                pltpu.SemaphoreType.DMA((spins * columns // 2,)),
            ]
        if keep:
            out_shape.append(jax.ShapeDtypeStruct(left_shape, jnp.bfloat16))
            out_specs.append(block)
        out = pl.pallas_call(
            functools.partial(
                add_shards, tuple(names), places, slots, totals is not None, given, last, share
            ),
            in_specs=[block] * len(operands),
            out_specs=out_specs,
            out_shape=out_shape,
            scratch_shapes=scratch,
            compiler_params=pltpu.CompilerParams(vmem_limit_bytes=40 * 1024 * 1024),
            cost_estimate=pl.CostEstimate(
                flops=4 * tall * wide * depth * len(names) * weight,
                bytes_accessed=wide * depth * 2 * len(names) + 8 * 4 * tall * wide,
                transcendentals=0,
            ),
        )(*operands)
        return (out[0], (slots, out[1])) if keep else out[0]

    def fence(totals):
        nonlocal arrays
        arrays, totals = lax.optimization_barrier((arrays, totals))
        return totals

    put("1a", hop_z(own, 2), "near", [("O", 2)])
    put("1b", hop_a(own), "near", [("A", 0)])
    put("1c", hop_z(own, 1), "near", [("O", 1)])
    put("1d", hop_b(own), "near", [("B", 0)])
    put("1e", hop_b(near("A", 0)), "near", [("AB", 0)])
    put("1f", swap(own), "far", [("O", 0)])
    put("9", own, "near", [("O", 0)])
    weights = fence(weights)

    def route(kernel, operands, counts, weight=0):
        block = pl.BlockSpec(memory_space=pltpu.VMEM)
        shapes = [(count,) * (count > 1) + own.shape for count in counts]
        routed = pl.pallas_call(
            kernel,
            in_specs=[block] * len(operands),
            out_specs=[block] * len(counts),
            out_shape=[jax.ShapeDtypeStruct(shape, own.dtype) for shape in shapes],
            compiler_params=pltpu.CompilerParams(vmem_limit_bytes=24 * 1024 * 1024),
            cost_estimate=pl.CostEstimate(flops=weight, bytes_accessed=0, transcendentals=0),
        )(*operands)
        return fence(routed)

    first = [("O", 0), ("A", 0), ("B", 0), ("AB", 0), ("O", 1), ("O", 2)]
    second = [("AB", 1), ("AB", 2), ("O", 3), ("A", 1), ("A", 2), ("B", 1), ("B", 2)]
    third = [("A", 3), ("AB", 3), ("B", 3)]
    stack, both, mixed = route(route_second, [near(*kind) for kind in first[1:]], (5, 2, 1))
    totals = add([("near", *kind) for kind in first], None)
    o3, ab2, a12, b12 = hop_z(near("O", 2), 1), hop_mixed(mixed), hop_a(both), hop_b(both)
    put("2a", swap(stack), "far", first[1:])
    totals = fence(totals)

    put("2b", hop_z(near("AB", 0), 1), "near", [("AB", 1)])
    totals = add([("far", *kind) for kind in first], totals)
    ab1 = arrays.pop("2b")
    put("2c", o3, "near", [("O", 3)])
    put("2d", ab2, "near", [("AB", 2)])
    totals = fence(totals)

    ab3, a3, b3 = hop_z(near("AB", 2), 1), hop_a(near("O", 3)), hop_b(near("O", 3))
    totals = add([("near", "O", 3)], totals, weight=45)
    arrays["2b"] = ab1
    put("2e", a12, "near", [("A", 1), ("A", 2)])
    put("2f", b12, "near", [("B", 1), ("B", 2)])
    totals = fence(totals)

    keys = ("2b", "2c", "2d", "2e", "2f")
    (stack,) = route(route_third, [arrays[key] for key in keys], (7,))
    far2 = swap(stack)
    names = [("near", *kind) for kind in second if kind != ("O", 3)]
    totals = add(names, totals)
    a3, ab3, totals = lax.optimization_barrier((a3, ab3, totals))
    (stack,) = route(route_last, [a3, ab3], (2,), weight=10**11)
    put("3a", stack, "near", third[:2])
    stack = swap(stack)
    put("3d", far2, "far", second)
    totals = add([("far", *kind) for kind in second], totals)
    put("3b", b3, "near", third[2:])
    totals = fence(totals)

    put("4a", stack, "far", third[:2])
    far3 = swap(near("B", 3))
    names = [("near", *kind) for kind in third]
    totals, (slots, left) = add(names, totals, keep=left_slots(names))
    put("4b", far3, "far", third[2:])
    totals, left = fence((totals, left))
    return add([("far", *kind) for kind in third], totals, left=(slots, left), last=True)


def add_terms(place_ref, weights_ref, left_ref, right_ref, field_ref):
    @pl.when(pl.program_id(0) == 0)
    def _():
        field_ref[...] = jnp.zeros_like(field_ref)

    spins = left_ref.shape[2]
    groups, columns, per_block, depth = right_ref.shape[0], *right_ref.shape[2:]
    owns = [left_ref[0, 0, spin] for spin in range(spins)]
    left = left_sides(owns, weights_ref[0])
    for column in range(columns):
        right = right_ref[:, 0, column].reshape(groups * per_block, depth)
        term = product(left, right)
        for part in range(2):
            for spin in range(spins):
                start = (part * spins + spin) * per_block
                field_ref[(spin * columns + column) * 2 + part] += term[start : start + per_block]


def gather_whole(packed, place, weights, share):
    groups, _, deep, flat = (lax.axis_size(name) for name in AXES)
    sites = deep * flat
    _, per_block, depth = packed.shape
    columns = min(4, share // 2)
    spins = share // (2 * columns)
    near = lax.all_gather(packed, ("pair", "deep", "flat"))
    near = near.reshape(groups, sites, 4, per_block, depth)
    far = lax.ppermute(near, "core", [(0, 1), (1, 0)])
    wide = groups * per_block

    def half(right):
        return pl.pallas_call(
            add_terms,
            grid_spec=pltpu.PrefetchScalarGridSpec(
                num_scalar_prefetch=1,
                grid=(sites,),
                in_specs=[
                    pl.BlockSpec((1, 2, weights.shape[2]), lambda m, place: (m, 0, 0)),
                    pl.BlockSpec(
                        (1, 1, spins, per_block, depth),
                        lambda m, place: (place[0], m, place[4] // spins, 0, 0),
                    ),
                    pl.BlockSpec(
                        (groups, 1, columns, per_block, depth),
                        lambda m, place: (0, m, place[6] // columns, 0, 0),
                    ),
                ],
                out_specs=pl.BlockSpec((share, per_block, wide), lambda m, place: (0, 0, 0)),
            ),
            out_shape=jax.ShapeDtypeStruct((share, per_block, wide), jnp.float32),
            compiler_params=pltpu.CompilerParams(vmem_limit_bytes=40 * 1024 * 1024),
        )(place, weights, near, right)

    sides = [half(right).reshape(share, per_block, groups, per_block) for right in (near, far)]
    first = lax.axis_index("core") == 0
    even, odd = (jnp.where(first, a, b) for a, b in (sides, sides[::-1]))
    return jnp.stack([even, odd], 3).reshape(share, per_block, 2 * wide)


def shards(modes, momenta):
    groups, _, deep, flat = (lax.axis_size(name) for name in AXES)
    sites = deep * flat
    slots, steps, per_block, spin_colour, site_count = modes.shape
    share = steps * momenta.shape[0] * 32 // sites
    owned = (lax.axis_index("deep") * flat + lax.axis_index("flat")) * (share // 2)
    place = [lax.axis_index(name) for name in AXES]
    place = jnp.stack(place + [owned // 4 % 4, jnp.int32(flat), owned % 4]).astype(jnp.int32)

    mine = lax.dynamic_slice_in_dim(momenta, owned // 16, 1, 0)
    weights = phase_table(mine, jnp.int32(0), sites * site_count, LEXT)[0]
    weights = jnp.transpose(weights.reshape(2, sites, site_count), (1, 0, 2))

    if (groups, deep, flat) == (2, 4, 2) and steps == 1 and share in (8, 16, 32):
        own = jnp.transpose(modes[:, 0], (0, 2, 1, 3))
        return swap_in_windows(own, weights, share)
    packed = jnp.transpose(modes.reshape(slots, per_block, 4, 3, site_count), (2, 1, 0, 3, 4))
    packed = packed.reshape(4, per_block, slots * 3 * site_count)
    return gather_whole(packed, place, weights, share)


def solution(mesh):
    count, sites = mesh.shape["blk"], mesh.shape["site"]
    flat = 2 ** (int(math.log2(sites)) // 2)
    split = Mesh(mesh.devices.reshape(count // 2, 2, sites // flat, flat), AXES)
    placed = (P(None, None, ("pair", "core"), None, ("deep", "flat")), P())
    return jax.shard_map(
        shards,
        mesh=split,
        in_specs=placed,
        out_specs=P(("deep", "flat"), ("pair", "core"), None),
        check_vma=False,
    )
```

```python
import functools
import math

import jax
import jax.numpy as jnp
from jax import lax
from jax.experimental import pallas as pl
from jax.experimental.pallas import tpu as pltpu
from jax.sharding import Mesh, PartitionSpec as P

LEXT = 48

TWO_PI = 2.0 * math.pi

AXES = ("pair", "core", "deep", "flat")


def phase_table(momenta, first_site, site_count, extent):
    flat = first_site + jnp.arange(site_count, dtype=jnp.int32)
    coords = jnp.stack([flat % extent, flat // extent % extent, flat // (extent * extent)], 0)
    turns = jnp.mod(jnp.sum(momenta[:, :, None] * coords[None, :, :], axis=1), extent)
    angle = turns.astype(jnp.float32) * (TWO_PI / extent)
    return jnp.stack([jnp.cos(angle), jnp.sin(angle)], 1)


def left_sides(owns, weights):
    depth = owns[0].shape[1]
    half = depth // 2
    cosine = jnp.tile(weights[0:1], (1, depth // weights.shape[1]))
    sine = jnp.tile(weights[1:2], (1, depth // weights.shape[1]))
    cosine_rows = [[], []]
    sine_rows = [[], []]
    for own in owns:
        own = own.astype(jnp.float32)
        by_cos = (own * cosine).astype(jnp.bfloat16)
        by_sin = (own * sine).astype(jnp.bfloat16)
        cosine_rows[0].append(by_cos)
        cosine_rows[1].append(jnp.concatenate([-by_cos[:, half:], by_cos[:, :half]], 1))
        sine_rows[0].append(jnp.concatenate([-by_sin[:, half:], by_sin[:, :half]], 1))
        sine_rows[1].append(-by_sin)
    return jnp.concatenate(cosine_rows[0] + cosine_rows[1] + sine_rows[0] + sine_rows[1], 0)


def product(left, right):
    dims = (((1,), (1,)), ((), ()))
    terms = lax.dot_general(left, right, dims, preferred_element_type=jnp.float32)
    half = terms.shape[0] // 2
    return terms[:half] + terms[half:]


def add_shards(names, where, slots, has_totals, given, last, share, weights_ref, *refs):
    refs = list(refs)
    if last:
        sems, row_ref, far_ref = (refs.pop() for _ in range(3))
    left_ref = None if given else refs.pop()
    out_ref = refs.pop()
    totals_in = refs.pop() if has_totals else None
    left_ref = refs.pop() if given else left_ref

    def shard(name):
        index, slot = where[name]
        return refs[index] if slot is None else refs[index].at[slot]

    def spin_rows(name, spin):
        ref = shard(name)
        tiles = [ref[part, spin * colours + x] for part in range(2) for x in range(colours)]
        return jnp.concatenate(tiles, 1)

    pair, core, level, beside = (lax.axis_index(name) for name in AXES)
    flat = lax.axis_size("flat")
    _, spin_colour, per_block, _ = shard(names[0]).shape
    columns, colours = 4, spin_colour // 4
    first_s = lax.rem(lax.div((level * flat + beside) * (share // 2), 4), 4)
    spins = left_ref.shape[1] // (4 * per_block)

    if last:
        far_ref[...] = totals_in[1]
    elif has_totals:
        out_ref[...] = totals_in[...]
    else:
        out_ref[...] = jnp.zeros_like(out_ref)
    if not given:
        for slot, (dy, dz) in enumerate(slots):
            site = jnp.bitwise_xor(level, dz) * flat + jnp.bitwise_xor(beside, dy)
            if dy == 0:
                owns = [spin_rows(("near", "O", dz), first_s + s) for s in range(spins)]
            else:
                owns = [
                    jnp.where(
                        core == 0,
                        spin_rows(("near", "B", dz), first_s + s),
                        spin_rows(("near", "A", dz), first_s + s),
                    )
                    for s in range(spins)
                ]
            left_ref[slot] = left_sides(owns, weights_ref[site])

    for side, kind, dz in names:
        right = jnp.concatenate([spin_rows((side, kind, dz), r) for r in range(columns)], 0)
        turn = core if side == "near" else 1 - core
        dx, dy = {"O": (0, 0), "A": (1 - turn, turn), "B": (turn, 1 - turn), "AB": (1, 1)}[kind]
        if kind in ("O", "AB"):
            slot = slots.index((dy, dz))
        else:
            slot = slots.index((0, dz)) + dy
        term = product(left_ref[slot], right)
        if last:
            far_ref[dx] += term
        else:
            out_ref[0 if side == "near" else 1, dx] += term

    if last:
        lane = lax.broadcasted_iota(jnp.int32, (per_block, 2 * per_block), 1)
        copies = []
        for spin in range(spins):
            for column in range(0, columns, 2):
                first = (spin * columns + column) * 2
                across = pl.ds(column * per_block, 2 * per_block)
                for part in range(2):
                    top = (part * spins + spin) * per_block
                    for p in range(2):
                        dx = jnp.bitwise_xor(pair, p)
                        near = totals_in[0, dx, pl.ds(top, per_block), across]
                        far = far_ref[dx, pl.ds(top, per_block), across]
                        even = jnp.where(core == 0, near, far)
                        odd = jnp.where(core == 0, far, near)
                        place = pl.ds(p * 2 * per_block, 2 * per_block)
                        row_ref[first + part, :, place] = jnp.where(
                            lane < per_block, even, pltpu.roll(odd, per_block, 1)
                        )
                        row_ref[first + part + 2, :, place] = jnp.where(
                            lane < per_block, pltpu.roll(even, per_block, 1), odd
                        )
                rows = pl.ds(first, 4)
                copies.append(
                    pltpu.make_async_copy(row_ref.at[rows], out_ref.at[rows], sems.at[len(copies)])
                )
                copies[-1].start()
        for copy in copies:
            copy.wait()


def route_second(*refs):
    ab0_ref, o1_ref, o2_ref, stack_ref, both_ref, mixed_ref = refs[2:]
    core = lax.axis_index("core")
    for slot in range(5):
        stack_ref[slot] = refs[slot][...]
    both_ref[0] = o1_ref[...]
    both_ref[1] = o2_ref[...]

    @pl.when(core == 0)
    def _():
        mixed_ref[...] = o2_ref[...]

    @pl.when(core != 0)
    def _():
        mixed_ref[...] = ab0_ref[...]


def route_third(*refs):
    stack_ref = refs[-1]
    for slot in range(5):
        stack_ref[slot] = refs[slot][...]
    stack_ref[5:7] = refs[5][...]


def route_last(a3_ref, ab3_ref, stack_ref):
    stack_ref[0] = a3_ref[...]
    stack_ref[1] = ab3_ref[...]


def left_slots(names):
    needed = set()
    for _, kind, dz in names:
        needed |= {"O": {(0, dz)}, "AB": {(1, dz)}}.get(kind, {(0, dz), (1, dz)})
    return sorted(needed, key=lambda slot: (slot[1], slot[0]))


def swap_in_windows(own, weights, share):
    shape = tuple(lax.axis_size(name) for name in AXES)
    columns, per_block = 4, own.shape[2]
    depth = own.size // (columns * per_block)
    spins = share // (2 * columns)
    tall, wide = 2 * spins * per_block, columns * per_block
    strides = (shape[1] * shape[2] * shape[3], shape[2] * shape[3], shape[3], 1)

    def move(array, target):
        pairs = []
        for p in range(shape[0]):
            for c in range(shape[1]):
                for z in range(shape[2]):
                    for y in range(shape[3]):
                        ends = (p, c, z, y), target(p, c, z, y)
                        pairs.append(
                            tuple(sum(a * b for a, b in zip(end, strides)) for end in ends)
                        )
        return lax.ppermute(array, AXES, pairs)

    def hop_a(array):
        return move(array, lambda p, c, z, y: (p ^ 1, c, z, y) if c == 0 else (p, c, z, y ^ 1))

    def hop_b(array):
        return move(array, lambda p, c, z, y: (p, c, z, y ^ 1) if c == 0 else (p ^ 1, c, z, y))

    def hop_ab(array):
        return move(array, lambda p, c, z, y: (p ^ 1, c, z, y ^ 1))

    def hop_z(array, by):
        return move(array, lambda p, c, z, y: (p, c, z ^ by, y))

    def hop_mixed(array):
        return move(
            array, lambda p, c, z, y: (p ^ 1, c, z, y ^ 1) if c == 0 else (p, c, z ^ 2, y)
        )

    def swap(array):
        return move(array, lambda p, c, z, y: (p, c ^ 1, z, y))

    arrays = {}
    where = {}

    def put(key, array, side, kinds):
        arrays[key] = array
        for slot, (kind, dz) in enumerate(kinds):
            where[(side, kind, dz)] = (key, slot if len(kinds) > 1 else None)

    def near(kind, dz):
        key, slot = where[("near", kind, dz)]
        return arrays[key] if slot is None else arrays[key][slot]

    def add(names, totals, keep=None, left=None, last=False, weight=1):
        given = left is not None
        slots, left = left if given else (keep or left_slots(names), None)
        uses = list(names)
        for dy, dz in [] if given else slots:
            uses += [("near", kind, dz) for kind in (("A", "B") if dy else ("O",))]
        keys = sorted({where[name][0] for name in uses})
        places = {name: (keys.index(where[name][0]), where[name][1]) for name in uses}
        operands = [weights] + [arrays[key] for key in keys]
        operands += [each for each in (left, totals) if each is not None]
        total_shape = (2, 2, tall, wide)
        left_shape = (len(slots), 2 * tall, depth)
        block = pl.BlockSpec(memory_space=pltpu.VMEM)
        out_shape = [jax.ShapeDtypeStruct(total_shape, jnp.float32)]
        scratch = [] if given or keep else [pltpu.VMEM(left_shape, jnp.bfloat16)]
        out_specs = [block]
        if last:
            out_shape = [jax.ShapeDtypeStruct((share, per_block, 4 * per_block), jnp.float32)]
            out_specs = [pl.BlockSpec(memory_space=pl.ANY)]
            scratch = [
                pltpu.VMEM(total_shape[1:], jnp.float32),
                pltpu.VMEM(out_shape[0].shape, jnp.float32),
                pltpu.SemaphoreType.DMA((spins * columns // 2,)),
            ]
        if keep:
            out_shape.append(jax.ShapeDtypeStruct(left_shape, jnp.bfloat16))
            out_specs.append(block)
        out = pl.pallas_call(
            functools.partial(
                add_shards, tuple(names), places, slots, totals is not None, given, last, share
            ),
            in_specs=[block] * len(operands),
            out_specs=out_specs,
            out_shape=out_shape,
            scratch_shapes=scratch,
            compiler_params=pltpu.CompilerParams(vmem_limit_bytes=40 * 1024 * 1024),
            cost_estimate=pl.CostEstimate(
                flops=4 * tall * wide * depth * len(names) * weight,
                bytes_accessed=wide * depth * 2 * len(names) + 8 * 4 * tall * wide,
                transcendentals=0,
            ),
        )(*operands)
        return (out[0], (slots, out[1])) if keep else out[0]

    def fence(totals):
        nonlocal arrays
        arrays, totals = lax.optimization_barrier((arrays, totals))
        return totals

    put("1a", hop_z(own, 2), "near", [("O", 2)])
    put("1b", hop_a(own), "near", [("A", 0)])
    put("1c", hop_z(own, 1), "near", [("O", 1)])
    put("1d", hop_b(own), "near", [("B", 0)])
    put("1e", hop_b(near("A", 0)), "near", [("AB", 0)])
    put("1f", swap(own), "far", [("O", 0)])
    put("9", own, "near", [("O", 0)])
    weights = fence(weights)

    def route(kernel, operands, counts, weight=0):
        block = pl.BlockSpec(memory_space=pltpu.VMEM)
        shapes = [(count,) * (count > 1) + own.shape for count in counts]
        routed = pl.pallas_call(
            kernel,
            in_specs=[block] * len(operands),
            out_specs=[block] * len(counts),
            out_shape=[jax.ShapeDtypeStruct(shape, own.dtype) for shape in shapes],
            compiler_params=pltpu.CompilerParams(vmem_limit_bytes=24 * 1024 * 1024),
            cost_estimate=pl.CostEstimate(flops=weight, bytes_accessed=0, transcendentals=0),
        )(*operands)
        return fence(routed)

    first = [("O", 0), ("A", 0), ("B", 0), ("AB", 0), ("O", 1), ("O", 2)]
    second = [("AB", 1), ("AB", 2), ("O", 3), ("A", 1), ("A", 2), ("B", 1), ("B", 2)]
    third = [("A", 3), ("AB", 3), ("B", 3)]
    a1 = hop_a(near("O", 1))
    stack, both, mixed = route(route_second, [near(*kind) for kind in first[1:]], (5, 2, 1))
    totals = add([("near", *kind) for kind in first], None)
    o3, ab2, a2, b12 = hop_z(near("O", 2), 1), hop_mixed(mixed), hop_a(near("O", 2)), hop_b(both)
    put("2a", swap(stack), "far", first[1:])
    totals = fence(totals)

    put("2b", hop_z(near("AB", 0), 1), "near", [("AB", 1)])
    totals = add([("far", *kind) for kind in first], totals)
    ab1 = arrays.pop("2b")
    put("2bb", a1, "near", [("A", 1)])
    put("2c", o3, "near", [("O", 3)])
    put("2d", ab2, "near", [("AB", 2)])
    totals = fence(totals)

    ab3, a3, b3 = hop_z(near("AB", 2), 1), hop_a(near("O", 3)), hop_b(near("O", 3))
    totals = add([("near", "O", 3)], totals, weight=45)
    arrays["2b"] = ab1
    put("2e", a2, "near", [("A", 2)])
    put("2f", b12, "near", [("B", 1), ("B", 2)])
    totals = fence(totals)

    keys = ("2b", "2d", "2c", "2bb", "2e", "2f")
    (stack,) = route(route_third, [arrays[key] for key in keys], (7,))
    far2 = swap(stack)
    names = [("near", *kind) for kind in second if kind != ("O", 3)]
    totals = add(names, totals)
    a3, ab3, totals = lax.optimization_barrier((a3, ab3, totals))
    (stack,) = route(route_last, [a3, ab3], (2,), weight=10**11)
    put("3a", stack, "near", third[:2])
    stack = swap(stack)
    put("3d", far2, "far", second)
    totals = add([("far", *kind) for kind in second], totals)
    put("3b", b3, "near", third[2:])
    totals = fence(totals)

    put("4a", stack, "far", third[:2])
    far3 = swap(near("B", 3))
    names = [("near", *kind) for kind in third]
    totals, (slots, left) = add(names, totals, keep=left_slots(names))
    put("4b", far3, "far", third[2:])
    totals, left = fence((totals, left))
    return add([("far", *kind) for kind in third], totals, left=(slots, left), last=True)


def add_terms(place_ref, weights_ref, left_ref, right_ref, field_ref):
    @pl.when(pl.program_id(0) == 0)
    def _():
        field_ref[...] = jnp.zeros_like(field_ref)

    spins = left_ref.shape[2]
    groups, columns, per_block, depth = right_ref.shape[0], *right_ref.shape[2:]
    owns = [left_ref[0, 0, spin] for spin in range(spins)]
    left = left_sides(owns, weights_ref[0])
    for column in range(columns):
        right = right_ref[:, 0, column].reshape(groups * per_block, depth)
        term = product(left, right)
        for part in range(2):
            for spin in range(spins):
                start = (part * spins + spin) * per_block
                field_ref[(spin * columns + column) * 2 + part] += term[start : start + per_block]


def gather_whole(packed, place, weights, share):
    groups, _, deep, flat = (lax.axis_size(name) for name in AXES)
    sites = deep * flat
    _, per_block, depth = packed.shape
    columns = min(4, share // 2)
    spins = share // (2 * columns)
    near = lax.all_gather(packed, ("pair", "deep", "flat"))
    near = near.reshape(groups, sites, 4, per_block, depth)
    far = lax.ppermute(near, "core", [(0, 1), (1, 0)])
    wide = groups * per_block

    def half(right):
        return pl.pallas_call(
            add_terms,
            grid_spec=pltpu.PrefetchScalarGridSpec(
                num_scalar_prefetch=1,
                grid=(sites,),
                in_specs=[
                    pl.BlockSpec((1, 2, weights.shape[2]), lambda m, place: (m, 0, 0)),
                    pl.BlockSpec(
                        (1, 1, spins, per_block, depth),
                        lambda m, place: (place[0], m, place[4] // spins, 0, 0),
                    ),
                    pl.BlockSpec(
                        (groups, 1, columns, per_block, depth),
                        lambda m, place: (0, m, place[6] // columns, 0, 0),
                    ),
                ],
                out_specs=pl.BlockSpec((share, per_block, wide), lambda m, place: (0, 0, 0)),
            ),
            out_shape=jax.ShapeDtypeStruct((share, per_block, wide), jnp.float32),
            compiler_params=pltpu.CompilerParams(vmem_limit_bytes=40 * 1024 * 1024),
        )(place, weights, near, right)

    sides = [half(right).reshape(share, per_block, groups, per_block) for right in (near, far)]
    first = lax.axis_index("core") == 0
    even, odd = (jnp.where(first, a, b) for a, b in (sides, sides[::-1]))
    return jnp.stack([even, odd], 3).reshape(share, per_block, 2 * wide)


def shards(modes, momenta):
    groups, _, deep, flat = (lax.axis_size(name) for name in AXES)
    sites = deep * flat
    slots, steps, per_block, spin_colour, site_count = modes.shape
    share = steps * momenta.shape[0] * 32 // sites
    owned = (lax.axis_index("deep") * flat + lax.axis_index("flat")) * (share // 2)
    place = [lax.axis_index(name) for name in AXES]
    place = jnp.stack(place + [owned // 4 % 4, jnp.int32(flat), owned % 4]).astype(jnp.int32)

    mine = lax.dynamic_slice_in_dim(momenta, owned // 16, 1, 0)
    weights = phase_table(mine, jnp.int32(0), sites * site_count, LEXT)[0]
    weights = jnp.transpose(weights.reshape(2, sites, site_count), (1, 0, 2))

    if (groups, deep, flat) == (2, 4, 2) and steps == 1 and share in (8, 16, 32):
        own = jnp.transpose(modes[:, 0], (0, 2, 1, 3))
        return swap_in_windows(own, weights, share)
    packed = jnp.transpose(modes.reshape(slots, per_block, 4, 3, site_count), (2, 1, 0, 3, 4))
    packed = packed.reshape(4, per_block, slots * 3 * site_count)
    return gather_whole(packed, place, weights, share)


def solution(mesh):
    count, sites = mesh.shape["blk"], mesh.shape["site"]
    flat = 2 ** (int(math.log2(sites)) // 2)
    split = Mesh(mesh.devices.reshape(count // 2, 2, sites // flat, flat), AXES)
    placed = (P(None, None, ("pair", "core"), None, ("deep", "flat")), P())
    return jax.shard_map(
        shards,
        mesh=split,
        in_specs=placed,
        out_specs=P(("deep", "flat"), ("pair", "core"), None),
        check_vma=False,
    )
```

```python
import functools
import math

import jax
import jax.numpy as jnp
from jax import lax
from jax.experimental import pallas as pl
from jax.experimental.pallas import tpu as pltpu
from jax.sharding import Mesh, PartitionSpec as P

LEXT = 48

TWO_PI = 2.0 * math.pi

AXES = ("pair", "core", "deep", "flat")


def phase_table(momenta, first_site, site_count, extent):
    flat = first_site + jnp.arange(site_count, dtype=jnp.int32)
    coords = jnp.stack([flat % extent, flat // extent % extent, flat // (extent * extent)], 0)
    turns = jnp.mod(jnp.sum(momenta[:, :, None] * coords[None, :, :], axis=1), extent)
    angle = turns.astype(jnp.float32) * (TWO_PI / extent)
    return jnp.stack([jnp.cos(angle), jnp.sin(angle)], 1)


def left_sides(owns, weights):
    depth = owns[0].shape[1]
    half = depth // 2
    cosine = jnp.tile(weights[0:1], (1, depth // weights.shape[1]))
    sine = jnp.tile(weights[1:2], (1, depth // weights.shape[1]))
    cosine_rows = [[], []]
    sine_rows = [[], []]
    for own in owns:
        own = own.astype(jnp.float32)
        by_cos = (own * cosine).astype(jnp.bfloat16)
        by_sin = (own * sine).astype(jnp.bfloat16)
        cosine_rows[0].append(by_cos)
        cosine_rows[1].append(jnp.concatenate([-by_cos[:, half:], by_cos[:, :half]], 1))
        sine_rows[0].append(jnp.concatenate([-by_sin[:, half:], by_sin[:, :half]], 1))
        sine_rows[1].append(-by_sin)
    return jnp.concatenate(cosine_rows[0] + cosine_rows[1] + sine_rows[0] + sine_rows[1], 0)


def product(left, right):
    dims = (((1,), (1,)), ((), ()))
    terms = lax.dot_general(left, right, dims, preferred_element_type=jnp.float32)
    half = terms.shape[0] // 2
    return terms[:half] + terms[half:]


def add_shards(names, where, slots, has_totals, given, last, share, weights_ref, *refs):
    refs = list(refs)
    if last:
        sems, row_ref, far_ref = (refs.pop() for _ in range(3))
    left_ref = None if given else refs.pop()
    out_ref = refs.pop()
    totals_in = refs.pop() if has_totals else None
    left_ref = refs.pop() if given else left_ref

    def shard(name):
        index, slot = where[name]
        return refs[index] if slot is None else refs[index].at[slot]

    def spin_rows(name, spin):
        ref = shard(name)
        tiles = [ref[part, spin * colours + x] for part in range(2) for x in range(colours)]
        return jnp.concatenate(tiles, 1)

    pair, core, level, beside = (lax.axis_index(name) for name in AXES)
    flat = lax.axis_size("flat")
    _, spin_colour, per_block, _ = shard(names[0]).shape
    columns, colours = 4, spin_colour // 4
    first_s = lax.rem(lax.div((level * flat + beside) * (share // 2), 4), 4)
    spins = left_ref.shape[1] // (4 * per_block)

    if last:
        far_ref[...] = totals_in[1]
    elif has_totals:
        out_ref[...] = totals_in[...]
    else:
        out_ref[...] = jnp.zeros_like(out_ref)
    if not given:
        for slot, (dy, dz) in enumerate(slots):
            site = jnp.bitwise_xor(level, dz) * flat + jnp.bitwise_xor(beside, dy)
            if dy == 0:
                owns = [spin_rows(("near", "O", dz), first_s + s) for s in range(spins)]
            else:
                owns = [
                    jnp.where(
                        core == 0,
                        spin_rows(("near", "B", dz), first_s + s),
                        spin_rows(("near", "A", dz), first_s + s),
                    )
                    for s in range(spins)
                ]
            left_ref[slot] = left_sides(owns, weights_ref[site])

    for side, kind, dz in names:
        right = jnp.concatenate([spin_rows((side, kind, dz), r) for r in range(columns)], 0)
        turn = core if side == "near" else 1 - core
        dx, dy = {"O": (0, 0), "A": (1 - turn, turn), "B": (turn, 1 - turn), "AB": (1, 1)}[kind]
        if kind in ("O", "AB"):
            slot = slots.index((dy, dz))
        else:
            slot = slots.index((0, dz)) + dy
        term = product(left_ref[slot], right)
        if last:
            far_ref[dx] += term
        else:
            out_ref[0 if side == "near" else 1, dx] += term

    if last:
        lane = lax.broadcasted_iota(jnp.int32, (per_block, 2 * per_block), 1)
        copies = []
        for spin in range(spins):
            for column in range(0, columns, 2):
                first = (spin * columns + column) * 2
                across = pl.ds(column * per_block, 2 * per_block)
                for part in range(2):
                    top = (part * spins + spin) * per_block
                    for p in range(2):
                        dx = jnp.bitwise_xor(pair, p)
                        near = totals_in[0, dx, pl.ds(top, per_block), across]
                        far = far_ref[dx, pl.ds(top, per_block), across]
                        even = jnp.where(core == 0, near, far)
                        odd = jnp.where(core == 0, far, near)
                        place = pl.ds(p * 2 * per_block, 2 * per_block)
                        row_ref[first + part, :, place] = jnp.where(
                            lane < per_block, even, pltpu.roll(odd, per_block, 1)
                        )
                        row_ref[first + part + 2, :, place] = jnp.where(
                            lane < per_block, pltpu.roll(even, per_block, 1), odd
                        )
                rows = pl.ds(first, 4)
                copies.append(
                    pltpu.make_async_copy(row_ref.at[rows], out_ref.at[rows], sems.at[len(copies)])
                )
                copies[-1].start()
        for copy in copies:
            copy.wait()


def route_second(*refs):
    o1_ref, o2_ref, stack_ref, both_ref = refs[3:]
    for slot in range(5):
        stack_ref[slot] = refs[slot][...]
    both_ref[0] = o1_ref[...]
    both_ref[1] = o2_ref[...]


def route_third(ab2_ref, o3_ref, a12_ref, b12_ref, stack_ref, a1_ref):
    stack_ref[0] = ab2_ref[...]
    stack_ref[1] = o3_ref[...]
    stack_ref[2:4] = a12_ref[...]
    stack_ref[4:6] = b12_ref[...]
    a1_ref[...] = a12_ref[0]


def route_last(a3_ref, ab3_ref, stack_ref):
    stack_ref[0] = a3_ref[...]
    stack_ref[1] = ab3_ref[...]


def left_slots(names):
    needed = set()
    for _, kind, dz in names:
        needed |= {"O": {(0, dz)}, "AB": {(1, dz)}}.get(kind, {(0, dz), (1, dz)})
    return sorted(needed, key=lambda slot: (slot[1], slot[0]))


def swap_in_windows(own, weights, share):
    shape = tuple(lax.axis_size(name) for name in AXES)
    columns, per_block = 4, own.shape[2]
    depth = own.size // (columns * per_block)
    spins = share // (2 * columns)
    tall, wide = 2 * spins * per_block, columns * per_block
    strides = (shape[1] * shape[2] * shape[3], shape[2] * shape[3], shape[3], 1)

    def move(array, target):
        pairs = []
        for p in range(shape[0]):
            for c in range(shape[1]):
                for z in range(shape[2]):
                    for y in range(shape[3]):
                        ends = (p, c, z, y), target(p, c, z, y)
                        pairs.append(
                            tuple(sum(a * b for a, b in zip(end, strides)) for end in ends)
                        )
        return lax.ppermute(array, AXES, pairs)

    def hop_a(array):
        return move(array, lambda p, c, z, y: (p ^ 1, c, z, y) if c == 0 else (p, c, z, y ^ 1))

    def hop_b(array):
        return move(array, lambda p, c, z, y: (p, c, z, y ^ 1) if c == 0 else (p ^ 1, c, z, y))

    def hop_z(array, by):
        return move(array, lambda p, c, z, y: (p, c, z ^ by, y))

    def swap(array):
        return move(array, lambda p, c, z, y: (p, c ^ 1, z, y))

    arrays = {}
    where = {}

    def put(key, array, side, kinds):
        arrays[key] = array
        for slot, (kind, dz) in enumerate(kinds):
            where[(side, kind, dz)] = (key, slot if len(kinds) > 1 else None)

    def near(kind, dz):
        key, slot = where[("near", kind, dz)]
        return arrays[key] if slot is None else arrays[key][slot]

    def add(names, totals, keep=None, left=None, last=False, weight=1):
        given = left is not None
        slots, left = left if given else (keep or left_slots(names), None)
        uses = list(names)
        for dy, dz in [] if given else slots:
            uses += [("near", kind, dz) for kind in (("A", "B") if dy else ("O",))]
        keys = sorted({where[name][0] for name in uses})
        places = {name: (keys.index(where[name][0]), where[name][1]) for name in uses}
        operands = [weights] + [arrays[key] for key in keys]
        operands += [each for each in (left, totals) if each is not None]
        total_shape = (2, 2, tall, wide)
        left_shape = (len(slots), 2 * tall, depth)
        block = pl.BlockSpec(memory_space=pltpu.VMEM)
        out_shape = [jax.ShapeDtypeStruct(total_shape, jnp.float32)]
        scratch = [] if given or keep else [pltpu.VMEM(left_shape, jnp.bfloat16)]
        out_specs = [block]
        if last:
            out_shape = [jax.ShapeDtypeStruct((share, per_block, 4 * per_block), jnp.float32)]
            out_specs = [pl.BlockSpec(memory_space=pl.ANY)]
            scratch = [
                pltpu.VMEM(total_shape[1:], jnp.float32),
                pltpu.VMEM(out_shape[0].shape, jnp.float32),
                pltpu.SemaphoreType.DMA((spins * columns // 2,)),
            ]
        if keep:
            out_shape.append(jax.ShapeDtypeStruct(left_shape, jnp.bfloat16))
            out_specs.append(block)
        out = pl.pallas_call(
            functools.partial(
                add_shards, tuple(names), places, slots, totals is not None, given, last, share
            ),
            in_specs=[block] * len(operands),
            out_specs=out_specs,
            out_shape=out_shape,
            scratch_shapes=scratch,
            compiler_params=pltpu.CompilerParams(vmem_limit_bytes=40 * 1024 * 1024),
            cost_estimate=pl.CostEstimate(
                flops=4 * tall * wide * depth * len(names) * weight,
                bytes_accessed=wide * depth * 2 * len(names) + 8 * 4 * tall * wide,
                transcendentals=0,
            ),
        )(*operands)
        return (out[0], (slots, out[1])) if keep else out[0]

    def fence(totals):
        nonlocal arrays
        arrays, totals = lax.optimization_barrier((arrays, totals))
        return totals

    put("1a", hop_z(own, 2), "near", [("O", 2)])
    put("1b", hop_a(own), "near", [("A", 0)])
    put("1c", hop_z(own, 1), "near", [("O", 1)])
    put("1d", hop_b(own), "near", [("B", 0)])
    put("1e", hop_b(near("A", 0)), "near", [("AB", 0)])
    put("1f", swap(own), "far", [("O", 0)])
    put("9", own, "near", [("O", 0)])
    weights = fence(weights)

    def route(kernel, operands, counts, weight=0):
        block = pl.BlockSpec(memory_space=pltpu.VMEM)
        shapes = [(count,) * (count > 1) + own.shape for count in counts]
        routed = pl.pallas_call(
            kernel,
            in_specs=[block] * len(operands),
            out_specs=[block] * len(counts),
            out_shape=[jax.ShapeDtypeStruct(shape, own.dtype) for shape in shapes],
            compiler_params=pltpu.CompilerParams(vmem_limit_bytes=24 * 1024 * 1024),
            cost_estimate=pl.CostEstimate(flops=weight, bytes_accessed=0, transcendentals=0),
        )(*operands)
        return fence(routed)

    first = [("O", 0), ("A", 0), ("B", 0), ("AB", 0), ("O", 1), ("O", 2)]
    second = [("AB", 2), ("O", 3), ("A", 1), ("A", 2), ("B", 1), ("B", 2)]
    third = [("A", 3), ("B", 3)]
    fourth = [("AB", 3), ("AB", 1)]
    stack, both = route(route_second, [near(*kind) for kind in first[1:]], (5, 2))
    totals = add([("near", *kind) for kind in first], None)
    o3, ab2 = hop_z(near("O", 2), 1), hop_z(near("AB", 0), 2)
    a12, b12 = hop_a(both), hop_b(both)
    put("2a", swap(stack), "far", first[1:])
    totals = fence(totals)

    totals = add([("far", *kind) for kind in first], totals)
    put("2c", o3, "near", [("O", 3)])
    totals = fence(totals)

    a3, b3 = hop_a(near("O", 3)), hop_b(near("O", 3))
    totals = add([("near", "O", 3)], totals, weight=45)
    put("2d", ab2, "near", [("AB", 2)])
    put("2e", a12, "near", [("A", 1), ("A", 2)])
    put("2f", b12, "near", [("B", 1), ("B", 2)])
    totals = fence(totals)

    ab3 = hop_z(near("AB", 2), 1)
    stack, a1 = route(route_third, [arrays[key] for key in ("2d", "2c", "2e", "2f")], (6, 1))
    far2, ab1 = swap(stack), hop_b(a1)
    names = [("near", *kind) for kind in second if kind != ("O", 3)]
    totals = add(names, totals)
    a3, b3, totals = lax.optimization_barrier((a3, b3, totals))
    (stack,) = route(route_last, [a3, b3], (2,), weight=10**11)
    put("3a", stack, "near", third)
    far3 = swap(stack)
    put("3d", far2, "far", second)
    names = [("far", *kind) for kind in second] + [("near", *kind) for kind in third]
    totals = add(names, totals)
    put("3b", ab3, "near", fourth[:1])
    put("3c", ab1, "near", fourth[1:])
    totals = fence(totals)

    far4 = [swap(near(*kind)) for kind in fourth]
    names = [("far", *kind) for kind in third + fourth]
    slots = left_slots(names)
    totals, (slots, left) = add([("near", *kind) for kind in fourth], totals, keep=slots)
    put("4a", far3, "far", third)
    put("4b", far4[0], "far", fourth[:1])
    put("4c", far4[1], "far", fourth[1:])
    totals, left = fence((totals, left))
    return add(names, totals, left=(slots, left), last=True)


def add_terms(place_ref, weights_ref, left_ref, right_ref, field_ref):
    @pl.when(pl.program_id(0) == 0)
    def _():
        field_ref[...] = jnp.zeros_like(field_ref)

    spins = left_ref.shape[2]
    groups, columns, per_block, depth = right_ref.shape[0], *right_ref.shape[2:]
    owns = [left_ref[0, 0, spin] for spin in range(spins)]
    left = left_sides(owns, weights_ref[0])
    for column in range(columns):
        right = right_ref[:, 0, column].reshape(groups * per_block, depth)
        term = product(left, right)
        for part in range(2):
            for spin in range(spins):
                start = (part * spins + spin) * per_block
                field_ref[(spin * columns + column) * 2 + part] += term[start : start + per_block]


def gather_whole(packed, place, weights, share):
    groups, _, deep, flat = (lax.axis_size(name) for name in AXES)
    sites = deep * flat
    _, per_block, depth = packed.shape
    columns = min(4, share // 2)
    spins = share // (2 * columns)
    near = lax.all_gather(packed, ("pair", "deep", "flat"))
    near = near.reshape(groups, sites, 4, per_block, depth)
    far = lax.ppermute(near, "core", [(0, 1), (1, 0)])
    wide = groups * per_block

    def half(right):
        return pl.pallas_call(
            add_terms,
            grid_spec=pltpu.PrefetchScalarGridSpec(
                num_scalar_prefetch=1,
                grid=(sites,),
                in_specs=[
                    pl.BlockSpec((1, 2, weights.shape[2]), lambda m, place: (m, 0, 0)),
                    pl.BlockSpec(
                        (1, 1, spins, per_block, depth),
                        lambda m, place: (place[0], m, place[4] // spins, 0, 0),
                    ),
                    pl.BlockSpec(
                        (groups, 1, columns, per_block, depth),
                        lambda m, place: (0, m, place[6] // columns, 0, 0),
                    ),
                ],
                out_specs=pl.BlockSpec((share, per_block, wide), lambda m, place: (0, 0, 0)),
            ),
            out_shape=jax.ShapeDtypeStruct((share, per_block, wide), jnp.float32),
            compiler_params=pltpu.CompilerParams(vmem_limit_bytes=40 * 1024 * 1024),
        )(place, weights, near, right)

    sides = [half(right).reshape(share, per_block, groups, per_block) for right in (near, far)]
    first = lax.axis_index("core") == 0
    even, odd = (jnp.where(first, a, b) for a, b in (sides, sides[::-1]))
    return jnp.stack([even, odd], 3).reshape(share, per_block, 2 * wide)


def shards(modes, momenta):
    groups, _, deep, flat = (lax.axis_size(name) for name in AXES)
    sites = deep * flat
    slots, steps, per_block, spin_colour, site_count = modes.shape
    share = steps * momenta.shape[0] * 32 // sites
    owned = (lax.axis_index("deep") * flat + lax.axis_index("flat")) * (share // 2)
    place = [lax.axis_index(name) for name in AXES]
    place = jnp.stack(place + [owned // 4 % 4, jnp.int32(flat), owned % 4]).astype(jnp.int32)

    mine = lax.dynamic_slice_in_dim(momenta, owned // 16, 1, 0)
    weights = phase_table(mine, jnp.int32(0), sites * site_count, LEXT)[0]
    weights = jnp.transpose(weights.reshape(2, sites, site_count), (1, 0, 2))

    if (groups, deep, flat) == (2, 4, 2) and steps == 1 and share in (8, 16, 32):
        own = jnp.transpose(modes[:, 0], (0, 2, 1, 3))
        return swap_in_windows(own, weights, share)
    packed = jnp.transpose(modes.reshape(slots, per_block, 4, 3, site_count), (2, 1, 0, 3, 4))
    packed = packed.reshape(4, per_block, slots * 3 * site_count)
    return gather_whole(packed, place, weights, share)


def solution(mesh):
    count, sites = mesh.shape["blk"], mesh.shape["site"]
    flat = 2 ** (int(math.log2(sites)) // 2)
    split = Mesh(mesh.devices.reshape(count // 2, 2, sites // flat, flat), AXES)
    placed = (P(None, None, ("pair", "core"), None, ("deep", "flat")), P())
    return jax.shard_map(
        shards,
        mesh=split,
        in_specs=placed,
        out_specs=P(("deep", "flat"), ("pair", "core"), None),
        check_vma=False,
    )
```

```python
import functools
import math

import jax
import jax.numpy as jnp
from jax import lax
from jax.experimental import pallas as pl
from jax.experimental.pallas import tpu as pltpu
from jax.sharding import Mesh, PartitionSpec as P

LEXT = 48

TWO_PI = 2.0 * math.pi

AXES = ("pair", "core", "deep", "flat")


def phase_table(momenta, first_site, site_count, extent):
    flat = first_site + jnp.arange(site_count, dtype=jnp.int32)
    coords = jnp.stack([flat % extent, flat // extent % extent, flat // (extent * extent)], 0)
    turns = jnp.mod(jnp.sum(momenta[:, :, None] * coords[None, :, :], axis=1), extent)
    angle = turns.astype(jnp.float32) * (TWO_PI / extent)
    return jnp.stack([jnp.cos(angle), jnp.sin(angle)], 1)


def left_sides(owns, weights):
    depth = owns[0].shape[1]
    half = depth // 2
    cosine = jnp.tile(weights[0:1], (1, depth // weights.shape[1]))
    sine = jnp.tile(weights[1:2], (1, depth // weights.shape[1]))
    cosine_rows = [[], []]
    sine_rows = [[], []]
    for own in owns:
        own = own.astype(jnp.float32)
        by_cos = (own * cosine).astype(jnp.bfloat16)
        by_sin = (own * sine).astype(jnp.bfloat16)
        cosine_rows[0].append(by_cos)
        cosine_rows[1].append(jnp.concatenate([-by_cos[:, half:], by_cos[:, :half]], 1))
        sine_rows[0].append(jnp.concatenate([-by_sin[:, half:], by_sin[:, :half]], 1))
        sine_rows[1].append(-by_sin)
    return jnp.concatenate(cosine_rows[0] + cosine_rows[1] + sine_rows[0] + sine_rows[1], 0)


def product(left, right):
    dims = (((1,), (1,)), ((), ()))
    terms = lax.dot_general(left, right, dims, preferred_element_type=jnp.float32)
    half = terms.shape[0] // 2
    return terms[:half] + terms[half:]


def add_shards(names, where, slots, has_totals, given, half, last, share, weights_ref, *refs):
    refs = list(refs)
    left_ref = None if given else refs.pop()
    if half:
        sems, row_ref, left_ref = left_ref, refs.pop(), refs.pop()
        field_ref = refs.pop()
    if last:
        sems, row_ref, far_ref, field_ref, _ = (refs.pop() for _ in range(5))
    else:
        out_ref = refs.pop()
    totals_in = refs.pop() if has_totals else None
    left_ref = refs.pop() if given else left_ref

    def shard(name):
        index, slot = where[name]
        return refs[index] if slot is None else refs[index].at[slot]

    def spin_rows(name, spin):
        ref = shard(name)
        tiles = [ref[part, spin * colours + x] for part in range(2) for x in range(colours)]
        return jnp.concatenate(tiles, 1)

    pair, core, level, beside = (lax.axis_index(name) for name in AXES)
    flat = lax.axis_size("flat")
    _, spin_colour, per_block, _ = shard(names[0]).shape
    columns, colours = 4, spin_colour // 4
    first_s = lax.rem(lax.div((level * flat + beside) * (share // 2), 4), 4)
    spins = left_ref.shape[1] // (4 * per_block)

    def send_columns(dx, near, far):
        lane = lax.broadcasted_iota(jnp.int32, (per_block, 2 * per_block), 1)
        start = pl.multiple_of(jnp.bitwise_xor(pair, dx) * (2 * per_block), 2 * per_block)
        copies = []
        for spin in range(spins):
            for column in range(0, columns, 2):
                first = (spin * columns + column) * 2
                across = slice(column * per_block, (column + 2) * per_block)
                for part in range(2):
                    top = (part * spins + spin) * per_block
                    one = near(slice(top, top + per_block), across)
                    two = far(slice(top, top + per_block), across)
                    even = jnp.where(core == 0, one, two)
                    odd = jnp.where(core == 0, two, one)
                    row_ref[first + part] = jnp.where(
                        lane < per_block, even, pltpu.roll(odd, per_block, 1)
                    )
                    row_ref[first + part + 2] = jnp.where(
                        lane < per_block, pltpu.roll(even, per_block, 1), odd
                    )
                four = pl.ds(first, 4)
                target = field_ref.at[four, :, pl.ds(start, 2 * per_block)]
                copies.append(
                    pltpu.make_async_copy(row_ref.at[four], target, sems.at[len(copies)])
                )
                copies[-1].start()
        return copies

    def term(name):
        side, kind, dz = name
        right = jnp.concatenate([spin_rows(name, r) for r in range(columns)], 0)
        turn = core if side == "near" else 1 - core
        dx, dy = {"O": (0, 0), "A": (1 - turn, turn), "B": (turn, 1 - turn), "AB": (1, 1)}[kind]
        if kind in ("O", "AB"):
            slot = slots.index((dy, dz))
        else:
            slot = slots.index((0, dz)) + dy
        return dx, product(left_ref[slot], right)

    if last:
        far_ref[...] = totals_in[1, 1] + sum(term(name)[1] for name in names)
        copies = send_columns(
            1,
            lambda rows, across: totals_in[0, 1, rows, across],
            lambda rows, across: far_ref[rows, across],
        )
        for copy in copies:
            copy.wait()
        return

    if has_totals:
        out_ref[...] = totals_in[...]
    else:
        out_ref[...] = jnp.zeros_like(out_ref)
    if not given:
        for slot, (dy, dz) in enumerate(slots):
            site = jnp.bitwise_xor(level, dz) * flat + jnp.bitwise_xor(beside, dy)
            if dy == 0:
                owns = [spin_rows(("near", "O", dz), first_s + s) for s in range(spins)]
            else:
                owns = [
                    jnp.where(
                        core == 0,
                        spin_rows(("near", "B", dz), first_s + s),
                        spin_rows(("near", "A", dz), first_s + s),
                    )
                    for s in range(spins)
                ]
            left_ref[slot] = left_sides(owns, weights_ref[site])
    for name in names:
        dx, added = term(name)
        out_ref[0 if name[0] == "near" else 1, dx] += added
    if half:
        copies = send_columns(
            0,
            lambda rows, across: out_ref[0, 0, rows, across],
            lambda rows, across: out_ref[1, 0, rows, across],
        )
        for copy in copies:
            copy.wait()


def route_second(*refs):
    o1_ref, o2_ref, stack_ref, both_ref = refs[3:]
    for slot in range(5):
        stack_ref[slot] = refs[slot][...]
    both_ref[0] = o1_ref[...]
    both_ref[1] = o2_ref[...]


def route_third(ab2_ref, o3_ref, a12_ref, b12_ref, stack_ref, a1_ref):
    stack_ref[0] = ab2_ref[...]
    stack_ref[1] = o3_ref[...]
    stack_ref[2:4] = a12_ref[...]
    stack_ref[4:6] = b12_ref[...]
    a1_ref[...] = a12_ref[0]


def route_last(a3_ref, ab3_ref, stack_ref):
    stack_ref[0] = a3_ref[...]
    stack_ref[1] = ab3_ref[...]


def left_slots(names):
    needed = set()
    for _, kind, dz in names:
        needed |= {"O": {(0, dz)}, "AB": {(1, dz)}}.get(kind, {(0, dz), (1, dz)})
    return sorted(needed, key=lambda slot: (slot[1], slot[0]))


def swap_in_windows(own, weights, share):
    shape = tuple(lax.axis_size(name) for name in AXES)
    columns, per_block = 4, own.shape[2]
    depth = own.size // (columns * per_block)
    spins = share // (2 * columns)
    tall, wide = 2 * spins * per_block, columns * per_block
    strides = (shape[1] * shape[2] * shape[3], shape[2] * shape[3], shape[3], 1)

    def move(array, target):
        pairs = []
        for p in range(shape[0]):
            for c in range(shape[1]):
                for z in range(shape[2]):
                    for y in range(shape[3]):
                        ends = (p, c, z, y), target(p, c, z, y)
                        pairs.append(
                            tuple(sum(a * b for a, b in zip(end, strides)) for end in ends)
                        )
        return lax.ppermute(array, AXES, pairs)

    def hop_a(array):
        return move(array, lambda p, c, z, y: (p ^ 1, c, z, y) if c == 0 else (p, c, z, y ^ 1))

    def hop_b(array):
        return move(array, lambda p, c, z, y: (p, c, z, y ^ 1) if c == 0 else (p ^ 1, c, z, y))

    def hop_z(array, by):
        return move(array, lambda p, c, z, y: (p, c, z ^ by, y))

    def swap(array):
        return move(array, lambda p, c, z, y: (p, c ^ 1, z, y))

    arrays = {}
    where = {}

    def put(key, array, side, kinds):
        arrays[key] = array
        for slot, (kind, dz) in enumerate(kinds):
            where[(side, kind, dz)] = (key, slot if len(kinds) > 1 else None)

    def near(kind, dz):
        key, slot = where[("near", kind, dz)]
        return arrays[key] if slot is None else arrays[key][slot]

    def add(names, totals, keep=None, left=None, half=False, field=None, weight=1):
        given, last = left is not None, field is not None
        slots, left = left if given else (keep or left_slots(names), None)
        uses = list(names)
        for dy, dz in [] if given else slots:
            uses += [("near", kind, dz) for kind in (("A", "B") if dy else ("O",))]
        keys = sorted({where[name][0] for name in uses})
        places = {name: (keys.index(where[name][0]), where[name][1]) for name in uses}
        operands = [weights] + [arrays[key] for key in keys]
        operands += [each for each in (left, totals, field) if each is not None]
        total_shape = (2, 2, tall, wide)
        left_shape = (len(slots), 2 * tall, depth)
        field_shape = (share, per_block, 4 * per_block)
        block, apart = (pl.BlockSpec(memory_space=space) for space in (pltpu.VMEM, pltpu.HBM))
        in_specs, outs, scratch, aliases = [block] * len(operands), [], [], {}
        if last:
            in_specs[-1] = apart
            aliases = {len(operands) - 1: 0}
            scratch.append(pltpu.VMEM(total_shape[2:], jnp.float32))
        else:
            outs.append((total_shape, jnp.float32, block))
        if half or last:
            outs.append((field_shape, jnp.float32, apart))
            scratch.append(pltpu.VMEM((*field_shape[:2], 2 * per_block), jnp.float32))
            scratch.append(pltpu.SemaphoreType.DMA((spins * columns // 2,)))
        if keep:
            outs.append((left_shape, jnp.bfloat16, block))
        elif not given:
            scratch.append(pltpu.VMEM(left_shape, jnp.bfloat16))
        out = pl.pallas_call(
            functools.partial(
                add_shards, tuple(names), places, slots, totals is not None, given, half, last, share
            ),
            in_specs=in_specs,
            out_specs=[spec for _, _, spec in outs],
            out_shape=[jax.ShapeDtypeStruct(shape, dtype) for shape, dtype, _ in outs],
            scratch_shapes=scratch,
            input_output_aliases=aliases,
            compiler_params=pltpu.CompilerParams(vmem_limit_bytes=40 * 1024 * 1024),
            cost_estimate=pl.CostEstimate(
                flops=4 * tall * wide * depth * len(names) * weight,
                bytes_accessed=wide * depth * 2 * len(names) + 8 * 4 * tall * wide,
                transcendentals=0,
            ),
        )(*operands)
        return (*out[:-1], (slots, out[-1])) if keep else out[0]

    def fence(totals):
        nonlocal arrays
        arrays, totals = lax.optimization_barrier((arrays, totals))
        return totals

    put("1a", hop_z(own, 2), "near", [("O", 2)])
    put("1b", hop_a(own), "near", [("A", 0)])
    put("1c", hop_z(own, 1), "near", [("O", 1)])
    put("1d", hop_b(own), "near", [("B", 0)])
    put("1e", hop_b(near("A", 0)), "near", [("AB", 0)])
    put("1f", swap(own), "far", [("O", 0)])
    put("9", own, "near", [("O", 0)])
    weights = fence(weights)

    def route(kernel, operands, counts, weight=0):
        block = pl.BlockSpec(memory_space=pltpu.VMEM)
        shapes = [(count,) * (count > 1) + own.shape for count in counts]
        routed = pl.pallas_call(
            kernel,
            in_specs=[block] * len(operands),
            out_specs=[block] * len(counts),
            out_shape=[jax.ShapeDtypeStruct(shape, own.dtype) for shape in shapes],
            compiler_params=pltpu.CompilerParams(vmem_limit_bytes=24 * 1024 * 1024),
            cost_estimate=pl.CostEstimate(flops=weight, bytes_accessed=0, transcendentals=0),
        )(*operands)
        return fence(routed)

    first = [("O", 0), ("A", 0), ("B", 0), ("AB", 0), ("O", 1), ("O", 2)]
    second = [("AB", 2), ("O", 3), ("A", 1), ("A", 2), ("B", 1), ("B", 2)]
    third = [("A", 3), ("B", 3)]
    fourth = [("AB", 3), ("AB", 1)]
    stack, both = route(route_second, [near(*kind) for kind in first[1:]], (5, 2))
    totals = add([("near", *kind) for kind in first], None)
    o3, ab2 = hop_z(near("O", 2), 1), hop_z(near("AB", 0), 2)
    a12, b12 = hop_a(both), hop_b(both)
    put("2a", swap(stack), "far", first[1:])
    totals = fence(totals)

    totals = add([("far", *kind) for kind in first], totals)
    put("2c", o3, "near", [("O", 3)])
    totals = fence(totals)

    a3, b3 = hop_a(near("O", 3)), hop_b(near("O", 3))
    totals = add([("near", "O", 3)], totals, weight=45)
    put("2d", ab2, "near", [("AB", 2)])
    put("2e", a12, "near", [("A", 1), ("A", 2)])
    put("2f", b12, "near", [("B", 1), ("B", 2)])
    totals = fence(totals)

    ab3 = hop_z(near("AB", 2), 1)
    stack, a1 = route(route_third, [arrays[key] for key in ("2d", "2c", "2e", "2f")], (6, 1))
    far2, ab1 = swap(stack), hop_b(a1)
    names = [("near", *kind) for kind in second if kind != ("O", 3)]
    totals = add(names, totals)
    a3, b3, totals = lax.optimization_barrier((a3, b3, totals))
    (stack,) = route(route_last, [a3, b3], (2,), weight=10**11)
    put("3a", stack, "near", third)
    far3 = swap(stack)
    put("3d", far2, "far", second)
    names = [("far", *kind) for kind in second] + [("near", *kind) for kind in third]
    totals = add(names, totals, weight=10)
    put("3b", ab3, "near", fourth[:1])
    put("3c", ab1, "near", fourth[1:])
    totals = fence(totals)

    far4 = [swap(near(*kind)) for kind in fourth]
    put("4a", far3, "far", third)
    names = [("far", *kind) for kind in third] + [("near", *kind) for kind in fourth]
    totals, field, (slots, left) = add(names, totals, keep=left_slots(names), half=True)
    put("4b", far4[0], "far", fourth[:1])
    put("4c", far4[1], "far", fourth[1:])
    totals, left, field = fence((totals, left, field))
    return add([("far", *kind) for kind in fourth], totals, left=(slots, left), field=field)


def add_terms(place_ref, weights_ref, left_ref, right_ref, field_ref):
    @pl.when(pl.program_id(0) == 0)
    def _():
        field_ref[...] = jnp.zeros_like(field_ref)

    spins = left_ref.shape[2]
    groups, columns, per_block, depth = right_ref.shape[0], *right_ref.shape[2:]
    owns = [left_ref[0, 0, spin] for spin in range(spins)]
    left = left_sides(owns, weights_ref[0])
    for column in range(columns):
        right = right_ref[:, 0, column].reshape(groups * per_block, depth)
        term = product(left, right)
        for part in range(2):
            for spin in range(spins):
                start = (part * spins + spin) * per_block
                field_ref[(spin * columns + column) * 2 + part] += term[start : start + per_block]


def gather_whole(packed, place, weights, share):
    groups, _, deep, flat = (lax.axis_size(name) for name in AXES)
    sites = deep * flat
    _, per_block, depth = packed.shape
    columns = min(4, share // 2)
    spins = share // (2 * columns)
    near = lax.all_gather(packed, ("pair", "deep", "flat"))
    near = near.reshape(groups, sites, 4, per_block, depth)
    far = lax.ppermute(near, "core", [(0, 1), (1, 0)])
    wide = groups * per_block

    def half(right):
        return pl.pallas_call(
            add_terms,
            grid_spec=pltpu.PrefetchScalarGridSpec(
                num_scalar_prefetch=1,
                grid=(sites,),
                in_specs=[
                    pl.BlockSpec((1, 2, weights.shape[2]), lambda m, place: (m, 0, 0)),
                    pl.BlockSpec(
                        (1, 1, spins, per_block, depth),
                        lambda m, place: (place[0], m, place[4] // spins, 0, 0),
                    ),
                    pl.BlockSpec(
                        (groups, 1, columns, per_block, depth),
                        lambda m, place: (0, m, place[6] // columns, 0, 0),
                    ),
                ],
                out_specs=pl.BlockSpec((share, per_block, wide), lambda m, place: (0, 0, 0)),
            ),
            out_shape=jax.ShapeDtypeStruct((share, per_block, wide), jnp.float32),
            compiler_params=pltpu.CompilerParams(vmem_limit_bytes=40 * 1024 * 1024),
        )(place, weights, near, right)

    sides = [half(right).reshape(share, per_block, groups, per_block) for right in (near, far)]
    first = lax.axis_index("core") == 0
    even, odd = (jnp.where(first, a, b) for a, b in (sides, sides[::-1]))
    return jnp.stack([even, odd], 3).reshape(share, per_block, 2 * wide)


def shards(modes, momenta):
    groups, _, deep, flat = (lax.axis_size(name) for name in AXES)
    sites = deep * flat
    slots, steps, per_block, spin_colour, site_count = modes.shape
    share = steps * momenta.shape[0] * 32 // sites
    owned = (lax.axis_index("deep") * flat + lax.axis_index("flat")) * (share // 2)
    place = [lax.axis_index(name) for name in AXES]
    place = jnp.stack(place + [owned // 4 % 4, jnp.int32(flat), owned % 4]).astype(jnp.int32)

    mine = lax.dynamic_slice_in_dim(momenta, owned // 16, 1, 0)
    weights = phase_table(mine, jnp.int32(0), sites * site_count, LEXT)[0]
    weights = jnp.transpose(weights.reshape(2, sites, site_count), (1, 0, 2))

    if (groups, deep, flat) == (2, 4, 2) and steps == 1 and share in (8, 16, 32):
        own = jnp.transpose(modes[:, 0], (0, 2, 1, 3))
        return swap_in_windows(own, weights, share)
    packed = jnp.transpose(modes.reshape(slots, per_block, 4, 3, site_count), (2, 1, 0, 3, 4))
    packed = packed.reshape(4, per_block, slots * 3 * site_count)
    return gather_whole(packed, place, weights, share)


def solution(mesh):
    count, sites = mesh.shape["blk"], mesh.shape["site"]
    flat = 2 ** (int(math.log2(sites)) // 2)
    split = Mesh(mesh.devices.reshape(count // 2, 2, sites // flat, flat), AXES)
    placed = (P(None, None, ("pair", "core"), None, ("deep", "flat")), P())
    return jax.shard_map(
        shards,
        mesh=split,
        in_specs=placed,
        out_specs=P(("deep", "flat"), ("pair", "core"), None),
        check_vma=False,
    )
```

```python
import functools
import math

import jax
import jax.numpy as jnp
from jax import lax
from jax.experimental import pallas as pl
from jax.experimental.pallas import tpu as pltpu
from jax.sharding import Mesh, PartitionSpec as P

LEXT = 48

TWO_PI = 2.0 * math.pi

AXES = ("pair", "core", "deep", "flat")


def phase_table(momenta, first_site, site_count, extent):
    flat = first_site + jnp.arange(site_count, dtype=jnp.int32)
    coords = jnp.stack([flat % extent, flat // extent % extent, flat // (extent * extent)], 0)
    turns = jnp.mod(jnp.sum(momenta[:, :, None] * coords[None, :, :], axis=1), extent)
    angle = turns.astype(jnp.float32) * (TWO_PI / extent)
    return jnp.stack([jnp.cos(angle), jnp.sin(angle)], 1)


def left_sides(owns, weights):
    depth = owns[0].shape[1]
    half = depth // 2
    cosine = jnp.tile(weights[0:1], (1, depth // weights.shape[1]))
    sine = jnp.tile(weights[1:2], (1, depth // weights.shape[1]))
    cosine_rows = [[], []]
    sine_rows = [[], []]
    for own in owns:
        own = own.astype(jnp.float32)
        by_cos = (own * cosine).astype(jnp.bfloat16)
        by_sin = (own * sine).astype(jnp.bfloat16)
        cosine_rows[0].append(by_cos)
        cosine_rows[1].append(jnp.concatenate([-by_cos[:, half:], by_cos[:, :half]], 1))
        sine_rows[0].append(jnp.concatenate([-by_sin[:, half:], by_sin[:, :half]], 1))
        sine_rows[1].append(-by_sin)
    return jnp.concatenate(cosine_rows[0] + cosine_rows[1] + sine_rows[0] + sine_rows[1], 0)


def product(left, right):
    dims = (((1,), (1,)), ((), ()))
    terms = lax.dot_general(left, right, dims, preferred_element_type=jnp.float32)
    half = terms.shape[0] // 2
    return terms[:half] + terms[half:]


def add_shards(names, where, slots, has_totals, given, half, last, share, weights_ref, *refs):
    refs = list(refs)
    left_ref = None if given else refs.pop()
    if half:
        sems, row_ref, field_ref = (refs.pop() for _ in range(3))
    if last:
        sems, row_ref, far_ref, field_ref, _ = (refs.pop() for _ in range(5))
    else:
        out_ref = refs.pop()
    totals_in = refs.pop() if has_totals else None
    left_ref = refs.pop() if given else left_ref

    def shard(name):
        index, slot = where[name]
        return refs[index] if slot is None else refs[index].at[slot]

    def spin_rows(name, spin):
        ref = shard(name)
        tiles = [ref[part, spin * colours + x] for part in range(2) for x in range(colours)]
        return jnp.concatenate(tiles, 1)

    pair, core, level, beside = (lax.axis_index(name) for name in AXES)
    flat = lax.axis_size("flat")
    _, spin_colour, per_block, _ = shard(names[0]).shape
    columns, colours = 4, spin_colour // 4
    first_s = lax.rem(lax.div((level * flat + beside) * (share // 2), 4), 4)
    spins = left_ref.shape[1] // (4 * per_block)

    def send_columns(dx, near, far):
        lane = lax.broadcasted_iota(jnp.int32, (per_block, 2 * per_block), 1)
        start = pl.multiple_of(jnp.bitwise_xor(pair, dx) * (2 * per_block), 2 * per_block)
        copies = []
        for spin in range(spins):
            for column in range(0, columns, 2):
                first = (spin * columns + column) * 2
                across = slice(column * per_block, (column + 2) * per_block)
                for part in range(2):
                    top = (part * spins + spin) * per_block
                    one = near(slice(top, top + per_block), across)
                    two = far(slice(top, top + per_block), across)
                    even = jnp.where(core == 0, one, two)
                    odd = jnp.where(core == 0, two, one)
                    row_ref[first + part] = jnp.where(
                        lane < per_block, even, pltpu.roll(odd, per_block, 1)
                    )
                    row_ref[first + part + 2] = jnp.where(
                        lane < per_block, pltpu.roll(even, per_block, 1), odd
                    )
                four = pl.ds(first, 4)
                target = field_ref.at[four, :, pl.ds(start, 2 * per_block)]
                copies.append(
                    pltpu.make_async_copy(row_ref.at[four], target, sems.at[len(copies)])
                )
                copies[-1].start()
        return copies

    def term(name):
        side, kind, dz = name
        right = jnp.concatenate([spin_rows(name, r) for r in range(columns)], 0)
        turn = core if side == "near" else 1 - core
        dx, dy = {"O": (0, 0), "A": (1 - turn, turn), "B": (turn, 1 - turn), "AB": (1, 1)}[kind]
        if kind in ("O", "AB"):
            slot = slots.index((dy, dz))
        else:
            slot = slots.index((0, dz)) + dy
        return dx, product(left_ref[slot], right)

    if last:
        far_ref[...] = totals_in[1, 1] + sum(term(name)[1] for name in names)
        copies = send_columns(
            1,
            lambda rows, across: totals_in[0, 1, rows, across],
            lambda rows, across: far_ref[rows, across],
        )
        for copy in copies:
            copy.wait()
        return

    if has_totals:
        out_ref[...] = totals_in[...]
    else:
        out_ref[...] = jnp.zeros_like(out_ref)
    if not given:
        for slot, (dy, dz) in enumerate(slots):
            site = jnp.bitwise_xor(level, dz) * flat + jnp.bitwise_xor(beside, dy)
            if dy == 0:
                owns = [spin_rows(("near", "O", dz), first_s + s) for s in range(spins)]
            else:
                owns = [
                    jnp.where(
                        core == 0,
                        spin_rows(("near", "B", dz), first_s + s),
                        spin_rows(("near", "A", dz), first_s + s),
                    )
                    for s in range(spins)
                ]
            left_ref[slot] = left_sides(owns, weights_ref[site])
    for name in names:
        dx, added = term(name)
        out_ref[0 if name[0] == "near" else 1, dx] += added
    if half:
        copies = send_columns(
            0,
            lambda rows, across: out_ref[0, 0, rows, across],
            lambda rows, across: out_ref[1, 0, rows, across],
        )
        for copy in copies:
            copy.wait()


def route_second(*refs):
    o1_ref, o2_ref, stack_ref, both_ref = refs[3:]
    for slot in range(5):
        stack_ref[slot] = refs[slot][...]
    both_ref[0] = o1_ref[...]
    both_ref[1] = o2_ref[...]


def route_third(ab2_ref, o3_ref, a12_ref, b12_ref, stack_ref, a1_ref):
    stack_ref[0] = ab2_ref[...]
    stack_ref[1] = o3_ref[...]
    stack_ref[2:4] = a12_ref[...]
    stack_ref[4:6] = b12_ref[...]
    a1_ref[...] = a12_ref[0]


def route_last(a3_ref, ab3_ref, stack_ref):
    stack_ref[0] = a3_ref[...]
    stack_ref[1] = ab3_ref[...]


def left_slots(names):
    needed = set()
    for _, kind, dz in names:
        needed |= {"O": {(0, dz)}, "AB": {(1, dz)}}.get(kind, {(0, dz), (1, dz)})
    return sorted(needed, key=lambda slot: (slot[1], slot[0]))


def swap_in_windows(own, weights, share):
    shape = tuple(lax.axis_size(name) for name in AXES)
    columns, per_block = 4, own.shape[2]
    depth = own.size // (columns * per_block)
    spins = share // (2 * columns)
    tall, wide = 2 * spins * per_block, columns * per_block
    strides = (shape[1] * shape[2] * shape[3], shape[2] * shape[3], shape[3], 1)

    def move(array, target):
        pairs = []
        for p in range(shape[0]):
            for c in range(shape[1]):
                for z in range(shape[2]):
                    for y in range(shape[3]):
                        ends = (p, c, z, y), target(p, c, z, y)
                        pairs.append(
                            tuple(sum(a * b for a, b in zip(end, strides)) for end in ends)
                        )
        return lax.ppermute(array, AXES, pairs)

    def hop_a(array):
        return move(array, lambda p, c, z, y: (p ^ 1, c, z, y) if c == 0 else (p, c, z, y ^ 1))

    def hop_b(array):
        return move(array, lambda p, c, z, y: (p, c, z, y ^ 1) if c == 0 else (p ^ 1, c, z, y))

    def hop_z(array, by):
        return move(array, lambda p, c, z, y: (p, c, z ^ by, y))

    def swap(array):
        return move(array, lambda p, c, z, y: (p, c ^ 1, z, y))

    arrays = {}
    where = {}

    def put(key, array, side, kinds):
        arrays[key] = array
        for slot, (kind, dz) in enumerate(kinds):
            where[(side, kind, dz)] = (key, slot if len(kinds) > 1 else None)

    def near(kind, dz):
        key, slot = where[("near", kind, dz)]
        return arrays[key] if slot is None else arrays[key][slot]

    def add(names, totals, keep=None, left=None, half=False, field=None, weight=1):
        given, last = left is not None, field is not None
        slots, left = left if given else (keep or left_slots(names), None)
        uses = list(names)
        for dy, dz in [] if given else slots:
            uses += [("near", kind, dz) for kind in (("A", "B") if dy else ("O",))]
        keys = sorted({where[name][0] for name in uses})
        places = {name: (keys.index(where[name][0]), where[name][1]) for name in uses}
        operands = [weights] + [arrays[key] for key in keys]
        operands += [each for each in (left, totals, field) if each is not None]
        total_shape = (2, 2, tall, wide)
        left_shape = (len(slots), 2 * tall, depth)
        field_shape = (share, per_block, 4 * per_block)
        block, apart = (pl.BlockSpec(memory_space=space) for space in (pltpu.VMEM, pltpu.HBM))
        in_specs, outs, scratch, aliases = [block] * len(operands), [], [], {}
        if last:
            in_specs[-1] = apart
            aliases = {len(operands) - 1: 0}
            scratch.append(pltpu.VMEM(total_shape[2:], jnp.float32))
        else:
            outs.append((total_shape, jnp.float32, block))
        if half or last:
            outs.append((field_shape, jnp.float32, apart))
            scratch.append(pltpu.VMEM((*field_shape[:2], 2 * per_block), jnp.float32))
            scratch.append(pltpu.SemaphoreType.DMA((spins * columns // 2,)))
        if keep:
            outs.append((left_shape, jnp.bfloat16, block))
        elif not given:
            scratch.append(pltpu.VMEM(left_shape, jnp.bfloat16))
        out = pl.pallas_call(
            functools.partial(
                add_shards, tuple(names), places, slots, totals is not None, given, half, last, share
            ),
            in_specs=in_specs,
            out_specs=[spec for _, _, spec in outs],
            out_shape=[jax.ShapeDtypeStruct(shape, dtype) for shape, dtype, _ in outs],
            scratch_shapes=scratch,
            input_output_aliases=aliases,
            compiler_params=pltpu.CompilerParams(vmem_limit_bytes=40 * 1024 * 1024),
            cost_estimate=pl.CostEstimate(
                flops=4 * tall * wide * depth * len(names) * weight,
                bytes_accessed=wide * depth * 2 * len(names) + 8 * 4 * tall * wide,
                transcendentals=0,
            ),
        )(*operands)
        if keep:
            return out[0], (slots, out[1])
        return out if half else out[0]

    def fence(totals):
        nonlocal arrays
        arrays, totals = lax.optimization_barrier((arrays, totals))
        return totals

    put("1a", hop_z(own, 2), "near", [("O", 2)])
    put("1b", hop_a(own), "near", [("A", 0)])
    put("1c", hop_z(own, 1), "near", [("O", 1)])
    put("1d", hop_b(own), "near", [("B", 0)])
    put("1e", hop_b(near("A", 0)), "near", [("AB", 0)])
    put("1f", swap(own), "far", [("O", 0)])
    put("9", own, "near", [("O", 0)])
    weights = fence(weights)

    def route(kernel, operands, counts, weight=0):
        block = pl.BlockSpec(memory_space=pltpu.VMEM)
        shapes = [(count,) * (count > 1) + own.shape for count in counts]
        routed = pl.pallas_call(
            kernel,
            in_specs=[block] * len(operands),
            out_specs=[block] * len(counts),
            out_shape=[jax.ShapeDtypeStruct(shape, own.dtype) for shape in shapes],
            compiler_params=pltpu.CompilerParams(vmem_limit_bytes=24 * 1024 * 1024),
            cost_estimate=pl.CostEstimate(flops=weight, bytes_accessed=0, transcendentals=0),
        )(*operands)
        return fence(routed)

    first = [("O", 0), ("A", 0), ("B", 0), ("AB", 0), ("O", 1), ("O", 2)]
    second = [("AB", 2), ("O", 3), ("A", 1), ("A", 2), ("B", 1), ("B", 2)]
    third = [("A", 3), ("B", 3)]
    fourth = [("AB", 3), ("AB", 1)]
    stack, both = route(route_second, [near(*kind) for kind in first[1:]], (5, 2))
    totals = add([("near", *kind) for kind in first], None)
    o3, ab2 = hop_z(near("O", 2), 1), hop_z(near("AB", 0), 2)
    a12, b12 = hop_a(both), hop_b(both)
    put("2a", swap(stack), "far", first[1:])
    totals = fence(totals)

    totals = add([("far", *kind) for kind in first], totals)
    put("2c", o3, "near", [("O", 3)])
    totals = fence(totals)

    a3, b3 = hop_a(near("O", 3)), hop_b(near("O", 3))
    totals = add([("near", "O", 3)], totals, weight=45)
    put("2d", ab2, "near", [("AB", 2)])
    put("2e", a12, "near", [("A", 1), ("A", 2)])
    put("2f", b12, "near", [("B", 1), ("B", 2)])
    totals = fence(totals)

    ab3 = hop_z(near("AB", 2), 1)
    stack, a1 = route(route_third, [arrays[key] for key in ("2d", "2c", "2e", "2f")], (6, 1))
    far2, ab1 = swap(stack), hop_b(a1)
    names = [("near", *kind) for kind in second if kind != ("O", 3)]
    totals = add(names, totals)
    a3, b3, totals = lax.optimization_barrier((a3, b3, totals))
    (stack,) = route(route_last, [a3, b3], (2,), weight=10**11)
    put("3a", stack, "near", third)
    far3 = swap(stack)
    put("3d", far2, "far", second)
    names = [("far", *kind) for kind in second] + [("near", *kind) for kind in third]
    totals = add(names, totals, weight=10)
    put("3e", far3, "far", third)
    names = [("far", *kind) for kind in third]
    totals, field = add(names, totals, half=True)
    put("3b", ab3, "near", fourth[:1])
    put("3c", ab1, "near", fourth[1:])
    totals, field = fence((totals, field))

    far4 = [swap(near(*kind)) for kind in fourth]
    names = [("near", *kind) for kind in fourth]
    totals, (slots, left) = add(names, totals, keep=left_slots(names))
    put("4b", far4[0], "far", fourth[:1])
    put("4c", far4[1], "far", fourth[1:])
    totals, left, field = fence((totals, left, field))
    return add([("far", *kind) for kind in fourth], totals, left=(slots, left), field=field)


def add_terms(place_ref, weights_ref, left_ref, right_ref, field_ref):
    @pl.when(pl.program_id(0) == 0)
    def _():
        field_ref[...] = jnp.zeros_like(field_ref)

    spins = left_ref.shape[2]
    groups, columns, per_block, depth = right_ref.shape[0], *right_ref.shape[2:]
    owns = [left_ref[0, 0, spin] for spin in range(spins)]
    left = left_sides(owns, weights_ref[0])
    for column in range(columns):
        right = right_ref[:, 0, column].reshape(groups * per_block, depth)
        term = product(left, right)
        for part in range(2):
            for spin in range(spins):
                start = (part * spins + spin) * per_block
                field_ref[(spin * columns + column) * 2 + part] += term[start : start + per_block]


def gather_whole(packed, place, weights, share):
    groups, _, deep, flat = (lax.axis_size(name) for name in AXES)
    sites = deep * flat
    _, per_block, depth = packed.shape
    columns = min(4, share // 2)
    spins = share // (2 * columns)
    near = lax.all_gather(packed, ("pair", "deep", "flat"))
    near = near.reshape(groups, sites, 4, per_block, depth)
    far = lax.ppermute(near, "core", [(0, 1), (1, 0)])
    wide = groups * per_block

    def half(right):
        return pl.pallas_call(
            add_terms,
            grid_spec=pltpu.PrefetchScalarGridSpec(
                num_scalar_prefetch=1,
                grid=(sites,),
                in_specs=[
                    pl.BlockSpec((1, 2, weights.shape[2]), lambda m, place: (m, 0, 0)),
                    pl.BlockSpec(
                        (1, 1, spins, per_block, depth),
                        lambda m, place: (place[0], m, place[4] // spins, 0, 0),
                    ),
                    pl.BlockSpec(
                        (groups, 1, columns, per_block, depth),
                        lambda m, place: (0, m, place[6] // columns, 0, 0),
                    ),
                ],
                out_specs=pl.BlockSpec((share, per_block, wide), lambda m, place: (0, 0, 0)),
            ),
            out_shape=jax.ShapeDtypeStruct((share, per_block, wide), jnp.float32),
            compiler_params=pltpu.CompilerParams(vmem_limit_bytes=40 * 1024 * 1024),
        )(place, weights, near, right)

    sides = [half(right).reshape(share, per_block, groups, per_block) for right in (near, far)]
    first = lax.axis_index("core") == 0
    even, odd = (jnp.where(first, a, b) for a, b in (sides, sides[::-1]))
    return jnp.stack([even, odd], 3).reshape(share, per_block, 2 * wide)


def shards(modes, momenta):
    groups, _, deep, flat = (lax.axis_size(name) for name in AXES)
    sites = deep * flat
    slots, steps, per_block, spin_colour, site_count = modes.shape
    share = steps * momenta.shape[0] * 32 // sites
    owned = (lax.axis_index("deep") * flat + lax.axis_index("flat")) * (share // 2)
    place = [lax.axis_index(name) for name in AXES]
    place = jnp.stack(place + [owned // 4 % 4, jnp.int32(flat), owned % 4]).astype(jnp.int32)

    mine = lax.dynamic_slice_in_dim(momenta, owned // 16, 1, 0)
    weights = phase_table(mine, jnp.int32(0), sites * site_count, LEXT)[0]
    weights = jnp.transpose(weights.reshape(2, sites, site_count), (1, 0, 2))

    if (groups, deep, flat) == (2, 4, 2) and steps == 1 and share in (8, 16, 32):
        own = jnp.transpose(modes[:, 0], (0, 2, 1, 3))
        return swap_in_windows(own, weights, share)
    packed = jnp.transpose(modes.reshape(slots, per_block, 4, 3, site_count), (2, 1, 0, 3, 4))
    packed = packed.reshape(4, per_block, slots * 3 * site_count)
    return gather_whole(packed, place, weights, share)


def solution(mesh):
    count, sites = mesh.shape["blk"], mesh.shape["site"]
    flat = 2 ** (int(math.log2(sites)) // 2)
    split = Mesh(mesh.devices.reshape(count // 2, 2, sites // flat, flat), AXES)
    placed = (P(None, None, ("pair", "core"), None, ("deep", "flat")), P())
    return jax.shard_map(
        shards,
        mesh=split,
        in_specs=placed,
        out_specs=P(("deep", "flat"), ("pair", "core"), None),
        check_vma=False,
    )
```

```python
import functools
import math

import jax
import jax.numpy as jnp
from jax import lax
from jax.experimental import pallas as pl
from jax.experimental.pallas import tpu as pltpu
from jax.sharding import Mesh, PartitionSpec as P

LEXT = 48

TWO_PI = 2.0 * math.pi

AXES = ("pair", "core", "deep", "flat")


def phase_table(momenta, first_site, site_count, extent):
    flat = first_site + jnp.arange(site_count, dtype=jnp.int32)
    coords = jnp.stack([flat % extent, flat // extent % extent, flat // (extent * extent)], 0)
    turns = jnp.mod(jnp.sum(momenta[:, :, None] * coords[None, :, :], axis=1), extent)
    angle = turns.astype(jnp.float32) * (TWO_PI / extent)
    return jnp.stack([jnp.cos(angle), jnp.sin(angle)], 1)


def left_sides(owns, weights):
    depth = owns[0].shape[1]
    half = depth // 2
    cosine = jnp.tile(weights[0:1], (1, depth // weights.shape[1]))
    sine = jnp.tile(weights[1:2], (1, depth // weights.shape[1]))
    cosine_rows = [[], []]
    sine_rows = [[], []]
    for own in owns:
        own = own.astype(jnp.float32)
        by_cos = (own * cosine).astype(jnp.bfloat16)
        by_sin = (own * sine).astype(jnp.bfloat16)
        cosine_rows[0].append(by_cos)
        cosine_rows[1].append(jnp.concatenate([-by_cos[:, half:], by_cos[:, :half]], 1))
        sine_rows[0].append(jnp.concatenate([-by_sin[:, half:], by_sin[:, :half]], 1))
        sine_rows[1].append(-by_sin)
    return jnp.concatenate(cosine_rows[0] + cosine_rows[1] + sine_rows[0] + sine_rows[1], 0)


def product(left, right):
    dims = (((1,), (1,)), ((), ()))
    terms = lax.dot_general(left, right, dims, preferred_element_type=jnp.float32)
    half = terms.shape[0] // 2
    return terms[:half] + terms[half:]


def add_shards(names, where, slots, has_totals, given, half, last, share, weights_ref, *refs):
    refs = list(refs)
    left_ref = None if given else refs.pop()
    if half:
        sems, row_ref, left_ref = left_ref, refs.pop(), refs.pop()
        field_ref = refs.pop()
    if last:
        sems, row_ref, far_ref, field_ref, _ = (refs.pop() for _ in range(5))
    else:
        out_ref = refs.pop()
    totals_in = refs.pop() if has_totals else None
    left_ref = refs.pop() if given else left_ref

    def shard(name):
        index, slot = where[name]
        return refs[index] if slot is None else refs[index].at[slot]

    def spin_rows(name, spin):
        ref = shard(name)
        tiles = [ref[part, spin * colours + x] for part in range(2) for x in range(colours)]
        return jnp.concatenate(tiles, 1)

    pair, core, level, beside = (lax.axis_index(name) for name in AXES)
    flat = lax.axis_size("flat")
    _, spin_colour, per_block, _ = shard(names[0]).shape
    columns, colours = 4, spin_colour // 4
    first_s = lax.rem(lax.div((level * flat + beside) * (share // 2), 4), 4)
    spins = left_ref.shape[1] // (4 * per_block)

    def send_columns(dx, near, far):
        lane = lax.broadcasted_iota(jnp.int32, (per_block, 2 * per_block), 1)
        start = pl.multiple_of(jnp.bitwise_xor(pair, dx) * (2 * per_block), 2 * per_block)
        copies = []
        for spin in range(spins):
            for column in range(0, columns, 2):
                first = (spin * columns + column) * 2
                across = slice(column * per_block, (column + 2) * per_block)
                for part in range(2):
                    top = (part * spins + spin) * per_block
                    one = near(slice(top, top + per_block), across)
                    two = far(slice(top, top + per_block), across)
                    even = jnp.where(core == 0, one, two)
                    odd = jnp.where(core == 0, two, one)
                    row_ref[first + part] = jnp.where(
                        lane < per_block, even, pltpu.roll(odd, per_block, 1)
                    )
                    row_ref[first + part + 2] = jnp.where(
                        lane < per_block, pltpu.roll(even, per_block, 1), odd
                    )
                four = pl.ds(first, 4)
                target = field_ref.at[four, :, pl.ds(start, 2 * per_block)]
                copies.append(
                    pltpu.make_async_copy(row_ref.at[four], target, sems.at[len(copies)])
                )
                copies[-1].start()
        return copies

    def term(name):
        side, kind, dz = name
        right = jnp.concatenate([spin_rows(name, r) for r in range(columns)], 0)
        turn = core if side == "near" else 1 - core
        dx, dy = {"O": (0, 0), "A": (1 - turn, turn), "B": (turn, 1 - turn), "AB": (1, 1)}[kind]
        if kind in ("O", "AB"):
            slot = slots.index((dy, dz))
        else:
            slot = slots.index((0, dz)) + dy
        return dx, product(left_ref[slot], right)

    if last:
        far_ref[...] = totals_in[1, 1] + sum(term(name)[1] for name in names)
        copies = send_columns(
            1,
            lambda rows, across: totals_in[0, 1, rows, across],
            lambda rows, across: far_ref[rows, across],
        )
        for copy in copies:
            copy.wait()
        return

    if has_totals:
        out_ref[...] = totals_in[...]
    else:
        out_ref[...] = jnp.zeros_like(out_ref)
    if not given:
        for slot, (dy, dz) in enumerate(slots):
            site = jnp.bitwise_xor(level, dz) * flat + jnp.bitwise_xor(beside, dy)
            if dy == 0:
                owns = [spin_rows(("near", "O", dz), first_s + s) for s in range(spins)]
            else:
                owns = [
                    jnp.where(
                        core == 0,
                        spin_rows(("near", "B", dz), first_s + s),
                        spin_rows(("near", "A", dz), first_s + s),
                    )
                    for s in range(spins)
                ]
            left_ref[slot] = left_sides(owns, weights_ref[site])
    copies = []
    for index, name in enumerate(names):
        if half and index == half:
            copies = send_columns(
                0,
                lambda rows, across: out_ref[0, 0, rows, across],
                lambda rows, across: out_ref[1, 0, rows, across],
            )
        dx, added = term(name)
        out_ref[0 if name[0] == "near" else 1, dx] += added
    for copy in copies:
        copy.wait()


def route_second(*refs):
    o1_ref, o2_ref, stack_ref, both_ref = refs[3:]
    for slot in range(5):
        stack_ref[slot] = refs[slot][...]
    both_ref[0] = o1_ref[...]
    both_ref[1] = o2_ref[...]


def route_third(ab2_ref, o3_ref, a12_ref, b12_ref, stack_ref, a1_ref):
    stack_ref[0] = ab2_ref[...]
    stack_ref[1] = o3_ref[...]
    stack_ref[2:4] = a12_ref[...]
    stack_ref[4:6] = b12_ref[...]
    a1_ref[...] = a12_ref[0]


def route_last(a3_ref, ab3_ref, stack_ref):
    stack_ref[0] = a3_ref[...]
    stack_ref[1] = ab3_ref[...]


def left_slots(names):
    needed = set()
    for _, kind, dz in names:
        needed |= {"O": {(0, dz)}, "AB": {(1, dz)}}.get(kind, {(0, dz), (1, dz)})
    return sorted(needed, key=lambda slot: (slot[1], slot[0]))


def swap_in_windows(own, weights, share):
    shape = tuple(lax.axis_size(name) for name in AXES)
    columns, per_block = 4, own.shape[2]
    depth = own.size // (columns * per_block)
    spins = share // (2 * columns)
    tall, wide = 2 * spins * per_block, columns * per_block
    strides = (shape[1] * shape[2] * shape[3], shape[2] * shape[3], shape[3], 1)

    def move(array, target):
        pairs = []
        for p in range(shape[0]):
            for c in range(shape[1]):
                for z in range(shape[2]):
                    for y in range(shape[3]):
                        ends = (p, c, z, y), target(p, c, z, y)
                        pairs.append(
                            tuple(sum(a * b for a, b in zip(end, strides)) for end in ends)
                        )
        return lax.ppermute(array, AXES, pairs)

    def hop_a(array):
        return move(array, lambda p, c, z, y: (p ^ 1, c, z, y) if c == 0 else (p, c, z, y ^ 1))

    def hop_b(array):
        return move(array, lambda p, c, z, y: (p, c, z, y ^ 1) if c == 0 else (p ^ 1, c, z, y))

    def hop_z(array, by):
        return move(array, lambda p, c, z, y: (p, c, z ^ by, y))

    def swap(array):
        return move(array, lambda p, c, z, y: (p, c ^ 1, z, y))

    arrays = {}
    where = {}

    def put(key, array, side, kinds):
        arrays[key] = array
        for slot, (kind, dz) in enumerate(kinds):
            where[(side, kind, dz)] = (key, slot if len(kinds) > 1 else None)

    def near(kind, dz):
        key, slot = where[("near", kind, dz)]
        return arrays[key] if slot is None else arrays[key][slot]

    def add(names, totals, keep=None, left=None, half=0, field=None, weight=1):
        given, last = left is not None, field is not None
        slots, left = left if given else (keep or left_slots(names), None)
        uses = list(names)
        for dy, dz in [] if given else slots:
            uses += [("near", kind, dz) for kind in (("A", "B") if dy else ("O",))]
        keys = sorted({where[name][0] for name in uses})
        places = {name: (keys.index(where[name][0]), where[name][1]) for name in uses}
        operands = [weights] + [arrays[key] for key in keys]
        operands += [each for each in (left, totals, field) if each is not None]
        total_shape = (2, 2, tall, wide)
        left_shape = (len(slots), 2 * tall, depth)
        field_shape = (share, per_block, 4 * per_block)
        block, apart = (pl.BlockSpec(memory_space=space) for space in (pltpu.VMEM, pltpu.HBM))
        in_specs, outs, scratch, aliases = [block] * len(operands), [], [], {}
        if last:
            in_specs[-1] = apart
            aliases = {len(operands) - 1: 0}
            scratch.append(pltpu.VMEM(total_shape[2:], jnp.float32))
        else:
            outs.append((total_shape, jnp.float32, block))
        if half or last:
            outs.append((field_shape, jnp.float32, apart))
            scratch.append(pltpu.VMEM((*field_shape[:2], 2 * per_block), jnp.float32))
            scratch.append(pltpu.SemaphoreType.DMA((spins * columns // 2,)))
        if keep:
            outs.append((left_shape, jnp.bfloat16, block))
        elif not given:
            scratch.append(pltpu.VMEM(left_shape, jnp.bfloat16))
        out = pl.pallas_call(
            functools.partial(
                add_shards, tuple(names), places, slots, totals is not None, given, half, last, share
            ),
            in_specs=in_specs,
            out_specs=[spec for _, _, spec in outs],
            out_shape=[jax.ShapeDtypeStruct(shape, dtype) for shape, dtype, _ in outs],
            scratch_shapes=scratch,
            input_output_aliases=aliases,
            compiler_params=pltpu.CompilerParams(vmem_limit_bytes=40 * 1024 * 1024),
            cost_estimate=pl.CostEstimate(
                flops=4 * tall * wide * depth * len(names) * weight,
                bytes_accessed=wide * depth * 2 * len(names) + 8 * 4 * tall * wide,
                transcendentals=0,
            ),
        )(*operands)
        return (*out[:-1], (slots, out[-1])) if keep else out[0]

    def fence(totals):
        nonlocal arrays
        arrays, totals = lax.optimization_barrier((arrays, totals))
        return totals

    put("1a", hop_z(own, 2), "near", [("O", 2)])
    put("1b", hop_a(own), "near", [("A", 0)])
    put("1c", hop_z(own, 1), "near", [("O", 1)])
    put("1d", hop_b(own), "near", [("B", 0)])
    put("1e", hop_b(near("A", 0)), "near", [("AB", 0)])
    put("1f", swap(own), "far", [("O", 0)])
    put("9", own, "near", [("O", 0)])
    weights = fence(weights)

    def route(kernel, operands, counts, weight=0):
        block = pl.BlockSpec(memory_space=pltpu.VMEM)
        shapes = [(count,) * (count > 1) + own.shape for count in counts]
        routed = pl.pallas_call(
            kernel,
            in_specs=[block] * len(operands),
            out_specs=[block] * len(counts),
            out_shape=[jax.ShapeDtypeStruct(shape, own.dtype) for shape in shapes],
            compiler_params=pltpu.CompilerParams(vmem_limit_bytes=24 * 1024 * 1024),
            cost_estimate=pl.CostEstimate(flops=weight, bytes_accessed=0, transcendentals=0),
        )(*operands)
        return fence(routed)

    first = [("O", 0), ("A", 0), ("B", 0), ("AB", 0), ("O", 1), ("O", 2)]
    second = [("AB", 2), ("O", 3), ("A", 1), ("A", 2), ("B", 1), ("B", 2)]
    third = [("A", 3), ("B", 3)]
    fourth = [("AB", 3), ("AB", 1)]
    stack, both = route(route_second, [near(*kind) for kind in first[1:]], (5, 2))
    totals = add([("near", *kind) for kind in first], None)
    o3, ab2 = hop_z(near("O", 2), 1), hop_z(near("AB", 0), 2)
    a12, b12 = hop_a(both), hop_b(both)
    put("2a", swap(stack), "far", first[1:])
    totals = fence(totals)

    totals = add([("far", *kind) for kind in first], totals)
    put("2c", o3, "near", [("O", 3)])
    totals = fence(totals)

    a3, b3 = hop_a(near("O", 3)), hop_b(near("O", 3))
    totals = add([("near", "O", 3)], totals, weight=45)
    put("2d", ab2, "near", [("AB", 2)])
    put("2e", a12, "near", [("A", 1), ("A", 2)])
    put("2f", b12, "near", [("B", 1), ("B", 2)])
    totals = fence(totals)

    ab3 = hop_z(near("AB", 2), 1)
    stack, a1 = route(route_third, [arrays[key] for key in ("2d", "2c", "2e", "2f")], (6, 1))
    far2, ab1 = swap(stack), hop_b(a1)
    names = [("near", *kind) for kind in second if kind != ("O", 3)]
    totals = add(names, totals)
    a3, b3, totals = lax.optimization_barrier((a3, b3, totals))
    (stack,) = route(route_last, [a3, b3], (2,), weight=10**11)
    put("3a", stack, "near", third)
    far3 = swap(stack)
    put("3d", far2, "far", second)
    names = [("far", *kind) for kind in second] + [("near", *kind) for kind in third]
    totals = add(names, totals, weight=10)
    put("3b", ab3, "near", fourth[:1])
    put("3c", ab1, "near", fourth[1:])
    totals = fence(totals)

    far4 = [swap(near(*kind)) for kind in fourth]
    put("4a", far3, "far", third)
    names = [("far", *kind) for kind in third] + [("near", *kind) for kind in fourth]
    totals, field, (slots, left) = add(names, totals, keep=left_slots(names), half=len(third))
    put("4b", far4[0], "far", fourth[:1])
    put("4c", far4[1], "far", fourth[1:])
    totals, left, field = fence((totals, left, field))
    return add([("far", *kind) for kind in fourth], totals, left=(slots, left), field=field)


def add_terms(place_ref, weights_ref, left_ref, right_ref, field_ref):
    @pl.when(pl.program_id(0) == 0)
    def _():
        field_ref[...] = jnp.zeros_like(field_ref)

    spins = left_ref.shape[2]
    groups, columns, per_block, depth = right_ref.shape[0], *right_ref.shape[2:]
    owns = [left_ref[0, 0, spin] for spin in range(spins)]
    left = left_sides(owns, weights_ref[0])
    for column in range(columns):
        right = right_ref[:, 0, column].reshape(groups * per_block, depth)
        term = product(left, right)
        for part in range(2):
            for spin in range(spins):
                start = (part * spins + spin) * per_block
                field_ref[(spin * columns + column) * 2 + part] += term[start : start + per_block]


def gather_whole(packed, place, weights, share):
    groups, _, deep, flat = (lax.axis_size(name) for name in AXES)
    sites = deep * flat
    _, per_block, depth = packed.shape
    columns = min(4, share // 2)
    spins = share // (2 * columns)
    near = lax.all_gather(packed, ("pair", "deep", "flat"))
    near = near.reshape(groups, sites, 4, per_block, depth)
    far = lax.ppermute(near, "core", [(0, 1), (1, 0)])
    wide = groups * per_block

    def half(right):
        return pl.pallas_call(
            add_terms,
            grid_spec=pltpu.PrefetchScalarGridSpec(
                num_scalar_prefetch=1,
                grid=(sites,),
                in_specs=[
                    pl.BlockSpec((1, 2, weights.shape[2]), lambda m, place: (m, 0, 0)),
                    pl.BlockSpec(
                        (1, 1, spins, per_block, depth),
                        lambda m, place: (place[0], m, place[4] // spins, 0, 0),
                    ),
                    pl.BlockSpec(
                        (groups, 1, columns, per_block, depth),
                        lambda m, place: (0, m, place[6] // columns, 0, 0),
                    ),
                ],
                out_specs=pl.BlockSpec((share, per_block, wide), lambda m, place: (0, 0, 0)),
            ),
            out_shape=jax.ShapeDtypeStruct((share, per_block, wide), jnp.float32),
            compiler_params=pltpu.CompilerParams(vmem_limit_bytes=40 * 1024 * 1024),
        )(place, weights, near, right)

    sides = [half(right).reshape(share, per_block, groups, per_block) for right in (near, far)]
    first = lax.axis_index("core") == 0
    even, odd = (jnp.where(first, a, b) for a, b in (sides, sides[::-1]))
    return jnp.stack([even, odd], 3).reshape(share, per_block, 2 * wide)


def shards(modes, momenta):
    groups, _, deep, flat = (lax.axis_size(name) for name in AXES)
    sites = deep * flat
    slots, steps, per_block, spin_colour, site_count = modes.shape
    share = steps * momenta.shape[0] * 32 // sites
    owned = (lax.axis_index("deep") * flat + lax.axis_index("flat")) * (share // 2)
    place = [lax.axis_index(name) for name in AXES]
    place = jnp.stack(place + [owned // 4 % 4, jnp.int32(flat), owned % 4]).astype(jnp.int32)

    mine = lax.dynamic_slice_in_dim(momenta, owned // 16, 1, 0)
    weights = phase_table(mine, jnp.int32(0), sites * site_count, LEXT)[0]
    weights = jnp.transpose(weights.reshape(2, sites, site_count), (1, 0, 2))

    if (groups, deep, flat) == (2, 4, 2) and steps == 1 and share in (8, 16, 32):
        own = jnp.transpose(modes[:, 0], (0, 2, 1, 3))
        return swap_in_windows(own, weights, share)
    packed = jnp.transpose(modes.reshape(slots, per_block, 4, 3, site_count), (2, 1, 0, 3, 4))
    packed = packed.reshape(4, per_block, slots * 3 * site_count)
    return gather_whole(packed, place, weights, share)


def solution(mesh):
    count, sites = mesh.shape["blk"], mesh.shape["site"]
    flat = 2 ** (int(math.log2(sites)) // 2)
    split = Mesh(mesh.devices.reshape(count // 2, 2, sites // flat, flat), AXES)
    placed = (P(None, None, ("pair", "core"), None, ("deep", "flat")), P())
    return jax.shard_map(
        shards,
        mesh=split,
        in_specs=placed,
        out_specs=P(("deep", "flat"), ("pair", "core"), None),
        check_vma=False,
    )
```

```python
import functools
import math

import jax
import jax.numpy as jnp
from jax import lax
from jax.experimental import pallas as pl
from jax.experimental.pallas import tpu as pltpu
from jax.sharding import Mesh, PartitionSpec as P

LEXT = 48

TWO_PI = 2.0 * math.pi

AXES = ("pair", "core", "deep", "flat")


def phase_table(momenta, first_site, site_count, extent):
    flat = first_site + jnp.arange(site_count, dtype=jnp.int32)
    coords = jnp.stack([flat % extent, flat // extent % extent, flat // (extent * extent)], 0)
    turns = jnp.mod(jnp.sum(momenta[:, :, None] * coords[None, :, :], axis=1), extent)
    angle = turns.astype(jnp.float32) * (TWO_PI / extent)
    return jnp.stack([jnp.cos(angle), jnp.sin(angle)], 1)


def left_sides(owns, weights):
    depth = owns[0].shape[1]
    half = depth // 2
    cosine = jnp.tile(weights[0:1], (1, depth // weights.shape[1]))
    sine = jnp.tile(weights[1:2], (1, depth // weights.shape[1]))
    cosine_rows = [[], []]
    sine_rows = [[], []]
    for own in owns:
        own = own.astype(jnp.float32)
        by_cos = (own * cosine).astype(jnp.bfloat16)
        by_sin = (own * sine).astype(jnp.bfloat16)
        cosine_rows[0].append(by_cos)
        cosine_rows[1].append(jnp.concatenate([-by_cos[:, half:], by_cos[:, :half]], 1))
        sine_rows[0].append(jnp.concatenate([-by_sin[:, half:], by_sin[:, :half]], 1))
        sine_rows[1].append(-by_sin)
    return jnp.concatenate(cosine_rows[0] + cosine_rows[1] + sine_rows[0] + sine_rows[1], 0)


def product(left, right):
    dims = (((1,), (1,)), ((), ()))
    terms = lax.dot_general(left, right, dims, preferred_element_type=jnp.float32)
    half = terms.shape[0] // 2
    return terms[:half] + terms[half:]


def add_shards(names, where, slots, has_totals, given, half, last, share, weights_ref, *refs):
    refs = list(refs)
    left_ref = None if given else refs.pop()
    if half:
        sems, row_ref, left_ref = left_ref, refs.pop(), refs.pop()
        field_ref = refs.pop()
    if last:
        sems, row_ref, far_ref, field_ref, _ = (refs.pop() for _ in range(5))
    else:
        out_ref = refs.pop()
    totals_in = refs.pop() if has_totals else None
    left_ref = refs.pop() if given else left_ref

    def shard(name):
        index, slot = where[name]
        return refs[index] if slot is None else refs[index].at[slot]

    def spin_rows(name, spin):
        ref = shard(name)
        tiles = [ref[part, spin * colours + x] for part in range(2) for x in range(colours)]
        return jnp.concatenate(tiles, 1)

    pair, core, level, beside = (lax.axis_index(name) for name in AXES)
    flat = lax.axis_size("flat")
    _, spin_colour, per_block, _ = shard(names[0]).shape
    columns, colours = 4, spin_colour // 4
    first_s = lax.rem(lax.div((level * flat + beside) * (share // 2), 4), 4)
    spins = left_ref.shape[1] // (4 * per_block)

    def send_columns(dx, near, far):
        lane = lax.broadcasted_iota(jnp.int32, (per_block, 2 * per_block), 1)
        start = pl.multiple_of(jnp.bitwise_xor(pair, dx) * (2 * per_block), 2 * per_block)
        copies = []
        for spin in range(spins):
            for column in range(0, columns, 2):
                first = (spin * columns + column) * 2
                across = slice(column * per_block, (column + 2) * per_block)
                for part in range(2):
                    top = (part * spins + spin) * per_block
                    one = near(slice(top, top + per_block), across)
                    two = far(slice(top, top + per_block), across)
                    even = jnp.where(core == 0, one, two)
                    odd = jnp.where(core == 0, two, one)
                    row_ref[first + part] = jnp.where(
                        lane < per_block, even, pltpu.roll(odd, per_block, 1)
                    )
                    row_ref[first + part + 2] = jnp.where(
                        lane < per_block, pltpu.roll(even, per_block, 1), odd
                    )
                four = pl.ds(first, 4)
                target = field_ref.at[four, :, pl.ds(start, 2 * per_block)]
                copies.append(
                    pltpu.make_async_copy(row_ref.at[four], target, sems.at[len(copies)])
                )
                copies[-1].start()
        return copies

    def term(name):
        side, kind, dz = name
        right = jnp.concatenate([spin_rows(name, r) for r in range(columns)], 0)
        turn = core if side == "near" else 1 - core
        dx, dy = {"O": (0, 0), "A": (1 - turn, turn), "B": (turn, 1 - turn), "AB": (1, 1)}[kind]
        if kind in ("O", "AB"):
            slot = slots.index((dy, dz))
        else:
            slot = slots.index((0, dz)) + dy
        return dx, product(left_ref[slot], right)

    if last:
        far_ref[...] = totals_in[1, 1] + sum(term(name)[1] for name in names)
        copies = send_columns(
            1,
            lambda rows, across: totals_in[0, 1, rows, across],
            lambda rows, across: far_ref[rows, across],
        )
        for copy in copies:
            copy.wait()
        return

    if has_totals:
        out_ref[...] = totals_in[...]
    else:
        out_ref[...] = jnp.zeros_like(out_ref)
    if not given:
        for slot, (dy, dz) in enumerate(slots):
            site = jnp.bitwise_xor(level, dz) * flat + jnp.bitwise_xor(beside, dy)
            if dy == 0:
                owns = [spin_rows(("near", "O", dz), first_s + s) for s in range(spins)]
            else:
                owns = [
                    jnp.where(
                        core == 0,
                        spin_rows(("near", "B", dz), first_s + s),
                        spin_rows(("near", "A", dz), first_s + s),
                    )
                    for s in range(spins)
                ]
            left_ref[slot] = left_sides(owns, weights_ref[site])
    for name in names:
        dx, added = term(name)
        out_ref[0 if name[0] == "near" else 1, dx] += added
    if half:
        copies = send_columns(
            0,
            lambda rows, across: out_ref[0, 0, rows, across],
            lambda rows, across: out_ref[1, 0, rows, across],
        )
        for copy in copies:
            copy.wait()


def route_second(*refs):
    o1_ref, o2_ref, stack_ref, both_ref = refs[3:]
    for slot in range(5):
        stack_ref[slot] = refs[slot][...]
    both_ref[0] = o1_ref[...]
    both_ref[1] = o2_ref[...]


def route_third(ab2_ref, o3_ref, a12_ref, b12_ref, stack_ref, a1_ref):
    stack_ref[0] = ab2_ref[...]
    stack_ref[1] = o3_ref[...]
    stack_ref[2:4] = a12_ref[...]
    stack_ref[4:6] = b12_ref[...]
    a1_ref[...] = a12_ref[0]


def route_last(a3_ref, ab3_ref, stack_ref):
    stack_ref[0] = a3_ref[...]
    stack_ref[1] = ab3_ref[...]


def left_slots(names):
    needed = set()
    for _, kind, dz in names:
        needed |= {"O": {(0, dz)}, "AB": {(1, dz)}}.get(kind, {(0, dz), (1, dz)})
    return sorted(needed, key=lambda slot: (slot[1], slot[0]))


def swap_in_windows(own, weights, share):
    shape = tuple(lax.axis_size(name) for name in AXES)
    columns, per_block = 4, own.shape[2]
    depth = own.size // (columns * per_block)
    spins = share // (2 * columns)
    tall, wide = 2 * spins * per_block, columns * per_block
    strides = (shape[1] * shape[2] * shape[3], shape[2] * shape[3], shape[3], 1)

    def move(array, target):
        pairs = []
        for p in range(shape[0]):
            for c in range(shape[1]):
                for z in range(shape[2]):
                    for y in range(shape[3]):
                        ends = (p, c, z, y), target(p, c, z, y)
                        pairs.append(
                            tuple(sum(a * b for a, b in zip(end, strides)) for end in ends)
                        )
        return lax.ppermute(array, AXES, pairs)

    def hop_a(array):
        return move(array, lambda p, c, z, y: (p ^ 1, c, z, y) if c == 0 else (p, c, z, y ^ 1))

    def hop_b(array):
        return move(array, lambda p, c, z, y: (p, c, z, y ^ 1) if c == 0 else (p ^ 1, c, z, y))

    def hop_z(array, by):
        return move(array, lambda p, c, z, y: (p, c, z ^ by, y))

    def swap(array):
        return move(array, lambda p, c, z, y: (p, c ^ 1, z, y))

    arrays = {}
    where = {}

    def put(key, array, side, kinds):
        arrays[key] = array
        for slot, (kind, dz) in enumerate(kinds):
            where[(side, kind, dz)] = (key, slot if len(kinds) > 1 else None)

    def near(kind, dz):
        key, slot = where[("near", kind, dz)]
        return arrays[key] if slot is None else arrays[key][slot]

    def add(names, totals, keep=None, left=None, half=False, field=None, weight=1):
        given, last = left is not None, field is not None
        slots, left = left if given else (keep or left_slots(names), None)
        uses = list(names)
        for dy, dz in [] if given else slots:
            uses += [("near", kind, dz) for kind in (("A", "B") if dy else ("O",))]
        keys = sorted({where[name][0] for name in uses})
        places = {name: (keys.index(where[name][0]), where[name][1]) for name in uses}
        operands = [weights] + [arrays[key] for key in keys]
        operands += [each for each in (left, totals, field) if each is not None]
        total_shape = (2, 2, tall, wide)
        left_shape = (len(slots), 2 * tall, depth)
        field_shape = (share, per_block, 4 * per_block)
        block, apart = (pl.BlockSpec(memory_space=space) for space in (pltpu.VMEM, pltpu.HBM))
        in_specs, outs, scratch, aliases = [block] * len(operands), [], [], {}
        if last:
            in_specs[-1] = apart
            aliases = {len(operands) - 1: 0}
            scratch.append(pltpu.VMEM(total_shape[2:], jnp.float32))
        else:
            outs.append((total_shape, jnp.float32, block))
        if half or last:
            outs.append((field_shape, jnp.float32, apart))
            scratch.append(pltpu.VMEM((*field_shape[:2], 2 * per_block), jnp.float32))
            scratch.append(pltpu.SemaphoreType.DMA((spins * columns // 2,)))
        if keep:
            outs.append((left_shape, jnp.bfloat16, block))
        elif not given:
            scratch.append(pltpu.VMEM(left_shape, jnp.bfloat16))
        out = pl.pallas_call(
            functools.partial(
                add_shards, tuple(names), places, slots, totals is not None, given, half, last, share
            ),
            in_specs=in_specs,
            out_specs=[spec for _, _, spec in outs],
            out_shape=[jax.ShapeDtypeStruct(shape, dtype) for shape, dtype, _ in outs],
            scratch_shapes=scratch,
            input_output_aliases=aliases,
            compiler_params=pltpu.CompilerParams(vmem_limit_bytes=40 * 1024 * 1024),
            cost_estimate=pl.CostEstimate(
                flops=4 * tall * wide * depth * len(names) * weight,
                bytes_accessed=wide * depth * 2 * len(names) + 8 * 4 * tall * wide,
                transcendentals=0,
            ),
        )(*operands)
        return (*out[:-1], (slots, out[-1])) if keep else out[0]

    def fence(totals):
        nonlocal arrays
        arrays, totals = lax.optimization_barrier((arrays, totals))
        return totals

    put("1a", hop_z(own, 2), "near", [("O", 2)])
    put("1b", hop_a(own), "near", [("A", 0)])
    put("1c", hop_z(own, 1), "near", [("O", 1)])
    put("1d", hop_b(own), "near", [("B", 0)])
    put("1e", hop_b(near("A", 0)), "near", [("AB", 0)])
    put("1f", swap(own), "far", [("O", 0)])
    put("9", own, "near", [("O", 0)])
    weights = fence(weights)

    def route(kernel, operands, counts, weight=0):
        block = pl.BlockSpec(memory_space=pltpu.VMEM)
        shapes = [(count,) * (count > 1) + own.shape for count in counts]
        routed = pl.pallas_call(
            kernel,
            in_specs=[block] * len(operands),
            out_specs=[block] * len(counts),
            out_shape=[jax.ShapeDtypeStruct(shape, own.dtype) for shape in shapes],
            compiler_params=pltpu.CompilerParams(vmem_limit_bytes=24 * 1024 * 1024),
            cost_estimate=pl.CostEstimate(flops=weight, bytes_accessed=0, transcendentals=0),
        )(*operands)
        return fence(routed)

    first = [("O", 0), ("A", 0), ("B", 0), ("AB", 0), ("O", 1), ("O", 2)]
    second = [("AB", 2), ("O", 3), ("A", 1), ("A", 2), ("B", 1), ("B", 2)]
    third = [("A", 3), ("B", 3)]
    fourth = [("AB", 3), ("AB", 1)]
    stack, both = route(route_second, [near(*kind) for kind in first[1:]], (5, 2))
    totals = add([("near", *kind) for kind in first], None)
    o3, ab2 = hop_z(near("O", 2), 1), hop_z(near("AB", 0), 2)
    a12, b12 = hop_a(both), hop_b(both)
    put("2a", swap(stack), "far", first[1:])
    totals = fence(totals)

    totals = add([("far", *kind) for kind in first], totals)
    put("2c", o3, "near", [("O", 3)])
    totals = fence(totals)

    a3, b3 = hop_a(near("O", 3)), hop_b(near("O", 3))
    totals = add([("near", "O", 3)], totals)
    put("2d", ab2, "near", [("AB", 2)])
    put("2e", a12, "near", [("A", 1), ("A", 2)])
    put("2f", b12, "near", [("B", 1), ("B", 2)])
    totals = fence(totals)

    ab3 = hop_z(near("AB", 2), 1)
    stack, a1 = route(route_third, [arrays[key] for key in ("2d", "2c", "2e", "2f")], (6, 1))
    far2, ab1 = swap(stack), hop_b(a1)
    names = [("near", *kind) for kind in second if kind != ("O", 3)]
    totals = add(names, totals)
    a3, b3, totals = lax.optimization_barrier((a3, b3, totals))
    (stack,) = route(route_last, [a3, b3], (2,), weight=10**11)
    put("3a", stack, "near", third)
    far3 = swap(stack)
    put("3d", far2, "far", second)
    names = [("far", *kind) for kind in second] + [("near", *kind) for kind in third]
    totals = add(names, totals, weight=10)
    put("3b", ab3, "near", fourth[:1])
    put("3c", ab1, "near", fourth[1:])
    totals = fence(totals)

    far4 = [swap(near(*kind)) for kind in fourth]
    put("4a", far3, "far", third)
    names = [("far", *kind) for kind in third] + [("near", *kind) for kind in fourth]
    totals, field, (slots, left) = add(names, totals, keep=left_slots(names), half=True)
    put("4b", far4[0], "far", fourth[:1])
    put("4c", far4[1], "far", fourth[1:])
    totals, left, field = fence((totals, left, field))
    return add([("far", *kind) for kind in fourth], totals, left=(slots, left), field=field)


def add_terms(place_ref, weights_ref, left_ref, right_ref, field_ref):
    @pl.when(pl.program_id(0) == 0)
    def _():
        field_ref[...] = jnp.zeros_like(field_ref)

    spins = left_ref.shape[2]
    groups, columns, per_block, depth = right_ref.shape[0], *right_ref.shape[2:]
    owns = [left_ref[0, 0, spin] for spin in range(spins)]
    left = left_sides(owns, weights_ref[0])
    for column in range(columns):
        right = right_ref[:, 0, column].reshape(groups * per_block, depth)
        term = product(left, right)
        for part in range(2):
            for spin in range(spins):
                start = (part * spins + spin) * per_block
                field_ref[(spin * columns + column) * 2 + part] += term[start : start + per_block]


def gather_whole(packed, place, weights, share):
    groups, _, deep, flat = (lax.axis_size(name) for name in AXES)
    sites = deep * flat
    _, per_block, depth = packed.shape
    columns = min(4, share // 2)
    spins = share // (2 * columns)
    near = lax.all_gather(packed, ("pair", "deep", "flat"))
    near = near.reshape(groups, sites, 4, per_block, depth)
    far = lax.ppermute(near, "core", [(0, 1), (1, 0)])
    wide = groups * per_block

    def half(right):
        return pl.pallas_call(
            add_terms,
            grid_spec=pltpu.PrefetchScalarGridSpec(
                num_scalar_prefetch=1,
                grid=(sites,),
                in_specs=[
                    pl.BlockSpec((1, 2, weights.shape[2]), lambda m, place: (m, 0, 0)),
                    pl.BlockSpec(
                        (1, 1, spins, per_block, depth),
                        lambda m, place: (place[0], m, place[4] // spins, 0, 0),
                    ),
                    pl.BlockSpec(
                        (groups, 1, columns, per_block, depth),
                        lambda m, place: (0, m, place[6] // columns, 0, 0),
                    ),
                ],
                out_specs=pl.BlockSpec((share, per_block, wide), lambda m, place: (0, 0, 0)),
            ),
            out_shape=jax.ShapeDtypeStruct((share, per_block, wide), jnp.float32),
            compiler_params=pltpu.CompilerParams(vmem_limit_bytes=40 * 1024 * 1024),
        )(place, weights, near, right)

    sides = [half(right).reshape(share, per_block, groups, per_block) for right in (near, far)]
    first = lax.axis_index("core") == 0
    even, odd = (jnp.where(first, a, b) for a, b in (sides, sides[::-1]))
    return jnp.stack([even, odd], 3).reshape(share, per_block, 2 * wide)


def shards(modes, momenta):
    groups, _, deep, flat = (lax.axis_size(name) for name in AXES)
    sites = deep * flat
    slots, steps, per_block, spin_colour, site_count = modes.shape
    share = steps * momenta.shape[0] * 32 // sites
    owned = (lax.axis_index("deep") * flat + lax.axis_index("flat")) * (share // 2)
    place = [lax.axis_index(name) for name in AXES]
    place = jnp.stack(place + [owned // 4 % 4, jnp.int32(flat), owned % 4]).astype(jnp.int32)

    mine = lax.dynamic_slice_in_dim(momenta, owned // 16, 1, 0)
    weights = phase_table(mine, jnp.int32(0), sites * site_count, LEXT)[0]
    weights = jnp.transpose(weights.reshape(2, sites, site_count), (1, 0, 2))

    if (groups, deep, flat) == (2, 4, 2) and steps == 1 and share in (8, 16, 32):
        own = jnp.transpose(modes[:, 0], (0, 2, 1, 3))
        return swap_in_windows(own, weights, share)
    packed = jnp.transpose(modes.reshape(slots, per_block, 4, 3, site_count), (2, 1, 0, 3, 4))
    packed = packed.reshape(4, per_block, slots * 3 * site_count)
    return gather_whole(packed, place, weights, share)


def solution(mesh):
    count, sites = mesh.shape["blk"], mesh.shape["site"]
    flat = 2 ** (int(math.log2(sites)) // 2)
    split = Mesh(mesh.devices.reshape(count // 2, 2, sites // flat, flat), AXES)
    placed = (P(None, None, ("pair", "core"), None, ("deep", "flat")), P())
    return jax.shard_map(
        shards,
        mesh=split,
        in_specs=placed,
        out_specs=P(("deep", "flat"), ("pair", "core"), None),
        check_vma=False,
    )
```

```python
import functools
import math

import jax
import jax.numpy as jnp
from jax import lax
from jax.experimental import pallas as pl
from jax.experimental.pallas import tpu as pltpu
from jax.sharding import Mesh, PartitionSpec as P

LEXT = 48

TWO_PI = 2.0 * math.pi

AXES = ("pair", "core", "deep", "flat")


def phase_table(momenta, first_site, site_count, extent):
    flat = first_site + jnp.arange(site_count, dtype=jnp.int32)
    coords = jnp.stack([flat % extent, flat // extent % extent, flat // (extent * extent)], 0)
    turns = jnp.mod(jnp.sum(momenta[:, :, None] * coords[None, :, :], axis=1), extent)
    angle = turns.astype(jnp.float32) * (TWO_PI / extent)
    return jnp.stack([jnp.cos(angle), jnp.sin(angle)], 1)


def left_sides(owns, weights):
    depth = owns[0].shape[1]
    half = depth // 2
    cosine = jnp.tile(weights[0:1], (1, depth // weights.shape[1]))
    sine = jnp.tile(weights[1:2], (1, depth // weights.shape[1]))
    cosine_rows = [[], []]
    sine_rows = [[], []]
    for own in owns:
        own = own.astype(jnp.float32)
        by_cos = (own * cosine).astype(jnp.bfloat16)
        by_sin = (own * sine).astype(jnp.bfloat16)
        cosine_rows[0].append(by_cos)
        cosine_rows[1].append(jnp.concatenate([-by_cos[:, half:], by_cos[:, :half]], 1))
        sine_rows[0].append(jnp.concatenate([-by_sin[:, half:], by_sin[:, :half]], 1))
        sine_rows[1].append(-by_sin)
    return jnp.concatenate(cosine_rows[0] + cosine_rows[1] + sine_rows[0] + sine_rows[1], 0)


def product(left, right):
    dims = (((1,), (1,)), ((), ()))
    terms = lax.dot_general(left, right, dims, preferred_element_type=jnp.float32)
    half = terms.shape[0] // 2
    return terms[:half] + terms[half:]


def add_shards(names, where, slots, has_totals, given, half, last, share, weights_ref, *refs):
    refs = list(refs)
    left_ref = None if given else refs.pop()
    if half:
        sems, row_ref, field_ref = (refs.pop() for _ in range(3))
    if last:
        sems, row_ref, far_ref, field_ref, _ = (refs.pop() for _ in range(5))
    else:
        out_ref = refs.pop()
    totals_in = refs.pop() if has_totals else None
    left_ref = refs.pop() if given else left_ref

    def shard(name):
        index, slot = where[name]
        return refs[index] if slot is None else refs[index].at[slot]

    def spin_rows(name, spin):
        ref = shard(name)
        tiles = [ref[part, spin * colours + x] for part in range(2) for x in range(colours)]
        return jnp.concatenate(tiles, 1)

    pair, core, level, beside = (lax.axis_index(name) for name in AXES)
    flat = lax.axis_size("flat")
    _, spin_colour, per_block, _ = shard(names[0]).shape
    columns, colours = 4, spin_colour // 4
    first_s = lax.rem(lax.div((level * flat + beside) * (share // 2), 4), 4)
    spins = left_ref.shape[1] // (4 * per_block)

    def send_columns(dx, near, far):
        lane = lax.broadcasted_iota(jnp.int32, (per_block, 2 * per_block), 1)
        start = pl.multiple_of(jnp.bitwise_xor(pair, dx) * (2 * per_block), 2 * per_block)
        copies = []
        for spin in range(spins):
            for column in range(0, columns, 2):
                first = (spin * columns + column) * 2
                across = slice(column * per_block, (column + 2) * per_block)
                for part in range(2):
                    top = (part * spins + spin) * per_block
                    one = near(slice(top, top + per_block), across)
                    two = far(slice(top, top + per_block), across)
                    even = jnp.where(core == 0, one, two)
                    odd = jnp.where(core == 0, two, one)
                    row_ref[first + part] = jnp.where(
                        lane < per_block, even, pltpu.roll(odd, per_block, 1)
                    )
                    row_ref[first + part + 2] = jnp.where(
                        lane < per_block, pltpu.roll(even, per_block, 1), odd
                    )
                four = pl.ds(first, 4)
                target = field_ref.at[four, :, pl.ds(start, 2 * per_block)]
                copies.append(
                    pltpu.make_async_copy(row_ref.at[four], target, sems.at[len(copies)])
                )
                copies[-1].start()
        return copies

    def term(name):
        side, kind, dz = name
        right = jnp.concatenate([spin_rows(name, r) for r in range(columns)], 0)
        turn = core if side == "near" else 1 - core
        dx, dy = {"O": (0, 0), "A": (1 - turn, turn), "B": (turn, 1 - turn), "AB": (1, 1)}[kind]
        if kind in ("O", "AB"):
            slot = slots.index((dy, dz))
        else:
            slot = slots.index((0, dz)) + dy
        return dx, product(left_ref[slot], right)

    if last:
        far_ref[...] = totals_in[1, 1] + sum(term(name)[1] for name in names)
        copies = send_columns(
            1,
            lambda rows, across: totals_in[0, 1, rows, across],
            lambda rows, across: far_ref[rows, across],
        )
        for copy in copies:
            copy.wait()
        return

    if has_totals:
        out_ref[...] = totals_in[...]
    else:
        out_ref[...] = jnp.zeros_like(out_ref)
    if not given:
        for slot, (dy, dz) in enumerate(slots):
            site = jnp.bitwise_xor(level, dz) * flat + jnp.bitwise_xor(beside, dy)
            if dy == 0:
                owns = [spin_rows(("near", "O", dz), first_s + s) for s in range(spins)]
            else:
                owns = [
                    jnp.where(
                        core == 0,
                        spin_rows(("near", "B", dz), first_s + s),
                        spin_rows(("near", "A", dz), first_s + s),
                    )
                    for s in range(spins)
                ]
            left_ref[slot] = left_sides(owns, weights_ref[site])
    copies = []
    for index, name in enumerate(names):
        if half and index == half:
            copies = send_columns(
                0,
                lambda rows, across: out_ref[0, 0, rows, across],
                lambda rows, across: out_ref[1, 0, rows, across],
            )
        dx, added = term(name)
        out_ref[0 if name[0] == "near" else 1, dx] += added
    for copy in copies:
        copy.wait()


def route_second(*refs):
    o1_ref, o2_ref, stack_ref, both_ref = refs[3:]
    for slot in range(5):
        stack_ref[slot] = refs[slot][...]
    both_ref[0] = o1_ref[...]
    both_ref[1] = o2_ref[...]


def route_third(ab2_ref, o3_ref, a12_ref, b12_ref, stack_ref, a1_ref):
    stack_ref[0] = ab2_ref[...]
    stack_ref[1] = o3_ref[...]
    stack_ref[2:4] = a12_ref[...]
    stack_ref[4:6] = b12_ref[...]
    a1_ref[...] = a12_ref[0]


def route_last(a3_ref, ab3_ref, stack_ref):
    stack_ref[0] = a3_ref[...]
    stack_ref[1] = ab3_ref[...]


def left_slots(names):
    needed = set()
    for _, kind, dz in names:
        needed |= {"O": {(0, dz)}, "AB": {(1, dz)}}.get(kind, {(0, dz), (1, dz)})
    return sorted(needed, key=lambda slot: (slot[1], slot[0]))


def swap_in_windows(own, weights, share):
    shape = tuple(lax.axis_size(name) for name in AXES)
    columns, per_block = 4, own.shape[2]
    depth = own.size // (columns * per_block)
    spins = share // (2 * columns)
    tall, wide = 2 * spins * per_block, columns * per_block
    strides = (shape[1] * shape[2] * shape[3], shape[2] * shape[3], shape[3], 1)

    def move(array, target):
        pairs = []
        for p in range(shape[0]):
            for c in range(shape[1]):
                for z in range(shape[2]):
                    for y in range(shape[3]):
                        ends = (p, c, z, y), target(p, c, z, y)
                        pairs.append(
                            tuple(sum(a * b for a, b in zip(end, strides)) for end in ends)
                        )
        return lax.ppermute(array, AXES, pairs)

    def hop_a(array):
        return move(array, lambda p, c, z, y: (p ^ 1, c, z, y) if c == 0 else (p, c, z, y ^ 1))

    def hop_b(array):
        return move(array, lambda p, c, z, y: (p, c, z, y ^ 1) if c == 0 else (p ^ 1, c, z, y))

    def hop_z(array, by):
        return move(array, lambda p, c, z, y: (p, c, z ^ by, y))

    def swap(array):
        return move(array, lambda p, c, z, y: (p, c ^ 1, z, y))

    arrays = {}
    where = {}

    def put(key, array, side, kinds):
        arrays[key] = array
        for slot, (kind, dz) in enumerate(kinds):
            where[(side, kind, dz)] = (key, slot if len(kinds) > 1 else None)

    def near(kind, dz):
        key, slot = where[("near", kind, dz)]
        return arrays[key] if slot is None else arrays[key][slot]

    def add(names, totals, keep=None, left=None, half=0, field=None, weight=1):
        given, last = left is not None, field is not None
        slots, left = left if given else (keep or left_slots(names), None)
        uses = list(names)
        for dy, dz in [] if given else slots:
            uses += [("near", kind, dz) for kind in (("A", "B") if dy else ("O",))]
        keys = sorted({where[name][0] for name in uses})
        places = {name: (keys.index(where[name][0]), where[name][1]) for name in uses}
        operands = [weights] + [arrays[key] for key in keys]
        operands += [each for each in (left, totals, field) if each is not None]
        total_shape = (2, 2, tall, wide)
        left_shape = (len(slots), 2 * tall, depth)
        field_shape = (share, per_block, 4 * per_block)
        block, apart = (pl.BlockSpec(memory_space=space) for space in (pltpu.VMEM, pltpu.HBM))
        in_specs, outs, scratch, aliases = [block] * len(operands), [], [], {}
        if last:
            in_specs[-1] = apart
            aliases = {len(operands) - 1: 0}
            scratch.append(pltpu.VMEM(total_shape[2:], jnp.float32))
        else:
            outs.append((total_shape, jnp.float32, block))
        if half or last:
            outs.append((field_shape, jnp.float32, apart))
            scratch.append(pltpu.VMEM((*field_shape[:2], 2 * per_block), jnp.float32))
            scratch.append(pltpu.SemaphoreType.DMA((spins * columns // 2,)))
        if keep:
            outs.append((left_shape, jnp.bfloat16, block))
        elif not given:
            scratch.append(pltpu.VMEM(left_shape, jnp.bfloat16))
        out = pl.pallas_call(
            functools.partial(
                add_shards, tuple(names), places, slots, totals is not None, given, half, last, share
            ),
            in_specs=in_specs,
            out_specs=[spec for _, _, spec in outs],
            out_shape=[jax.ShapeDtypeStruct(shape, dtype) for shape, dtype, _ in outs],
            scratch_shapes=scratch,
            input_output_aliases=aliases,
            compiler_params=pltpu.CompilerParams(vmem_limit_bytes=40 * 1024 * 1024),
            cost_estimate=pl.CostEstimate(
                flops=4 * tall * wide * depth * len(names) * weight,
                bytes_accessed=wide * depth * 2 * len(names) + 8 * 4 * tall * wide,
                transcendentals=0,
            ),
        )(*operands)
        if keep:
            return out[0], (slots, out[1])
        return out if half else out[0]

    def fence(totals):
        nonlocal arrays
        arrays, totals = lax.optimization_barrier((arrays, totals))
        return totals

    put("1a", hop_z(own, 2), "near", [("O", 2)])
    put("1b", hop_a(own), "near", [("A", 0)])
    put("1c", hop_z(own, 1), "near", [("O", 1)])
    put("1d", hop_b(own), "near", [("B", 0)])
    put("1e", hop_b(near("A", 0)), "near", [("AB", 0)])
    put("1f", swap(own), "far", [("O", 0)])
    put("9", own, "near", [("O", 0)])
    weights = fence(weights)

    def route(kernel, operands, counts, weight=0):
        block = pl.BlockSpec(memory_space=pltpu.VMEM)
        shapes = [(count,) * (count > 1) + own.shape for count in counts]
        routed = pl.pallas_call(
            kernel,
            in_specs=[block] * len(operands),
            out_specs=[block] * len(counts),
            out_shape=[jax.ShapeDtypeStruct(shape, own.dtype) for shape in shapes],
            compiler_params=pltpu.CompilerParams(vmem_limit_bytes=24 * 1024 * 1024),
            cost_estimate=pl.CostEstimate(flops=weight, bytes_accessed=0, transcendentals=0),
        )(*operands)
        return fence(routed)

    first = [("O", 0), ("A", 0), ("B", 0), ("AB", 0), ("O", 1), ("O", 2)]
    second = [("AB", 2), ("O", 3), ("A", 1), ("A", 2), ("B", 1), ("B", 2)]
    third = [("A", 3), ("B", 3)]
    fourth = [("AB", 3), ("AB", 1)]
    stack, both = route(route_second, [near(*kind) for kind in first[1:]], (5, 2))
    totals = add([("near", *kind) for kind in first], None)
    o3, ab2 = hop_z(near("O", 2), 1), hop_z(near("AB", 0), 2)
    a12, b12 = hop_a(both), hop_b(both)
    put("2a", swap(stack), "far", first[1:])
    totals = fence(totals)

    totals = add([("far", *kind) for kind in first], totals)
    put("2c", o3, "near", [("O", 3)])
    totals = fence(totals)

    a3, b3 = hop_a(near("O", 3)), hop_b(near("O", 3))
    totals = add([("near", "O", 3)], totals, weight=45)
    put("2d", ab2, "near", [("AB", 2)])
    put("2e", a12, "near", [("A", 1), ("A", 2)])
    put("2f", b12, "near", [("B", 1), ("B", 2)])
    totals = fence(totals)

    ab3 = hop_z(near("AB", 2), 1)
    stack, a1 = route(route_third, [arrays[key] for key in ("2d", "2c", "2e", "2f")], (6, 1))
    far2, ab1 = swap(stack), hop_b(a1)
    names = [("near", *kind) for kind in second if kind != ("O", 3)]
    totals = add(names, totals)
    a3, b3, totals = lax.optimization_barrier((a3, b3, totals))
    (stack,) = route(route_last, [a3, b3], (2,), weight=10**11)
    put("3a", stack, "near", third)
    far3 = swap(stack)
    put("3d", far2, "far", second)
    names = [("far", *kind) for kind in second] + [("near", *kind) for kind in third]
    totals, (slots, left) = add(names, totals, keep=left_slots(names), weight=10)
    put("3b", ab3, "near", fourth[:1])
    put("3c", ab1, "near", fourth[1:])
    totals, left = fence((totals, left))

    far4 = [swap(near(*kind)) for kind in fourth]
    put("4a", far3, "far", third)
    names = [("far", *kind) for kind in third] + [("near", *kind) for kind in fourth]
    totals, field = add(names, totals, left=(slots, left), half=len(third))
    put("4b", far4[0], "far", fourth[:1])
    put("4c", far4[1], "far", fourth[1:])
    totals, left, field = fence((totals, left, field))
    return add([("far", *kind) for kind in fourth], totals, left=(slots, left), field=field)


def add_terms(place_ref, weights_ref, left_ref, right_ref, field_ref):
    @pl.when(pl.program_id(0) == 0)
    def _():
        field_ref[...] = jnp.zeros_like(field_ref)

    spins = left_ref.shape[2]
    groups, columns, per_block, depth = right_ref.shape[0], *right_ref.shape[2:]
    owns = [left_ref[0, 0, spin] for spin in range(spins)]
    left = left_sides(owns, weights_ref[0])
    for column in range(columns):
        right = right_ref[:, 0, column].reshape(groups * per_block, depth)
        term = product(left, right)
        for part in range(2):
            for spin in range(spins):
                start = (part * spins + spin) * per_block
                field_ref[(spin * columns + column) * 2 + part] += term[start : start + per_block]


def gather_whole(packed, place, weights, share):
    groups, _, deep, flat = (lax.axis_size(name) for name in AXES)
    sites = deep * flat
    _, per_block, depth = packed.shape
    columns = min(4, share // 2)
    spins = share // (2 * columns)
    near = lax.all_gather(packed, ("pair", "deep", "flat"))
    near = near.reshape(groups, sites, 4, per_block, depth)
    far = lax.ppermute(near, "core", [(0, 1), (1, 0)])
    wide = groups * per_block

    def half(right):
        return pl.pallas_call(
            add_terms,
            grid_spec=pltpu.PrefetchScalarGridSpec(
                num_scalar_prefetch=1,
                grid=(sites,),
                in_specs=[
                    pl.BlockSpec((1, 2, weights.shape[2]), lambda m, place: (m, 0, 0)),
                    pl.BlockSpec(
                        (1, 1, spins, per_block, depth),
                        lambda m, place: (place[0], m, place[4] // spins, 0, 0),
                    ),
                    pl.BlockSpec(
                        (groups, 1, columns, per_block, depth),
                        lambda m, place: (0, m, place[6] // columns, 0, 0),
                    ),
                ],
                out_specs=pl.BlockSpec((share, per_block, wide), lambda m, place: (0, 0, 0)),
            ),
            out_shape=jax.ShapeDtypeStruct((share, per_block, wide), jnp.float32),
            compiler_params=pltpu.CompilerParams(vmem_limit_bytes=40 * 1024 * 1024),
        )(place, weights, near, right)

    sides = [half(right).reshape(share, per_block, groups, per_block) for right in (near, far)]
    first = lax.axis_index("core") == 0
    even, odd = (jnp.where(first, a, b) for a, b in (sides, sides[::-1]))
    return jnp.stack([even, odd], 3).reshape(share, per_block, 2 * wide)


def shards(modes, momenta):
    groups, _, deep, flat = (lax.axis_size(name) for name in AXES)
    sites = deep * flat
    slots, steps, per_block, spin_colour, site_count = modes.shape
    share = steps * momenta.shape[0] * 32 // sites
    owned = (lax.axis_index("deep") * flat + lax.axis_index("flat")) * (share // 2)
    place = [lax.axis_index(name) for name in AXES]
    place = jnp.stack(place + [owned // 4 % 4, jnp.int32(flat), owned % 4]).astype(jnp.int32)

    mine = lax.dynamic_slice_in_dim(momenta, owned // 16, 1, 0)
    weights = phase_table(mine, jnp.int32(0), sites * site_count, LEXT)[0]
    weights = jnp.transpose(weights.reshape(2, sites, site_count), (1, 0, 2))

    if (groups, deep, flat) == (2, 4, 2) and steps == 1 and share in (8, 16, 32):
        own = jnp.transpose(modes[:, 0], (0, 2, 1, 3))
        return swap_in_windows(own, weights, share)
    packed = jnp.transpose(modes.reshape(slots, per_block, 4, 3, site_count), (2, 1, 0, 3, 4))
    packed = packed.reshape(4, per_block, slots * 3 * site_count)
    return gather_whole(packed, place, weights, share)


def solution(mesh):
    count, sites = mesh.shape["blk"], mesh.shape["site"]
    flat = 2 ** (int(math.log2(sites)) // 2)
    split = Mesh(mesh.devices.reshape(count // 2, 2, sites // flat, flat), AXES)
    placed = (P(None, None, ("pair", "core"), None, ("deep", "flat")), P())
    return jax.shard_map(
        shards,
        mesh=split,
        in_specs=placed,
        out_specs=P(("deep", "flat"), ("pair", "core"), None),
        check_vma=False,
    )
```

```python
import functools
import math

import jax
import jax.numpy as jnp
from jax import lax
from jax.experimental import pallas as pl
from jax.experimental.pallas import tpu as pltpu
from jax.sharding import Mesh, PartitionSpec as P

LEXT = 48

TWO_PI = 2.0 * math.pi

AXES = ("pair", "core", "deep", "flat")


def phase_table(momenta, first_site, site_count, extent):
    flat = first_site + jnp.arange(site_count, dtype=jnp.int32)
    coords = jnp.stack([flat % extent, flat // extent % extent, flat // (extent * extent)], 0)
    turns = jnp.mod(jnp.sum(momenta[:, :, None] * coords[None, :, :], axis=1), extent)
    angle = turns.astype(jnp.float32) * (TWO_PI / extent)
    return jnp.stack([jnp.cos(angle), jnp.sin(angle)], 1)


def left_sides(owns, weights):
    depth = owns[0].shape[1]
    half = depth // 2
    cosine = jnp.tile(weights[0:1], (1, depth // weights.shape[1]))
    sine = jnp.tile(weights[1:2], (1, depth // weights.shape[1]))
    cosine_rows = [[], []]
    sine_rows = [[], []]
    for own in owns:
        own = own.astype(jnp.float32)
        by_cos = (own * cosine).astype(jnp.bfloat16)
        by_sin = (own * sine).astype(jnp.bfloat16)
        cosine_rows[0].append(by_cos)
        cosine_rows[1].append(jnp.concatenate([-by_cos[:, half:], by_cos[:, :half]], 1))
        sine_rows[0].append(jnp.concatenate([-by_sin[:, half:], by_sin[:, :half]], 1))
        sine_rows[1].append(-by_sin)
    return jnp.concatenate(cosine_rows[0] + cosine_rows[1] + sine_rows[0] + sine_rows[1], 0)


def product(left, right):
    dims = (((1,), (1,)), ((), ()))
    terms = lax.dot_general(left, right, dims, preferred_element_type=jnp.float32)
    half = terms.shape[0] // 2
    return terms[:half] + terms[half:]


def add_shards(names, where, slots, has_totals, given, half, last, share, weights_ref, *refs):
    refs = list(refs)
    left_ref = None if given else refs.pop()
    if half:
        sems, row_ref, field_ref = (refs.pop() for _ in range(3))
    if last:
        sems, row_ref, far_ref, field_ref, _ = (refs.pop() for _ in range(5))
    else:
        out_ref = refs.pop()
    totals_in = refs.pop() if has_totals else None
    left_ref = refs.pop() if given else left_ref

    def shard(name):
        index, slot = where[name]
        return refs[index] if slot is None else refs[index].at[slot]

    def spin_rows(name, spin):
        ref = shard(name)
        tiles = [ref[part, spin * colours + x] for part in range(2) for x in range(colours)]
        return jnp.concatenate(tiles, 1)

    pair, core, level, beside = (lax.axis_index(name) for name in AXES)
    flat = lax.axis_size("flat")
    _, spin_colour, per_block, _ = shard(names[0]).shape
    columns, colours = 4, spin_colour // 4
    first_s = lax.rem(lax.div((level * flat + beside) * (share // 2), 4), 4)
    spins = left_ref.shape[1] // (4 * per_block)

    def send_columns(dx, near, far):
        lane = lax.broadcasted_iota(jnp.int32, (per_block, 2 * per_block), 1)
        start = pl.multiple_of(jnp.bitwise_xor(pair, dx) * (2 * per_block), 2 * per_block)

        def place(even, odd):
            for spin in range(spins):
                for column in range(0, columns, 2):
                    first = (spin * columns + column) * 2
                    across = slice(column * per_block, (column + 2) * per_block)
                    for part in range(2):
                        top = (part * spins + spin) * per_block
                        rows = slice(top, top + per_block)
                        one, two = even(rows, across), odd(rows, across)
                        row_ref[first + part] = jnp.where(
                            lane < per_block, one, pltpu.roll(two, per_block, 1)
                        )
                        row_ref[first + part + 2] = jnp.where(
                            lane < per_block, pltpu.roll(one, per_block, 1), two
                        )

        @pl.when(core == 0)
        def _():
            place(near, far)

        @pl.when(core != 0)
        def _():
            place(far, near)

        copies = []
        for index in range(spins * columns // 2):
            four = pl.ds(4 * index, 4)
            target = field_ref.at[four, :, pl.ds(start, 2 * per_block)]
            copies.append(pltpu.make_async_copy(row_ref.at[four], target, sems.at[index]))
            copies[-1].start()
        return copies

    def term(name):
        side, kind, dz = name
        right = jnp.concatenate([spin_rows(name, r) for r in range(columns)], 0)
        turn = core if side == "near" else 1 - core
        dx, dy = {"O": (0, 0), "A": (1 - turn, turn), "B": (turn, 1 - turn), "AB": (1, 1)}[kind]
        if kind in ("O", "AB"):
            slot = slots.index((dy, dz))
        else:
            slot = slots.index((0, dz)) + dy
        return dx, product(left_ref[slot], right)

    if last:
        far_ref[...] = totals_in[1, 1] + sum(term(name)[1] for name in names)
        copies = send_columns(
            1,
            lambda rows, across: totals_in[0, 1, rows, across],
            lambda rows, across: far_ref[rows, across],
        )
        for copy in copies:
            copy.wait()
        return

    if has_totals:
        out_ref[...] = totals_in[...]
    else:
        out_ref[...] = jnp.zeros_like(out_ref)
    if not given:
        for slot, (dy, dz) in enumerate(slots):
            site = jnp.bitwise_xor(level, dz) * flat + jnp.bitwise_xor(beside, dy)
            if dy == 0:
                owns = [spin_rows(("near", "O", dz), first_s + s) for s in range(spins)]
            else:
                owns = [
                    jnp.where(
                        core == 0,
                        spin_rows(("near", "B", dz), first_s + s),
                        spin_rows(("near", "A", dz), first_s + s),
                    )
                    for s in range(spins)
                ]
            left_ref[slot] = left_sides(owns, weights_ref[site])
    copies = []
    for index, name in enumerate(names):
        if half and index == half:
            copies = send_columns(
                0,
                lambda rows, across: out_ref[0, 0, rows, across],
                lambda rows, across: out_ref[1, 0, rows, across],
            )
        dx, added = term(name)
        out_ref[0 if name[0] == "near" else 1, dx] += added
    for copy in copies:
        copy.wait()


def route_second(*refs):
    o1_ref, o2_ref, stack_ref, both_ref = refs[3:]
    for slot in range(5):
        stack_ref[slot] = refs[slot][...]
    both_ref[0] = o1_ref[...]
    both_ref[1] = o2_ref[...]


def route_third(ab2_ref, o3_ref, a12_ref, b12_ref, stack_ref, a1_ref):
    stack_ref[0] = ab2_ref[...]
    stack_ref[1] = o3_ref[...]
    stack_ref[2:4] = a12_ref[...]
    stack_ref[4:6] = b12_ref[...]
    a1_ref[...] = a12_ref[0]


def route_last(a3_ref, ab3_ref, stack_ref):
    stack_ref[0] = a3_ref[...]
    stack_ref[1] = ab3_ref[...]


def left_slots(names):
    needed = set()
    for _, kind, dz in names:
        needed |= {"O": {(0, dz)}, "AB": {(1, dz)}}.get(kind, {(0, dz), (1, dz)})
    return sorted(needed, key=lambda slot: (slot[1], slot[0]))


def swap_in_windows(own, weights, share):
    shape = tuple(lax.axis_size(name) for name in AXES)
    columns, per_block = 4, own.shape[2]
    depth = own.size // (columns * per_block)
    spins = share // (2 * columns)
    tall, wide = 2 * spins * per_block, columns * per_block
    strides = (shape[1] * shape[2] * shape[3], shape[2] * shape[3], shape[3], 1)

    def move(array, target):
        pairs = []
        for p in range(shape[0]):
            for c in range(shape[1]):
                for z in range(shape[2]):
                    for y in range(shape[3]):
                        ends = (p, c, z, y), target(p, c, z, y)
                        pairs.append(
                            tuple(sum(a * b for a, b in zip(end, strides)) for end in ends)
                        )
        return lax.ppermute(array, AXES, pairs)

    def hop_a(array):
        return move(array, lambda p, c, z, y: (p ^ 1, c, z, y) if c == 0 else (p, c, z, y ^ 1))

    def hop_b(array):
        return move(array, lambda p, c, z, y: (p, c, z, y ^ 1) if c == 0 else (p ^ 1, c, z, y))

    def hop_z(array, by):
        return move(array, lambda p, c, z, y: (p, c, z ^ by, y))

    def swap(array):
        return move(array, lambda p, c, z, y: (p, c ^ 1, z, y))

    arrays = {}
    where = {}

    def put(key, array, side, kinds):
        arrays[key] = array
        for slot, (kind, dz) in enumerate(kinds):
            where[(side, kind, dz)] = (key, slot if len(kinds) > 1 else None)

    def near(kind, dz):
        key, slot = where[("near", kind, dz)]
        return arrays[key] if slot is None else arrays[key][slot]

    def add(names, totals, keep=None, left=None, half=0, field=None, weight=1):
        given, last = left is not None, field is not None
        slots, left = left if given else (keep or left_slots(names), None)
        uses = list(names)
        for dy, dz in [] if given else slots:
            uses += [("near", kind, dz) for kind in (("A", "B") if dy else ("O",))]
        keys = sorted({where[name][0] for name in uses})
        places = {name: (keys.index(where[name][0]), where[name][1]) for name in uses}
        operands = [weights] + [arrays[key] for key in keys]
        operands += [each for each in (left, totals, field) if each is not None]
        total_shape = (2, 2, tall, wide)
        left_shape = (len(slots), 2 * tall, depth)
        field_shape = (share, per_block, 4 * per_block)
        block, apart = (pl.BlockSpec(memory_space=space) for space in (pltpu.VMEM, pltpu.HBM))
        in_specs, outs, scratch, aliases = [block] * len(operands), [], [], {}
        if last:
            in_specs[-1] = apart
            aliases = {len(operands) - 1: 0}
            scratch.append(pltpu.VMEM(total_shape[2:], jnp.float32))
        else:
            outs.append((total_shape, jnp.float32, block))
        if half or last:
            outs.append((field_shape, jnp.float32, apart))
            scratch.append(pltpu.VMEM((*field_shape[:2], 2 * per_block), jnp.float32))
            scratch.append(pltpu.SemaphoreType.DMA((spins * columns // 2,)))
        if keep:
            outs.append((left_shape, jnp.bfloat16, block))
        elif not given:
            scratch.append(pltpu.VMEM(left_shape, jnp.bfloat16))
        out = pl.pallas_call(
            functools.partial(
                add_shards, tuple(names), places, slots, totals is not None, given, half, last, share
            ),
            in_specs=in_specs,
            out_specs=[spec for _, _, spec in outs],
            out_shape=[jax.ShapeDtypeStruct(shape, dtype) for shape, dtype, _ in outs],
            scratch_shapes=scratch,
            input_output_aliases=aliases,
            compiler_params=pltpu.CompilerParams(vmem_limit_bytes=40 * 1024 * 1024),
            cost_estimate=pl.CostEstimate(
                flops=4 * tall * wide * depth * len(names) * weight,
                bytes_accessed=wide * depth * 2 * len(names) + 8 * 4 * tall * wide,
                transcendentals=0,
            ),
        )(*operands)
        if keep:
            return out[0], (slots, out[1])
        return out if half else out[0]

    def fence(totals):
        nonlocal arrays
        arrays, totals = lax.optimization_barrier((arrays, totals))
        return totals

    put("1a", hop_z(own, 2), "near", [("O", 2)])
    put("1b", hop_a(own), "near", [("A", 0)])
    put("1c", hop_z(own, 1), "near", [("O", 1)])
    put("1d", hop_b(own), "near", [("B", 0)])
    put("1e", hop_b(near("A", 0)), "near", [("AB", 0)])
    put("1f", swap(own), "far", [("O", 0)])
    put("9", own, "near", [("O", 0)])
    weights = fence(weights)

    def route(kernel, operands, counts, weight=0):
        block = pl.BlockSpec(memory_space=pltpu.VMEM)
        shapes = [(count,) * (count > 1) + own.shape for count in counts]
        routed = pl.pallas_call(
            kernel,
            in_specs=[block] * len(operands),
            out_specs=[block] * len(counts),
            out_shape=[jax.ShapeDtypeStruct(shape, own.dtype) for shape in shapes],
            compiler_params=pltpu.CompilerParams(vmem_limit_bytes=24 * 1024 * 1024),
            cost_estimate=pl.CostEstimate(flops=weight, bytes_accessed=0, transcendentals=0),
        )(*operands)
        return fence(routed)

    first = [("O", 0), ("A", 0), ("B", 0), ("AB", 0), ("O", 1), ("O", 2)]
    second = [("AB", 2), ("O", 3), ("A", 1), ("A", 2), ("B", 1), ("B", 2)]
    third = [("A", 3), ("B", 3)]
    fourth = [("AB", 3), ("AB", 1)]
    stack, both = route(route_second, [near(*kind) for kind in first[1:]], (5, 2))
    totals = add([("near", *kind) for kind in first], None)
    o3, ab2 = hop_z(near("O", 2), 1), hop_z(near("AB", 0), 2)
    a12, b12 = hop_a(both), hop_b(both)
    put("2a", swap(stack), "far", first[1:])
    totals = fence(totals)

    totals = add([("far", *kind) for kind in first], totals)
    put("2c", o3, "near", [("O", 3)])
    totals = fence(totals)

    a3, b3 = hop_a(near("O", 3)), hop_b(near("O", 3))
    totals = add([("near", "O", 3)], totals, weight=45)
    put("2d", ab2, "near", [("AB", 2)])
    put("2e", a12, "near", [("A", 1), ("A", 2)])
    put("2f", b12, "near", [("B", 1), ("B", 2)])
    totals = fence(totals)

    ab3 = hop_z(near("AB", 2), 1)
    stack, a1 = route(route_third, [arrays[key] for key in ("2d", "2c", "2e", "2f")], (6, 1))
    far2, ab1 = swap(stack), hop_b(a1)
    names = [("near", *kind) for kind in second if kind != ("O", 3)]
    totals = add(names, totals)
    a3, b3, totals = lax.optimization_barrier((a3, b3, totals))
    (stack,) = route(route_last, [a3, b3], (2,), weight=10**11)
    put("3a", stack, "near", third)
    far3 = swap(stack)
    put("3d", far2, "far", second)
    names = [("far", *kind) for kind in second] + [("near", *kind) for kind in third]
    totals, (slots, left) = add(names, totals, keep=left_slots(names), weight=10)
    put("3b", ab3, "near", fourth[:1])
    put("3c", ab1, "near", fourth[1:])
    totals, left = fence((totals, left))

    far4 = [swap(near(*kind)) for kind in fourth]
    put("4a", far3, "far", third)
    names = [("far", *kind) for kind in third] + [("near", *kind) for kind in fourth]
    totals, field = add(names, totals, left=(slots, left), half=len(third))
    put("4b", far4[0], "far", fourth[:1])
    put("4c", far4[1], "far", fourth[1:])
    totals, left, field = fence((totals, left, field))
    return add([("far", *kind) for kind in fourth], totals, left=(slots, left), field=field)


def add_terms(place_ref, weights_ref, left_ref, right_ref, field_ref):
    @pl.when(pl.program_id(0) == 0)
    def _():
        field_ref[...] = jnp.zeros_like(field_ref)

    spins = left_ref.shape[2]
    groups, columns, per_block, depth = right_ref.shape[0], *right_ref.shape[2:]
    owns = [left_ref[0, 0, spin] for spin in range(spins)]
    left = left_sides(owns, weights_ref[0])
    for column in range(columns):
        right = right_ref[:, 0, column].reshape(groups * per_block, depth)
        term = product(left, right)
        for part in range(2):
            for spin in range(spins):
                start = (part * spins + spin) * per_block
                field_ref[(spin * columns + column) * 2 + part] += term[start : start + per_block]


def gather_whole(packed, place, weights, share):
    groups, _, deep, flat = (lax.axis_size(name) for name in AXES)
    sites = deep * flat
    _, per_block, depth = packed.shape
    columns = min(4, share // 2)
    spins = share // (2 * columns)
    near = lax.all_gather(packed, ("pair", "deep", "flat"))
    near = near.reshape(groups, sites, 4, per_block, depth)
    far = lax.ppermute(near, "core", [(0, 1), (1, 0)])
    wide = groups * per_block

    def half(right):
        return pl.pallas_call(
            add_terms,
            grid_spec=pltpu.PrefetchScalarGridSpec(
                num_scalar_prefetch=1,
                grid=(sites,),
                in_specs=[
                    pl.BlockSpec((1, 2, weights.shape[2]), lambda m, place: (m, 0, 0)),
                    pl.BlockSpec(
                        (1, 1, spins, per_block, depth),
                        lambda m, place: (place[0], m, place[4] // spins, 0, 0),
                    ),
                    pl.BlockSpec(
                        (groups, 1, columns, per_block, depth),
                        lambda m, place: (0, m, place[6] // columns, 0, 0),
                    ),
                ],
                out_specs=pl.BlockSpec((share, per_block, wide), lambda m, place: (0, 0, 0)),
            ),
            out_shape=jax.ShapeDtypeStruct((share, per_block, wide), jnp.float32),
            compiler_params=pltpu.CompilerParams(vmem_limit_bytes=40 * 1024 * 1024),
        )(place, weights, near, right)

    sides = [half(right).reshape(share, per_block, groups, per_block) for right in (near, far)]
    first = lax.axis_index("core") == 0
    even, odd = (jnp.where(first, a, b) for a, b in (sides, sides[::-1]))
    return jnp.stack([even, odd], 3).reshape(share, per_block, 2 * wide)


def shards(modes, momenta):
    groups, _, deep, flat = (lax.axis_size(name) for name in AXES)
    sites = deep * flat
    slots, steps, per_block, spin_colour, site_count = modes.shape
    share = steps * momenta.shape[0] * 32 // sites
    owned = (lax.axis_index("deep") * flat + lax.axis_index("flat")) * (share // 2)
    place = [lax.axis_index(name) for name in AXES]
    place = jnp.stack(place + [owned // 4 % 4, jnp.int32(flat), owned % 4]).astype(jnp.int32)

    mine = lax.dynamic_slice_in_dim(momenta, owned // 16, 1, 0)
    weights = phase_table(mine, jnp.int32(0), sites * site_count, LEXT)[0]
    weights = jnp.transpose(weights.reshape(2, sites, site_count), (1, 0, 2))

    if (groups, deep, flat) == (2, 4, 2) and steps == 1 and share in (8, 16, 32):
        own = jnp.transpose(modes[:, 0], (0, 2, 1, 3))
        return swap_in_windows(own, weights, share)
    packed = jnp.transpose(modes.reshape(slots, per_block, 4, 3, site_count), (2, 1, 0, 3, 4))
    packed = packed.reshape(4, per_block, slots * 3 * site_count)
    return gather_whole(packed, place, weights, share)


def solution(mesh):
    count, sites = mesh.shape["blk"], mesh.shape["site"]
    flat = 2 ** (int(math.log2(sites)) // 2)
    split = Mesh(mesh.devices.reshape(count // 2, 2, sites // flat, flat), AXES)
    placed = (P(None, None, ("pair", "core"), None, ("deep", "flat")), P())
    return jax.shard_map(
        shards,
        mesh=split,
        in_specs=placed,
        out_specs=P(("deep", "flat"), ("pair", "core"), None),
        check_vma=False,
    )
```

```python
import functools
import math

import jax
import jax.numpy as jnp
from jax import lax
from jax.experimental import pallas as pl
from jax.experimental.pallas import tpu as pltpu
from jax.sharding import Mesh, PartitionSpec as P

LEXT = 48

TWO_PI = 2.0 * math.pi

AXES = ("pair", "core", "deep", "flat")


def phase_table(momenta, first_site, site_count, extent):
    flat = first_site + jnp.arange(site_count, dtype=jnp.int32)
    coords = jnp.stack([flat % extent, flat // extent % extent, flat // (extent * extent)], 0)
    turns = jnp.mod(jnp.sum(momenta[:, :, None] * coords[None, :, :], axis=1), extent)
    angle = turns.astype(jnp.float32) * (TWO_PI / extent)
    return jnp.stack([jnp.cos(angle), jnp.sin(angle)], 1)


def left_sides(owns, weights):
    depth = owns[0].shape[1]
    half = depth // 2
    cosine = jnp.tile(weights[0:1], (1, depth // weights.shape[1]))
    sine = jnp.tile(weights[1:2], (1, depth // weights.shape[1]))
    cosine_rows = [[], []]
    sine_rows = [[], []]
    for own in owns:
        own = own.astype(jnp.float32)
        by_cos = (own * cosine).astype(jnp.bfloat16)
        by_sin = (own * sine).astype(jnp.bfloat16)
        cosine_rows[0].append(by_cos)
        cosine_rows[1].append(jnp.concatenate([-by_cos[:, half:], by_cos[:, :half]], 1))
        sine_rows[0].append(jnp.concatenate([-by_sin[:, half:], by_sin[:, :half]], 1))
        sine_rows[1].append(-by_sin)
    return jnp.concatenate(cosine_rows[0] + cosine_rows[1] + sine_rows[0] + sine_rows[1], 0)


def product(left, right):
    dims = (((1,), (1,)), ((), ()))
    terms = lax.dot_general(left, right, dims, preferred_element_type=jnp.float32)
    half = terms.shape[0] // 2
    return terms[:half] + terms[half:]


def add_shards(names, where, slots, has_totals, given, half, last, share, weights_ref, *refs):
    refs = list(refs)
    left_ref = None if given else refs.pop()
    if half:
        sems, row_ref, field_ref = (refs.pop() for _ in range(3))
    if last:
        sems, row_ref, far_ref, field_ref, _ = (refs.pop() for _ in range(5))
    else:
        out_ref = refs.pop()
    totals_in = refs.pop() if has_totals else None
    left_ref = refs.pop() if given else left_ref

    def shard(name):
        index, slot = where[name]
        return refs[index] if slot is None else refs[index].at[slot]

    def spin_rows(name, spin):
        ref = shard(name)
        tiles = [ref[part, spin * colours + x] for part in range(2) for x in range(colours)]
        return jnp.concatenate(tiles, 1)

    pair, core, level, beside = (lax.axis_index(name) for name in AXES)
    flat = lax.axis_size("flat")
    _, spin_colour, per_block, _ = shard(names[0]).shape
    columns, colours = 4, spin_colour // 4
    first_s = lax.rem(lax.div((level * flat + beside) * (share // 2), 4), 4)
    spins = left_ref.shape[1] // (4 * per_block)

    def send_columns(dx, near, far):
        lane = lax.broadcasted_iota(jnp.int32, (per_block, 2 * per_block), 1)
        start = pl.multiple_of(jnp.bitwise_xor(pair, dx) * (2 * per_block), 2 * per_block)
        copies = []
        for spin in range(spins):
            for column in range(0, columns, 2):
                first = (spin * columns + column) * 2
                across = slice(column * per_block, (column + 2) * per_block)
                for part in range(2):
                    top = (part * spins + spin) * per_block
                    one = near(slice(top, top + per_block), across)
                    two = far(slice(top, top + per_block), across)
                    even = jnp.where(core == 0, one, two)
                    odd = jnp.where(core == 0, two, one)
                    row_ref[first + part] = jnp.where(
                        lane < per_block, even, pltpu.roll(odd, per_block, 1)
                    )
                    row_ref[first + part + 2] = jnp.where(
                        lane < per_block, pltpu.roll(even, per_block, 1), odd
                    )
                four = pl.ds(first, 4)
                target = field_ref.at[four, :, pl.ds(start, 2 * per_block)]
                copies.append(
                    pltpu.make_async_copy(row_ref.at[four], target, sems.at[len(copies)])
                )
                copies[-1].start()
        return copies

    def term(name):
        side, kind, dz = name
        right = jnp.concatenate([spin_rows(name, r) for r in range(columns)], 0)
        turn = core if side == "near" else 1 - core
        dx, dy = {"O": (0, 0), "A": (1 - turn, turn), "B": (turn, 1 - turn), "AB": (1, 1)}[kind]
        if kind in ("O", "AB"):
            slot = slots.index((dy, dz))
        else:
            slot = slots.index((0, dz)) + dy
        return dx, product(left_ref[slot], right)

    if last:
        far_ref[...] = totals_in[1, 1] + sum(term(name)[1] for name in names)
        copies = send_columns(
            1,
            lambda rows, across: totals_in[0, 1, rows, across],
            lambda rows, across: far_ref[rows, across],
        )
        for copy in copies:
            copy.wait()
        return

    if has_totals:
        out_ref[...] = totals_in[...]
    else:
        out_ref[...] = jnp.zeros_like(out_ref)
    if not given:
        for slot, (dy, dz) in enumerate(slots):
            site = jnp.bitwise_xor(level, dz) * flat + jnp.bitwise_xor(beside, dy)
            if dy == 0:
                owns = [spin_rows(("near", "O", dz), first_s + s) for s in range(spins)]
            else:
                owns = [
                    jnp.where(
                        core == 0,
                        spin_rows(("near", "B", dz), first_s + s),
                        spin_rows(("near", "A", dz), first_s + s),
                    )
                    for s in range(spins)
                ]
            left_ref[slot] = left_sides(owns, weights_ref[site])
    copies = []
    if half:
        copies = send_columns(
            0,
            lambda rows, across: totals_in[0, 0, rows, across],
            lambda rows, across: totals_in[1, 0, rows, across],
        )
    for name in names:
        dx, added = term(name)
        out_ref[0 if name[0] == "near" else 1, dx] += added
    for copy in copies:
        copy.wait()


def route_second(*refs):
    o1_ref, o2_ref, stack_ref, both_ref = refs[3:]
    for slot in range(5):
        stack_ref[slot] = refs[slot][...]
    both_ref[0] = o1_ref[...]
    both_ref[1] = o2_ref[...]


def route_third(ab2_ref, o3_ref, a12_ref, b12_ref, stack_ref, a1_ref):
    stack_ref[0] = ab2_ref[...]
    stack_ref[1] = o3_ref[...]
    stack_ref[2:4] = a12_ref[...]
    stack_ref[4:6] = b12_ref[...]
    a1_ref[...] = a12_ref[0]


def route_last(a3_ref, ab3_ref, stack_ref):
    stack_ref[0] = a3_ref[...]
    stack_ref[1] = ab3_ref[...]


def left_slots(names):
    needed = set()
    for _, kind, dz in names:
        needed |= {"O": {(0, dz)}, "AB": {(1, dz)}}.get(kind, {(0, dz), (1, dz)})
    return sorted(needed, key=lambda slot: (slot[1], slot[0]))


def swap_in_windows(own, weights, share):
    shape = tuple(lax.axis_size(name) for name in AXES)
    columns, per_block = 4, own.shape[2]
    depth = own.size // (columns * per_block)
    spins = share // (2 * columns)
    tall, wide = 2 * spins * per_block, columns * per_block
    strides = (shape[1] * shape[2] * shape[3], shape[2] * shape[3], shape[3], 1)

    def move(array, target):
        pairs = []
        for p in range(shape[0]):
            for c in range(shape[1]):
                for z in range(shape[2]):
                    for y in range(shape[3]):
                        ends = (p, c, z, y), target(p, c, z, y)
                        pairs.append(
                            tuple(sum(a * b for a, b in zip(end, strides)) for end in ends)
                        )
        return lax.ppermute(array, AXES, pairs)

    def hop_a(array):
        return move(array, lambda p, c, z, y: (p ^ 1, c, z, y) if c == 0 else (p, c, z, y ^ 1))

    def hop_b(array):
        return move(array, lambda p, c, z, y: (p, c, z, y ^ 1) if c == 0 else (p ^ 1, c, z, y))

    def hop_z(array, by):
        return move(array, lambda p, c, z, y: (p, c, z ^ by, y))

    def swap(array):
        return move(array, lambda p, c, z, y: (p, c ^ 1, z, y))

    arrays = {}
    where = {}

    def put(key, array, side, kinds):
        arrays[key] = array
        for slot, (kind, dz) in enumerate(kinds):
            where[(side, kind, dz)] = (key, slot if len(kinds) > 1 else None)

    def near(kind, dz):
        key, slot = where[("near", kind, dz)]
        return arrays[key] if slot is None else arrays[key][slot]

    def add(names, totals, keep=None, left=None, half=False, field=None, weight=1):
        given, last = left is not None, field is not None
        slots, left = left if given else (keep or left_slots(names), None)
        uses = list(names)
        for dy, dz in [] if given else slots:
            uses += [("near", kind, dz) for kind in (("A", "B") if dy else ("O",))]
        keys = sorted({where[name][0] for name in uses})
        places = {name: (keys.index(where[name][0]), where[name][1]) for name in uses}
        operands = [weights] + [arrays[key] for key in keys]
        operands += [each for each in (left, totals, field) if each is not None]
        total_shape = (2, 2, tall, wide)
        left_shape = (len(slots), 2 * tall, depth)
        field_shape = (share, per_block, 4 * per_block)
        block, apart = (pl.BlockSpec(memory_space=space) for space in (pltpu.VMEM, pltpu.HBM))
        in_specs, outs, scratch, aliases = [block] * len(operands), [], [], {}
        if last:
            in_specs[-1] = apart
            aliases = {len(operands) - 1: 0}
            scratch.append(pltpu.VMEM(total_shape[2:], jnp.float32))
        else:
            outs.append((total_shape, jnp.float32, block))
        if half or last:
            outs.append((field_shape, jnp.float32, apart))
            scratch.append(pltpu.VMEM((*field_shape[:2], 2 * per_block), jnp.float32))
            scratch.append(pltpu.SemaphoreType.DMA((spins * columns // 2,)))
        if keep:
            outs.append((left_shape, jnp.bfloat16, block))
        elif not given:
            scratch.append(pltpu.VMEM(left_shape, jnp.bfloat16))
        out = pl.pallas_call(
            functools.partial(
                add_shards, tuple(names), places, slots, totals is not None, given, half, last, share
            ),
            in_specs=in_specs,
            out_specs=[spec for _, _, spec in outs],
            out_shape=[jax.ShapeDtypeStruct(shape, dtype) for shape, dtype, _ in outs],
            scratch_shapes=scratch,
            input_output_aliases=aliases,
            compiler_params=pltpu.CompilerParams(vmem_limit_bytes=40 * 1024 * 1024),
            cost_estimate=pl.CostEstimate(
                flops=4 * tall * wide * depth * len(names) * weight,
                bytes_accessed=wide * depth * 2 * len(names) + 8 * 4 * tall * wide,
                transcendentals=0,
            ),
        )(*operands)
        if keep:
            return out[0], (slots, out[1])
        return out if half else out[0]

    def fence(totals):
        nonlocal arrays
        arrays, totals = lax.optimization_barrier((arrays, totals))
        return totals

    put("1a", hop_z(own, 2), "near", [("O", 2)])
    put("1b", hop_a(own), "near", [("A", 0)])
    put("1c", hop_z(own, 1), "near", [("O", 1)])
    put("1d", hop_b(own), "near", [("B", 0)])
    put("1e", hop_b(near("A", 0)), "near", [("AB", 0)])
    put("1f", swap(own), "far", [("O", 0)])
    put("9", own, "near", [("O", 0)])
    weights = fence(weights)

    def route(kernel, operands, counts, weight=0):
        block = pl.BlockSpec(memory_space=pltpu.VMEM)
        shapes = [(count,) * (count > 1) + own.shape for count in counts]
        routed = pl.pallas_call(
            kernel,
            in_specs=[block] * len(operands),
            out_specs=[block] * len(counts),
            out_shape=[jax.ShapeDtypeStruct(shape, own.dtype) for shape in shapes],
            compiler_params=pltpu.CompilerParams(vmem_limit_bytes=24 * 1024 * 1024),
            cost_estimate=pl.CostEstimate(flops=weight, bytes_accessed=0, transcendentals=0),
        )(*operands)
        return fence(routed)

    first = [("O", 0), ("A", 0), ("B", 0), ("AB", 0), ("O", 1), ("O", 2)]
    second = [("AB", 2), ("O", 3), ("A", 1), ("A", 2), ("B", 1), ("B", 2)]
    third = [("A", 3), ("B", 3)]
    fourth = [("AB", 3), ("AB", 1)]
    stack, both = route(route_second, [near(*kind) for kind in first[1:]], (5, 2))
    totals = add([("near", *kind) for kind in first], None)
    o3, ab2 = hop_z(near("O", 2), 1), hop_z(near("AB", 0), 2)
    a12, b12 = hop_a(both), hop_b(both)
    put("2a", swap(stack), "far", first[1:])
    totals = fence(totals)

    totals = add([("far", *kind) for kind in first], totals)
    put("2c", o3, "near", [("O", 3)])
    totals = fence(totals)

    a3, b3 = hop_a(near("O", 3)), hop_b(near("O", 3))
    totals = add([("near", "O", 3)], totals, weight=45)
    put("2d", ab2, "near", [("AB", 2)])
    put("2e", a12, "near", [("A", 1), ("A", 2)])
    put("2f", b12, "near", [("B", 1), ("B", 2)])
    totals = fence(totals)

    ab3 = hop_z(near("AB", 2), 1)
    stack, a1 = route(route_third, [arrays[key] for key in ("2d", "2c", "2e", "2f")], (6, 1))
    far2, ab1 = swap(stack), hop_b(a1)
    names = [("near", *kind) for kind in second if kind != ("O", 3)]
    totals = add(names, totals)
    a3, b3, totals = lax.optimization_barrier((a3, b3, totals))
    (stack,) = route(route_last, [a3, b3], (2,), weight=10**11)
    put("3a", stack, "near", third)
    far3 = swap(stack)
    put("3d", far2, "far", second)
    names = [("far", *kind) for kind in second] + [("near", *kind) for kind in third]
    totals, (slots, left) = add(names, totals, keep=left_slots(names), weight=10)
    put("3e", far3, "far", third)
    totals, left = fence((totals, left))
    totals = add([("far", *kind) for kind in third], totals, left=(slots, left))
    put("3b", ab3, "near", fourth[:1])
    put("3c", ab1, "near", fourth[1:])
    totals, left = fence((totals, left))

    far4 = [swap(near(*kind)) for kind in fourth]
    names = [("near", *kind) for kind in fourth]
    totals, field = add(names, totals, left=(slots, left), half=True)
    put("4b", far4[0], "far", fourth[:1])
    put("4c", far4[1], "far", fourth[1:])
    totals, left, field = fence((totals, left, field))
    return add([("far", *kind) for kind in fourth], totals, left=(slots, left), field=field)


def add_terms(place_ref, weights_ref, left_ref, right_ref, field_ref):
    @pl.when(pl.program_id(0) == 0)
    def _():
        field_ref[...] = jnp.zeros_like(field_ref)

    spins = left_ref.shape[2]
    groups, columns, per_block, depth = right_ref.shape[0], *right_ref.shape[2:]
    owns = [left_ref[0, 0, spin] for spin in range(spins)]
    left = left_sides(owns, weights_ref[0])
    for column in range(columns):
        right = right_ref[:, 0, column].reshape(groups * per_block, depth)
        term = product(left, right)
        for part in range(2):
            for spin in range(spins):
                start = (part * spins + spin) * per_block
                field_ref[(spin * columns + column) * 2 + part] += term[start : start + per_block]


def gather_whole(packed, place, weights, share):
    groups, _, deep, flat = (lax.axis_size(name) for name in AXES)
    sites = deep * flat
    _, per_block, depth = packed.shape
    columns = min(4, share // 2)
    spins = share // (2 * columns)
    near = lax.all_gather(packed, ("pair", "deep", "flat"))
    near = near.reshape(groups, sites, 4, per_block, depth)
    far = lax.ppermute(near, "core", [(0, 1), (1, 0)])
    wide = groups * per_block

    def half(right):
        return pl.pallas_call(
            add_terms,
            grid_spec=pltpu.PrefetchScalarGridSpec(
                num_scalar_prefetch=1,
                grid=(sites,),
                in_specs=[
                    pl.BlockSpec((1, 2, weights.shape[2]), lambda m, place: (m, 0, 0)),
                    pl.BlockSpec(
                        (1, 1, spins, per_block, depth),
                        lambda m, place: (place[0], m, place[4] // spins, 0, 0),
                    ),
                    pl.BlockSpec(
                        (groups, 1, columns, per_block, depth),
                        lambda m, place: (0, m, place[6] // columns, 0, 0),
                    ),
                ],
                out_specs=pl.BlockSpec((share, per_block, wide), lambda m, place: (0, 0, 0)),
            ),
            out_shape=jax.ShapeDtypeStruct((share, per_block, wide), jnp.float32),
            compiler_params=pltpu.CompilerParams(vmem_limit_bytes=40 * 1024 * 1024),
        )(place, weights, near, right)

    sides = [half(right).reshape(share, per_block, groups, per_block) for right in (near, far)]
    first = lax.axis_index("core") == 0
    even, odd = (jnp.where(first, a, b) for a, b in (sides, sides[::-1]))
    return jnp.stack([even, odd], 3).reshape(share, per_block, 2 * wide)


def shards(modes, momenta):
    groups, _, deep, flat = (lax.axis_size(name) for name in AXES)
    sites = deep * flat
    slots, steps, per_block, spin_colour, site_count = modes.shape
    share = steps * momenta.shape[0] * 32 // sites
    owned = (lax.axis_index("deep") * flat + lax.axis_index("flat")) * (share // 2)
    place = [lax.axis_index(name) for name in AXES]
    place = jnp.stack(place + [owned // 4 % 4, jnp.int32(flat), owned % 4]).astype(jnp.int32)

    mine = lax.dynamic_slice_in_dim(momenta, owned // 16, 1, 0)
    weights = phase_table(mine, jnp.int32(0), sites * site_count, LEXT)[0]
    weights = jnp.transpose(weights.reshape(2, sites, site_count), (1, 0, 2))

    if (groups, deep, flat) == (2, 4, 2) and steps == 1 and share in (8, 16, 32):
        own = jnp.transpose(modes[:, 0], (0, 2, 1, 3))
        return swap_in_windows(own, weights, share)
    packed = jnp.transpose(modes.reshape(slots, per_block, 4, 3, site_count), (2, 1, 0, 3, 4))
    packed = packed.reshape(4, per_block, slots * 3 * site_count)
    return gather_whole(packed, place, weights, share)


def solution(mesh):
    count, sites = mesh.shape["blk"], mesh.shape["site"]
    flat = 2 ** (int(math.log2(sites)) // 2)
    split = Mesh(mesh.devices.reshape(count // 2, 2, sites // flat, flat), AXES)
    placed = (P(None, None, ("pair", "core"), None, ("deep", "flat")), P())
    return jax.shard_map(
        shards,
        mesh=split,
        in_specs=placed,
        out_specs=P(("deep", "flat"), ("pair", "core"), None),
        check_vma=False,
    )
```

```python
import functools
import math

import jax
import jax.numpy as jnp
from jax import lax
from jax.experimental import pallas as pl
from jax.experimental.pallas import tpu as pltpu
from jax.sharding import Mesh, PartitionSpec as P

LEXT = 48

TWO_PI = 2.0 * math.pi

AXES = ("pair", "core", "deep", "flat")


def phase_table(momenta, first_site, site_count, extent):
    flat = first_site + jnp.arange(site_count, dtype=jnp.int32)
    coords = jnp.stack([flat % extent, flat // extent % extent, flat // (extent * extent)], 0)
    turns = jnp.mod(jnp.sum(momenta[:, :, None] * coords[None, :, :], axis=1), extent)
    angle = turns.astype(jnp.float32) * (TWO_PI / extent)
    return jnp.stack([jnp.cos(angle), jnp.sin(angle)], 1)


def left_sides(owns, weights):
    depth = owns[0].shape[1]
    half = depth // 2
    cosine = jnp.tile(weights[0:1], (1, depth // weights.shape[1]))
    sine = jnp.tile(weights[1:2], (1, depth // weights.shape[1]))
    cosine_rows = [[], []]
    sine_rows = [[], []]
    for own in owns:
        own = own.astype(jnp.float32)
        by_cos = (own * cosine).astype(jnp.bfloat16)
        by_sin = (own * sine).astype(jnp.bfloat16)
        cosine_rows[0].append(by_cos)
        cosine_rows[1].append(jnp.concatenate([-by_cos[:, half:], by_cos[:, :half]], 1))
        sine_rows[0].append(jnp.concatenate([-by_sin[:, half:], by_sin[:, :half]], 1))
        sine_rows[1].append(-by_sin)
    return jnp.concatenate(cosine_rows[0] + cosine_rows[1] + sine_rows[0] + sine_rows[1], 0)


def product(left, right):
    dims = (((1,), (1,)), ((), ()))
    terms = lax.dot_general(left, right, dims, preferred_element_type=jnp.float32)
    half = terms.shape[0] // 2
    return terms[:half] + terms[half:]


def add_shards(names, where, slots, has_totals, given, half, last, share, weights_ref, *refs):
    refs = list(refs)
    left_ref = None if given else refs.pop()
    if half:
        sems, row_ref, field_ref = (refs.pop() for _ in range(3))
    if last:
        sems, row_ref, far_ref, field_ref, _ = (refs.pop() for _ in range(5))
    else:
        out_ref = refs.pop()
    totals_in = refs.pop() if has_totals else None
    left_ref = refs.pop() if given else left_ref

    def shard(name):
        index, slot = where[name]
        return refs[index] if slot is None else refs[index].at[slot]

    def spin_rows(name, spin):
        ref = shard(name)
        tiles = [ref[part, spin * colours + x] for part in range(2) for x in range(colours)]
        return jnp.concatenate(tiles, 1)

    pair, core, level, beside = (lax.axis_index(name) for name in AXES)
    flat = lax.axis_size("flat")
    _, spin_colour, per_block, _ = shard(names[0]).shape
    columns, colours = 4, spin_colour // 4
    first_s = lax.rem(lax.div((level * flat + beside) * (share // 2), 4), 4)
    spins = left_ref.shape[1] // (4 * per_block)

    def send_columns(dx, near, far):
        lane = lax.broadcasted_iota(jnp.int32, (per_block, 2 * per_block), 1)
        start = pl.multiple_of(jnp.bitwise_xor(pair, dx) * (2 * per_block), 2 * per_block)
        copies = []
        for spin in range(spins):
            for column in range(0, columns, 2):
                first = (spin * columns + column) * 2
                across = slice(column * per_block, (column + 2) * per_block)
                for part in range(2):
                    top = (part * spins + spin) * per_block
                    one = near(slice(top, top + per_block), across)
                    two = far(slice(top, top + per_block), across)
                    even = jnp.where(core == 0, one, two)
                    odd = jnp.where(core == 0, two, one)
                    row_ref[first + part] = jnp.where(
                        lane < per_block, even, pltpu.roll(odd, per_block, 1)
                    )
                    row_ref[first + part + 2] = jnp.where(
                        lane < per_block, pltpu.roll(even, per_block, 1), odd
                    )
                four = pl.ds(first, 4)
                target = field_ref.at[four, :, pl.ds(start, 2 * per_block)]
                copies.append(
                    pltpu.make_async_copy(row_ref.at[four], target, sems.at[len(copies)])
                )
                copies[-1].start()
        return copies

    def term(name):
        side, kind, dz = name
        right = jnp.concatenate([spin_rows(name, r) for r in range(columns)], 0)
        turn = core if side == "near" else 1 - core
        dx, dy = {"O": (0, 0), "A": (1 - turn, turn), "B": (turn, 1 - turn), "AB": (1, 1)}[kind]
        if kind in ("O", "AB"):
            slot = slots.index((dy, dz))
        else:
            slot = slots.index((0, dz)) + dy
        return dx, product(left_ref[slot], right)

    if last:
        far_ref[...] = totals_in[1, 1] + sum(term(name)[1] for name in names)
        copies = send_columns(
            1,
            lambda rows, across: totals_in[0, 1, rows, across],
            lambda rows, across: far_ref[rows, across],
        )
        for copy in copies:
            copy.wait()
        return

    if has_totals:
        out_ref[...] = totals_in[...]
    else:
        out_ref[...] = jnp.zeros_like(out_ref)
    if not given:
        for slot, (dy, dz) in enumerate(slots):
            site = jnp.bitwise_xor(level, dz) * flat + jnp.bitwise_xor(beside, dy)
            if dy == 0:
                owns = [spin_rows(("near", "O", dz), first_s + s) for s in range(spins)]
            else:
                owns = [
                    jnp.where(
                        core == 0,
                        spin_rows(("near", "B", dz), first_s + s),
                        spin_rows(("near", "A", dz), first_s + s),
                    )
                    for s in range(spins)
                ]
            left_ref[slot] = left_sides(owns, weights_ref[site])
    copies = []
    if half:
        copies = send_columns(
            0,
            lambda rows, across: totals_in[0, 0, rows, across],
            lambda rows, across: totals_in[1, 0, rows, across],
        )
    for name in names:
        dx, added = term(name)
        out_ref[0 if name[0] == "near" else 1, dx] += added
    for copy in copies:
        copy.wait()


def route_second(*refs):
    o1_ref, o2_ref, stack_ref, both_ref = refs[3:]
    for slot in range(5):
        stack_ref[slot] = refs[slot][...]
    both_ref[0] = o1_ref[...]
    both_ref[1] = o2_ref[...]


def route_third(ab2_ref, o3_ref, a12_ref, b12_ref, stack_ref, a1_ref):
    stack_ref[0] = ab2_ref[...]
    stack_ref[1] = o3_ref[...]
    stack_ref[2:4] = a12_ref[...]
    stack_ref[4:6] = b12_ref[...]
    a1_ref[...] = a12_ref[0]


def route_last(a3_ref, ab3_ref, stack_ref):
    stack_ref[0] = a3_ref[...]
    stack_ref[1] = ab3_ref[...]


def left_slots(names):
    needed = set()
    for _, kind, dz in names:
        needed |= {"O": {(0, dz)}, "AB": {(1, dz)}}.get(kind, {(0, dz), (1, dz)})
    return sorted(needed, key=lambda slot: (slot[1], slot[0]))


def swap_in_windows(own, weights, share):
    shape = tuple(lax.axis_size(name) for name in AXES)
    columns, per_block = 4, own.shape[2]
    depth = own.size // (columns * per_block)
    spins = share // (2 * columns)
    tall, wide = 2 * spins * per_block, columns * per_block
    strides = (shape[1] * shape[2] * shape[3], shape[2] * shape[3], shape[3], 1)

    def move(array, target):
        pairs = []
        for p in range(shape[0]):
            for c in range(shape[1]):
                for z in range(shape[2]):
                    for y in range(shape[3]):
                        ends = (p, c, z, y), target(p, c, z, y)
                        pairs.append(
                            tuple(sum(a * b for a, b in zip(end, strides)) for end in ends)
                        )
        return lax.ppermute(array, AXES, pairs)

    def hop_a(array):
        return move(array, lambda p, c, z, y: (p ^ 1, c, z, y) if c == 0 else (p, c, z, y ^ 1))

    def hop_b(array):
        return move(array, lambda p, c, z, y: (p, c, z, y ^ 1) if c == 0 else (p ^ 1, c, z, y))

    def hop_z(array, by):
        return move(array, lambda p, c, z, y: (p, c, z ^ by, y))

    def swap(array):
        return move(array, lambda p, c, z, y: (p, c ^ 1, z, y))

    arrays = {}
    where = {}

    def put(key, array, side, kinds):
        arrays[key] = array
        for slot, (kind, dz) in enumerate(kinds):
            where[(side, kind, dz)] = (key, slot if len(kinds) > 1 else None)

    def near(kind, dz):
        key, slot = where[("near", kind, dz)]
        return arrays[key] if slot is None else arrays[key][slot]

    def add(names, totals, keep=None, left=None, half=False, field=None, weight=1):
        given, last = left is not None, field is not None
        slots, left = left if given else (keep or left_slots(names), None)
        uses = list(names)
        for dy, dz in [] if given else slots:
            uses += [("near", kind, dz) for kind in (("A", "B") if dy else ("O",))]
        keys = sorted({where[name][0] for name in uses})
        places = {name: (keys.index(where[name][0]), where[name][1]) for name in uses}
        operands = [weights] + [arrays[key] for key in keys]
        operands += [each for each in (left, totals, field) if each is not None]
        total_shape = (2, 2, tall, wide)
        left_shape = (len(slots), 2 * tall, depth)
        field_shape = (share, per_block, 4 * per_block)
        block, apart = (pl.BlockSpec(memory_space=space) for space in (pltpu.VMEM, pltpu.HBM))
        in_specs, outs, scratch, aliases = [block] * len(operands), [], [], {}
        if last:
            in_specs[-1] = apart
            aliases = {len(operands) - 1: 0}
            scratch.append(pltpu.VMEM(total_shape[2:], jnp.float32))
        else:
            outs.append((total_shape, jnp.float32, block))
        if half or last:
            outs.append((field_shape, jnp.float32, apart))
            scratch.append(pltpu.VMEM((*field_shape[:2], 2 * per_block), jnp.float32))
            scratch.append(pltpu.SemaphoreType.DMA((spins * columns // 2,)))
        if keep:
            outs.append((left_shape, jnp.bfloat16, block))
        elif not given:
            scratch.append(pltpu.VMEM(left_shape, jnp.bfloat16))
        out = pl.pallas_call(
            functools.partial(
                add_shards, tuple(names), places, slots, totals is not None, given, half, last, share
            ),
            in_specs=in_specs,
            out_specs=[spec for _, _, spec in outs],
            out_shape=[jax.ShapeDtypeStruct(shape, dtype) for shape, dtype, _ in outs],
            scratch_shapes=scratch,
            input_output_aliases=aliases,
            compiler_params=pltpu.CompilerParams(vmem_limit_bytes=40 * 1024 * 1024),
            cost_estimate=pl.CostEstimate(
                flops=4 * tall * wide * depth * len(names) * weight,
                bytes_accessed=wide * depth * 2 * len(names) + 8 * 4 * tall * wide,
                transcendentals=0,
            ),
        )(*operands)
        if keep:
            return out[0], (slots, out[1])
        return out if half else out[0]

    def fence(totals):
        nonlocal arrays
        arrays, totals = lax.optimization_barrier((arrays, totals))
        return totals

    put("1a", hop_z(own, 2), "near", [("O", 2)])
    put("1b", hop_a(own), "near", [("A", 0)])
    put("1c", hop_z(own, 1), "near", [("O", 1)])
    put("1d", hop_b(own), "near", [("B", 0)])
    put("1e", hop_b(near("A", 0)), "near", [("AB", 0)])
    put("1f", swap(own), "far", [("O", 0)])
    put("9", own, "near", [("O", 0)])
    weights = fence(weights)

    def route(kernel, operands, counts, weight=0):
        block = pl.BlockSpec(memory_space=pltpu.VMEM)
        shapes = [(count,) * (count > 1) + own.shape for count in counts]
        routed = pl.pallas_call(
            kernel,
            in_specs=[block] * len(operands),
            out_specs=[block] * len(counts),
            out_shape=[jax.ShapeDtypeStruct(shape, own.dtype) for shape in shapes],
            compiler_params=pltpu.CompilerParams(vmem_limit_bytes=24 * 1024 * 1024),
            cost_estimate=pl.CostEstimate(flops=weight, bytes_accessed=0, transcendentals=0),
        )(*operands)
        return fence(routed)

    first = [("O", 0), ("A", 0), ("B", 0), ("AB", 0), ("O", 1), ("O", 2)]
    second = [("AB", 2), ("O", 3), ("A", 1), ("A", 2), ("B", 1), ("B", 2)]
    third = [("A", 3), ("B", 3)]
    fourth = [("AB", 3), ("AB", 1)]
    stack, both = route(route_second, [near(*kind) for kind in first[1:]], (5, 2))
    totals = add([("near", *kind) for kind in first], None)
    o3, ab2 = hop_z(near("O", 2), 1), hop_z(near("AB", 0), 2)
    a12, b12 = hop_a(both), hop_b(both)
    put("2a", swap(stack), "far", first[1:])
    totals = fence(totals)

    totals = add([("far", *kind) for kind in first], totals)
    put("2c", o3, "near", [("O", 3)])
    totals = fence(totals)

    a3, b3 = hop_a(near("O", 3)), hop_b(near("O", 3))
    totals = add([("near", "O", 3)], totals, weight=45)
    put("2d", ab2, "near", [("AB", 2)])
    put("2e", a12, "near", [("A", 1), ("A", 2)])
    put("2f", b12, "near", [("B", 1), ("B", 2)])
    totals = fence(totals)

    ab3 = hop_z(near("AB", 2), 1)
    stack, a1 = route(route_third, [arrays[key] for key in ("2d", "2c", "2e", "2f")], (6, 1))
    far2, ab1 = swap(stack), hop_b(a1)
    names = [("near", *kind) for kind in second if kind != ("O", 3)]
    totals = add(names, totals)
    a3, b3, totals = lax.optimization_barrier((a3, b3, totals))
    (stack,) = route(route_last, [a3, b3], (2,), weight=10**11)
    put("3a", stack, "near", third)
    far3 = swap(stack)
    put("3d", far2, "far", second)
    names = [("far", *kind) for kind in second] + [("near", *kind) for kind in third]
    totals, (slots, left) = add(names, totals, keep=left_slots(names), weight=10)
    put("3e", far3, "far", third)
    totals, left = fence((totals, left))
    totals = add([("far", *kind) for kind in third], totals, left=(slots, left))
    put("3b", ab3, "near", fourth[:1])
    put("3c", ab1, "near", fourth[1:])
    totals, left = fence((totals, left))

    (stack,) = route(route_last, [near(*kind) for kind in fourth], (2,))
    far4 = swap(stack)
    names = [("near", *kind) for kind in fourth]
    totals, field = add(names, totals, left=(slots, left), half=True)
    put("4b", far4, "far", fourth)
    totals, left, field = fence((totals, left, field))
    return add([("far", *kind) for kind in fourth], totals, left=(slots, left), field=field)


def add_terms(place_ref, weights_ref, left_ref, right_ref, field_ref):
    @pl.when(pl.program_id(0) == 0)
    def _():
        field_ref[...] = jnp.zeros_like(field_ref)

    spins = left_ref.shape[2]
    groups, columns, per_block, depth = right_ref.shape[0], *right_ref.shape[2:]
    owns = [left_ref[0, 0, spin] for spin in range(spins)]
    left = left_sides(owns, weights_ref[0])
    for column in range(columns):
        right = right_ref[:, 0, column].reshape(groups * per_block, depth)
        term = product(left, right)
        for part in range(2):
            for spin in range(spins):
                start = (part * spins + spin) * per_block
                field_ref[(spin * columns + column) * 2 + part] += term[start : start + per_block]


def gather_whole(packed, place, weights, share):
    groups, _, deep, flat = (lax.axis_size(name) for name in AXES)
    sites = deep * flat
    _, per_block, depth = packed.shape
    columns = min(4, share // 2)
    spins = share // (2 * columns)
    near = lax.all_gather(packed, ("pair", "deep", "flat"))
    near = near.reshape(groups, sites, 4, per_block, depth)
    far = lax.ppermute(near, "core", [(0, 1), (1, 0)])
    wide = groups * per_block

    def half(right):
        return pl.pallas_call(
            add_terms,
            grid_spec=pltpu.PrefetchScalarGridSpec(
                num_scalar_prefetch=1,
                grid=(sites,),
                in_specs=[
                    pl.BlockSpec((1, 2, weights.shape[2]), lambda m, place: (m, 0, 0)),
                    pl.BlockSpec(
                        (1, 1, spins, per_block, depth),
                        lambda m, place: (place[0], m, place[4] // spins, 0, 0),
                    ),
                    pl.BlockSpec(
                        (groups, 1, columns, per_block, depth),
                        lambda m, place: (0, m, place[6] // columns, 0, 0),
                    ),
                ],
                out_specs=pl.BlockSpec((share, per_block, wide), lambda m, place: (0, 0, 0)),
            ),
            out_shape=jax.ShapeDtypeStruct((share, per_block, wide), jnp.float32),
            compiler_params=pltpu.CompilerParams(vmem_limit_bytes=40 * 1024 * 1024),
        )(place, weights, near, right)

    sides = [half(right).reshape(share, per_block, groups, per_block) for right in (near, far)]
    first = lax.axis_index("core") == 0
    even, odd = (jnp.where(first, a, b) for a, b in (sides, sides[::-1]))
    return jnp.stack([even, odd], 3).reshape(share, per_block, 2 * wide)


def shards(modes, momenta):
    groups, _, deep, flat = (lax.axis_size(name) for name in AXES)
    sites = deep * flat
    slots, steps, per_block, spin_colour, site_count = modes.shape
    share = steps * momenta.shape[0] * 32 // sites
    owned = (lax.axis_index("deep") * flat + lax.axis_index("flat")) * (share // 2)
    place = [lax.axis_index(name) for name in AXES]
    place = jnp.stack(place + [owned // 4 % 4, jnp.int32(flat), owned % 4]).astype(jnp.int32)

    mine = lax.dynamic_slice_in_dim(momenta, owned // 16, 1, 0)
    weights = phase_table(mine, jnp.int32(0), sites * site_count, LEXT)[0]
    weights = jnp.transpose(weights.reshape(2, sites, site_count), (1, 0, 2))

    if (groups, deep, flat) == (2, 4, 2) and steps == 1 and share in (8, 16, 32):
        own = jnp.transpose(modes[:, 0], (0, 2, 1, 3))
        return swap_in_windows(own, weights, share)
    packed = jnp.transpose(modes.reshape(slots, per_block, 4, 3, site_count), (2, 1, 0, 3, 4))
    packed = packed.reshape(4, per_block, slots * 3 * site_count)
    return gather_whole(packed, place, weights, share)


def solution(mesh):
    count, sites = mesh.shape["blk"], mesh.shape["site"]
    flat = 2 ** (int(math.log2(sites)) // 2)
    split = Mesh(mesh.devices.reshape(count // 2, 2, sites // flat, flat), AXES)
    placed = (P(None, None, ("pair", "core"), None, ("deep", "flat")), P())
    return jax.shard_map(
        shards,
        mesh=split,
        in_specs=placed,
        out_specs=P(("deep", "flat"), ("pair", "core"), None),
        check_vma=False,
    )
```

```python
import functools
import math

import jax
import jax.numpy as jnp
from jax import lax
from jax.experimental import pallas as pl
from jax.experimental.pallas import tpu as pltpu
from jax.sharding import Mesh, PartitionSpec as P

LEXT = 48

TWO_PI = 2.0 * math.pi

AXES = ("pair", "core", "deep", "flat")


def phase_table(momenta, first_site, site_count, extent):
    flat = first_site + jnp.arange(site_count, dtype=jnp.int32)
    coords = jnp.stack([flat % extent, flat // extent % extent, flat // (extent * extent)], 0)
    turns = jnp.mod(jnp.sum(momenta[:, :, None] * coords[None, :, :], axis=1), extent)
    angle = turns.astype(jnp.float32) * (TWO_PI / extent)
    return jnp.stack([jnp.cos(angle), jnp.sin(angle)], 1)


def left_sides(owns, weights):
    depth = owns[0].shape[1]
    half = depth // 2
    cosine = jnp.tile(weights[0:1], (1, depth // weights.shape[1]))
    sine = jnp.tile(weights[1:2], (1, depth // weights.shape[1]))
    cosine_rows = [[], []]
    sine_rows = [[], []]
    for own in owns:
        own = own.astype(jnp.float32)
        by_cos = (own * cosine).astype(jnp.bfloat16)
        by_sin = (own * sine).astype(jnp.bfloat16)
        cosine_rows[0].append(by_cos)
        cosine_rows[1].append(jnp.concatenate([-by_cos[:, half:], by_cos[:, :half]], 1))
        sine_rows[0].append(jnp.concatenate([-by_sin[:, half:], by_sin[:, :half]], 1))
        sine_rows[1].append(-by_sin)
    return jnp.concatenate(cosine_rows[0] + cosine_rows[1] + sine_rows[0] + sine_rows[1], 0)


def product(left, right):
    dims = (((1,), (1,)), ((), ()))
    terms = lax.dot_general(left, right, dims, preferred_element_type=jnp.float32)
    half = terms.shape[0] // 2
    return terms[:half] + terms[half:]


def add_shards(names, where, slots, has_totals, given, half, last, share, weights_ref, *refs):
    refs = list(refs)
    left_ref = None if given else refs.pop()
    if half:
        sems, row_ref, field_ref = (refs.pop() for _ in range(3))
    if last:
        sems, row_ref, far_ref, field_ref, _ = (refs.pop() for _ in range(5))
    else:
        out_ref = refs.pop()
    totals_in = refs.pop() if has_totals else None
    left_ref = refs.pop() if given else left_ref

    def shard(name):
        index, slot = where[name]
        return refs[index] if slot is None else refs[index].at[slot]

    def spin_rows(name, spin):
        ref = shard(name)
        tiles = [ref[part, spin * colours + x] for part in range(2) for x in range(colours)]
        return jnp.concatenate(tiles, 1)

    pair, core, level, beside = (lax.axis_index(name) for name in AXES)
    flat = lax.axis_size("flat")
    _, spin_colour, per_block, _ = shard(names[0]).shape
    columns, colours = 4, spin_colour // 4
    first_s = lax.rem(lax.div((level * flat + beside) * (share // 2), 4), 4)
    spins = left_ref.shape[1] // (4 * per_block)

    def send_columns(dx, near, far):
        lane = lax.broadcasted_iota(jnp.int32, (per_block, 2 * per_block), 1)
        start = pl.multiple_of(jnp.bitwise_xor(pair, dx) * (2 * per_block), 2 * per_block)
        copies = []
        for spin in range(spins):
            for column in range(0, columns, 2):
                first = (spin * columns + column) * 2
                across = slice(column * per_block, (column + 2) * per_block)
                for part in range(2):
                    top = (part * spins + spin) * per_block
                    one = near(slice(top, top + per_block), across)
                    two = far(slice(top, top + per_block), across)
                    even = jnp.where(core == 0, one, two)
                    odd = jnp.where(core == 0, two, one)
                    row_ref[first + part] = jnp.where(
                        lane < per_block, even, pltpu.roll(odd, per_block, 1)
                    )
                    row_ref[first + part + 2] = jnp.where(
                        lane < per_block, pltpu.roll(even, per_block, 1), odd
                    )
        target = field_ref.at[:, :, pl.ds(start, 2 * per_block)]
        copies.append(pltpu.make_async_copy(row_ref, target, sems.at[0]))
        copies[-1].start()
        return copies

    def term(name):
        side, kind, dz = name
        right = jnp.concatenate([spin_rows(name, r) for r in range(columns)], 0)
        turn = core if side == "near" else 1 - core
        dx, dy = {"O": (0, 0), "A": (1 - turn, turn), "B": (turn, 1 - turn), "AB": (1, 1)}[kind]
        if kind in ("O", "AB"):
            slot = slots.index((dy, dz))
        else:
            slot = slots.index((0, dz)) + dy
        return dx, product(left_ref[slot], right)

    if last:
        far_ref[...] = totals_in[1, 1] + sum(term(name)[1] for name in names)
        copies = send_columns(
            1,
            lambda rows, across: totals_in[0, 1, rows, across],
            lambda rows, across: far_ref[rows, across],
        )
        for copy in copies:
            copy.wait()
        return

    if has_totals:
        out_ref[...] = totals_in[...]
    else:
        out_ref[...] = jnp.zeros_like(out_ref)
    if not given:
        for slot, (dy, dz) in enumerate(slots):
            site = jnp.bitwise_xor(level, dz) * flat + jnp.bitwise_xor(beside, dy)
            if dy == 0:
                owns = [spin_rows(("near", "O", dz), first_s + s) for s in range(spins)]
            else:
                owns = [
                    jnp.where(
                        core == 0,
                        spin_rows(("near", "B", dz), first_s + s),
                        spin_rows(("near", "A", dz), first_s + s),
                    )
                    for s in range(spins)
                ]
            left_ref[slot] = left_sides(owns, weights_ref[site])
    copies = []
    if half:
        copies = send_columns(
            0,
            lambda rows, across: totals_in[0, 0, rows, across],
            lambda rows, across: totals_in[1, 0, rows, across],
        )
    for name in names:
        dx, added = term(name)
        out_ref[0 if name[0] == "near" else 1, dx] += added
    for copy in copies:
        copy.wait()


def route_second(*refs):
    o1_ref, o2_ref, stack_ref, both_ref = refs[3:]
    for slot in range(5):
        stack_ref[slot] = refs[slot][...]
    both_ref[0] = o1_ref[...]
    both_ref[1] = o2_ref[...]


def route_third(ab2_ref, o3_ref, a12_ref, b12_ref, stack_ref, a1_ref):
    stack_ref[0] = ab2_ref[...]
    stack_ref[1] = o3_ref[...]
    stack_ref[2:4] = a12_ref[...]
    stack_ref[4:6] = b12_ref[...]
    a1_ref[...] = a12_ref[0]


def route_last(a3_ref, ab3_ref, stack_ref):
    stack_ref[0] = a3_ref[...]
    stack_ref[1] = ab3_ref[...]


def left_slots(names):
    needed = set()
    for _, kind, dz in names:
        needed |= {"O": {(0, dz)}, "AB": {(1, dz)}}.get(kind, {(0, dz), (1, dz)})
    return sorted(needed, key=lambda slot: (slot[1], slot[0]))


def swap_in_windows(own, weights, share):
    shape = tuple(lax.axis_size(name) for name in AXES)
    columns, per_block = 4, own.shape[2]
    depth = own.size // (columns * per_block)
    spins = share // (2 * columns)
    tall, wide = 2 * spins * per_block, columns * per_block
    strides = (shape[1] * shape[2] * shape[3], shape[2] * shape[3], shape[3], 1)

    def move(array, target):
        pairs = []
        for p in range(shape[0]):
            for c in range(shape[1]):
                for z in range(shape[2]):
                    for y in range(shape[3]):
                        ends = (p, c, z, y), target(p, c, z, y)
                        pairs.append(
                            tuple(sum(a * b for a, b in zip(end, strides)) for end in ends)
                        )
        return lax.ppermute(array, AXES, pairs)

    def hop_a(array):
        return move(array, lambda p, c, z, y: (p ^ 1, c, z, y) if c == 0 else (p, c, z, y ^ 1))

    def hop_b(array):
        return move(array, lambda p, c, z, y: (p, c, z, y ^ 1) if c == 0 else (p ^ 1, c, z, y))

    def hop_z(array, by):
        return move(array, lambda p, c, z, y: (p, c, z ^ by, y))

    def swap(array):
        return move(array, lambda p, c, z, y: (p, c ^ 1, z, y))

    arrays = {}
    where = {}

    def put(key, array, side, kinds):
        arrays[key] = array
        for slot, (kind, dz) in enumerate(kinds):
            where[(side, kind, dz)] = (key, slot if len(kinds) > 1 else None)

    def near(kind, dz):
        key, slot = where[("near", kind, dz)]
        return arrays[key] if slot is None else arrays[key][slot]

    def add(names, totals, keep=None, left=None, half=False, field=None, weight=1):
        given, last = left is not None, field is not None
        slots, left = left if given else (keep or left_slots(names), None)
        uses = list(names)
        for dy, dz in [] if given else slots:
            uses += [("near", kind, dz) for kind in (("A", "B") if dy else ("O",))]
        keys = sorted({where[name][0] for name in uses})
        places = {name: (keys.index(where[name][0]), where[name][1]) for name in uses}
        operands = [weights] + [arrays[key] for key in keys]
        operands += [each for each in (left, totals, field) if each is not None]
        total_shape = (2, 2, tall, wide)
        left_shape = (len(slots), 2 * tall, depth)
        field_shape = (share, per_block, 4 * per_block)
        block, apart = (pl.BlockSpec(memory_space=space) for space in (pltpu.VMEM, pltpu.HBM))
        in_specs, outs, scratch, aliases = [block] * len(operands), [], [], {}
        if last:
            in_specs[-1] = apart
            aliases = {len(operands) - 1: 0}
            scratch.append(pltpu.VMEM(total_shape[2:], jnp.float32))
        else:
            outs.append((total_shape, jnp.float32, block))
        if half or last:
            outs.append((field_shape, jnp.float32, apart))
            scratch.append(pltpu.VMEM((*field_shape[:2], 2 * per_block), jnp.float32))
            scratch.append(pltpu.SemaphoreType.DMA((spins * columns // 2,)))
        if keep:
            outs.append((left_shape, jnp.bfloat16, block))
        elif not given:
            scratch.append(pltpu.VMEM(left_shape, jnp.bfloat16))
        out = pl.pallas_call(
            functools.partial(
                add_shards, tuple(names), places, slots, totals is not None, given, half, last, share
            ),
            in_specs=in_specs,
            out_specs=[spec for _, _, spec in outs],
            out_shape=[jax.ShapeDtypeStruct(shape, dtype) for shape, dtype, _ in outs],
            scratch_shapes=scratch,
            input_output_aliases=aliases,
            compiler_params=pltpu.CompilerParams(vmem_limit_bytes=40 * 1024 * 1024),
            cost_estimate=pl.CostEstimate(
                flops=4 * tall * wide * depth * len(names) * weight,
                bytes_accessed=wide * depth * 2 * len(names) + 8 * 4 * tall * wide,
                transcendentals=0,
            ),
        )(*operands)
        if keep:
            return out[0], (slots, out[1])
        return out if half else out[0]

    def fence(totals):
        nonlocal arrays
        arrays, totals = lax.optimization_barrier((arrays, totals))
        return totals

    put("1a", hop_z(own, 2), "near", [("O", 2)])
    put("1b", hop_a(own), "near", [("A", 0)])
    put("1c", hop_z(own, 1), "near", [("O", 1)])
    put("1d", hop_b(own), "near", [("B", 0)])
    put("1e", hop_b(near("A", 0)), "near", [("AB", 0)])
    put("1f", swap(own), "far", [("O", 0)])
    put("9", own, "near", [("O", 0)])
    weights = fence(weights)

    def route(kernel, operands, counts, weight=0):
        block = pl.BlockSpec(memory_space=pltpu.VMEM)
        shapes = [(count,) * (count > 1) + own.shape for count in counts]
        routed = pl.pallas_call(
            kernel,
            in_specs=[block] * len(operands),
            out_specs=[block] * len(counts),
            out_shape=[jax.ShapeDtypeStruct(shape, own.dtype) for shape in shapes],
            compiler_params=pltpu.CompilerParams(vmem_limit_bytes=24 * 1024 * 1024),
            cost_estimate=pl.CostEstimate(flops=weight, bytes_accessed=0, transcendentals=0),
        )(*operands)
        return fence(routed)

    first = [("O", 0), ("A", 0), ("B", 0), ("AB", 0), ("O", 1), ("O", 2)]
    second = [("AB", 2), ("O", 3), ("A", 1), ("A", 2), ("B", 1), ("B", 2)]
    third = [("A", 3), ("B", 3)]
    fourth = [("AB", 3), ("AB", 1)]
    stack, both = route(route_second, [near(*kind) for kind in first[1:]], (5, 2))
    totals = add([("near", *kind) for kind in first], None)
    o3, ab2 = hop_z(near("O", 2), 1), hop_z(near("AB", 0), 2)
    a12, b12 = hop_a(both), hop_b(both)
    put("2a", swap(stack), "far", first[1:])
    totals = fence(totals)

    totals = add([("far", *kind) for kind in first], totals)
    put("2c", o3, "near", [("O", 3)])
    totals = fence(totals)

    a3, b3 = hop_a(near("O", 3)), hop_b(near("O", 3))
    totals = add([("near", "O", 3)], totals, weight=45)
    put("2d", ab2, "near", [("AB", 2)])
    put("2e", a12, "near", [("A", 1), ("A", 2)])
    put("2f", b12, "near", [("B", 1), ("B", 2)])
    totals = fence(totals)

    ab3 = hop_z(near("AB", 2), 1)
    stack, a1 = route(route_third, [arrays[key] for key in ("2d", "2c", "2e", "2f")], (6, 1))
    far2, ab1 = swap(stack), hop_b(a1)
    names = [("near", *kind) for kind in second if kind != ("O", 3)]
    totals = add(names, totals)
    a3, b3, totals = lax.optimization_barrier((a3, b3, totals))
    (stack,) = route(route_last, [a3, b3], (2,), weight=10**11)
    put("3a", stack, "near", third)
    far3 = swap(stack)
    put("3d", far2, "far", second)
    names = [("far", *kind) for kind in second] + [("near", *kind) for kind in third]
    totals, (slots, left) = add(names, totals, keep=left_slots(names), weight=10)
    put("3e", far3, "far", third)
    totals, left = fence((totals, left))
    totals = add([("far", *kind) for kind in third], totals, left=(slots, left))
    put("3b", ab3, "near", fourth[:1])
    put("3c", ab1, "near", fourth[1:])
    totals, left = fence((totals, left))

    far4 = [swap(near(*kind)) for kind in fourth]
    names = [("near", *kind) for kind in fourth]
    totals, field = add(names, totals, left=(slots, left), half=True)
    put("4b", far4[0], "far", fourth[:1])
    put("4c", far4[1], "far", fourth[1:])
    totals, left, field = fence((totals, left, field))
    return add([("far", *kind) for kind in fourth], totals, left=(slots, left), field=field)


def add_terms(place_ref, weights_ref, left_ref, right_ref, field_ref):
    @pl.when(pl.program_id(0) == 0)
    def _():
        field_ref[...] = jnp.zeros_like(field_ref)

    spins = left_ref.shape[2]
    groups, columns, per_block, depth = right_ref.shape[0], *right_ref.shape[2:]
    owns = [left_ref[0, 0, spin] for spin in range(spins)]
    left = left_sides(owns, weights_ref[0])
    for column in range(columns):
        right = right_ref[:, 0, column].reshape(groups * per_block, depth)
        term = product(left, right)
        for part in range(2):
            for spin in range(spins):
                start = (part * spins + spin) * per_block
                field_ref[(spin * columns + column) * 2 + part] += term[start : start + per_block]


def gather_whole(packed, place, weights, share):
    groups, _, deep, flat = (lax.axis_size(name) for name in AXES)
    sites = deep * flat
    _, per_block, depth = packed.shape
    columns = min(4, share // 2)
    spins = share // (2 * columns)
    near = lax.all_gather(packed, ("pair", "deep", "flat"))
    near = near.reshape(groups, sites, 4, per_block, depth)
    far = lax.ppermute(near, "core", [(0, 1), (1, 0)])
    wide = groups * per_block

    def half(right):
        return pl.pallas_call(
            add_terms,
            grid_spec=pltpu.PrefetchScalarGridSpec(
                num_scalar_prefetch=1,
                grid=(sites,),
                in_specs=[
                    pl.BlockSpec((1, 2, weights.shape[2]), lambda m, place: (m, 0, 0)),
                    pl.BlockSpec(
                        (1, 1, spins, per_block, depth),
                        lambda m, place: (place[0], m, place[4] // spins, 0, 0),
                    ),
                    pl.BlockSpec(
                        (groups, 1, columns, per_block, depth),
                        lambda m, place: (0, m, place[6] // columns, 0, 0),
                    ),
                ],
                out_specs=pl.BlockSpec((share, per_block, wide), lambda m, place: (0, 0, 0)),
            ),
            out_shape=jax.ShapeDtypeStruct((share, per_block, wide), jnp.float32),
            compiler_params=pltpu.CompilerParams(vmem_limit_bytes=40 * 1024 * 1024),
        )(place, weights, near, right)

    sides = [half(right).reshape(share, per_block, groups, per_block) for right in (near, far)]
    first = lax.axis_index("core") == 0
    even, odd = (jnp.where(first, a, b) for a, b in (sides, sides[::-1]))
    return jnp.stack([even, odd], 3).reshape(share, per_block, 2 * wide)


def shards(modes, momenta):
    groups, _, deep, flat = (lax.axis_size(name) for name in AXES)
    sites = deep * flat
    slots, steps, per_block, spin_colour, site_count = modes.shape
    share = steps * momenta.shape[0] * 32 // sites
    owned = (lax.axis_index("deep") * flat + lax.axis_index("flat")) * (share // 2)
    place = [lax.axis_index(name) for name in AXES]
    place = jnp.stack(place + [owned // 4 % 4, jnp.int32(flat), owned % 4]).astype(jnp.int32)

    mine = lax.dynamic_slice_in_dim(momenta, owned // 16, 1, 0)
    weights = phase_table(mine, jnp.int32(0), sites * site_count, LEXT)[0]
    weights = jnp.transpose(weights.reshape(2, sites, site_count), (1, 0, 2))

    if (groups, deep, flat) == (2, 4, 2) and steps == 1 and share in (8, 16, 32):
        own = jnp.transpose(modes[:, 0], (0, 2, 1, 3))
        return swap_in_windows(own, weights, share)
    packed = jnp.transpose(modes.reshape(slots, per_block, 4, 3, site_count), (2, 1, 0, 3, 4))
    packed = packed.reshape(4, per_block, slots * 3 * site_count)
    return gather_whole(packed, place, weights, share)


def solution(mesh):
    count, sites = mesh.shape["blk"], mesh.shape["site"]
    flat = 2 ** (int(math.log2(sites)) // 2)
    split = Mesh(mesh.devices.reshape(count // 2, 2, sites // flat, flat), AXES)
    placed = (P(None, None, ("pair", "core"), None, ("deep", "flat")), P())
    return jax.shard_map(
        shards,
        mesh=split,
        in_specs=placed,
        out_specs=P(("deep", "flat"), ("pair", "core"), None),
        check_vma=False,
    )
```
